32 devices in a mesh: ctx: 8 (over z, y), wsh: 4 (over x, core).
Axes of the slice: x: 2, y: 2, z: 4, core: 2. Of those that a mesh axis runs over, the one named last changes fastest.
Arguments:
- hidden_in: bfloat16 [4, 2048, 768], P('wsh', 'ctx'), may hold values from -6 to 6
- w_query: bfloat16 [768, 768], P('wsh'), may hold values from -0.09375 to 0.09375
- w_key: bfloat16 [768, 768], P('wsh'), may hold values from -0.09375 to 0.09375
- w_value: bfloat16 [768, 768], P('wsh'), may hold values from -0.21875 to 0.21875
- w_output: bfloat16 [768, 768], P('wsh'), may hold values from -3 to 3
- w_router: bfloat16 [768, 16], P('wsh'), may hold values from -0.109375 to 0.109375
- gain_attn: bfloat16 [768], P('wsh'), may hold values from 0.5 to 1.5
- gain_moe: bfloat16 [768], P('wsh'), may hold values from 0.5 to 1.5
- rel_bias: bfloat16 [32, 12], P('wsh'), may hold values from -124 to 124
- w_in: bfloat16 [16, 768, 3072], P('ctx', None, 'wsh'), may hold values from -0.21875 to 0.21875
- w_out: bfloat16 [16, 3072, 768], P('ctx', 'wsh'), may hold values from -2 to 2
- routes: int32 [4, 2048, 1], P('wsh', 'ctx'), may hold values from 0 to 15; in each aligned block of 256 rows (0 to 255, 256 to 511, ..., all dimensions but the last counted through in order) at most 32 rows name the same one
- block_pairs: int32 [8, 2], replicated, may hold values from 0 to 15, as said below
- cotangent: bfloat16 [4, 2048, 768], P('wsh', 'ctx'), may hold values from -6 to 6
Outputs:
- output: bfloat16 [4, 2048, 768], P('wsh', 'ctx')
- input_grad: bfloat16 [4, 2048, 768], P('wsh', 'ctx')
- grad_query: float32 [768, 768], P('wsh')
- grad_key: float32 [768, 768], P('wsh')
- grad_value: float32 [768, 768], P('wsh')
- grad_output: float32 [768, 768], P('wsh')
- grad_router: float32 [768, 16], P('wsh')
- grad_gain_attn: float32 [768], P('wsh')
- grad_gain_moe: float32 [768], P('wsh')
- grad_rel_bias: float32 [32, 12], P('wsh')
- grad_w_in: float32 [16, 768, 3072], P('ctx', None, 'wsh')
- grad_w_out: float32 [16, 3072, 768], P('ctx', 'wsh')
The draws below stay inside these ranges and needn't reach their ends.
Inputs may be any that keep to these rules, and one draw needn't show every extreme that they name: `block_pairs`: row c names the two blocks of 128 tokens that ctx index c holds, in the order of its rows: a block b and the block that is b places from the end; every block of a sequence is named once. `routes`: in the rows of one device no expert is named more than 32 times, and in some device's rows an expert is named exactly 32 times.
All inputs are finite; a program needn't handle non-finite values.
Results may differ from the reference program's by a relative error of at most 0.017.
Values may be sent and summed in bfloat16 or wider, within the bound.
A program may use at most 256 MiB of HBM per device.

```python
import math
import jax
import jax.numpy as jnp
import numpy as np
from jax import lax

D = 768
HEADS = 12
HEAD_DIM = 64
FF = 3072
BUCKETS = 32
BLK = 128
EXPERTS = 16
TOK_DEV = 256
LENGTH = 2048
SEQS = 4
MOST = 32
CAP = 144
N_CTX = 8


def draw_block_pairs(key, part):
    key = jax.random.fold_in(key, 7)
    first_key, second_key = jax.random.split(key)
    order = jax.random.permutation(first_key, N_CTX).astype(jnp.int32)
    flips = jax.random.randint(second_key, (N_CTX,), 0, 2).astype(jnp.int32)
    mirror = (2 * N_CTX - 1 - order).astype(jnp.int32)
    leading = jnp.where(flips == 1, mirror, order)
    trailing = jnp.where(flips == 1, order, mirror)
    return jnp.stack([leading, trailing], axis=1).astype(jnp.int32)


def draw_rel_bias(key, part):
    key = jax.random.fold_in(key, 11)
    rough_key, level_key, sign_key = jax.random.split(key, 3)
    rough = jnp.clip(jax.random.normal(rough_key, (BUCKETS, HEADS), jnp.float32), -4.0, 4.0)
    levels = jax.random.uniform(level_key, (HEADS,), jnp.float32, 100.0, 120.0)
    order = jax.random.permutation(sign_key, HEADS)
    signs = jnp.where(order % 2 == 0, 1.0, -1.0).astype(jnp.float32)
    return (rough + (signs * levels)[None, :]).astype(jnp.bfloat16)


def block_scale(key, dims, pieces, smallest, high):
    level, own = 1.0, jax.random.fold_in(key, 6)
    for dim, shards_of in pieces:
        steps = jnp.exp(jax.random.uniform(jax.random.fold_in(own, dim), (shards_of,), jnp.float32, smallest / len(pieces), high / len(pieces)))
        level = level * jnp.repeat(steps, dims[dim] // shards_of).reshape([-1 if axis == dim else 1 for axis in range(len(dims))])
    return level


def routed_block(rng, own, number, rows, number_of, top, reach, skew):
    ranking = jax.random.permutation(rng, number_of)
    crowded, ordinary = load_shares(number_of, rows * top, reach, skew, True), load_shares(number_of, rows * top, reach, skew, False)
    places = jnp.arange(number_of)

    def named(lengths, offset_by):
        used = int((lengths > 0).sum())
        fixed = max(1, used // 4)
        moved = fixed + (places - fixed + offset_by * (used - fixed)) % max(1, number_of - fixed)
        return jnp.zeros((number_of,), jnp.int32).at[ranking[jnp.where(places < fixed, places, moved)]].set(jnp.asarray(lengths, jnp.int32))

    lengths = jnp.where(number % 4 == 0, named(crowded, number // 4), named(ordinary, number - number // 4 - 1))
    mixed = jax.random.permutation(jax.random.fold_in(own, 3), number_of)
    giver, receiver = mixed[0:number_of // 2 * 2:2], mixed[1:number_of // 2 * 2:2]
    margin = jnp.minimum(lengths[giver] - 1, reach - lengths[receiver]) // 2
    margin = jnp.where((giver == ranking[0]) | (receiver == ranking[0]) | (lengths[receiver] == 0), 0, jnp.maximum(margin, 0))
    moved = jax.random.randint(jax.random.fold_in(own, 4), (number_of // 2,), 0, 1 << 20) % (margin + 1)
    lengths = lengths.at[giver].add(-moved).at[receiver].add(moved)
    items = jnp.searchsorted(jnp.cumsum(lengths), jnp.arange(rows * top), side="right").astype(jnp.int32)
    grid = items.reshape(top, rows).T
    grid = grid[jax.random.permutation(jax.random.fold_in(own, 1), rows)]
    offset_by = jax.random.randint(jax.random.fold_in(own, 2), (rows, 1), 0, top)
    return jnp.take_along_axis(grid, (jnp.arange(top)[None, :] + offset_by) % top, axis=1)


def load_shares(amount, total, most, lean, full):
    loads = [(1 << 20) // math.isqrt(standing ** lean) + 1 for standing in range(1, amount + 1)]
    largest = most if full else min(most, max(-(-total // amount), total * loads[0] // sum(loads)))
    least = 1 if total - largest >= amount - 1 else 0
    given, rest = [largest] + [least] * (amount - 1), total - largest - least * (amount - 1)
    while rest > 0:
        movable = [i for i in range(1, amount) if given[i] < largest] or [i for i in range(1, amount) if given[i] < most]
        pool, left = sum([loads[i] for i in movable]), rest
        for i in movable:
            more = min(most - given[i], max(1, left * loads[i] // pool), rest)
            given[i] = given[i] + more
            rest = rest - more
    return np.array(given)


def noise(rng, extent, deviation, reach, cuts=(), kind=jnp.bfloat16):
    array = deviation * jax.random.normal(rng, extent, jnp.float32)
    if cuts:
        array = array * block_scale(rng, extent, cuts, -0.22, 0.18)
    return jnp.clip(array, -reach, reach).astype(kind)


def setup_inputs(seed: int = 0) -> dict:
    streams_of = jax.random.split(jax.random.key(seed), 15)
    hidden_in = noise(streams_of[0], (SEQS, LENGTH, D), 1.0, 6.0, ((0, 4), (1, 8)))
    w_query = noise(streams_of[1], (D, D), (5 * D) ** -0.5, 0.09375, ((0, 4),))
    w_key = noise(streams_of[2], (D, D), (5 * D) ** -0.5, 0.09375, ((0, 4),))
    w_value = noise(streams_of[3], (D, D), D ** -0.5, 0.21875, ((0, 4),))
    w_output = noise(streams_of[4], (D, D), 4 ** -0.5, 3.0, ((0, 4),))
    w_router = noise(streams_of[5], (D, EXPERTS), (4 * D) ** -0.5, 0.109375, ((0, 4),))
    gain_attn = jnp.clip(1.0 + 0.1 * jax.random.normal(streams_of[6], (D,), jnp.float32), 0.5, 1.5).astype(jnp.bfloat16)
    gain_moe = jnp.clip(1.0 + 0.1 * jax.random.normal(streams_of[7], (D,), jnp.float32), 0.5, 1.5).astype(jnp.bfloat16)
    rel_bias = draw_rel_bias(jax.random.fold_in(streams_of[14], 71), 0)
    w_in = noise(streams_of[9], (EXPERTS, D, FF), D ** -0.5, 0.21875, ((0, 8), (2, 4)))
    w_out = noise(streams_of[10], (EXPERTS, FF, D), (FF // (2 * EXPERTS * EXPERTS) + 1) ** -0.5, 2.0, ((0, 8), (1, 4)))
    routes_keys = jax.random.split(jax.random.fold_in(streams_of[11], 1), SEQS * LENGTH // TOK_DEV)
    routes_turns = jax.random.permutation(jax.random.fold_in(streams_of[11], 3), SEQS * LENGTH // TOK_DEV)
    routes = jax.vmap(lambda own, number: routed_block(jax.random.fold_in(streams_of[11], 2), own, number, TOK_DEV, EXPERTS, 1, MOST, 2))(routes_keys, routes_turns).reshape((SEQS, LENGTH, 1))
    block_pairs = draw_block_pairs(jax.random.fold_in(streams_of[14], 71), 0)
    cotangent = noise(streams_of[13], (SEQS, LENGTH, D), 1.0, 6.0, ((0, 4), (1, 8)))
    return {"hidden_in": hidden_in, "w_query": w_query, "w_key": w_key, "w_value": w_value, "w_output": w_output, "w_router": w_router, "gain_attn": gain_attn, "gain_moe": gain_moe, "rel_bias": rel_bias, "w_in": w_in, "w_out": w_out, "routes": routes, "block_pairs": block_pairs, "cotangent": cotangent}


bucket_edges = [math.ceil(16 * 8 ** (marker / 16)) for marker in range(1, 16)]

@jax.custom_vjp
def low(v):
    return lax.optimization_barrier(v.astype(jnp.bfloat16)).astype(jnp.float32)

@jax.custom_vjp
def low_back(v):
    return v

def low_keep(v):
    return (low(v), None)

def low_pass(kept, grad):
    return (grad,)

def back_keep(v):
    return (v, None)

def back_low(kept, grad):
    return (low(grad),)
low.defvjp(low_keep, low_pass)
low_back.defvjp(back_keep, back_low)

def bucket_index(distance):
    gap_ahead = jnp.maximum(distance, 0)
    bucket_count = jnp.full(gap_ahead.shape, 16, jnp.int32)
    for threshold in bucket_edges:
        bucket_count = bucket_count + (gap_ahead >= threshold).astype(jnp.int32)
    return jnp.where(gap_ahead < 16, gap_ahead, bucket_count).astype(jnp.int32)

def rms_norm(values, gain_vec):
    return values * lax.rsqrt(lax.optimization_barrier(jnp.mean(values * values, axis=-1, keepdims=True)) + 1e-06) * gain_vec

def reference(hidden_in, w_query, w_key, w_value, w_output, w_router, gain_attn, gain_moe, rel_bias, w_in, w_out, routes, block_pairs, cotangent):
    highest = lax.Precision.HIGHEST
    positions = (block_pairs.reshape(-1)[:, None] * BLK + jnp.arange(BLK, dtype=jnp.int32)[None, :]).reshape(-1).astype(jnp.int32)
    query_block = min(512, LENGTH)
    pos_split = positions.reshape(LENGTH // query_block, query_block)
    params = tuple((item.astype(jnp.float32) for item in (w_query, w_key, w_value, w_output, w_router, gain_attn, gain_moe, rel_bias, w_in, w_out)))

    def attend(query_part, pos_part, key_heads, value_heads, bias_table):
        gap_mat = pos_part[:, None] - positions[None, :]
        scores = jnp.einsum('qhd,khd->hqk', query_part, key_heads, precision=highest)
        scores = scores + jnp.transpose(jnp.take(bias_table, bucket_index(gap_mat), axis=0), (2, 0, 1))
        scores = low_back(scores)
        scores = jnp.where((gap_mat >= 0)[None], scores, -1e+30)
        weights = low(jax.nn.softmax(scores, axis=-1))
        return jnp.einsum('hqk,khd->qhd', weights, value_heads, precision=highest)
    attend_saved = jax.checkpoint(attend)

    def forward(seq_rows, route_ids, mat_query, mat_key, mat_value, mat_output, mat_router, gain_one, gain_two, bias_table, mat_in, mat_out):
        normed_one = low(rms_norm(seq_rows, gain_one))
        queries = low(low_back(jnp.dot(normed_one, mat_query, precision=highest)))
        key_rows = low(low_back(jnp.dot(normed_one, mat_key, precision=highest)))
        value_rows = low(low_back(jnp.dot(normed_one, mat_value, precision=highest)))
        query_heads = queries.reshape(LENGTH // query_block, query_block, HEADS, HEAD_DIM)
        key_heads = key_rows.reshape(LENGTH, HEADS, HEAD_DIM)
        value_heads = value_rows.reshape(LENGTH, HEADS, HEAD_DIM)
        attn_blocks = lax.map(lambda pair_in: attend_saved(pair_in[0], pair_in[1], key_heads, value_heads, bias_table), (query_heads, pos_split))
        attn_rows = low(low_back(attn_blocks.reshape(LENGTH, D)))
        branch_attn = low_back(jnp.dot(attn_rows, mat_output, precision=highest))
        resid_mid = seq_rows + branch_attn
        normed_two = low(rms_norm(resid_mid, gain_two))
        logits = low_back(jnp.dot(normed_two, mat_router, precision=highest))
        probs = jax.nn.softmax(logits, axis=-1)
        chosen = route_ids[:, None] == jnp.arange(EXPERTS, dtype=jnp.int32)[None, :]
        gate_val = lax.optimization_barrier(jnp.sum(jnp.where(chosen, probs, 0.0), axis=-1))
        chosen_int = chosen.astype(jnp.int32)
        ranks = lax.optimization_barrier(jnp.sum((jnp.cumsum(chosen_int, axis=0) - chosen_int) * chosen_int, axis=-1))
        slots = jnp.where(ranks < CAP, route_ids * CAP + ranks, EXPERTS * CAP).astype(jnp.int32)
        holder = jnp.full((EXPERTS * CAP + 1,), LENGTH, jnp.int32).at[slots].set(jnp.arange(LENGTH, dtype=jnp.int32))[:EXPERTS * CAP]
        expert_in = low_back(normed_two)
        padded_in = jnp.concatenate([expert_in, jnp.zeros((1, D), jnp.float32)], axis=0)
        slot_rows = jnp.take(padded_in, holder, axis=0).reshape(EXPERTS, CAP, D)
        pre_act = low_back(jnp.einsum('ecd,edf->ecf', slot_rows, mat_in, precision=highest))
        hidden_act = low(jax.nn.gelu(pre_act, approximate=True))
        expert_out = low(low_back(jnp.einsum('ecf,efd->ecd', hidden_act, mat_out, precision=highest)))
        padded_out = jnp.concatenate([expert_out.reshape(EXPERTS * CAP, D), jnp.zeros((1, D), jnp.float32)], axis=0)
        token_out = jnp.take(padded_out, slots, axis=0)
        return resid_mid + gate_val[:, None] * token_out

    def one_sequence(carry, inputs):
        seq_rows, route_ids, grad_rows = inputs
        result, pullback = jax.vjp(lambda row_data, *weight_args: forward(row_data, route_ids, *weight_args), seq_rows, *params)
        gradients = pullback(grad_rows)
        return (tuple((total + added for total, added in zip(carry, gradients[1:]))), (result, gradients[0]))
    start_sums = tuple((jnp.zeros_like(item) for item in params))
    totals, (outputs, input_grads) = lax.scan(one_sequence, start_sums, (hidden_in.astype(jnp.float32), routes[..., 0], cotangent.astype(jnp.float32)))
    return (outputs.astype(jnp.bfloat16), input_grads.astype(jnp.bfloat16), totals[0], totals[1], totals[2], totals[3], totals[4], totals[5], totals[6], totals[7], totals[8], totals[9])
```

```python
import functools
import math

import jax
import jax.numpy as jnp
import numpy as np
from jax import lax
from jax.experimental import pallas as pl
from jax.experimental.pallas import tpu as pltpu
from jax.sharding import PartitionSpec as P

HEADS = 12
HEAD_DIM = 64
BLOCK = 128
PAIRS = HEADS // 2
NEAR = 2 * BLOCK
SPAN = 3 * BLOCK
epsilon = 1e-06
MASKED = -1e30
bucket_edges = [math.ceil(16 * 8 ** (marker / 16)) for marker in range(1, 16)]
F32 = jnp.float32
BF16 = jnp.bfloat16
HIGH = lax.Precision.HIGHEST


def bucket_of(distance):
    gap = np.maximum(distance, 0)
    count = np.full(gap.shape, 16, np.int32)
    for edge in bucket_edges:
        count = count + (gap >= edge)
    return np.where(gap < 16, gap, count)


def wrapped_lanes():
    lanes = np.arange(SPAN)
    return np.where(lanes < NEAR, lanes, lanes - SPAN)


def onehot_of(distance, buckets):
    return (bucket_of(distance)[:, None] == np.arange(buckets)[None, :]).astype(np.float32)


def dot(left, right, left_dim=1, right_dim=0):
    return lax.dot_general(
        left, right, (((left_dim,), (right_dim,)), ((), ())), preferred_element_type=F32
    )


def lane_ids(rows, lanes):
    return lax.broadcasted_iota(jnp.int32, (rows, lanes), 1)


def stack_heads(rows):
    first = lane_ids(rows.shape[0], BLOCK) < HEAD_DIM
    zero = jnp.zeros_like(rows)
    return jnp.concatenate([jnp.where(first, rows, zero), jnp.where(first, zero, rows)], axis=0)


def merge_heads(stacked):
    half = stacked.shape[0] // 2
    first = lane_ids(half, BLOCK) < HEAD_DIM
    return jnp.where(first, stacked[:half], stacked[half:])


def fold_lanes(tile, combine):
    return combine(tile[:, :BLOCK], tile[:, BLOCK:])


def near_bias(base_ref):
    tiles = []
    for head in range(2):
        row = jnp.broadcast_to(base_ref[0, head : head + 1, :], (BLOCK, SPAN))
        tiles.append(pltpu.roll(row, 0, 1, stride=1, stride_axis=0)[:, :NEAR])
    return jnp.concatenate(tiles, axis=0)


def aligned(row):
    return pl.ds(pl.multiple_of(row * BLOCK, BLOCK), NEAR)


def own_rows_at(block):
    return pl.ds(pl.multiple_of(block * BLOCK, BLOCK), BLOCK)


def project_kernel(source_ref, first_ref, second_ref, gain_ref, wq_ref, wk_ref, wv_ref, out_ref):
    rows = jnp.concatenate([first_ref[...], second_ref[...]], axis=0).astype(F32)
    inv = lax.rsqrt(jnp.mean(rows * rows, axis=-1, keepdims=True) + epsilon)
    normed = (rows * inv * gain_ref[...]).astype(BF16)
    width = wq_ref.shape[1]
    for place, weight in enumerate((wq_ref, wk_ref, wv_ref)):
        out_ref[:, place * width : (place + 1) * width] = dot(normed, weight[...]).astype(BF16)


def project(rows_all, source, gain, wq, wk, wv):
    length, width = rows_all.shape
    steps = (length // BLOCK + 2) // 2
    whole = pl.BlockSpec((width, width), lambda step, src: (0, 0))
    return pl.pallas_call(
        project_kernel,
        grid_spec=pltpu.PrefetchScalarGridSpec(
            num_scalar_prefetch=1,
            grid=(steps,),
            in_specs=[
                pl.BlockSpec((BLOCK, width), lambda step, src: (src[2 * step], 0)),
                pl.BlockSpec((BLOCK, width), lambda step, src: (src[2 * step + 1], 0)),
                pl.BlockSpec((1, width), lambda step, src: (0, 0)),
                whole,
                whole,
                whole,
            ],
            out_specs=pl.BlockSpec((NEAR, 3 * width), lambda step, src: (step, 0)),
        ),
        out_shape=jax.ShapeDtypeStruct((steps * NEAR, 3 * width), BF16),
        compiler_params=pltpu.CompilerParams(vmem_limit_bytes=40 << 20),
        name="project",
    )(source, rows_all, rows_all, gain, wq, wk, wv)


def back_kernel(source_ref, first_ref, second_ref, weight_ref, out_ref):
    rows = jnp.concatenate([first_ref[...], second_ref[...]], axis=0)
    out_ref[...] = dot(rows, weight_ref[...], 1, 1).astype(BF16)


def back_project(rows_all, source, weight):
    length, width = rows_all.shape
    steps = (length // BLOCK + 2) // 2
    return pl.pallas_call(
        back_kernel,
        grid_spec=pltpu.PrefetchScalarGridSpec(
            num_scalar_prefetch=1,
            grid=(steps,),
            in_specs=[
                pl.BlockSpec((BLOCK, width), lambda step, src: (src[2 * step], 0)),
                pl.BlockSpec((BLOCK, width), lambda step, src: (src[2 * step + 1], 0)),
                pl.BlockSpec((width, width), lambda step, src: (0, 0)),
            ],
            out_specs=pl.BlockSpec((NEAR, width), lambda step, src: (step, 0)),
        ),
        out_shape=jax.ShapeDtypeStruct((steps * NEAR, width), BF16),
        compiler_params=pltpu.CompilerParams(vmem_limit_bytes=40 << 20),
        name="back_project",
    )(source, rows_all, rows_all, weight)


def forward_kernel(place_ref, q_ref, k_ref, v_ref, base_ref, out_ref, exact_ref, lse_ref, scores_ref, bias_ref):
    bias_ref[...] = near_bias(base_ref)
    lanes = lane_ids(2 * BLOCK, NEAR)
    for own in range(2):
        block = place_ref[own]
        stacked = stack_heads(q_ref[own_rows_at(block + 1), :])
        scores = dot(stacked, k_ref[aligned(block), :], 1, 1) + bias_ref[...]
        scores = jnp.where(lanes + block * BLOCK < BLOCK, MASKED, scores)
        scores_ref[0] = scores
        chunks = jnp.maximum(block, 1) // 2

        def score_step(chunk, best):
            start = block - 2 * chunk
            part = dot(stacked, k_ref[aligned(start), :], 1, 1)
            part = jnp.where(lanes + start * BLOCK < BLOCK, MASKED, part)
            scores_ref[chunk] = part
            return jnp.maximum(best, fold_lanes(part, jnp.maximum))

        best = lax.fori_loop(1, chunks + 1, score_step, fold_lanes(scores, jnp.maximum))
        top = jnp.max(best, axis=-1, keepdims=True)

        def value_step(chunk, carry):
            total, summed = carry
            weights = jnp.exp(scores_ref[chunk] - top)
            high = weights.astype(BF16)
            low = (weights - high.astype(F32)).astype(BF16)
            values = v_ref[aligned(block - 2 * chunk), :]
            summed = summed + dot(jnp.concatenate([high, low], axis=0), values)
            return (total + fold_lanes(weights, jnp.add), summed)

        total, summed = lax.fori_loop(
            0,
            chunks + 1,
            value_step,
            (jnp.zeros((2 * BLOCK, BLOCK), F32), jnp.zeros((4 * BLOCK, BLOCK), F32)),
        )
        total = jnp.sum(total, axis=-1, keepdims=True)
        main = summed[: 2 * BLOCK] / total
        exact = main + summed[2 * BLOCK :] / total
        rows = pl.ds(own * BLOCK, BLOCK)
        out_ref[rows, :] = merge_heads(main).astype(BF16)
        exact_ref[rows, :] = merge_heads(exact)
        lse_ref[0, own] = jnp.broadcast_to(top + jnp.log(total), (2 * BLOCK, BLOCK))


def pair_specs(rows, width):
    pairs = width // BLOCK

    def column(offset):
        return pl.BlockSpec((rows, BLOCK), lambda pair, place: (0, offset + pair))

    return [column(0), column(pairs), column(2 * pairs)]


def attend_forward(places, qkv, base, width):
    rows = qkv.shape[0]
    chunks = rows // NEAR
    own = pl.BlockSpec((NEAR, BLOCK), lambda pair, place: (0, pair))
    return pl.pallas_call(
        forward_kernel,
        grid_spec=pltpu.PrefetchScalarGridSpec(
            num_scalar_prefetch=1,
            grid=(PAIRS,),
            in_specs=pair_specs(rows, width)
            + [pl.BlockSpec((1, 8, SPAN), lambda pair, place: (pair, 0, 0))],
            out_specs=[
                own,
                own,
                pl.BlockSpec((1, 2, NEAR, BLOCK), lambda pair, place: (pair, 0, 0, 0)),
            ],
            scratch_shapes=[
                pltpu.VMEM((chunks, NEAR, NEAR), F32),
                pltpu.VMEM((NEAR, NEAR), F32),
            ],
        ),
        out_shape=[
            jax.ShapeDtypeStruct((NEAR, width), BF16),
            jax.ShapeDtypeStruct((NEAR, width), F32),
            jax.ShapeDtypeStruct((PAIRS, 2, NEAR, BLOCK), F32),
        ],
        compiler_params=pltpu.CompilerParams(vmem_limit_bytes=40 << 20),
        name="attend_forward",
    )(places, qkv, qkv, qkv, base)


def query_kernel(
    place_ref, q_ref, k_ref, v_ref, base_ref, do_ref, exact_ref, lse_ref, dq_ref, sums_ref, bias_ref, near_ref
):
    bias_ref[...] = near_bias(base_ref)
    lanes = lane_ids(2 * BLOCK, NEAR)
    far = jnp.zeros((2 * BLOCK, BLOCK), F32)
    for own in range(2):
        block = place_ref[own]
        rows = pl.ds(own * BLOCK, BLOCK)
        stacked = stack_heads(q_ref[own_rows_at(block + 1), :])
        grads = stack_heads(do_ref[rows, :])
        exact = exact_ref[rows, :]
        product = grads.astype(F32) * jnp.concatenate([exact, exact], axis=0)
        delta = jnp.sum(product, axis=-1, keepdims=True)
        lse = lse_ref[0, own][:, :1]

        def grad_scores(scores, start):
            weights = jnp.exp(scores - lse)
            return weights * (dot(grads, v_ref[aligned(start), :], 1, 1) - delta)

        scores = dot(stacked, k_ref[aligned(block), :], 1, 1) + bias_ref[...]
        scores = jnp.where(lanes + block * BLOCK < BLOCK, MASKED, scores)
        near = grad_scores(scores, block)
        if own == 0:
            near_ref[...] = near
        else:
            near_ref[...] += near

        def step(chunk, carry):
            grad_q, far = carry
            start = block - 2 * chunk
            keys = k_ref[aligned(start), :]
            part = dot(stacked, keys, 1, 1)
            part = jnp.where(lanes + start * BLOCK < BLOCK, MASKED, part)
            grad_s = grad_scores(part, start)
            return (grad_q + dot(grad_s.astype(BF16), keys), far + fold_lanes(grad_s, jnp.add))

        grad_q, far = lax.fori_loop(
            1,
            jnp.maximum(block, 1) // 2 + 1,
            step,
            (dot(near.astype(BF16), k_ref[aligned(block), :]), far),
        )
        dq_ref[rows, :] = merge_heads(grad_q).astype(BF16)
    row_ids = lax.broadcasted_iota(jnp.int32, (BLOCK, SPAN), 0)
    for head in range(2):
        part = near_ref[head * BLOCK : (head + 1) * BLOCK, :]
        part = jnp.concatenate([part, jnp.zeros((BLOCK, BLOCK), F32)], axis=1)
        for bit in range(BLOCK.bit_length() - 1):
            moved = pltpu.roll(part, SPAN - (1 << bit), 1)
            part = jnp.where((row_ids >> bit) & 1 == 1, moved, part)
        sums_ref[0, head : head + 1, :] = jnp.sum(part, axis=0, keepdims=True)
        far_part = jnp.sum(far[head * BLOCK : (head + 1) * BLOCK], axis=0, keepdims=True)
        sums_ref[0, 2 + head : 3 + head, :] = jnp.concatenate(
            [far_part, jnp.zeros((1, NEAR), F32)], axis=1
        )
    sums_ref[0, 4:8, :] = jnp.zeros((4, SPAN), F32)


def attend_queries(places, qkv, base, grad_out, exact, lse):
    rows, width = qkv.shape[0], grad_out.shape[1]
    own = pl.BlockSpec((NEAR, BLOCK), lambda pair, place: (0, pair))
    row_spec = pl.BlockSpec((1, 8, SPAN), lambda pair, place: (pair, 0, 0))
    return pl.pallas_call(
        query_kernel,
        grid_spec=pltpu.PrefetchScalarGridSpec(
            num_scalar_prefetch=1,
            grid=(PAIRS,),
            in_specs=pair_specs(rows, width)
            + [
                row_spec,
                own,
                own,
                pl.BlockSpec((1, 2, NEAR, BLOCK), lambda pair, place: (pair, 0, 0, 0)),
            ],
            out_specs=[own, row_spec],
            scratch_shapes=[pltpu.VMEM((NEAR, NEAR), F32), pltpu.VMEM((NEAR, NEAR), F32)],
        ),
        out_shape=[
            jax.ShapeDtypeStruct((NEAR, width), BF16),
            jax.ShapeDtypeStruct((PAIRS, 8, SPAN), F32),
        ],
        compiler_params=pltpu.CompilerParams(vmem_limit_bytes=40 << 20),
        name="attend_queries",
    )(places, qkv, qkv, qkv, base, grad_out, exact, lse)


def key_kernel(place_ref, q_ref, k_ref, v_ref, base_ref, do_ref, stats_ref, dk_ref, dv_ref, bias_ref):
    bias_ref[...] = near_bias(base_ref)
    blocks = q_ref.shape[0] // BLOCK - 2
    lanes = lane_ids(2 * BLOCK, NEAR)

    def spread(row, start):
        window = stats_ref[0, row : row + 2, aligned(start)]
        return jnp.concatenate(
            [
                jnp.broadcast_to(window[:1], (BLOCK, NEAR)),
                jnp.broadcast_to(window[1:], (BLOCK, NEAR)),
            ],
            axis=0,
        )

    for own in range(2):
        block = place_ref[own]
        rows = pl.ds(own * BLOCK, BLOCK)
        keys = stack_heads(k_ref[own_rows_at(block + 1), :])
        values = stack_heads(v_ref[own_rows_at(block + 1), :])

        def grads(scores, start):
            queries, grad_out = q_ref[aligned(start), :], do_ref[aligned(start), :]
            scores = jnp.where((start == blocks) & (lanes >= BLOCK), MASKED, scores)
            weights = jnp.exp(scores - spread(0, start))
            grad_s = weights * (dot(values, grad_out, 1, 1) - spread(2, start))
            return dot(grad_s.astype(BF16), queries), dot(weights.astype(BF16), grad_out)

        def step(chunk, carry):
            start = block + 1 + 2 * chunk
            more_k, more_v = grads(dot(keys, q_ref[aligned(start), :], 1, 1), start)
            return (carry[0] + more_k, carry[1] + more_v)

        near = dot(keys, q_ref[aligned(block + 1), :], 1, 1) + bias_ref[...]
        chunks = jnp.maximum(blocks - 1 - block, 0) // 2
        grad_k, grad_v = lax.fori_loop(1, chunks + 1, step, grads(near, block + 1))
        dk_ref[rows, :] = merge_heads(grad_k).astype(BF16)
        dv_ref[rows, :] = merge_heads(grad_v).astype(BF16)


def attend_keys(places, qkv, base, grad_out, stats):
    rows, width = grad_out.shape
    own = pl.BlockSpec((NEAR, BLOCK), lambda pair, place: (0, pair))
    return pl.pallas_call(
        key_kernel,
        grid_spec=pltpu.PrefetchScalarGridSpec(
            num_scalar_prefetch=1,
            grid=(PAIRS,),
            in_specs=pair_specs(rows, width)
            + [
                pl.BlockSpec((1, 8, SPAN), lambda pair, place: (pair, 0, 0)),
                pl.BlockSpec((rows, BLOCK), lambda pair, place: (0, pair)),
                pl.BlockSpec((1, 8, rows), lambda pair, place: (pair, 0, 0)),
            ],
            out_specs=[own, own],
            scratch_shapes=[pltpu.VMEM((NEAR, NEAR), F32)],
        ),
        out_shape=[jax.ShapeDtypeStruct((NEAR, width), BF16)] * 2,
        compiler_params=pltpu.CompilerParams(vmem_limit_bytes=40 << 20),
        name="attend_keys",
    )(places, qkv, qkv, qkv, base, grad_out, stats)


def gelu_tanh(values):
    return jax.nn.gelu(values, approximate=True)


def rms_forward(values, gain_vec):
    inv_rms = lax.rsqrt(jnp.mean(values * values, axis=-1, keepdims=True) + epsilon)
    return (values * inv_rms * gain_vec, inv_rms)


def rms_backward(values, inv_rms, gain_vec, upstream):
    grad_gain = jnp.sum(upstream * values * inv_rms, axis=0)
    scaled = upstream * gain_vec
    grad_values = inv_rms * scaled - values * inv_rms**3 * jnp.mean(
        scaled * values, axis=-1, keepdims=True
    )
    return (grad_values, grad_gain)


def per_device(
    hidden_in,
    w_query,
    w_key,
    w_value,
    w_output,
    w_router,
    gain_attn,
    gain_moe,
    rel_bias,
    w_in,
    w_out,
    routes,
    block_pairs,
    cotangent,
):
    tokens, width = hidden_in.shape[1:]
    ctx_count, wsh_count = lax.axis_size("ctx"), lax.axis_size("wsh")
    ctx_rank, wsh_rank = lax.axis_index("ctx"), lax.axis_index("wsh")
    length = tokens * ctx_count
    blocks = length // BLOCK
    experts, exp_dev = w_router.shape[1], w_in.shape[0]
    slot_most = 2 * tokens // experts
    capacity = (9 * length // (8 * experts) + 7) // 8 * 8

    def over(axis, array, dim=0):
        return lax.all_gather(array, axis, axis=dim, tiled=True)

    rows_all = over("ctx", hidden_in[0])
    small = jnp.concatenate([w_router, gain_attn[:, None], gain_moe[:, None]], axis=1)
    small = jnp.concatenate(
        [small, jnp.pad(rel_bias, ((0, 0), (0, small.shape[1] - HEADS)))], axis=0
    )
    small = lax.all_gather(small, "wsh", axis=0, tiled=False)
    share = width // wsh_count
    vectors = small[:, :share].reshape(width, experts + 2)
    full_router = vectors[:, :experts]
    gain_one = vectors[:, experts].astype(F32)
    gain_two = vectors[:, experts + 1].astype(F32)
    full_bias = small[:, share:, :HEADS].reshape(-1, HEADS)
    full_query, full_key = over("wsh", w_query), over("wsh", w_key)
    full_value, full_output = over("wsh", w_value), over("wsh", w_output)

    order = block_pairs.reshape(-1)
    places = lax.dynamic_slice_in_dim(order, 2 * ctx_rank, 2)
    ids = jnp.arange(blocks, dtype=jnp.int32)
    inverse = jnp.sum(jnp.where(order[None, :] == ids[:, None], ids[None, :], 0), axis=1)
    source = jnp.pad(inverse, (1, 1))

    buckets = full_bias.shape[0]
    lanes = wrapped_lanes()
    query_hot = onehot_of(BLOCK - lanes, buckets)
    key_hot = onehot_of(lanes, buckets)

    def base_rows(hot, distance):
        table = dot(full_bias, jnp.asarray(hot, BF16), 0, 1)
        table = table - full_bias[buckets - 1].astype(F32)[:, None]
        table = jnp.where(jnp.asarray(distance >= 0)[None, :], table, MASKED)
        return jnp.pad(table.reshape(PAIRS, 2, SPAN), ((0, 0), (0, 6), (0, 0)))

    query_base = base_rows(query_hot, BLOCK - lanes)
    key_base = base_rows(key_hot, lanes)

    route_ids = routes[0, :, 0]
    chosen = route_ids[:, None] == jnp.arange(experts, dtype=jnp.int32)[None, :]
    earlier = jnp.asarray(np.tril(np.ones((tokens, tokens), np.float32), -1), BF16)
    before = dot(earlier, chosen.astype(BF16))
    local_rank = jnp.sum(jnp.where(chosen, before, 0.0), axis=-1).astype(jnp.int32)
    counts = lax.all_gather(jnp.sum(chosen.astype(jnp.int32), axis=0), "ctx", axis=0, tiled=False)
    income = lax.dynamic_slice_in_dim(counts, exp_dev * ctx_rank, exp_dev, 1)
    local_slot = route_ids * slot_most + local_rank
    placement = (
        jnp.arange(experts * slot_most, dtype=jnp.int32)[:, None] == local_slot[None, :]
    ).astype(BF16)
    offsets = jnp.cumsum(income, axis=0) - income
    slot_index = jnp.arange(slot_most, dtype=jnp.int32)
    target = offsets.T[:, :, None] + slot_index[None, None, :]
    target = jnp.where(slot_index[None, None, :] < income.T[:, :, None], target, capacity)
    target = target.reshape(exp_dev, ctx_count * slot_most)
    cap_map = (
        target[:, None, :] == jnp.arange(capacity, dtype=jnp.int32)[None, :, None]
    ).astype(BF16)

    def dispatch(rows):
        outgoing = dot(placement, rows).astype(BF16)
        outgoing = outgoing.reshape(ctx_count, exp_dev * slot_most, width)
        incoming = lax.all_to_all(outgoing, "ctx", split_axis=0, concat_axis=0, tiled=True)
        incoming = incoming.reshape(ctx_count, exp_dev, slot_most, width)
        return jnp.stack(
            [
                dot(cap_map[e], incoming[:, e].reshape(ctx_count * slot_most, width)).astype(BF16)
                for e in range(exp_dev)
            ]
        )

    def bring_back(slots):
        returning = jnp.stack(
            [
                dot(cap_map[e], slots[e], 0, 0)
                .astype(BF16)
                .reshape(ctx_count, slot_most, width)
                for e in range(exp_dev)
            ],
            axis=1,
        ).reshape(ctx_count, exp_dev * slot_most, width)
        returned = lax.all_to_all(returning, "ctx", split_axis=0, concat_axis=0, tiled=True)
        return dot(placement, returned.reshape(experts * slot_most, width), 0, 0)

    def spread_slots(slots):
        return jnp.swapaxes(
            lax.all_gather(slots, "wsh", axis=0, tiled=False), 0, 1
        ).reshape(exp_dev, wsh_count * capacity, width)

    def sum_slots(parts):
        parts = parts.astype(BF16).reshape(exp_dev, wsh_count, capacity, width)
        return lax.psum_scatter(jnp.swapaxes(parts, 0, 1), "wsh", scatter_dimension=0, tiled=False)

    grad_rows = cotangent[0]
    own_g = dispatch(grad_rows)
    all_g = spread_slots(own_g)

    qkv = project(rows_all, source, gain_one[None, :], full_query, full_key, full_value)
    attn_low, attn_exact, lse = attend_forward(places, qkv, query_base, width)

    resid_in = hidden_in[0].astype(F32)
    resid_mid = resid_in + dot(attn_low, full_output)
    normed_two, inv_two = rms_forward(resid_mid, gain_two)
    normed_two = normed_two.astype(BF16)
    own_x = dispatch(normed_two)
    all_x = spread_slots(own_x)

    expert_ids = exp_dev * ctx_rank + jnp.arange(exp_dev, dtype=jnp.int32)
    expert_hot = (
        expert_ids[:, None] == jnp.arange(experts, dtype=jnp.int32)[None, :]
    ).astype(F32)[:, None, :]

    def router(rows):
        logits = jnp.einsum("ecd,dr->ecr", rows, full_router, preferred_element_type=F32)
        probs = jax.nn.softmax(logits, axis=-1)
        return probs, jnp.sum(probs * expert_hot, axis=-1, keepdims=True)

    gate_all = router(all_x)[1]
    grad_slots = (gate_all * all_g.astype(F32)).astype(BF16)
    pre_act = jnp.einsum("ecd,edf->ecf", all_x, w_in, preferred_element_type=F32)
    hidden_act = gelu_tanh(pre_act).astype(BF16)
    out_part = jnp.einsum("ecf,efd->ecd", hidden_act, w_out, preferred_element_type=F32)
    own_out = sum_slots(out_part)
    grad_hidden = jnp.einsum("ecd,efd->ecf", grad_slots, w_out, preferred_element_type=F32)
    grad_pre = jax.vjp(gelu_tanh, pre_act)[1](grad_hidden)[0].astype(BF16)
    in_part = jnp.einsum("ecf,edf->ecd", grad_pre, w_in, preferred_element_type=F32)
    own_dx = sum_slots(in_part)
    grad_w_out = jnp.einsum("ecf,ecd->efd", hidden_act, grad_slots, preferred_element_type=F32)
    grad_w_in = jnp.einsum("ecd,ecf->edf", all_x, grad_pre, preferred_element_type=F32)

    probs, gate_own = router(own_x)
    grad_gate = jnp.sum(own_g.astype(F32) * own_out.astype(F32), axis=-1, keepdims=True)
    grad_logits = (gate_own * grad_gate * (expert_hot - probs)).astype(BF16)
    grad_router = jnp.einsum("ecd,ecr->dr", own_x, grad_logits, preferred_element_type=F32)
    grad_slots_in = own_dx.astype(F32) + jnp.einsum(
        "ecr,dr->ecd", grad_logits, full_router, preferred_element_type=F32
    )
    grad_normed_two = bring_back(grad_slots_in.astype(BF16))
    token_out = bring_back(own_out)

    logits = dot(normed_two, full_router)
    gate_val = jnp.sum(jnp.where(chosen, jax.nn.softmax(logits, axis=-1), 0.0), axis=-1)
    output_rows = resid_mid + gate_val[:, None] * token_out

    upstream = grad_rows.astype(F32)
    grad_mid_norm, grad_gain_m = rms_backward(resid_mid, inv_two, gain_two, grad_normed_two)
    grad_mid = upstream + grad_mid_norm
    grad_branch = grad_mid.astype(BF16)
    branch_all = over("ctx", grad_branch)
    grad_wo = dot(attn_low, grad_branch, 0, 0)
    grad_heads = dot(grad_branch, full_output, 1, 1).astype(BF16)
    head_hot = jnp.asarray(
        (np.arange(width)[:, None] // HEAD_DIM == np.arange(HEADS)[None, :]).astype(np.float32)
    )
    delta = jnp.dot(grad_heads.astype(F32) * attn_exact, head_hot, precision=HIGH)
    lse_rows = lse[..., 0].reshape(PAIRS, 2, 2, BLOCK)
    lse_rows = jnp.transpose(lse_rows, (1, 0, 2, 3))
    delta_rows = jnp.transpose(delta.T.reshape(PAIRS, 2, 2, BLOCK), (2, 0, 1, 3))
    stats = jnp.concatenate([lse_rows, delta_rows], axis=2)
    stats = over("ctx", stats)
    stats = jnp.transpose(jnp.take(stats, source, axis=0), (1, 2, 0, 3))
    stats = jnp.pad(
        stats.reshape(PAIRS, 4, (blocks + 2) * BLOCK), ((0, 0), (0, 4), (0, 0))
    )

    grad_q, sums = attend_queries(places, qkv, query_base, grad_heads, attn_exact, lse)
    near_sums = sums[:, :2].reshape(HEADS, SPAN)
    far_sums = jnp.sum(sums[:, 2:4].reshape(HEADS, SPAN), axis=1)
    grad_table = jnp.dot(jnp.asarray(query_hot.T), near_sums.T, precision=HIGH)
    grad_table = grad_table.at[buckets - 1].add(far_sums)

    heads_all = back_project(branch_all, source, full_output)
    grad_k, grad_v = attend_keys(places, qkv, key_base, heads_all, stats)

    normed_one, inv_one = rms_forward(resid_in, gain_one)
    normed_one = normed_one.astype(BF16)
    grad_normed_one = dot(grad_q, full_query, 1, 1)
    grad_normed_one = grad_normed_one + dot(grad_k, full_key, 1, 1)
    grad_normed_one = grad_normed_one + dot(grad_v, full_value, 1, 1)
    grad_in_norm, grad_gain_a = rms_backward(resid_in, inv_one, gain_one, grad_normed_one)
    grad_input = (grad_mid + grad_in_norm).astype(BF16)

    def reduce_weight(grad):
        part = lax.psum_scatter(grad.astype(BF16), "wsh", scatter_dimension=0, tiled=True)
        return lax.psum(part, "ctx").astype(F32)

    grad_wq = dot(normed_one, grad_q, 0, 0)
    grad_wk = dot(normed_one, grad_k, 0, 0)
    grad_wv = dot(normed_one, grad_v, 0, 0)
    shares = [reduce_weight(grad) for grad in (grad_wq, grad_wk, grad_wv, grad_wo)]
    columns = jnp.concatenate(
        [grad_router, grad_gain_a[:, None], grad_gain_m[:, None]], axis=1
    )
    table = jnp.pad(grad_table, ((0, 0), (0, columns.shape[1] - HEADS)))
    summed = lax.psum(jnp.concatenate([columns, table], axis=0), ("ctx", "wsh"))
    own_columns = lax.dynamic_slice_in_dim(summed[:width], wsh_rank * share, share, 0)
    bucket_share = buckets // wsh_count
    own_table = lax.dynamic_slice_in_dim(
        summed[width:, :HEADS], wsh_rank * bucket_share, bucket_share, 0
    )
    return (
        output_rows.astype(BF16)[None],
        grad_input[None],
        *shares,
        own_columns[:, :experts],
        own_columns[:, experts],
        own_columns[:, experts + 1],
        own_table,
        grad_w_in,
        grad_w_out,
    )


def solution(mesh):
    in_specs = (
        P("wsh", "ctx", None),
        P("wsh", None),
        P("wsh", None),
        P("wsh", None),
        P("wsh", None),
        P("wsh", None),
        P("wsh"),
        P("wsh"),
        P("wsh", None),
        P("ctx", None, "wsh"),
        P("ctx", "wsh", None),
        P("wsh", "ctx", None),
        P(),
        P("wsh", "ctx", None),
    )
    out_specs = (
        P("wsh", "ctx", None),
        P("wsh", "ctx", None),
        P("wsh", None),
        P("wsh", None),
        P("wsh", None),
        P("wsh", None),
        P("wsh", None),
        P("wsh"),
        P("wsh"),
        P("wsh", None),
        P("ctx", None, "wsh"),
        P("ctx", "wsh", None),
    )
    return jax.shard_map(
        per_device, mesh=mesh, in_specs=in_specs, out_specs=out_specs, check_vma=False
    )
```

```python
import functools
import math

import jax
import jax.numpy as jnp
import numpy as np
from jax import lax
from jax.experimental import pallas as pl
from jax.experimental.pallas import tpu as pltpu
from jax.sharding import PartitionSpec as P

HEADS = 12
HEAD_DIM = 64
BLOCK = 128
PAIRS = HEADS // 2
NEAR = 2 * BLOCK
SPAN = 3 * BLOCK
epsilon = 1e-06
MASKED = -1e30
bucket_edges = [math.ceil(16 * 8 ** (marker / 16)) for marker in range(1, 16)]
F32 = jnp.float32
BF16 = jnp.bfloat16
HIGH = lax.Precision.HIGHEST


def bucket_of(distance):
    gap = np.maximum(distance, 0)
    count = np.full(gap.shape, 16, np.int32)
    for edge in bucket_edges:
        count = count + (gap >= edge)
    return np.where(gap < 16, gap, count)


def wrapped_lanes():
    lanes = np.arange(SPAN)
    return np.where(lanes < NEAR, lanes, lanes - SPAN)


def onehot_of(distance, buckets):
    return (bucket_of(distance)[:, None] == np.arange(buckets)[None, :]).astype(np.float32)


def dot(left, right, left_dim=1, right_dim=0):
    return lax.dot_general(
        left, right, (((left_dim,), (right_dim,)), ((), ())), preferred_element_type=F32
    )


def lane_ids(rows, lanes):
    return lax.broadcasted_iota(jnp.int32, (rows, lanes), 1)


def stack_heads(rows):
    first = lane_ids(rows.shape[0], BLOCK) < HEAD_DIM
    zero = jnp.zeros_like(rows)
    return jnp.concatenate([jnp.where(first, rows, zero), jnp.where(first, zero, rows)], axis=0)


def merge_heads(stacked):
    half = stacked.shape[0] // 2
    first = lane_ids(half, BLOCK) < HEAD_DIM
    return jnp.where(first, stacked[:half], stacked[half:])


def fold_lanes(tile, combine):
    return combine(tile[:, :BLOCK], tile[:, BLOCK:])


def near_bias(base_ref):
    tiles = []
    for head in range(2):
        row = jnp.broadcast_to(base_ref[0, head : head + 1, :], (BLOCK, SPAN))
        tiles.append(pltpu.roll(row, 0, 1, stride=1, stride_axis=0)[:, :NEAR])
    return jnp.concatenate(tiles, axis=0)


def rows_at(block):
    return pl.ds(pl.multiple_of(block * BLOCK, BLOCK), BLOCK)


def two_tiles(ref, source_ref, tile):
    return jnp.concatenate(
        [ref[rows_at(source_ref[tile]), :], ref[rows_at(source_ref[tile + 1]), :]], axis=0
    )


class LineGather:
    def __init__(self, axis, lines, across, views, own, sems):
        self.axis, self.lines, self.across = axis, lines, across
        self.views, self.own, self.sems = views, own, sems
        self.me = lax.axis_index(axis)
        self.line, self.column = self.me // across, self.me % across

    def copy(self, part, block, peer, kind, place, own=False):
        send, recv = self.sems
        view = self.views[part](block)
        return pltpu.make_async_remote_copy(
            src_ref=self.own[part] if own else view,
            dst_ref=view,
            send_sem=send.at[part, kind, place],
            recv_sem=recv.at[part, kind, place],
            device_id={self.axis: peer},
            device_id_type=pl.DeviceIdType.MESH,
        )

    def line_send(self, part, way, step):
        place = self.line - way * step
        ahead = self.line + way
        there = (place >= 0) & (place < self.lines) & (ahead >= 0) & (ahead < self.lines)
        copy = self.copy(
            part,
            place * self.across + self.column,
            ahead * self.across + self.column,
            (1 - way) // 2,
            step,
            own=step == 0,
        )
        return there, copy

    def line_recv(self, part, way, step):
        place = self.line - way * (step + 1)
        there = (place >= 0) & (place < self.lines)
        block = place * self.across + self.column
        return there, block, self.copy(part, block, self.me, (1 - way) // 2, step)

    def cross_send(self, part, block, ahead, own=False):
        peer = self.line * self.across + (self.column + ahead) % self.across
        return self.copy(part, block, peer, 1 + ahead, block // self.across, own)

    def cross_recv(self, part, line, ahead):
        block = line * self.across + (self.column + self.across - ahead) % self.across
        return self.copy(part, block, self.me, 1 + ahead, line)

    def begin(self, part):
        for way in (1, -1):
            there, copy = self.line_send(part, way, 0)
            pl.when(there)(copy.start)
        for ahead in range(1, self.across):
            self.cross_send(part, self.me, ahead, own=True).start()

    def advance(self, part, step):
        for way in (1, -1):
            there, block, arrived = self.line_recv(part, way, step)

            @pl.when(there)
            def _():
                arrived.wait_recv()
                for ahead in range(1, self.across):
                    self.cross_send(part, block, ahead).start()

            if step + 2 < self.lines:
                there, copy = self.line_send(part, way, step + 1)
                pl.when(there)(copy.start)

    def wait_cross(self, part):
        for ahead in range(1, self.across):
            for line in range(self.lines):
                self.cross_recv(part, line, ahead).wait_recv()

    def finish(self):
        for part in range(len(self.views)):
            for step in range(self.lines - 1):
                for way in (1, -1):
                    there, copy = self.line_send(part, way, step)
                    pl.when(there)(copy.wait_send)
            for ahead in range(1, self.across):
                for line in range(self.lines):
                    self.cross_send(part, line * self.across + self.column, ahead).wait_send()


def gather_sems(parts, lines, across):
    return [pltpu.SemaphoreType.DMA((parts, 1 + across, lines))] * 2


def greet(counts):
    barrier = pltpu.get_barrier_semaphore()
    for axis, count in zip(("ctx", "wsh"), counts):
        me = lax.axis_index(axis)
        for ahead in range(1, count):
            pl.semaphore_signal(
                barrier,
                inc=1,
                device_id={axis: (me + ahead) % count},
                device_id_type=pl.DeviceIdType.MESH,
            )
    pl.semaphore_wait(barrier, sum(counts) - 2)


class Exchange:
    def __init__(self, count, experts, most, sems, source, target):
        self.count, self.experts, self.most = count, experts, most
        self.send, self.recv = sems
        self.source, self.target = source, target
        self.me = lax.axis_index("ctx")

    def rows(self, place):
        return pl.ds(pl.multiple_of(place * self.most, self.most), self.most)

    def copy(self, expert, ahead, outward):
        peer = (self.me + ahead) % self.count if outward else (self.me + self.count - ahead) % self.count
        return pltpu.make_async_remote_copy(
            src_ref=self.source(expert, peer),
            dst_ref=self.target(expert, self.me),
            send_sem=self.send.at[expert, ahead - 1],
            recv_sem=self.recv.at[expert, ahead - 1],
            device_id={"ctx": peer},
            device_id_type=pl.DeviceIdType.MESH,
        )

    def start(self, expert):
        for ahead in range(1, self.count):
            self.copy(expert, ahead, True).start()
        self.target(expert, self.me)[...] = self.source(expert, self.me)[...]

    def wait(self, expert):
        for ahead in range(1, self.count):
            peer = (self.me + self.count - ahead) % self.count
            pltpu.make_async_remote_copy(
                src_ref=self.source(expert, peer),
                dst_ref=self.target(expert, peer),
                send_sem=self.send.at[expert, ahead - 1],
                recv_sem=self.recv.at[expert, ahead - 1],
                device_id={"ctx": peer},
                device_id_type=pl.DeviceIdType.MESH,
            ).wait_recv()

    def finish(self, expert):
        for ahead in range(1, self.count):
            self.copy(expert, ahead, True).wait_send()


def exchange_sems(count, experts):
    return [pltpu.SemaphoreType.DMA((experts, count - 1))] * 2


def cap_map(target_ref, expert, capacity):
    slots = target_ref.shape[1]
    rows = lax.broadcasted_iota(jnp.int32, (capacity, slots), 0)
    return (rows == jnp.broadcast_to(target_ref[expert : expert + 1, :], rows.shape)).astype(F32).astype(BF16)


def placement_of(slot_ref, slots):
    rows = lax.broadcasted_iota(jnp.int32, (slots, slot_ref.shape[1]), 0)
    return (rows == jnp.broadcast_to(slot_ref[0:1, :], rows.shape)).astype(F32).astype(BF16)


def grid_of(count):
    lines = 4 if count % 4 == 0 else 1
    return lines, count // lines


def route_slots(routes_ref, chosen_ref, most):
    experts, tokens = chosen_ref.shape
    ids = lax.broadcasted_iota(jnp.int32, (experts, tokens), 0)
    routes = jnp.broadcast_to(routes_ref[0:1, :], ids.shape)
    chosen = (ids == routes).astype(F32)
    chosen_ref[...] = chosen
    earlier = lax.broadcasted_iota(jnp.int32, (tokens, tokens), 0) < lax.broadcasted_iota(
        jnp.int32, (tokens, tokens), 1
    )
    before = dot(chosen.astype(BF16), earlier.astype(F32).astype(BF16))
    rank = jnp.sum(chosen * before, axis=0, keepdims=True).astype(jnp.int32)
    return routes_ref[0:1, :] * most + rank, jnp.sum(chosen, axis=1, keepdims=True)


def project_kernel(
    counts,
    capacity,
    rows_ref,
    wq_ref,
    wk_ref,
    wv_ref,
    wo_ref,
    small_ref,
    routes_ref,
    grad_ref,
    qkv_out,
    weights_out,
    small_out,
    slot_out,
    target_out,
    own_out,
    held,
    weights,
    smalls,
    gain,
    ready,
    chosen,
    tallies,
    grad_rows,
    outgoing,
    incoming,
    row_send,
    row_recv,
    weight_send,
    weight_recv,
    grad_send,
    grad_recv,
    tally_send,
    tally_recv,
    out_sems,
    local_sems,
):
    ctx_count, wsh_count = counts
    experts = chosen.shape[0]
    exp_dev = experts // ctx_count
    lanes = experts
    tokens, width = rows_ref.shape
    share = wq_ref.shape[0]
    lines, across = grid_of(ctx_count)
    pairs = wsh_count // 2

    def shard(block):
        return pl.ds(pl.multiple_of(block * share, 16), share)

    def weight_view(place):
        return lambda block: weights.at[place, shard(block), :]

    rows = LineGather(
        "ctx", lines, across, [lambda block: held.at[block]], [rows_ref], (row_send, row_recv)
    )
    mats = LineGather(
        "wsh",
        pairs,
        2,
        [lambda block: smalls.at[shard(block), :]] + [weight_view(place) for place in range(4)],
        [small_ref, wq_ref, wk_ref, wv_ref, wo_ref],
        (weight_send, weight_recv),
    )
    own_copies = [
        pltpu.make_async_copy(ref, view(index), local_sems.at[2 + place])
        for place, (ref, view, index) in enumerate(
            zip(
                [rows_ref] + mats.own,
                rows.views + mats.views,
                [rows.me] + [mats.me] * 5,
            )
        )
    ]
    grad_copy = pltpu.make_async_copy(grad_ref, grad_rows, local_sems.at[8])
    grad_copy.start()
    for copy in own_copies:
        copy.start()
    greet(counts)
    rows.begin(0)
    for part in range(5):
        mats.begin(part)
    most = incoming.shape[1] // ctx_count
    slot, tally = route_slots(routes_ref, chosen, most)
    slot_out[...] = jnp.broadcast_to(slot, slot_out.shape)
    tallies[rows.me] = jnp.broadcast_to(tally, (experts, BLOCK))
    counted = Exchange(
        ctx_count,
        1,
        most,
        (tally_send, tally_recv),
        lambda expert, peer: tallies.at[rows.me],
        lambda expert, peer: tallies.at[peer],
    )
    for ahead in range(1, ctx_count):
        counted.copy(0, ahead, True).start()
    grad_copy.wait()
    outgoing[...] = dot(placement_of(slot_out, experts * most), grad_rows[...]).astype(BF16)
    grads = Exchange(
        ctx_count,
        exp_dev,
        most,
        (grad_send, grad_recv),
        lambda expert, peer: outgoing.at[grads.rows(peer * exp_dev + expert), :],
        lambda expert, peer: incoming.at[expert, grads.rows(peer), :],
    )
    for copy in own_copies:
        copy.wait()
    for step in range(max(lines, pairs) - 1):
        if step < lines - 1:
            rows.advance(0, step)
        if step == 0:
            for expert in range(exp_dev):
                grads.start(expert)
        if step >= lines - 2 or step < pairs - 1:
            for part in range(5):
                if step < pairs - 1:
                    mats.advance(part, step)
    for part in range(5):
        mats.wait_cross(part)
    weights_copy = pltpu.make_async_copy(weights, weights_out, local_sems.at[0])
    weights_copy.start()
    small_copy = pltpu.make_async_copy(smalls, small_out, local_sems.at[1])
    small_copy.start()
    gain[...] = jnp.transpose(smalls[...].astype(F32))[lanes : lanes + 8, :]
    upper = rows.line // max(lines // 2, 1)

    def put(slot, block):
        place = pl.ds(pl.multiple_of(block * tokens, tokens), tokens)
        return pltpu.make_async_copy(ready.at[slot], qkv_out.at[place, :], out_sems.at[slot])

    def order(step):
        ahead, line = step // lines, step % lines
        line = line + upper * (lines - 1 - 2 * line)
        return line, ahead, line * across + (rows.column + across - ahead) % across

    def step_body(step, carry):
        line, ahead, block = order(step)
        slot = step % 2
        for skip in range(1, across):

            @pl.when(ahead == skip)
            def _():
                rows.cross_recv(0, line, skip).wait_recv()

        @pl.when(step >= 2)
        def _():
            put(slot, order(step - 2)[2]).wait()

        values = held[block].astype(F32)
        inv = lax.rsqrt(jnp.mean(values * values, axis=-1, keepdims=True) + epsilon)
        normed = (values * inv * gain[0:1, :]).astype(BF16)
        for place in range(3):
            ready[slot, :, place * width : (place + 1) * width] = dot(
                normed, weights[place]
            ).astype(BF16)
        put(slot, block).start()
        return carry

    lax.fori_loop(0, ctx_count, step_body, 0)
    for step in (ctx_count - 2, ctx_count - 1):
        put(step % 2, order(step)[2]).wait()
    counted.wait(0)
    lane = lane_ids(1, ctx_count * most)
    for expert in range(exp_dev):
        offset = jnp.zeros((1, 1), F32)
        target = jnp.full((1, ctx_count * most), capacity, jnp.int32)
        for source in range(ctx_count):
            count = tallies[source, pl.ds(rows.me * exp_dev + expert, 1), 0:1]
            inside = (lane >= source * most) & (
                lane < source * most + jnp.broadcast_to(count.astype(jnp.int32), lane.shape)
            )
            place = lane - source * most + jnp.broadcast_to(offset.astype(jnp.int32), lane.shape)
            target = jnp.where(inside, place, target)
            offset = offset + count
        target_out[expert : expert + 1, :] = target
    target_out[exp_dev:, :] = jnp.zeros_like(target_out[exp_dev:, :])
    for expert in range(exp_dev):
        grads.wait(expert)
        own_out[expert] = dot(cap_map(target_out, expert, capacity), incoming[expert]).astype(BF16)
    weights_copy.wait()
    small_copy.wait()
    counted.finish(0)
    for expert in range(exp_dev):
        grads.finish(expert)
    rows.finish()
    mats.finish()


def project(counts, capacity, experts, most, rows, weights, small, routes, grad):
    tokens, width = rows.shape
    ctx_count, wsh_count = counts
    exp_dev = experts // ctx_count
    length = tokens * ctx_count
    lines, across = grid_of(ctx_count)
    vmem = pl.BlockSpec(memory_space=pltpu.VMEM)
    anywhere = pl.BlockSpec(memory_space=pl.ANY)
    return pl.pallas_call(
        functools.partial(project_kernel, counts, capacity),
        in_specs=[anywhere] * 6 + [vmem, anywhere],
        out_specs=[anywhere] * 3 + [vmem] * 3,
        out_shape=[
            jax.ShapeDtypeStruct((length, 3 * width), BF16),
            jax.ShapeDtypeStruct((4, width, width), BF16),
            jax.ShapeDtypeStruct((width, small.shape[1]), BF16),
            jax.ShapeDtypeStruct((8, tokens), jnp.int32),
            jax.ShapeDtypeStruct((8, ctx_count * most), jnp.int32),
            jax.ShapeDtypeStruct((exp_dev, capacity, width), BF16),
        ],
        scratch_shapes=[
            pltpu.VMEM((ctx_count, tokens, width), BF16),
            pltpu.VMEM((4, width, width), BF16),
            pltpu.VMEM((width, small.shape[1]), BF16),
            pltpu.VMEM((8, width), F32),
            pltpu.VMEM((2, tokens, 3 * width), BF16),
            pltpu.VMEM((experts, tokens), F32),
            pltpu.VMEM((ctx_count, experts, BLOCK), F32),
            pltpu.VMEM((tokens, width), BF16),
            pltpu.VMEM((experts * most, width), BF16),
            pltpu.VMEM((exp_dev, ctx_count * most, width), BF16),
            *gather_sems(1, lines, across),
            *gather_sems(5, wsh_count // 2, 2),
            *exchange_sems(ctx_count, exp_dev),
            *exchange_sems(ctx_count, 1),
            pltpu.SemaphoreType.DMA((2,)),
            pltpu.SemaphoreType.DMA((9,)),
        ],
        compiler_params=pltpu.CompilerParams(
            collective_id=0, has_side_effects=True, vmem_limit_bytes=40 << 20
        ),
        name="project",
    )(rows, *weights, small, routes, grad)


def gelu_parts(values):
    slope, cubic = math.sqrt(2 / math.pi), 0.044715
    square = values * values
    bent = jnp.tanh(slope * (values + cubic * values * square))
    outer = 0.5 * (1.0 + bent)
    derivative = outer + 0.5 * values * (1.0 - bent * bent) * slope * (1.0 + 3 * cubic * square)
    return values * outer, derivative


def choose(rows, router, experts, expert):
    logits = dot(rows, router)
    lanes = lane_ids(rows.shape[0], router.shape[1])
    logits = jnp.where(lanes < experts, logits, MASKED)
    weights = jnp.exp(logits - jnp.max(logits, axis=-1, keepdims=True))
    probs = weights / jnp.sum(weights, axis=-1, keepdims=True)
    hot = (lanes == expert).astype(F32)
    return probs, hot, jnp.sum(probs * hot, axis=-1, keepdims=True)


def middle_kernel(
    counts,
    experts,
    spread_here,
    attn_ref,
    exact_ref,
    hidden_ref,
    grad_ref,
    weights_ref,
    w_in_ref,
    w_out_ref,
    own_g_ref,
    small_ref,
    slot_ref,
    target_ref,
    lse_ref,
    routes_ref,
    output_out,
    grad_mid_out,
    grad_heads_out,
    heads_all_out,
    stats_out,
    grad_wo_out,
    grad_router_out,
    grad_gain_out,
    grad_in_out,
    grad_out_out,
    attn,
    exact,
    hidden,
    grad,
    wo,
    w_in,
    w_out,
    resid,
    incoming,
    own_x,
    all_x,
    all_g,
    hid,
    du,
    parts,
    from_mate,
    from_far,
    returning,
    home,
    branch,
    stats,
    stage_in,
    stage_out,
    heads_stage,
    fetch_sems,
    out_sems,
    heads_sems,
    x_send,
    x_recv,
    g_send,
    g_recv,
    go_send,
    go_recv,
    back_send,
    back_recv,
    mate_send,
    mate_recv,
    far_send,
    far_recv,
    branch_send,
    branch_recv,
):
    ctx_count, wsh_count = counts
    tokens, width = hidden.shape
    exp_dev, capacity = own_x.shape[:2]
    most = incoming.shape[1] // ctx_count
    lines, across = grid_of(ctx_count)
    pairs = wsh_count // 2
    me = lax.axis_index("ctx")
    home_row = me if spread_here else 0
    sources = (
        (attn_ref, attn),
        (weights_ref.at[3], wo),
        (hidden_ref, hidden),
        (grad_ref, grad),
        (w_in_ref, w_in),
        (w_out_ref, w_out),
        (exact_ref, exact),
    )
    fetches = [
        pltpu.make_async_copy(src, dst, fetch_sems.at[place])
        for place, (src, dst) in enumerate(sources)
    ]
    for fetch in fetches:
        fetch.start()
    views = [
        (lambda buffer, expert: lambda block: buffer.at[expert, block])(buffer, expert)
        for buffer in (all_g, all_x)
        for expert in range(exp_dev)
    ]
    gather_g = LineGather(
        "wsh",
        pairs,
        2,
        views[:exp_dev],
        [own_g_ref.at[expert] for expert in range(exp_dev)],
        (g_send, g_recv),
    )
    gather_x = LineGather(
        "wsh",
        pairs,
        2,
        views[exp_dev:],
        [own_x.at[expert] for expert in range(exp_dev)],
        (x_send, x_recv),
    )
    wsh_me, my_line, my_core = gather_x.me, gather_x.line, gather_x.column
    greet(counts)
    for expert in range(exp_dev):
        gather_g.begin(expert)
        all_g[expert, wsh_me] = own_g_ref[expert]

    small_t = jnp.transpose(small_ref[...].astype(F32))[experts : experts + 8, :]
    gain_two = small_t[1:2, :]
    router = jnp.where(
        lane_ids(width, small_ref.shape[1]) < experts, small_ref[...], jnp.zeros_like(small_ref)
    )
    for fetch in fetches[:3]:
        fetch.wait()
    resid[...] = hidden[...].astype(F32) + dot(attn[...], wo[...])
    inv_two = lax.rsqrt(jnp.mean(resid[...] * resid[...], axis=-1, keepdims=True) + epsilon)
    normed_two = (resid[...] * inv_two * gain_two).astype(BF16)
    placement = placement_of(slot_ref, experts * most)
    returning[0] = dot(placement, normed_two).astype(BF16)
    forth = Exchange(
        ctx_count,
        exp_dev,
        most,
        (go_send, go_recv),
        lambda expert, peer: returning.at[0, forth.rows(peer * exp_dev + expert), :],
        lambda expert, peer: incoming.at[expert, forth.rows(peer), :],
    )
    for expert in range(exp_dev):
        forth.start(expert)
    gate = choose(normed_two, router, experts, routes_ref[...])[2]
    for expert in range(exp_dev):
        for step in range(pairs - 1):
            gather_g.advance(expert, step)
    gather_g.finish()
    for fetch in fetches[3:]:
        fetch.wait()

    def mate_copy(array, expert, line):
        mine = line * 2 + 1 - my_core
        return pltpu.make_async_remote_copy(
            src_ref=parts.at[array, expert, mine],
            dst_ref=from_mate.at[array, expert, line],
            send_sem=mate_send.at[array, expert, line],
            recv_sem=mate_recv.at[array, expert, line],
            device_id={"wsh": my_line * 2 + 1 - my_core},
            device_id_type=pl.DeviceIdType.MESH,
        )

    def far_copy(array, expert, ahead):
        line = (my_line + ahead) % pairs
        return pltpu.make_async_remote_copy(
            src_ref=parts.at[array, expert, line * 2 + my_core],
            dst_ref=from_far.at[array, expert, ahead - 1],
            send_sem=far_send.at[array, expert, ahead - 1],
            recv_sem=far_recv.at[array, expert, ahead - 1],
            device_id={"wsh": line * 2 + my_core},
            device_id_type=pl.DeviceIdType.MESH,
        )

    def work(expert, step):
        line = (my_line + step // 2) % pairs
        core = (my_core + step % 2) % 2
        block = line * 2 + core

        @pl.when(step % 2 == 1)
        def _():
            gather_x.cross_recv(expert, line, 1).wait_recv()
            gather_g.cross_recv(expert, line, 1).wait_recv()

        rows = all_x[expert, block]
        active, slope = gelu_parts(dot(rows, w_in[expert]))
        active = active.astype(BF16)
        hid[expert, block] = active
        parts[0, expert, block] = dot(active, w_out[expert]).astype(BF16)
        share = choose(rows, router, experts, exp_dev * me + expert)[2]
        grads = (share * all_g[expert, block].astype(F32)).astype(BF16)
        all_g[expert, block] = grads
        grad_u = (dot(grads, w_out[expert], 1, 1) * slope).astype(BF16)
        du[expert, block] = grad_u
        parts[1, expert, block] = dot(grad_u, w_in[expert], 1, 1).astype(BF16)

        @pl.when(step % 2 == 1)
        def _():
            mate_copy(0, expert, line).start()
            mate_copy(1, expert, line).start()

    def fold(expert, ahead):
        line = (my_line + ahead) % pairs
        for array in range(2):
            mate_copy(array, expert, line).wait_recv()
            if ahead > 0:
                both = parts[array, expert, line * 2 + my_core].astype(F32) + from_mate[
                    array, expert, line
                ].astype(F32)
                parts[array, expert, line * 2 + my_core] = both.astype(BF16)
                far_copy(array, expert, ahead).start()

    for expert in range(exp_dev):
        forth.wait(expert)
        own_x[expert] = dot(cap_map(target_ref, expert, capacity), incoming[expert]).astype(BF16)
        gather_x.begin(expert)
        all_x[expert, wsh_me] = own_x[expert]
        lax.fori_loop(0, 2, lambda step, carry: (work(expert, step), carry)[1], 0)
        for step in range(pairs - 1):
            gather_x.advance(expert, step)
        lax.fori_loop(2, wsh_count, lambda step, carry: (work(expert, step), carry)[1], 0)
        for ahead in range(1, pairs):
            fold(expert, ahead)

    back = [
        Exchange(
            ctx_count,
            exp_dev,
            most,
            (back_send.at[array], back_recv.at[array]),
            (
                lambda array: lambda expert, peer: returning.at[
                    array, forth.rows(expert * ctx_count + peer), :
                ]
            )(array),
            (
                lambda array: lambda expert, peer: home.at[
                    array, forth.rows(peer * exp_dev + expert), :
                ]
            )(array),
        )
        for array in range(2)
    ]
    for expert in range(exp_dev):
        forth.finish(expert)
    for expert in range(exp_dev):
        expert_rows = pl.ds(expert * ctx_count * most, ctx_count * most)
        fold(expert, 0)
        sums = []
        for array in range(2):
            line = my_line * 2 + my_core
            total = parts[array, expert, line].astype(F32) + from_mate[
                array, expert, my_line
            ].astype(F32)
            for ahead in range(1, pairs):
                far_copy(array, expert, ahead).wait_recv()
                total = total + from_far[array, expert, ahead - 1].astype(F32)
            sums.append(total)
        out_rows = sums[0].astype(BF16)
        rows = own_x[expert]
        probs, hot, share = choose(rows, router, experts, exp_dev * me + expert)
        slot_g = own_g_ref[expert].astype(F32)
        grad_gate = jnp.sum(slot_g * out_rows.astype(F32), axis=-1, keepdims=True)
        grad_logits = (share * grad_gate * (hot - probs)).astype(BF16)
        grad_rows = sums[1].astype(BF16).astype(F32) + dot(grad_logits, router, 1, 1)
        spread = cap_map(target_ref, expert, capacity)
        returning[1, expert_rows] = dot(spread, grad_rows.astype(BF16), 0, 0).astype(BF16)
        back[1].start(expert)
        returning[0, expert_rows] = dot(spread, out_rows, 0, 0).astype(BF16)
        router_part = dot(grad_logits, rows, 0, 0)[:experts]
        if expert == 0:
            grad_router_out[...] = router_part
        else:
            grad_router_out[...] += router_part
    for expert in range(exp_dev):
        back[0].start(expert)
    grad_up = grad[...].astype(F32)
    for expert in range(exp_dev):
        back[1].wait(expert)
    grad_normed = dot(placement_of(slot_ref, experts * most), home[1], 0, 0)
    scaled = grad_normed * gain_two
    mean = jnp.mean(scaled * resid[...], axis=-1, keepdims=True)
    gain_part = jnp.sum(grad_normed * resid[...] * inv_two, axis=0, keepdims=True)
    grad_gain_out[...] = jnp.broadcast_to(gain_part, grad_gain_out.shape)
    grad_mid = grad_up + inv_two * scaled - resid[...] * inv_two * inv_two * inv_two * mean
    grad_mid_out[...] = grad_mid
    branch[home_row] = grad_mid.astype(BF16)

    gather_d = LineGather(
        "ctx",
        lines,
        across,
        [lambda block: branch.at[block], lambda block: stats.at[block]],
        [branch.at[me], stats.at[me]],
        (branch_send, branch_recv),
    )
    if spread_here:
        gather_d.begin(0)
    grad_heads = dot(branch[home_row], wo[...], 1, 1).astype(BF16)
    grad_heads_out[...] = grad_heads
    product = grad_heads.astype(F32) * exact[...]
    heads = lax.broadcasted_iota(jnp.int32, (width, BLOCK), 0) // HEAD_DIM
    head_hot = (heads == lane_ids(width, BLOCK)).astype(F32)
    delta = jnp.transpose(
        lax.dot_general(
            product, head_hot, (((1,), (0,)), ((), ())), precision=HIGH, preferred_element_type=F32
        )
    )
    for pair in range(PAIRS):
        stats[home_row, pair] = lse_ref[pair]
        stats[home_row, pair, 2:4, :] = delta[2 * pair : 2 * pair + 2, :]
    if spread_here:
        gather_d.begin(1)

    def in_copy(expert):
        return pltpu.make_async_copy(stage_in, grad_in_out.at[expert], out_sems.at[1])

    def out_copy(expert):
        return pltpu.make_async_copy(stage_out, grad_out_out.at[expert], out_sems.at[0])

    group = min(wsh_count, 4)

    def slot_sum(stage, left, right, expert):
        def part(turn):
            blocks = pl.ds(turn * group, group)
            return dot(
                left[expert, blocks].reshape(group * capacity, left.shape[3]),
                right[expert, blocks].reshape(group * capacity, right.shape[3]),
                0,
                0,
            )

        stage[...] = part(0)
        if wsh_count > group:

            def add(turn, carry):
                stage[...] += part(turn)
                return carry

            lax.fori_loop(1, wsh_count // group, add, 0)

    def grads_of(expert):
        if expert:
            out_copy(expert - 1).wait()
        slot_sum(stage_out, hid, all_g, expert)
        out_copy(expert).start()
        if expert:
            in_copy(expert - 1).wait()
        slot_sum(stage_in, all_x, du, expert)
        in_copy(expert).start()

    grad_wo_out[...] = dot(attn[...], branch[home_row], 0, 0).astype(BF16)
    for step in range(lines - 1):
        if spread_here:
            for part in range(2):
                gather_d.advance(part, step)
        if step < exp_dev:
            grads_of(step)
    for expert in range(min(lines - 1, exp_dev), exp_dev):
        grads_of(expert)
    for expert in range(exp_dev):
        back[0].wait(expert)
    token_out = dot(placement_of(slot_ref, experts * most), home[0], 0, 0)
    output_out[...] = (resid[...] + gate * token_out).astype(BF16)
    upper = gather_d.line // max(lines // 2, 1)

    def order(step):
        ahead, line = step // lines, step % lines
        line = line + upper * (lines - 1 - 2 * line)
        return line, ahead, line * across + (gather_d.column + across - ahead) % across

    def put(slot, block):
        place = pl.ds(pl.multiple_of(block * tokens, tokens), tokens)
        return pltpu.make_async_copy(
            heads_stage.at[slot], heads_all_out.at[place, :], heads_sems.at[slot]
        )

    def heads_step(step, carry):
        line, ahead, block = order(step)
        slot = step % 2
        for skip in range(1, across):

            @pl.when(ahead == skip)
            def _():
                gather_d.cross_recv(0, line, skip).wait_recv()
                gather_d.cross_recv(1, line, skip).wait_recv()

        @pl.when(step >= 2)
        def _():
            put(slot, order(step - 2)[2]).wait()

        heads_stage[slot] = dot(branch[block], wo[...], 1, 1).astype(BF16)
        put(slot, block).start()
        return carry

    if spread_here:
        lax.fori_loop(0, ctx_count, heads_step, 0)
    stats_copy = pltpu.make_async_copy(stats, stats_out, fetch_sems.at[0])
    stats_copy.start()
    if spread_here:
        for step in (ctx_count - 2, ctx_count - 1):
            put(step % 2, order(step)[2]).wait()
    else:
        heads_stage[0] = branch[0]
        own_branch = pltpu.make_async_copy(heads_stage.at[0], heads_all_out, heads_sems.at[0])
        own_branch.start()
        own_branch.wait()
    out_copy(exp_dev - 1).wait()
    in_copy(exp_dev - 1).wait()
    stats_copy.wait()
    for expert in range(exp_dev):
        for array in range(2):
            back[array].finish(expert)
            for line in range(pairs):
                mate_copy(array, expert, line).wait_send()
            for ahead in range(1, pairs):
                far_copy(array, expert, ahead).wait_send()
    gather_x.finish()
    if spread_here:
        gather_d.finish()


def middle(
    counts,
    experts,
    attn,
    exact,
    hidden,
    grad,
    weights,
    w_in,
    w_out,
    own_g,
    small,
    slots,
    targets,
    lse_rows,
    routes,
):
    ctx_count, wsh_count = counts
    tokens, width = hidden.shape
    exp_dev, capacity = own_g.shape[:2]
    units = w_in.shape[2]
    slot_count = targets.shape[1]
    all_slots = experts * (slot_count // ctx_count)
    lines, across = grid_of(ctx_count)
    pairs = wsh_count // 2
    vmem = pl.BlockSpec(memory_space=pltpu.VMEM)
    anywhere = pl.BlockSpec(memory_space=pl.ANY)
    slot_rows = (exp_dev, wsh_count, capacity)
    spread_here = wsh_count <= 4
    held = ctx_count if spread_here else 1
    return pl.pallas_call(
        functools.partial(middle_kernel, counts, experts, spread_here),
        in_specs=[anywhere] * 7 + [vmem] * 6,
        out_specs=[vmem] * 3 + [anywhere] * 2 + [vmem] * 3 + [anywhere] * 2,
        out_shape=[
            jax.ShapeDtypeStruct((tokens, width), BF16),
            jax.ShapeDtypeStruct((tokens, width), F32),
            jax.ShapeDtypeStruct((tokens, width), BF16),
            jax.ShapeDtypeStruct((tokens * held, width), BF16),
            jax.ShapeDtypeStruct((held, PAIRS, 8, tokens), F32),
            jax.ShapeDtypeStruct((width, width), BF16),
            jax.ShapeDtypeStruct((experts, width), F32),
            jax.ShapeDtypeStruct((8, width), F32),
            jax.ShapeDtypeStruct((exp_dev, width, units), F32),
            jax.ShapeDtypeStruct((exp_dev, units, width), F32),
        ],
        scratch_shapes=[
            pltpu.VMEM((tokens, width), BF16),
            pltpu.VMEM((tokens, width), F32),
            pltpu.VMEM((tokens, width), BF16),
            pltpu.VMEM((tokens, width), BF16),
            pltpu.VMEM((width, width), BF16),
            pltpu.VMEM(w_in.shape, BF16),
            pltpu.VMEM(w_out.shape, BF16),
            pltpu.VMEM((tokens, width), F32),
            pltpu.VMEM((exp_dev, slot_count, width), BF16),
            pltpu.VMEM((exp_dev, capacity, width), BF16),
            pltpu.VMEM((*slot_rows, width), BF16),
            pltpu.VMEM((*slot_rows, width), BF16),
            pltpu.VMEM((*slot_rows, units), BF16),
            pltpu.VMEM((*slot_rows, units), BF16),
            pltpu.VMEM((2, *slot_rows, width), BF16),
            pltpu.VMEM((2, exp_dev, pairs, capacity, width), BF16),
            pltpu.VMEM((2, exp_dev, max(pairs - 1, 1), capacity, width), BF16),
            pltpu.VMEM((2, all_slots, width), BF16),
            pltpu.VMEM((2, all_slots, width), BF16),
            pltpu.VMEM((held, tokens, width), BF16),
            pltpu.VMEM((held, PAIRS, 8, tokens), F32),
            pltpu.VMEM((width, units), F32),
            pltpu.VMEM((units, width), F32),
            pltpu.VMEM((2, tokens, width), BF16),
            pltpu.SemaphoreType.DMA((7,)),
            pltpu.SemaphoreType.DMA((2,)),
            pltpu.SemaphoreType.DMA((2,)),
            *gather_sems(exp_dev, pairs, 2),
            *gather_sems(exp_dev, pairs, 2),
            *exchange_sems(ctx_count, exp_dev),
            pltpu.SemaphoreType.DMA((2, exp_dev, ctx_count - 1)),
            pltpu.SemaphoreType.DMA((2, exp_dev, ctx_count - 1)),
            pltpu.SemaphoreType.DMA((2, exp_dev, pairs)),
            pltpu.SemaphoreType.DMA((2, exp_dev, pairs)),
            pltpu.SemaphoreType.DMA((2, exp_dev, max(pairs - 1, 1))),
            pltpu.SemaphoreType.DMA((2, exp_dev, max(pairs - 1, 1))),
            *gather_sems(2, lines, across),
        ],
        compiler_params=pltpu.CompilerParams(
            collective_id=1, has_side_effects=True, vmem_limit_bytes=(56 if spread_here else 62) << 20
        ),
        name="middle",
    )(
        attn,
        exact,
        hidden,
        grad,
        weights,
        w_in,
        w_out,
        own_g,
        small,
        slots,
        targets,
        lse_rows,
        routes,
    )


def forward_kernel(place_ref, source_ref, q_ref, k_ref, v_ref, base_ref, out_ref, exact_ref, lse_ref, row_ref, scores_ref, bias_ref):
    bias_ref[...] = near_bias(base_ref)
    lanes = lane_ids(2 * BLOCK, NEAR)
    for own in range(2):
        block = place_ref[own]
        stacked = stack_heads(q_ref[rows_at(source_ref[block + 1]), :])
        scores = dot(stacked, two_tiles(k_ref, source_ref, block), 1, 1) + bias_ref[...]
        scores = jnp.where(lanes + block * BLOCK < BLOCK, MASKED, scores)
        scores_ref[0] = scores
        chunks = jnp.maximum(block, 1) // 2

        def score_step(chunk, best):
            start = block - 2 * chunk
            part = dot(stacked, two_tiles(k_ref, source_ref, start), 1, 1)
            part = jnp.where(lanes + start * BLOCK < BLOCK, MASKED, part)
            scores_ref[chunk] = part
            return jnp.maximum(best, fold_lanes(part, jnp.maximum))

        best = lax.fori_loop(1, chunks + 1, score_step, fold_lanes(scores, jnp.maximum))
        top = jnp.max(best, axis=-1, keepdims=True)

        def value_step(chunk, carry):
            total, summed = carry
            weights = jnp.exp(scores_ref[chunk] - top)
            high = weights.astype(BF16)
            low = (weights - high.astype(F32)).astype(BF16)
            values = two_tiles(v_ref, source_ref, block - 2 * chunk)
            summed = summed + dot(jnp.concatenate([high, low], axis=0), values)
            return (total + fold_lanes(weights, jnp.add), summed)

        total, summed = lax.fori_loop(
            0,
            chunks + 1,
            value_step,
            (jnp.zeros((2 * BLOCK, BLOCK), F32), jnp.zeros((4 * BLOCK, BLOCK), F32)),
        )
        total = jnp.sum(total, axis=-1, keepdims=True)
        main = summed[: 2 * BLOCK] / total
        exact = main + summed[2 * BLOCK :] / total
        rows = pl.ds(own * BLOCK, BLOCK)
        out_ref[rows, :] = merge_heads(main).astype(BF16)
        exact_ref[rows, :] = merge_heads(exact)
        lse = jnp.broadcast_to(top + jnp.log(total), (2 * BLOCK, BLOCK))
        lse_ref[0, own] = lse
        lse = jnp.transpose(lse)
        for head in range(2):
            row_ref[0, head : head + 1, own * BLOCK : (own + 1) * BLOCK] = lse[
                :1, head * BLOCK : (head + 1) * BLOCK
            ]
    row_ref[0, 2:8, :] = jnp.zeros((6, NEAR), F32)


def pair_specs(rows, width):
    pairs = width // BLOCK

    def column(offset):
        return pl.BlockSpec((rows, BLOCK), lambda pair, place, source: (0, offset + pair))

    return [column(0), column(pairs), column(2 * pairs)]


def attend_forward(places, source, qkv, base, width):
    rows = qkv.shape[0]
    chunks = rows // NEAR
    own = pl.BlockSpec((NEAR, BLOCK), lambda pair, place, source: (0, pair))
    return pl.pallas_call(
        forward_kernel,
        grid_spec=pltpu.PrefetchScalarGridSpec(
            num_scalar_prefetch=2,
            grid=(PAIRS,),
            in_specs=pair_specs(rows, width)
            + [pl.BlockSpec((1, 8, SPAN), lambda pair, place, source: (pair, 0, 0))],
            out_specs=[
                own,
                own,
                pl.BlockSpec((1, 2, NEAR, BLOCK), lambda pair, place, source: (pair, 0, 0, 0)),
                pl.BlockSpec((1, 8, NEAR), lambda pair, place, source: (pair, 0, 0)),
            ],
            scratch_shapes=[
                pltpu.VMEM((chunks, NEAR, NEAR), F32),
                pltpu.VMEM((NEAR, NEAR), F32),
            ],
        ),
        out_shape=[
            jax.ShapeDtypeStruct((NEAR, width), BF16),
            jax.ShapeDtypeStruct((NEAR, width), F32),
            jax.ShapeDtypeStruct((PAIRS, 2, NEAR, BLOCK), F32),
            jax.ShapeDtypeStruct((PAIRS, 8, NEAR), F32),
        ],
        compiler_params=pltpu.CompilerParams(vmem_limit_bytes=40 << 20),
        name="attend_forward",
    )(places, source, qkv, qkv, qkv, base)


def query_kernel(
    place_ref, source_ref, q_ref, k_ref, v_ref, base_ref, do_ref, exact_ref, lse_ref, dq_ref, sums_ref, bias_ref, near_ref
):
    bias_ref[...] = near_bias(base_ref)
    lanes = lane_ids(2 * BLOCK, NEAR)
    far = jnp.zeros((2 * BLOCK, BLOCK), F32)
    for own in range(2):
        block = place_ref[own]
        rows = pl.ds(own * BLOCK, BLOCK)
        stacked = stack_heads(q_ref[rows_at(source_ref[block + 1]), :])
        grads = stack_heads(do_ref[rows, :])
        exact = exact_ref[rows, :]
        product = grads.astype(F32) * jnp.concatenate([exact, exact], axis=0)
        delta = jnp.sum(product, axis=-1, keepdims=True)
        lse = lse_ref[0, own][:, :1]

        def grad_scores(scores, start):
            weights = jnp.exp(scores - lse)
            return weights * (dot(grads, two_tiles(v_ref, source_ref, start), 1, 1) - delta)

        scores = dot(stacked, two_tiles(k_ref, source_ref, block), 1, 1) + bias_ref[...]
        scores = jnp.where(lanes + block * BLOCK < BLOCK, MASKED, scores)
        near = grad_scores(scores, block)
        if own == 0:
            near_ref[...] = near
        else:
            near_ref[...] += near

        def step(chunk, carry):
            grad_q, far = carry
            start = block - 2 * chunk
            keys = two_tiles(k_ref, source_ref, start)
            part = dot(stacked, keys, 1, 1)
            part = jnp.where(lanes + start * BLOCK < BLOCK, MASKED, part)
            grad_s = grad_scores(part, start)
            return (grad_q + dot(grad_s.astype(BF16), keys), far + fold_lanes(grad_s, jnp.add))

        grad_q, far = lax.fori_loop(
            1,
            jnp.maximum(block, 1) // 2 + 1,
            step,
            (dot(near.astype(BF16), two_tiles(k_ref, source_ref, block)), far),
        )
        dq_ref[rows, :] = merge_heads(grad_q).astype(BF16)
    row_ids = lax.broadcasted_iota(jnp.int32, (BLOCK, SPAN), 0)
    for head in range(2):
        part = near_ref[head * BLOCK : (head + 1) * BLOCK, :]
        part = jnp.concatenate([part, jnp.zeros((BLOCK, BLOCK), F32)], axis=1)
        for bit in range(BLOCK.bit_length() - 1):
            moved = pltpu.roll(part, SPAN - (1 << bit), 1)
            part = jnp.where((row_ids >> bit) & 1 == 1, moved, part)
        sums_ref[0, head : head + 1, :] = jnp.sum(part, axis=0, keepdims=True)
        far_part = jnp.sum(far[head * BLOCK : (head + 1) * BLOCK], axis=0, keepdims=True)
        sums_ref[0, 2 + head : 3 + head, :] = jnp.concatenate(
            [far_part, jnp.zeros((1, NEAR), F32)], axis=1
        )
    sums_ref[0, 4:8, :] = jnp.zeros((4, SPAN), F32)


def attend_queries(places, source, qkv, base, grad_out, exact, lse):
    rows, width = qkv.shape[0], grad_out.shape[1]
    own = pl.BlockSpec((NEAR, BLOCK), lambda pair, place, source: (0, pair))
    row_spec = pl.BlockSpec((1, 8, SPAN), lambda pair, place, source: (pair, 0, 0))
    return pl.pallas_call(
        query_kernel,
        grid_spec=pltpu.PrefetchScalarGridSpec(
            num_scalar_prefetch=2,
            grid=(PAIRS,),
            in_specs=pair_specs(rows, width)
            + [
                row_spec,
                own,
                own,
                pl.BlockSpec((1, 2, NEAR, BLOCK), lambda pair, place, source: (pair, 0, 0, 0)),
            ],
            out_specs=[own, row_spec],
            scratch_shapes=[pltpu.VMEM((NEAR, NEAR), F32), pltpu.VMEM((NEAR, NEAR), F32)],
        ),
        out_shape=[
            jax.ShapeDtypeStruct((NEAR, width), BF16),
            jax.ShapeDtypeStruct((PAIRS, 8, SPAN), F32),
        ],
        compiler_params=pltpu.CompilerParams(vmem_limit_bytes=40 << 20),
        name="attend_queries",
    )(places, source, qkv, qkv, qkv, base, grad_out, exact, lse)


def key_kernel(place_ref, source_ref, q_ref, k_ref, v_ref, base_ref, do_ref, stats_ref, dk_ref, dv_ref, bias_ref):
    bias_ref[...] = near_bias(base_ref)
    blocks = q_ref.shape[0] // BLOCK
    lanes = lane_ids(2 * BLOCK, NEAR)

    def spread(row, start):
        window = jnp.concatenate(
            [
                stats_ref[source_ref[tile] // 2, 0, row : row + 2, rows_at(source_ref[tile] % 2)]
                for tile in (start, start + 1)
            ],
            axis=1,
        )
        return jnp.concatenate(
            [
                jnp.broadcast_to(window[:1], (BLOCK, NEAR)),
                jnp.broadcast_to(window[1:], (BLOCK, NEAR)),
            ],
            axis=0,
        )

    for own in range(2):
        block = place_ref[own]
        rows = pl.ds(own * BLOCK, BLOCK)
        keys = stack_heads(k_ref[rows_at(source_ref[block + 1]), :])
        values = stack_heads(v_ref[rows_at(source_ref[block + 1]), :])

        def grads(scores, start):
            queries, grad_out = two_tiles(q_ref, source_ref, start), two_tiles(do_ref, source_ref, start)
            scores = jnp.where((start == blocks) & (lanes >= BLOCK), MASKED, scores)
            weights = jnp.exp(scores - spread(0, start))
            grad_s = weights * (dot(values, grad_out, 1, 1) - spread(2, start))
            return dot(grad_s.astype(BF16), queries), dot(weights.astype(BF16), grad_out)

        def step(chunk, carry):
            start = block + 1 + 2 * chunk
            more_k, more_v = grads(dot(keys, two_tiles(q_ref, source_ref, start), 1, 1), start)
            return (carry[0] + more_k, carry[1] + more_v)

        near = dot(keys, two_tiles(q_ref, source_ref, block + 1), 1, 1) + bias_ref[...]
        chunks = jnp.maximum(blocks - 1 - block, 0) // 2
        grad_k, grad_v = lax.fori_loop(1, chunks + 1, step, grads(near, block + 1))
        dk_ref[rows, :] = merge_heads(grad_k).astype(BF16)
        dv_ref[rows, :] = merge_heads(grad_v).astype(BF16)


def attend_keys(places, source, qkv, base, grad_out, stats):
    rows, width = grad_out.shape
    own = pl.BlockSpec((NEAR, BLOCK), lambda pair, place, source: (0, pair))
    return pl.pallas_call(
        key_kernel,
        grid_spec=pltpu.PrefetchScalarGridSpec(
            num_scalar_prefetch=2,
            grid=(PAIRS,),
            in_specs=pair_specs(rows, width)
            + [
                pl.BlockSpec((1, 8, SPAN), lambda pair, place, source: (pair, 0, 0)),
                pl.BlockSpec((rows, BLOCK), lambda pair, place, source: (0, pair)),
                pl.BlockSpec(
                    (rows // NEAR, 1, 8, NEAR), lambda pair, place, source: (0, pair, 0, 0)
                ),
            ],
            out_specs=[own, own],
            scratch_shapes=[pltpu.VMEM((NEAR, NEAR), F32)],
        ),
        out_shape=[jax.ShapeDtypeStruct((NEAR, width), BF16)] * 2,
        compiler_params=pltpu.CompilerParams(vmem_limit_bytes=40 << 20),
        name="attend_keys",
    )(places, source, qkv, qkv, qkv, base, grad_out, stats)


BITS = {"core": ("wsh", 1), "x": ("wsh", 2), "y": ("ctx", 1), "near": ("ctx", 2), "far": ("ctx", 4)}
ORDERS = (
    ("core", "x", "near", "y", "far"),
    ("core", "x", "y", "near", "far"),
    ("core", "y", "near", "x", "far"),
    ("core", "near", "y", "x", "far"),
)


def halved_shapes(order, share, width):
    shapes, blocks, rows, columns = [], 4, share, width
    for name in order:
        if name in ("core", "x"):
            blocks //= 2
        elif name == "y":
            columns //= 2
        else:
            rows //= 2
        shapes.append((blocks, rows, columns))
    return shapes


def partner(name):
    axis, bit = BITS[name]
    me = lax.axis_index(axis)
    side = (me // bit) % 2
    return axis, me + bit * (1 - 2 * side), side


def tail_kernel(
    experts,
    dq_ref,
    dk_ref,
    dv_ref,
    hidden_ref,
    grad_mid_ref,
    weights_ref,
    grad_wo_ref,
    small_ref,
    router_ref,
    gain_ref,
    sums_ref,
    hot_ref,
    input_grad_out,
    wq_out,
    wk_out,
    wv_out,
    wo_out,
    router_out,
    gains_out,
    table_out,
    weights,
    hidden,
    grad_mid,
    grad_wo,
    total,
    gathered,
    pack,
    pack_recv,
    *rest,
):
    steps = len(BITS)
    sends = [rest[matrix * steps : (matrix + 1) * steps] for matrix in range(4)]
    rest = rest[4 * steps :]
    recvs = [rest[matrix * steps : (matrix + 1) * steps] for matrix in range(4)]
    fetch_sems, half_send, half_recv, whole_send, whole_recv, pack_send, pack_sem = rest[4 * steps :]
    tokens, width = dq_ref.shape
    share = total.shape[2]
    sources = (
        (hidden_ref, hidden),
        (grad_wo_ref, grad_wo),
        (weights_ref.at[pl.ds(0, 3)], weights),
        (grad_mid_ref, grad_mid),
    )
    fetches = [
        pltpu.make_async_copy(src, dst, fetch_sems.at[place])
        for place, (src, dst) in enumerate(sources)
    ]
    for fetch in fetches:
        fetch.start()
    barrier = pltpu.get_barrier_semaphore()
    for name in BITS:
        axis, peer, side = partner(name)
        pl.semaphore_signal(
            barrier, inc=1, device_id={axis: peer}, device_id_type=pl.DeviceIdType.MESH
        )
    pl.semaphore_wait(barrier, steps)

    def remote(source, target, send, recv, name):
        axis, peer, side = partner(name)
        return pltpu.make_async_remote_copy(
            src_ref=source,
            dst_ref=target,
            send_sem=send,
            recv_sem=recv,
            device_id={axis: peer},
            device_id_type=pl.DeviceIdType.MESH,
        )

    regions = []
    for order in ORDERS:
        blocks, row, column, kept = [0, 1, 2, 3], 0, 0, []
        rows, columns = share, width
        for name in order:
            side = partner(name)[2]
            if name == "core":
                pair = [(line * 2 + side, line * 2 + 1 - side) for line in range(2)]
                keep = ([a for a, b in pair], row, column)
                sent = ([b for a, b in pair], row, column)
            elif name == "x":
                core = partner("core")[2]
                keep = ([side * 2 + core], row, column)
                sent = ([(1 - side) * 2 + core], row, column)
            elif name == "y":
                columns //= 2
                keep = (blocks, row, column + side * columns)
                sent = (blocks, row, column + (1 - side) * columns)
            else:
                rows //= 2
                keep = (blocks, row + side * rows, column)
                sent = (blocks, row + (1 - side) * rows, column)
            blocks, row, column = keep
            kept.append((keep, sent))
        regions.append(kept)

    def spans(matrix, step, region):
        shape = sends[matrix][step].shape
        blocks, row, column = region
        row_part = pl.ds(row if isinstance(row, int) else pl.multiple_of(row, 16), shape[1])
        column_part = pl.ds(
            column if isinstance(column, int) else pl.multiple_of(column, BLOCK), shape[2]
        )
        return blocks, row_part, column_part

    def half_copy(matrix, step):
        return remote(
            sends[matrix][step],
            recvs[matrix][step],
            half_send.at[matrix, step],
            half_recv.at[matrix, step],
            ORDERS[matrix][step],
        )

    def give(matrix, step):
        blocks, row_part, column_part = spans(matrix, step, regions[matrix][step][1])
        for place, block in enumerate(blocks):
            sends[matrix][step][place] = total[matrix, block, row_part, column_part].astype(BF16)
        half_copy(matrix, step).start()

    def take(matrix, step):
        half_copy(matrix, step).wait_recv()
        blocks, row_part, column_part = spans(matrix, step, regions[matrix][step][0])
        for place, block in enumerate(blocks):
            total[matrix, block, row_part, column_part] += recvs[matrix][step][place].astype(F32)

    def whole_view(matrix, step):
        keep = regions[matrix][step][0]
        blocks, row_part, column_part = spans(matrix, step, keep)
        return gathered.at[matrix, row_part, column_part]

    wholes = [[name for name in order if BITS[name][0] == "ctx"] for order in ORDERS]

    def whole_copy(matrix, back):
        name = wholes[matrix][2 - back]
        step = ORDERS[matrix].index(name)
        blocks, row, column = regions[matrix][step][0]
        shape = sends[matrix][step].shape
        row_part = pl.ds(row if isinstance(row, int) else pl.multiple_of(row, 16), shape[1])
        column_part = pl.ds(
            column if isinstance(column, int) else pl.multiple_of(column, BLOCK), shape[2]
        )
        view = gathered.at[matrix, row_part, column_part]
        return remote(view, view, whole_send.at[matrix, back], whole_recv.at[matrix, back], name)

    fetches[0].wait()
    resid = hidden[...].astype(F32)
    inv = lax.rsqrt(jnp.mean(resid * resid, axis=-1, keepdims=True) + epsilon)
    gain = jnp.transpose(small_ref[...].astype(F32))[experts : experts + 1, :]
    normed = (resid * inv * gain).astype(BF16)
    for matrix, ref in ((1, dq_ref), (2, dk_ref), (3, dv_ref)):
        part = dot(normed, ref[...], 0, 0)
        for block in range(4):
            total[matrix, block] = part[block * share : (block + 1) * share]
        give(matrix, 0)
    fetches[1].wait()
    for block in range(4):
        total[0, block] = grad_wo[block * share : (block + 1) * share, :].astype(F32)
    give(0, 0)
    fetches[2].wait()
    grad_normed = dot(dq_ref[...], weights[0], 1, 1)
    grad_normed = grad_normed + dot(dk_ref[...], weights[1], 1, 1)
    grad_normed = grad_normed + dot(dv_ref[...], weights[2], 1, 1)
    pack[...] = jnp.zeros_like(pack)
    pack[:experts, :] = router_ref[...]
    pack[experts : experts + 1, :] = jnp.sum(grad_normed * resid * inv, axis=0, keepdims=True)
    pack[experts + 1 : experts + 2, :] = gain_ref[0:1, :]
    last = lane_ids(2, BLOCK) == hot_ref.shape[1] - 1
    for pair in range(PAIRS):
        near = lax.dot_general(
            sums_ref[pair, 0:2, :],
            hot_ref[...],
            (((1,), (0,)), ((), ())),
            precision=HIGH,
            preferred_element_type=F32,
        )
        near = jnp.concatenate([near, jnp.zeros((2, BLOCK - near.shape[1]), F32)], axis=1)
        distant = jnp.sum(sums_ref[pair, 2:4, :], axis=1, keepdims=True)
        place = experts + 8 + 2 * pair
        pack[place : place + 2, :BLOCK] = near + jnp.where(last, distant, 0.0)

    def pack_copy(step):
        return remote(
            pack_recv.at[0, step],
            pack_recv.at[1, step],
            pack_send.at[step],
            pack_sem.at[step],
            list(BITS)[step],
        )

    for step in range(steps):
        pack_recv[0, step] = pack[...]
        pack_copy(step).start()
        for matrix in (1, 2, 3, 0):
            take(matrix, step)
            if step + 1 < steps:
                give(matrix, step + 1)
        if step == 0:
            fetches[3].wait()
            scaled = grad_normed * gain
            mean = jnp.mean(scaled * resid, axis=-1, keepdims=True)
            grad_in = grad_mid[...] + inv * scaled - resid * inv * inv * inv * mean
            input_grad_out[...] = grad_in.astype(BF16)
        pack_copy(step).wait_recv()
        pack[...] += pack_recv[1, step]

    outs = (wo_out, wq_out, wk_out, wv_out)
    mine = lax.axis_index("wsh")
    for matrix in range(4):
        keep = regions[matrix][steps - 1][0]
        blocks, row_part, column_part = spans(matrix, steps - 1, keep)
        gathered[matrix, row_part, column_part] = total[
            matrix, blocks[0], row_part, column_part
        ].astype(BF16)
        whole_copy(matrix, 0).start()
    for back in range(3):
        for matrix in range(4):
            whole_copy(matrix, back).wait_recv()
            if back < 2:
                whole_copy(matrix, back + 1).start()
            else:
                outs[matrix][...] = gathered[matrix].astype(F32)
        if back == 0:
            buckets = table_out.shape[0]
            for block in range(4):

                @pl.when(mine == block)
                def _():
                    rows = pack[: experts + 8, block * share : (block + 1) * share]
                    turned = jnp.transpose(rows)
                    router_out[...] = turned[:, :experts]
                    gains_out[...] = rows[experts : experts + 8]
                    table = jnp.transpose(pack[experts + 8 :, :BLOCK])
                    table_out[...] = table[block * buckets : (block + 1) * buckets, :HEADS]

    for step in range(steps):
        pack_copy(step).wait_send()
        for matrix in range(4):
            half_copy(matrix, step).wait_send()
    for back in range(3):
        for matrix in range(4):
            whole_copy(matrix, back).wait_send()


def tail(experts, dq, dk, dv, hidden, grad_mid, weights, grad_wo, small, router, gains, sums, hot, share, buckets):
    tokens, width = dq.shape
    vmem = pl.BlockSpec(memory_space=pltpu.VMEM)
    anywhere = pl.BlockSpec(memory_space=pl.ANY)
    steps = len(BITS)
    pieces = [shape for order in ORDERS for shape in halved_shapes(order, share, width)]
    buffers = [pltpu.VMEM(shape, BF16) for shape in pieces]
    rows = experts + 8 + 16
    dma = pltpu.SemaphoreType.DMA
    return pl.pallas_call(
        functools.partial(tail_kernel, experts),
        in_specs=[vmem] * 3 + [anywhere] * 4 + [vmem] * 5,
        out_specs=[vmem] * 8,
        out_shape=[
            jax.ShapeDtypeStruct((tokens, width), BF16),
            *[jax.ShapeDtypeStruct((share, width), F32)] * 4,
            jax.ShapeDtypeStruct((share, experts), F32),
            jax.ShapeDtypeStruct((8, share), F32),
            jax.ShapeDtypeStruct((buckets, HEADS), F32),
        ],
        scratch_shapes=[
            pltpu.VMEM((3, width, width), BF16),
            pltpu.VMEM((tokens, width), BF16),
            pltpu.VMEM((tokens, width), F32),
            pltpu.VMEM((width, width), BF16),
            pltpu.VMEM((4, 4, share, width), F32),
            pltpu.VMEM((4, share, width), BF16),
            pltpu.VMEM((rows, width), F32),
            pltpu.VMEM((2, steps, rows, width), F32),
            *buffers,
            *buffers,
            dma((4,)),
            dma((4, steps)),
            dma((4, steps)),
            dma((4, 3)),
            dma((4, 3)),
            dma((steps,)),
            dma((steps,)),
        ],
        compiler_params=pltpu.CompilerParams(
            collective_id=2, has_side_effects=True, vmem_limit_bytes=56 << 20
        ),
        name="tail",
    )(dq, dk, dv, hidden, grad_mid, weights, grad_wo, small, router, gains, sums, hot)


def rms_forward(values, gain_vec):
    inv_rms = lax.rsqrt(jnp.mean(values * values, axis=-1, keepdims=True) + epsilon)
    return (values * inv_rms * gain_vec, inv_rms)


def rms_backward(values, inv_rms, gain_vec, upstream):
    grad_gain = jnp.sum(upstream * values * inv_rms, axis=0)
    scaled = upstream * gain_vec
    grad_values = inv_rms * scaled - values * inv_rms**3 * jnp.mean(
        scaled * values, axis=-1, keepdims=True
    )
    return (grad_values, grad_gain)


def per_device(
    hidden_in,
    w_query,
    w_key,
    w_value,
    w_output,
    w_router,
    gain_attn,
    gain_moe,
    rel_bias,
    w_in,
    w_out,
    routes,
    block_pairs,
    cotangent,
):
    tokens, width = hidden_in.shape[1:]
    ctx_count, wsh_count = lax.axis_size("ctx"), lax.axis_size("wsh")
    ctx_rank, wsh_rank = lax.axis_index("ctx"), lax.axis_index("wsh")
    length = tokens * ctx_count
    blocks = length // BLOCK
    experts, exp_dev = w_router.shape[1], w_in.shape[0]
    slot_most = 2 * tokens // experts
    capacity = (9 * length // (8 * experts) + 7) // 8 * 8

    def over(axis, array, dim=0):
        return lax.all_gather(array, axis, axis=dim, tiled=True)

    share = width // wsh_count
    small = jnp.concatenate(
        [
            w_router,
            gain_attn[:, None],
            gain_moe[:, None],
            jnp.pad(rel_bias, ((0, share - rel_bias.shape[0]), (0, 0))),
        ],
        axis=1,
    )
    small = jnp.pad(small, ((0, 0), (0, BLOCK - small.shape[1])))
    qkv, weights, small, slot_rows, targets, own_g = project(
        (ctx_count, wsh_count),
        capacity,
        experts,
        slot_most,
        hidden_in[0],
        (w_query, w_key, w_value, w_output),
        small,
        routes.reshape(1, tokens),
        cotangent[0],
    )
    full_query, full_key, full_value, full_output = (weights[place] for place in range(4))
    full_router = small[:, :experts]
    gain_one = small[:, experts].astype(F32)
    gain_two = small[:, experts + 1].astype(F32)
    full_bias = small.reshape(wsh_count, share, BLOCK)[
        :, : rel_bias.shape[0], experts + 2 : experts + 2 + HEADS
    ].reshape(-1, HEADS)

    order = block_pairs.reshape(-1)
    places = lax.dynamic_slice_in_dim(order, 2 * ctx_rank, 2)
    ids = jnp.arange(blocks, dtype=jnp.int32)
    inverse = jnp.sum(jnp.where(order[None, :] == ids[:, None], ids[None, :], 0), axis=1)
    source = jnp.pad(inverse, (1, 1))

    buckets = full_bias.shape[0]
    lanes = wrapped_lanes()
    query_hot = onehot_of(BLOCK - lanes, buckets)
    key_hot = onehot_of(lanes, buckets)

    def base_rows(hot, distance):
        table = dot(full_bias, jnp.asarray(hot, BF16), 0, 1)
        table = table - full_bias[buckets - 1].astype(F32)[:, None]
        table = jnp.where(jnp.asarray(distance >= 0)[None, :], table, MASKED)
        return jnp.pad(table.reshape(PAIRS, 2, SPAN), ((0, 0), (0, 6), (0, 0)))

    query_base = base_rows(query_hot, BLOCK - lanes)
    key_base = base_rows(key_hot, lanes)

    attn_low, attn_exact, lse, lse_rows = attend_forward(places, source, qkv, query_base, width)
    (
        output_rows,
        grad_mid,
        grad_heads,
        heads_all,
        stats,
        grad_wo,
        grad_router,
        grad_gain_m,
        grad_w_in,
        grad_w_out,
    ) = middle(
        (ctx_count, wsh_count),
        experts,
        attn_low,
        attn_exact,
        hidden_in[0],
        cotangent[0],
        weights,
        w_in,
        w_out,
        own_g,
        small,
        slot_rows,
        targets,
        lse_rows,
        routes.reshape(tokens, 1),
    )

    if heads_all.shape[0] == tokens:
        heads_all = dot(over("ctx", heads_all), full_output, 1, 1).astype(BF16)
        stats = over("ctx", stats)

    grad_q, sums = attend_queries(places, source, qkv, query_base, grad_heads, attn_exact, lse)
    grad_k, grad_v = attend_keys(places, source, qkv, key_base, heads_all, stats)

    bucket_share = buckets // wsh_count
    if ctx_count == 8 and wsh_count == 4 and share % 64 == 0:
        grad_input, grad_a, grad_b, grad_c, grad_d, own_router, own_gains, own_table = tail(
            experts,
            grad_q,
            grad_k,
            grad_v,
            hidden_in[0],
            grad_mid,
            weights,
            grad_wo,
            small,
            grad_router,
            grad_gain_m,
            sums,
            jnp.asarray(query_hot),
            share,
            bucket_share,
        )
        return (
            output_rows[None],
            grad_input[None],
            grad_a,
            grad_b,
            grad_c,
            grad_d,
            own_router,
            own_gains[0],
            own_gains[1],
            own_table,
            grad_w_in,
            grad_w_out,
        )

    near_sums = sums[:, :2].reshape(HEADS, SPAN)
    far_sums = jnp.sum(sums[:, 2:4].reshape(HEADS, SPAN), axis=1)
    grad_table = jnp.dot(jnp.asarray(query_hot.T), near_sums.T, precision=HIGH)
    grad_table = grad_table.at[buckets - 1].add(far_sums)

    resid_in = hidden_in[0].astype(F32)
    normed_one, inv_one = rms_forward(resid_in, gain_one)
    normed_one = normed_one.astype(BF16)
    grad_normed_one = dot(grad_q, full_query, 1, 1)
    grad_normed_one = grad_normed_one + dot(grad_k, full_key, 1, 1)
    grad_normed_one = grad_normed_one + dot(grad_v, full_value, 1, 1)
    grad_in_norm, grad_gain_a = rms_backward(resid_in, inv_one, gain_one, grad_normed_one)
    grad_input = (grad_mid + grad_in_norm).astype(BF16)

    def reduce_weight(grad):
        part = lax.psum_scatter(grad.astype(BF16), "wsh", scatter_dimension=0, tiled=True)
        return lax.psum(part, "ctx").astype(F32)

    grad_wq = dot(normed_one, grad_q, 0, 0)
    grad_wk = dot(normed_one, grad_k, 0, 0)
    grad_wv = dot(normed_one, grad_v, 0, 0)
    shares = [reduce_weight(grad) for grad in (grad_wq, grad_wk, grad_wv, grad_wo)]
    columns = jnp.concatenate(
        [grad_router.T, grad_gain_a[:, None], grad_gain_m[0][:, None]], axis=1
    )
    table = jnp.pad(grad_table, ((0, 0), (0, columns.shape[1] - HEADS)))
    summed = lax.psum(jnp.concatenate([columns, table], axis=0), ("ctx", "wsh"))
    own_columns = lax.dynamic_slice_in_dim(summed[:width], wsh_rank * share, share, 0)
    own_table = lax.dynamic_slice_in_dim(
        summed[width:, :HEADS], wsh_rank * bucket_share, bucket_share, 0
    )
    return (
        output_rows.astype(BF16)[None],
        grad_input[None],
        *shares,
        own_columns[:, :experts],
        own_columns[:, experts],
        own_columns[:, experts + 1],
        own_table,
        grad_w_in,
        grad_w_out,
    )


def solution(mesh):
    in_specs = (
        P("wsh", "ctx", None),
        P("wsh", None),
        P("wsh", None),
        P("wsh", None),
        P("wsh", None),
        P("wsh", None),
        P("wsh"),
        P("wsh"),
        P("wsh", None),
        P("ctx", None, "wsh"),
        P("ctx", "wsh", None),
        P("wsh", "ctx", None),
        P(),
        P("wsh", "ctx", None),
    )
    out_specs = (
        P("wsh", "ctx", None),
        P("wsh", "ctx", None),
        P("wsh", None),
        P("wsh", None),
        P("wsh", None),
        P("wsh", None),
        P("wsh", None),
        P("wsh"),
        P("wsh"),
        P("wsh", None),
        P("ctx", None, "wsh"),
        P("ctx", "wsh", None),
    )
    return jax.shard_map(
        per_device, mesh=mesh, in_specs=in_specs, out_specs=out_specs, check_vma=False
    )
```

```python
import functools
import math

import jax
import jax.numpy as jnp
import numpy as np
from jax import lax
from jax.experimental import pallas as pl
from jax.experimental.pallas import tpu as pltpu
from jax.sharding import PartitionSpec as P

HEADS = 12
HEAD_DIM = 64
BLOCK = 128
PAIRS = HEADS // 2
NEAR = 2 * BLOCK
SPAN = 3 * BLOCK
epsilon = 1e-06
MASKED = -1e30
bucket_edges = [math.ceil(16 * 8 ** (marker / 16)) for marker in range(1, 16)]
F32 = jnp.float32
BF16 = jnp.bfloat16
HIGH = lax.Precision.HIGHEST


def bucket_of(distance):
    gap = np.maximum(distance, 0)
    count = np.full(gap.shape, 16, np.int32)
    for edge in bucket_edges:
        count = count + (gap >= edge)
    return np.where(gap < 16, gap, count)


def wrapped_lanes():
    lanes = np.arange(SPAN)
    return np.where(lanes < NEAR, lanes, lanes - SPAN)


def onehot_of(distance, buckets):
    return (bucket_of(distance)[:, None] == np.arange(buckets)[None, :]).astype(np.float32)


def dot(left, right, left_dim=1, right_dim=0):
    return lax.dot_general(
        left, right, (((left_dim,), (right_dim,)), ((), ())), preferred_element_type=F32
    )


def lane_ids(rows, lanes):
    return lax.broadcasted_iota(jnp.int32, (rows, lanes), 1)


def stack_heads(rows):
    first = lane_ids(rows.shape[0], BLOCK) < HEAD_DIM
    zero = jnp.zeros_like(rows)
    return jnp.concatenate([jnp.where(first, rows, zero), jnp.where(first, zero, rows)], axis=0)


def merge_heads(stacked):
    half = stacked.shape[0] // 2
    first = lane_ids(half, BLOCK) < HEAD_DIM
    return jnp.where(first, stacked[:half], stacked[half:])


def fold_lanes(tile, combine):
    return combine(tile[:, :BLOCK], tile[:, BLOCK:])


def near_bias(base_ref, place=0):
    tiles = []
    for head in range(2):
        row = jnp.broadcast_to(base_ref[place, head : head + 1, :], (BLOCK, SPAN))
        tiles.append(pltpu.roll(row, 0, 1, stride=1, stride_axis=0)[:, :NEAR])
    return jnp.concatenate(tiles, axis=0)


def rows_at(block):
    return pl.ds(pl.multiple_of(block * BLOCK, BLOCK), BLOCK)


def two_tiles(ref, plan_ref, tile):
    tile = SOURCE + tile
    return jnp.concatenate(
        [ref[rows_at(plan_ref[tile]), :], ref[rows_at(plan_ref[tile + 1]), :]], axis=0
    )


class LineGather:
    def __init__(self, axis, lines, across, views, own, sems):
        self.axis, self.lines, self.across = axis, lines, across
        self.views, self.own, self.sems = views, own, sems
        self.me = lax.axis_index(axis)
        self.line, self.column = self.me // across, self.me % across

    def copy(self, part, block, peer, kind, place, own=False):
        send, recv = self.sems
        view = self.views[part](block)
        return pltpu.make_async_remote_copy(
            src_ref=self.own[part] if own else view,
            dst_ref=view,
            send_sem=send.at[part, kind, place],
            recv_sem=recv.at[part, kind, place],
            device_id={self.axis: peer},
            device_id_type=pl.DeviceIdType.MESH,
        )

    def line_send(self, part, way, step):
        place = self.line - way * step
        ahead = self.line + way
        there = (place >= 0) & (place < self.lines) & (ahead >= 0) & (ahead < self.lines)
        copy = self.copy(
            part,
            place * self.across + self.column,
            ahead * self.across + self.column,
            (1 - way) // 2,
            step,
            own=step == 0,
        )
        return there, copy

    def line_recv(self, part, way, step):
        place = self.line - way * (step + 1)
        there = (place >= 0) & (place < self.lines)
        block = place * self.across + self.column
        return there, block, self.copy(part, block, self.me, (1 - way) // 2, step)

    def cross_send(self, part, block, ahead, own=False):
        peer = self.line * self.across + (self.column + ahead) % self.across
        return self.copy(part, block, peer, 1 + ahead, block // self.across, own)

    def cross_recv(self, part, line, ahead):
        block = line * self.across + (self.column + self.across - ahead) % self.across
        return self.copy(part, block, self.me, 1 + ahead, line)

    def begin(self, part):
        for way in (1, -1):
            there, copy = self.line_send(part, way, 0)
            pl.when(there)(copy.start)
        for ahead in range(1, self.across):
            self.cross_send(part, self.me, ahead, own=True).start()

    def advance(self, part, step):
        for way in (1, -1):
            there, block, arrived = self.line_recv(part, way, step)

            @pl.when(there)
            def _():
                arrived.wait_recv()
                for ahead in range(1, self.across):
                    self.cross_send(part, block, ahead).start()

            if step + 2 < self.lines:
                there, copy = self.line_send(part, way, step + 1)
                pl.when(there)(copy.start)

    def wait_cross(self, part):
        for ahead in range(1, self.across):
            for line in range(self.lines):
                self.cross_recv(part, line, ahead).wait_recv()

    def finish(self):
        for part in range(len(self.views)):
            for step in range(self.lines - 1):
                for way in (1, -1):
                    there, copy = self.line_send(part, way, step)
                    pl.when(there)(copy.wait_send)
            for ahead in range(1, self.across):
                for line in range(self.lines):
                    self.cross_send(part, line * self.across + self.column, ahead).wait_send()


def gather_sems(parts, lines, across):
    return [pltpu.SemaphoreType.DMA((parts, 1 + across, lines))] * 2


def greet(counts):
    barrier = pltpu.get_barrier_semaphore()
    for axis, count in zip(("ctx", "wsh"), counts):
        me = lax.axis_index(axis)
        for ahead in range(1, count):
            pl.semaphore_signal(
                barrier,
                inc=1,
                device_id={axis: (me + ahead) % count},
                device_id_type=pl.DeviceIdType.MESH,
            )
    pl.semaphore_wait(barrier, sum(counts) - 2)


class Exchange:
    def __init__(self, count, experts, most, sems, source, target):
        self.count, self.experts, self.most = count, experts, most
        self.send, self.recv = sems
        self.source, self.target = source, target
        self.me = lax.axis_index("ctx")

    def rows(self, place):
        return pl.ds(pl.multiple_of(place * self.most, self.most), self.most)

    def copy(self, expert, ahead, outward):
        peer = (self.me + ahead) % self.count if outward else (self.me + self.count - ahead) % self.count
        return pltpu.make_async_remote_copy(
            src_ref=self.source(expert, peer),
            dst_ref=self.target(expert, self.me),
            send_sem=self.send.at[expert, ahead - 1],
            recv_sem=self.recv.at[expert, ahead - 1],
            device_id={"ctx": peer},
            device_id_type=pl.DeviceIdType.MESH,
        )

    def start(self, expert):
        for ahead in range(1, self.count):
            self.copy(expert, ahead, True).start()
        self.target(expert, self.me)[...] = self.source(expert, self.me)[...]

    def wait(self, expert):
        for ahead in range(1, self.count):
            peer = (self.me + self.count - ahead) % self.count
            pltpu.make_async_remote_copy(
                src_ref=self.source(expert, peer),
                dst_ref=self.target(expert, peer),
                send_sem=self.send.at[expert, ahead - 1],
                recv_sem=self.recv.at[expert, ahead - 1],
                device_id={"ctx": peer},
                device_id_type=pl.DeviceIdType.MESH,
            ).wait_recv()

    def finish(self, expert):
        for ahead in range(1, self.count):
            self.copy(expert, ahead, True).wait_send()


def exchange_sems(count, experts):
    return [pltpu.SemaphoreType.DMA((experts, count - 1))] * 2


def cap_map(target_ref, expert, capacity):
    slots = target_ref.shape[1]
    rows = lax.broadcasted_iota(jnp.int32, (capacity, slots), 0)
    return (rows == jnp.broadcast_to(target_ref[expert : expert + 1, :], rows.shape)).astype(F32).astype(BF16)


def placement_of(slot_ref, slots):
    rows = lax.broadcasted_iota(jnp.int32, (slots, slot_ref.shape[1]), 0)
    return (rows == jnp.broadcast_to(slot_ref[0:1, :], rows.shape)).astype(F32).astype(BF16)


def grid_of(count):
    lines = 4 if count % 4 == 0 else 1
    return lines, count // lines


def route_slots(routes_ref, chosen_ref, most):
    experts, tokens = chosen_ref.shape
    ids = lax.broadcasted_iota(jnp.int32, (experts, tokens), 0)
    routes = jnp.broadcast_to(routes_ref[0:1, :], ids.shape)
    chosen = (ids == routes).astype(F32)
    chosen_ref[...] = chosen
    earlier = lax.broadcasted_iota(jnp.int32, (tokens, tokens), 0) < lax.broadcasted_iota(
        jnp.int32, (tokens, tokens), 1
    )
    before = dot(chosen.astype(BF16), earlier.astype(F32).astype(BF16))
    rank = jnp.sum(chosen * before, axis=0, keepdims=True).astype(jnp.int32)
    return routes_ref[0:1, :] * most + rank, jnp.sum(chosen, axis=1, keepdims=True)


SOURCE = 2


def plan_start(blocks):
    return SOURCE + blocks + 2


def plan_size(blocks):
    return plan_start(blocks) + 4 + 3 * (blocks + 1)


def write_plan(pairs_ref, plan, me):
    blocks = 2 * pairs_ref.shape[0]
    half = blocks // 2
    own = [pairs_ref[me, side] for side in range(2)]
    plan[0], plan[1] = own[0], own[1]
    plan[SOURCE] = jnp.int32(0)
    plan[SOURCE + blocks + 1] = jnp.int32(0)

    def place(position, carry):
        found = jnp.int32(0)
        for row in range(blocks):
            found = found + jnp.where(pairs_ref[row // 2, row % 2] == position, row, 0)
        plan[SOURCE + 1 + position] = found
        return carry

    lax.fori_loop(0, blocks, place, 0)
    early, late = jnp.minimum(own[0], own[1]), jnp.maximum(own[0], own[1])
    first = jnp.where(own[0] < own[1], 0, 1).astype(jnp.int32)
    start = plan_start(blocks)
    plan[start], plan[start + 1] = first, 1 - first
    plan[start + 2], plan[start + 3] = early, late
    start = start + 4
    for step in range(blocks + 1):
        rest = step - (half + 2)
        if step <= half:
            tile, owner = late - step, jnp.int32(1)
        elif step == half + 1:
            tile, owner = early, jnp.int32(0)
        else:
            tile = jnp.where(rest < early, early - 1 - rest, late - half - 1 - (rest - early))
            owner = jnp.where(rest < early, 0, 1).astype(jnp.int32)
        tile = jnp.minimum(jnp.maximum(tile, 0), blocks - 1)
        plan[start + step] = plan[SOURCE + 1 + tile]
        plan[start + blocks + 1 + step] = owner
        plan[start + 2 * blocks + 2 + step] = plan[SOURCE + blocks - tile]


def project_kernel(
    counts,
    capacity,
    rows_ref,
    wq_ref,
    wk_ref,
    wv_ref,
    wo_ref,
    small_ref,
    routes_ref,
    pairs_ref,
    query_hot_ref,
    key_hot_ref,
    grad_ref,
    qkv_out,
    weights_out,
    small_out,
    slot_out,
    target_out,
    own_out,
    plan_out,
    query_base_out,
    key_base_out,
    held,
    weights,
    smalls,
    gain,
    ready,
    chosen,
    tallies,
    grad_rows,
    outgoing,
    incoming,
    row_send,
    row_recv,
    weight_send,
    weight_recv,
    grad_send,
    grad_recv,
    tally_send,
    tally_recv,
    out_sems,
    local_sems,
):
    ctx_count, wsh_count = counts
    experts = chosen.shape[0]
    exp_dev = experts // ctx_count
    lanes = experts
    tokens, width = rows_ref.shape
    share = wq_ref.shape[0]
    lines, across = grid_of(ctx_count)
    pairs = wsh_count // 2

    def shard(block):
        return pl.ds(pl.multiple_of(block * share, 16), share)

    def weight_view(place):
        return lambda block: weights.at[place, shard(block), :]

    rows = LineGather(
        "ctx", lines, across, [lambda block: held.at[block]], [rows_ref], (row_send, row_recv)
    )
    mats = LineGather(
        "wsh",
        pairs,
        2,
        [lambda block: smalls.at[shard(block), :]] + [weight_view(place) for place in range(4)],
        [small_ref, wq_ref, wk_ref, wv_ref, wo_ref],
        (weight_send, weight_recv),
    )
    own_copies = [
        pltpu.make_async_copy(ref, view(index), local_sems.at[2 + place])
        for place, (ref, view, index) in enumerate(
            zip(
                [rows_ref] + mats.own,
                rows.views + mats.views,
                [rows.me] + [mats.me] * 5,
            )
        )
    ]
    grad_copy = pltpu.make_async_copy(grad_ref, grad_rows, local_sems.at[8])
    grad_copy.start()
    for copy in own_copies:
        copy.start()
    greet(counts)
    rows.begin(0)
    for part in range(5):
        mats.begin(part)
    most = incoming.shape[1] // ctx_count
    slot, tally = route_slots(routes_ref, chosen, most)
    slot_out[...] = jnp.broadcast_to(slot, slot_out.shape)
    tallies[rows.me] = jnp.broadcast_to(tally, (experts, BLOCK))
    counted = Exchange(
        ctx_count,
        1,
        most,
        (tally_send, tally_recv),
        lambda expert, peer: tallies.at[rows.me],
        lambda expert, peer: tallies.at[peer],
    )
    for ahead in range(1, ctx_count):
        counted.copy(0, ahead, True).start()
    grad_copy.wait()
    outgoing[...] = dot(placement_of(slot_out, experts * most), grad_rows[...]).astype(BF16)
    grads = Exchange(
        ctx_count,
        exp_dev,
        most,
        (grad_send, grad_recv),
        lambda expert, peer: outgoing.at[grads.rows(peer * exp_dev + expert), :],
        lambda expert, peer: incoming.at[expert, grads.rows(peer), :],
    )
    for copy in own_copies:
        copy.wait()
    for step in range(max(lines, pairs) - 1):
        if step < lines - 1:
            rows.advance(0, step)
        if step == 0:
            for expert in range(exp_dev):
                grads.start(expert)
        if step >= lines - 2 or step < pairs - 1:
            for part in range(5):
                if step < pairs - 1:
                    mats.advance(part, step)
    for part in range(5):
        mats.wait_cross(part)
    weights_copy = pltpu.make_async_copy(weights, weights_out, local_sems.at[0])
    weights_copy.start()
    small_copy = pltpu.make_async_copy(smalls, small_out, local_sems.at[1])
    small_copy.start()
    gain[...] = jnp.transpose(smalls[...].astype(F32))[lanes : lanes + 8, :]
    upper = rows.line // max(lines // 2, 1)

    def put(slot, block):
        place = pl.ds(pl.multiple_of(block * tokens, tokens), tokens)
        return pltpu.make_async_copy(ready.at[slot], qkv_out.at[place, :], out_sems.at[slot])

    def order(step):
        ahead, line = step // lines, step % lines
        line = line + upper * (lines - 1 - 2 * line)
        return line, ahead, line * across + (rows.column + across - ahead) % across

    def step_body(step, carry):
        line, ahead, block = order(step)
        slot = step % 2
        for skip in range(1, across):

            @pl.when(ahead == skip)
            def _():
                rows.cross_recv(0, line, skip).wait_recv()

        @pl.when(step >= 2)
        def _():
            put(slot, order(step - 2)[2]).wait()

        values = held[block].astype(F32)
        inv = lax.rsqrt(jnp.mean(values * values, axis=-1, keepdims=True) + epsilon)
        normed = (values * inv * gain[0:1, :]).astype(BF16)
        for place in range(3):
            ready[slot, :, place * width : (place + 1) * width] = dot(
                normed, weights[place]
            ).astype(BF16)
        put(slot, block).start()
        return carry

    lax.fori_loop(0, ctx_count, step_body, 0)
    for step in (ctx_count - 2, ctx_count - 1):
        put(step % 2, order(step)[2]).wait()
    write_plan(pairs_ref, plan_out, rows.me)
    turned = jnp.transpose(smalls[...].astype(F32))
    for hot_ref, base_out, sign in (
        (query_hot_ref, query_base_out, -1),
        (key_hot_ref, key_base_out, 1),
    ):
        table = dot(turned.astype(BF16), hot_ref[...])
        lane = lane_ids(BLOCK, SPAN)
        lane = jnp.where(lane < NEAR, lane, lane - SPAN)
        gap = lane if sign > 0 else BLOCK - lane
        last = jnp.max(jnp.where(gap == NEAR - 1, table, -jnp.inf), axis=1, keepdims=True)
        table = jnp.where(gap >= 0, table - last, MASKED)
        for pair in range(PAIRS):
            start = experts + 2 + 2 * pair
            base_out[pair] = jnp.zeros((8, SPAN), F32)
            base_out[pair, 0:2, :] = table[start : start + 2]
    counted.wait(0)
    lane = lane_ids(1, ctx_count * most)
    for expert in range(exp_dev):
        offset = jnp.zeros((1, 1), F32)
        target = jnp.full((1, ctx_count * most), capacity, jnp.int32)
        for source in range(ctx_count):
            count = tallies[source, pl.ds(rows.me * exp_dev + expert, 1), 0:1]
            inside = (lane >= source * most) & (
                lane < source * most + jnp.broadcast_to(count.astype(jnp.int32), lane.shape)
            )
            place = lane - source * most + jnp.broadcast_to(offset.astype(jnp.int32), lane.shape)
            target = jnp.where(inside, place, target)
            offset = offset + count
        target_out[expert : expert + 1, :] = target
    target_out[exp_dev:, :] = jnp.zeros_like(target_out[exp_dev:, :])
    for expert in range(exp_dev):
        grads.wait(expert)
        own_out[expert] = dot(cap_map(target_out, expert, capacity), incoming[expert]).astype(BF16)
    weights_copy.wait()
    small_copy.wait()
    counted.finish(0)
    for expert in range(exp_dev):
        grads.finish(expert)
    rows.finish()
    mats.finish()


def project(
    counts, capacity, experts, most, rows, weights, small, routes, pairs, query_hot, key_hot, grad
):
    tokens, width = rows.shape
    ctx_count, wsh_count = counts
    exp_dev = experts // ctx_count
    length = tokens * ctx_count
    lines, across = grid_of(ctx_count)
    vmem = pl.BlockSpec(memory_space=pltpu.VMEM)
    anywhere = pl.BlockSpec(memory_space=pl.ANY)
    smem = pl.BlockSpec(memory_space=pltpu.SMEM)
    return pl.pallas_call(
        functools.partial(project_kernel, counts, capacity),
        in_specs=[anywhere] * 6 + [vmem, smem, vmem, vmem, anywhere],
        out_specs=[anywhere] * 3 + [vmem] * 3 + [smem] + [vmem] * 2,
        out_shape=[
            jax.ShapeDtypeStruct((length, 3 * width), BF16),
            jax.ShapeDtypeStruct((4, width, width), BF16),
            jax.ShapeDtypeStruct((width, small.shape[1]), BF16),
            jax.ShapeDtypeStruct((8, tokens), jnp.int32),
            jax.ShapeDtypeStruct((8, ctx_count * most), jnp.int32),
            jax.ShapeDtypeStruct((exp_dev, capacity, width), BF16),
            jax.ShapeDtypeStruct((plan_size(2 * ctx_count),), jnp.int32),
            jax.ShapeDtypeStruct((PAIRS, 8, SPAN), F32),
            jax.ShapeDtypeStruct((PAIRS, 8, SPAN), F32),
        ],
        scratch_shapes=[
            pltpu.VMEM((ctx_count, tokens, width), BF16),
            pltpu.VMEM((4, width, width), BF16),
            pltpu.VMEM((width, small.shape[1]), BF16),
            pltpu.VMEM((8, width), F32),
            pltpu.VMEM((2, tokens, 3 * width), BF16),
            pltpu.VMEM((experts, tokens), F32),
            pltpu.VMEM((ctx_count, experts, BLOCK), F32),
            pltpu.VMEM((tokens, width), BF16),
            pltpu.VMEM((experts * most, width), BF16),
            pltpu.VMEM((exp_dev, ctx_count * most, width), BF16),
            *gather_sems(1, lines, across),
            *gather_sems(5, wsh_count // 2, 2),
            *exchange_sems(ctx_count, exp_dev),
            *exchange_sems(ctx_count, 1),
            pltpu.SemaphoreType.DMA((2,)),
            pltpu.SemaphoreType.DMA((9,)),
        ],
        compiler_params=pltpu.CompilerParams(
            collective_id=0, has_side_effects=True, vmem_limit_bytes=60 << 20
        ),
        name="project",
    )(rows, *weights, small, routes, pairs, query_hot, key_hot, grad)


def gelu_parts(values):
    slope, cubic = math.sqrt(2 / math.pi), 0.044715
    square = values * values
    bent = jnp.tanh(slope * (values + cubic * values * square))
    outer = 0.5 * (1.0 + bent)
    derivative = outer + 0.5 * values * (1.0 - bent * bent) * slope * (1.0 + 3 * cubic * square)
    return values * outer, derivative


def choose(rows, router, experts, expert):
    logits = dot(rows, router)
    lanes = lane_ids(rows.shape[0], router.shape[1])
    logits = jnp.where(lanes < experts, logits, MASKED)
    weights = jnp.exp(logits - jnp.max(logits, axis=-1, keepdims=True))
    probs = weights / jnp.sum(weights, axis=-1, keepdims=True)
    hot = (lanes == expert).astype(F32)
    return probs, hot, jnp.sum(probs * hot, axis=-1, keepdims=True)


def middle_kernel(
    counts,
    experts,
    spread_here,
    attn_ref,
    exact_ref,
    hidden_ref,
    grad_ref,
    weights_ref,
    w_in_ref,
    w_out_ref,
    own_g_ref,
    small_ref,
    slot_ref,
    target_ref,
    lse_ref,
    routes_ref,
    base_ref,
    plan_ref,
    qkv_ref,
    lse_all_ref,
    output_out,
    grad_mid_out,
    grad_heads_out,
    heads_all_out,
    stats_out,
    grad_wo_out,
    grad_router_out,
    grad_gain_out,
    dq_out,
    sums_out,
    grad_in_out,
    grad_out_out,
    qkv,
    lse_all,
    stacked_q,
    stacked_g,
    lse_rep,
    delta_rep,
    bias,
    near,
    attn,
    exact,
    heads,
    exact_blocks,
    hidden,
    grad,
    wo,
    w_in,
    w_out,
    resid,
    incoming,
    own_x,
    all_x,
    all_g,
    hid,
    du,
    parts,
    from_mate,
    from_far,
    returning,
    home,
    branch,
    stats,
    stage_in,
    stage_out,
    heads_stage,
    fetch_sems,
    out_sems,
    heads_sems,
    x_send,
    x_recv,
    g_send,
    g_recv,
    go_send,
    go_recv,
    back_send,
    back_recv,
    mate_send,
    mate_recv,
    far_send,
    far_recv,
    branch_send,
    branch_recv,
):
    ctx_count, wsh_count = counts
    tokens, width = hidden.shape
    exp_dev, capacity = own_x.shape[:2]
    most = incoming.shape[1] // ctx_count
    lines, across = grid_of(ctx_count)
    pairs = wsh_count // 2
    me = lax.axis_index("ctx")
    home_row = me if spread_here else 0
    sources = (
        (attn_ref, attn),
        (weights_ref.at[3], wo),
        (hidden_ref, hidden),
        (grad_ref, grad),
        (w_in_ref, w_in),
        (w_out_ref, w_out),
        (exact_ref, exact),
    )
    if spread_here:
        sources = sources + ((qkv_ref, qkv), (lse_all_ref, lse_all))
    fetches = [
        pltpu.make_async_copy(src, dst, fetch_sems.at[place])
        for place, (src, dst) in enumerate(sources)
    ]
    for fetch in fetches:
        fetch.start()
    views = [
        (lambda buffer, expert: lambda block: buffer.at[expert, block])(buffer, expert)
        for buffer in (all_g, all_x)
        for expert in range(exp_dev)
    ]
    gather_g = LineGather(
        "wsh",
        pairs,
        2,
        views[:exp_dev],
        [own_g_ref.at[expert] for expert in range(exp_dev)],
        (g_send, g_recv),
    )
    gather_x = LineGather(
        "wsh",
        pairs,
        2,
        views[exp_dev:],
        [own_x.at[expert] for expert in range(exp_dev)],
        (x_send, x_recv),
    )
    wsh_me, my_line, my_core = gather_x.me, gather_x.line, gather_x.column
    greet(counts)
    for expert in range(exp_dev):
        gather_g.begin(expert)
        all_g[expert, wsh_me] = own_g_ref[expert]

    small_t = jnp.transpose(small_ref[...].astype(F32))[experts : experts + 8, :]
    gain_two = small_t[1:2, :]
    router = jnp.where(
        lane_ids(width, small_ref.shape[1]) < experts, small_ref[...], jnp.zeros_like(small_ref)
    )
    for fetch in fetches[:3]:
        fetch.wait()
    resid[...] = hidden[...].astype(F32) + dot(attn[...], wo[...])
    inv_two = lax.rsqrt(jnp.mean(resid[...] * resid[...], axis=-1, keepdims=True) + epsilon)
    normed_two = (resid[...] * inv_two * gain_two).astype(BF16)
    units = w_in.shape[2]
    placement = placement_of(slot_ref, experts * most)
    returning[0] = dot(placement, normed_two).astype(BF16)
    forth = Exchange(
        ctx_count,
        exp_dev,
        most,
        (go_send, go_recv),
        lambda expert, peer: returning.at[0, forth.rows(peer * exp_dev + expert), :],
        lambda expert, peer: incoming.at[expert, forth.rows(peer), :],
    )
    forth.start(0)
    gate = choose(normed_two, router, experts, routes_ref[...])[2]
    for expert in range(exp_dev):
        for step in range(pairs - 1):
            gather_g.advance(expert, step)
    gather_g.finish()
    for fetch in fetches[3:]:
        fetch.wait()

    def mate_copy(array, expert, line):
        mine = line * 2 + 1 - my_core
        return pltpu.make_async_remote_copy(
            src_ref=parts.at[array, expert, mine],
            dst_ref=from_mate.at[array, expert, line],
            send_sem=mate_send.at[array, expert, line],
            recv_sem=mate_recv.at[array, expert, line],
            device_id={"wsh": my_line * 2 + 1 - my_core},
            device_id_type=pl.DeviceIdType.MESH,
        )

    def far_copy(array, expert, ahead):
        line = (my_line + ahead) % pairs
        return pltpu.make_async_remote_copy(
            src_ref=parts.at[array, expert, line * 2 + my_core],
            dst_ref=from_far.at[array, expert, ahead - 1],
            send_sem=far_send.at[array, expert, ahead - 1],
            recv_sem=far_recv.at[array, expert, ahead - 1],
            device_id={"wsh": line * 2 + my_core},
            device_id_type=pl.DeviceIdType.MESH,
        )

    def work(expert, ahead):
        line = (my_line + ahead) % pairs
        both = pl.ds(line * 2, 2)
        gather_x.cross_recv(expert, line, 1).wait_recv()
        gather_g.cross_recv(expert, line, 1).wait_recv()
        rows = all_x[expert, both].reshape(2 * capacity, width)
        active, slope = gelu_parts(dot(rows, w_in[expert]))
        active = active.astype(BF16)
        hid[expert, both] = active.reshape(2, capacity, units)
        part = dot(active, w_out[expert]).astype(BF16)
        parts[0, expert, both] = part.reshape(2, capacity, width)
        mate_copy(0, expert, line).start()
        share = choose(rows, router, experts, exp_dev * me + expert)[2]
        grads = all_g[expert, both].reshape(2 * capacity, width).astype(F32)
        grads = (share * grads).astype(BF16)
        all_g[expert, both] = grads.reshape(2, capacity, width)
        grad_u = (dot(grads, w_out[expert], 1, 1) * slope).astype(BF16)
        du[expert, both] = grad_u.reshape(2, capacity, units)
        part = dot(grad_u, w_in[expert], 1, 1).astype(BF16)
        parts[1, expert, both] = part.reshape(2, capacity, width)
        mate_copy(1, expert, line).start()

    def fold(expert, ahead):
        line = (my_line + ahead) % pairs
        for array in range(2):
            mate_copy(array, expert, line).wait_recv()
            if ahead > 0:
                both = parts[array, expert, line * 2 + my_core].astype(F32) + from_mate[
                    array, expert, line
                ].astype(F32)
                parts[array, expert, line * 2 + my_core] = both.astype(BF16)
                far_copy(array, expert, ahead).start()

    for expert in range(exp_dev):
        forth.wait(expert)
        if expert + 1 < exp_dev:
            forth.start(expert + 1)
        own_x[expert] = dot(cap_map(target_ref, expert, capacity), incoming[expert]).astype(BF16)
        gather_x.begin(expert)
        all_x[expert, wsh_me] = own_x[expert]
        work(expert, 0)
        for step in range(pairs - 1):
            gather_x.advance(expert, step)

        def others(ahead, carry):
            work(expert, ahead)
            return carry

        if pairs == 2:
            work(expert, 1)
        else:
            lax.fori_loop(1, pairs, others, 0)
        for ahead in range(1, pairs):
            fold(expert, ahead)

    back = [
        Exchange(
            ctx_count,
            exp_dev,
            most,
            (back_send.at[array], back_recv.at[array]),
            (
                lambda array: lambda expert, peer: returning.at[
                    array, forth.rows(expert * ctx_count + peer), :
                ]
            )(array),
            (
                lambda array: lambda expert, peer: home.at[
                    array, forth.rows(peer * exp_dev + expert), :
                ]
            )(array),
        )
        for array in range(2)
    ]
    for expert in range(exp_dev):
        forth.finish(expert)
    for expert in range(exp_dev):
        expert_rows = pl.ds(expert * ctx_count * most, ctx_count * most)
        fold(expert, 0)
        sums = []
        for array in range(2):
            line = my_line * 2 + my_core
            total = parts[array, expert, line].astype(F32) + from_mate[
                array, expert, my_line
            ].astype(F32)
            for ahead in range(1, pairs):
                far_copy(array, expert, ahead).wait_recv()
                total = total + from_far[array, expert, ahead - 1].astype(F32)
            sums.append(total)
        out_rows = sums[0].astype(BF16)
        rows = own_x[expert]
        probs, hot, share = choose(rows, router, experts, exp_dev * me + expert)
        slot_g = own_g_ref[expert].astype(F32)
        grad_gate = jnp.sum(slot_g * out_rows.astype(F32), axis=-1, keepdims=True)
        grad_logits = (share * grad_gate * (hot - probs)).astype(BF16)
        grad_rows = sums[1].astype(BF16).astype(F32) + dot(grad_logits, router, 1, 1)
        spread = cap_map(target_ref, expert, capacity)
        returning[1, expert_rows] = dot(spread, grad_rows.astype(BF16), 0, 0).astype(BF16)
        back[1].start(expert)
        returning[0, expert_rows] = dot(spread, out_rows, 0, 0).astype(BF16)
        if expert + 1 < exp_dev:
            back[0].start(expert)
        router_part = dot(grad_logits, rows, 0, 0)[:experts]
        if expert == 0:
            grad_router_out[...] = router_part
        else:
            grad_router_out[...] += router_part
    def in_copy(expert):
        return pltpu.make_async_copy(stage_in, grad_in_out.at[expert], out_sems.at[1])

    def out_copy(expert):
        return pltpu.make_async_copy(stage_out, grad_out_out.at[expert], out_sems.at[0])

    group = min(wsh_count, 4)

    def slot_sum(stage, left, right, expert):
        def part(turn):
            blocks = pl.ds(turn * group, group)
            return dot(
                left[expert, blocks].reshape(group * capacity, left.shape[3]),
                right[expert, blocks].reshape(group * capacity, right.shape[3]),
                0,
                0,
            )

        stage[...] = part(0)
        if wsh_count > group:

            def add(turn, carry):
                stage[...] += part(turn)
                return carry

            lax.fori_loop(1, wsh_count // group, add, 0)

    def grads_of(expert):
        if expert:
            out_copy(expert - 1).wait()
        slot_sum(stage_out, hid, all_g, expert)
        out_copy(expert).start()
        if expert:
            in_copy(expert - 1).wait()
        slot_sum(stage_in, all_x, du, expert)
        in_copy(expert).start()

    for expert in range(exp_dev):
        grads_of(expert)
    grad_up = grad[...].astype(F32)
    for expert in range(exp_dev):
        back[1].wait(expert)
    back[0].start(exp_dev - 1)
    grad_normed = dot(placement_of(slot_ref, experts * most), home[1], 0, 0)
    scaled = grad_normed * gain_two
    mean = jnp.mean(scaled * resid[...], axis=-1, keepdims=True)
    gain_part = jnp.sum(grad_normed * resid[...] * inv_two, axis=0, keepdims=True)
    grad_gain_out[...] = jnp.broadcast_to(gain_part, grad_gain_out.shape)
    grad_mid = grad_up + inv_two * scaled - resid[...] * inv_two * inv_two * inv_two * mean
    grad_mid_out[...] = grad_mid
    branch[home_row] = grad_mid.astype(BF16)

    gather_d = LineGather(
        "ctx",
        lines,
        across,
        [lambda block: branch.at[block], lambda block: stats.at[block]],
        [branch.at[me], stats.at[me]],
        (branch_send, branch_recv),
    )
    if spread_here:
        gather_d.begin(0)
    grad_heads = dot(branch[home_row], wo[...], 1, 1).astype(BF16)
    grad_heads_out[...] = grad_heads
    if spread_here:
        for own in range(2):
            heads[own] = grad_heads[own * BLOCK : (own + 1) * BLOCK]
            exact_blocks[own] = exact[own * BLOCK : (own + 1) * BLOCK, :]
    product = grad_heads.astype(F32) * exact[...]
    head_of = lax.broadcasted_iota(jnp.int32, (width, BLOCK), 0) // HEAD_DIM
    head_hot = (head_of == lane_ids(width, BLOCK)).astype(F32)
    delta = jnp.transpose(
        lax.dot_general(
            product, head_hot, (((1,), (0,)), ((), ())), precision=HIGH, preferred_element_type=F32
        )
    )
    for pair in range(PAIRS):
        stats[home_row, pair] = lse_ref[pair]
        stats[home_row, pair, 2:4, :] = delta[2 * pair : 2 * pair + 2, :]
    if spread_here:
        gather_d.begin(1)

    grad_wo_out[...] = dot(attn[...], branch[home_row], 0, 0).astype(BF16)

    plan_from = plan_start(2 * ctx_count)
    half = ctx_count

    def query_pair(pair, carry):
        pair_lanes = pl.ds(pl.multiple_of(pair * BLOCK, BLOCK), BLOCK)

        def tile(part, step):
            lanes = pl.ds(pl.multiple_of(part * width + pair * BLOCK, BLOCK), BLOCK)
            return qkv[plan_ref[plan_from + 4 + step], :, lanes]

        bias[...] = near_bias(base_ref, pair)
        for place in range(2):
            own = plan_ref[plan_from + place]
            stacked_q[place] = stack_heads(tile(0, 0 if place else half + 1))
            grads = stack_heads(heads[own, :, pair_lanes])
            stacked_g[place] = grads
            own_exact = exact_blocks[own, :, pair_lanes]
            product = grads.astype(F32) * jnp.concatenate([own_exact, own_exact], axis=0)
            delta_rep[place] = jnp.broadcast_to(
                jnp.sum(product, axis=-1, keepdims=True), (2 * BLOCK, BLOCK)
            )
            lse_rep[place] = lse_all[pair, own]

        def score_grads(place, step, extra):
            keys = tile(1, step)
            scores = dot(stacked_q[place], keys, 1, 1)
            if extra is not None:
                scores = scores + extra
            weights = jnp.exp(scores - lse_rep[place])
            grad_s = weights * (dot(stacked_g[place], tile(2, step), 1, 1) - delta_rep[place])
            return grad_s, dot(grad_s.astype(BF16), keys)

        diagonal, big = score_grads(1, 0, bias[:, BLOCK:])
        beside, more = score_grads(1, 1, bias[:, :BLOCK])
        big = big + more
        far = jnp.zeros((2 * BLOCK, BLOCK), F32)
        for step in range(2, half + 1):
            grad_s, more = score_grads(1, step, None)
            far, big = far + grad_s, big + more
        grad_s, small_part = score_grads(0, half + 1, bias[:, BLOCK:])
        near[:, BLOCK:] = diagonal + grad_s
        for step in range(half + 2, 2 * half + 1):
            place = plan_ref[plan_from + 4 + 2 * half + 1 + step]
            later = place.astype(F32)
            sooner = 1.0 - later
            extra = None
            if step == half + 2:
                extra = bias[:, :BLOCK] * sooner
            grad_s, more = score_grads(place, step, extra)
            if step == half + 2:
                near[:, :BLOCK] = beside + grad_s * sooner
                far = far + grad_s * later
            else:
                far = far + grad_s
            big = big + more * later
            small_part = small_part + more * sooner
        second = plan_ref[plan_from].astype(F32)
        small_part, big = merge_heads(small_part), merge_heads(big)
        first = 1.0 - second
        dq_out[:BLOCK, pair_lanes] = (small_part * first + big * second).astype(BF16)
        dq_out[BLOCK:, pair_lanes] = (big * first + small_part * second).astype(BF16)
        put_sums(sums_out, pair, near, far)
        return carry

    def query_pairs(turn):
        share = PAIRS // (lines - 1)
        lax.fori_loop(turn * share, (turn + 1) * share, query_pair, 0)

    for step in range(lines - 1):
        if spread_here:
            for part in range(2):
                gather_d.advance(part, step)
        if spread_here:
            query_pairs(step)
    for expert in range(exp_dev):
        back[0].wait(expert)
    token_out = dot(placement_of(slot_ref, experts * most), home[0], 0, 0)
    output_out[...] = (resid[...] + gate * token_out).astype(BF16)
    upper = gather_d.line // max(lines // 2, 1)

    def order(step):
        ahead, line = step // lines, step % lines
        line = line + upper * (lines - 1 - 2 * line)
        return line, ahead, line * across + (gather_d.column + across - ahead) % across

    def put(slot, block):
        place = pl.ds(pl.multiple_of(block * tokens, tokens), tokens)
        return pltpu.make_async_copy(
            heads_stage.at[slot], heads_all_out.at[place, :], heads_sems.at[slot]
        )

    def heads_step(step, carry):
        line, ahead, block = order(step)
        slot = step % 2
        for skip in range(1, across):

            @pl.when(ahead == skip)
            def _():
                gather_d.cross_recv(0, line, skip).wait_recv()
                gather_d.cross_recv(1, line, skip).wait_recv()

        @pl.when(step >= 2)
        def _():
            put(slot, order(step - 2)[2]).wait()

        heads_stage[slot] = dot(branch[block], wo[...], 1, 1).astype(BF16)
        put(slot, block).start()
        return carry

    if spread_here:
        lax.fori_loop(0, ctx_count, heads_step, 0)
    stats_copy = pltpu.make_async_copy(stats, stats_out, fetch_sems.at[0])
    stats_copy.start()
    if spread_here:
        for step in (ctx_count - 2, ctx_count - 1):
            put(step % 2, order(step)[2]).wait()
    else:
        heads_stage[0] = branch[0]
        own_branch = pltpu.make_async_copy(heads_stage.at[0], heads_all_out, heads_sems.at[0])
        own_branch.start()
        own_branch.wait()
    out_copy(exp_dev - 1).wait()
    in_copy(exp_dev - 1).wait()
    stats_copy.wait()
    for expert in range(exp_dev):
        for array in range(2):
            back[array].finish(expert)
            for line in range(pairs):
                mate_copy(array, expert, line).wait_send()
            for ahead in range(1, pairs):
                far_copy(array, expert, ahead).wait_send()
    gather_x.finish()
    if spread_here:
        gather_d.finish()


def middle(
    counts,
    experts,
    attn,
    exact,
    hidden,
    grad,
    weights,
    w_in,
    w_out,
    own_g,
    small,
    slots,
    targets,
    lse_rows,
    routes,
    base,
    plan,
    qkv,
    lse,
):
    ctx_count, wsh_count = counts
    tokens, width = hidden.shape
    exp_dev, capacity = own_g.shape[:2]
    units = w_in.shape[2]
    slot_count = targets.shape[1]
    all_slots = experts * (slot_count // ctx_count)
    lines, across = grid_of(ctx_count)
    pairs = wsh_count // 2
    vmem = pl.BlockSpec(memory_space=pltpu.VMEM)
    anywhere = pl.BlockSpec(memory_space=pl.ANY)
    slot_rows = (exp_dev, wsh_count, capacity)
    spread_here = wsh_count <= 4
    held = ctx_count if spread_here else 1
    score_rows = NEAR if spread_here else 16
    return pl.pallas_call(
        functools.partial(middle_kernel, counts, experts, spread_here),
        in_specs=[anywhere] * 7
        + [vmem] * 7
        + [pl.BlockSpec(memory_space=pltpu.SMEM)]
        + [anywhere] * 2,
        out_specs=[vmem] * 3 + [anywhere] * 2 + [vmem] * 5 + [anywhere] * 2,
        out_shape=[
            jax.ShapeDtypeStruct((tokens, width), BF16),
            jax.ShapeDtypeStruct((tokens, width), F32),
            jax.ShapeDtypeStruct((tokens, width), BF16),
            jax.ShapeDtypeStruct((tokens * held, width), BF16),
            jax.ShapeDtypeStruct((held, PAIRS, 8, tokens), F32),
            jax.ShapeDtypeStruct((width, width), BF16),
            jax.ShapeDtypeStruct((experts, width), F32),
            jax.ShapeDtypeStruct((8, width), F32),
            jax.ShapeDtypeStruct((tokens if spread_here else 16, width), BF16),
            jax.ShapeDtypeStruct((PAIRS, 8, SPAN), F32),
            jax.ShapeDtypeStruct((exp_dev, width, units), F32),
            jax.ShapeDtypeStruct((exp_dev, units, width), F32),
        ],
        scratch_shapes=[
            pltpu.VMEM(qkv.shape if spread_here else (1, 16, BLOCK), BF16),
            pltpu.VMEM(lse.shape if spread_here else (1, 2, 8, BLOCK), F32),
            pltpu.VMEM((2, score_rows, BLOCK), BF16),
            pltpu.VMEM((2, score_rows, BLOCK), BF16),
            pltpu.VMEM((2, score_rows, BLOCK), F32),
            pltpu.VMEM((2, score_rows, BLOCK), F32),
            pltpu.VMEM((score_rows, NEAR), F32),
            pltpu.VMEM((score_rows, NEAR), F32),
            pltpu.VMEM((tokens, width), BF16),
            pltpu.VMEM((tokens, width), F32),
            pltpu.VMEM((2, BLOCK if spread_here else 16, width), BF16),
            pltpu.VMEM((2, BLOCK if spread_here else 8, width), F32),
            pltpu.VMEM((tokens, width), BF16),
            pltpu.VMEM((tokens, width), BF16),
            pltpu.VMEM((width, width), BF16),
            pltpu.VMEM(w_in.shape, BF16),
            pltpu.VMEM(w_out.shape, BF16),
            pltpu.VMEM((tokens, width), F32),
            pltpu.VMEM((exp_dev, slot_count, width), BF16),
            pltpu.VMEM((exp_dev, capacity, width), BF16),
            pltpu.VMEM((*slot_rows, width), BF16),
            pltpu.VMEM((*slot_rows, width), BF16),
            pltpu.VMEM((*slot_rows, units), BF16),
            pltpu.VMEM((*slot_rows, units), BF16),
            pltpu.VMEM((2, *slot_rows, width), BF16),
            pltpu.VMEM((2, exp_dev, pairs, capacity, width), BF16),
            pltpu.VMEM((2, exp_dev, max(pairs - 1, 1), capacity, width), BF16),
            pltpu.VMEM((2, all_slots, width), BF16),
            pltpu.VMEM((2, all_slots, width), BF16),
            pltpu.VMEM((held, tokens, width), BF16),
            pltpu.VMEM((held, PAIRS, 8, tokens), F32),
            pltpu.VMEM((width, units), F32),
            pltpu.VMEM((units, width), F32),
            pltpu.VMEM((2, tokens, width), BF16),
            pltpu.SemaphoreType.DMA((9,)),
            pltpu.SemaphoreType.DMA((2,)),
            pltpu.SemaphoreType.DMA((2,)),
            *gather_sems(exp_dev, pairs, 2),
            *gather_sems(exp_dev, pairs, 2),
            *exchange_sems(ctx_count, exp_dev),
            pltpu.SemaphoreType.DMA((2, exp_dev, ctx_count - 1)),
            pltpu.SemaphoreType.DMA((2, exp_dev, ctx_count - 1)),
            pltpu.SemaphoreType.DMA((2, exp_dev, pairs)),
            pltpu.SemaphoreType.DMA((2, exp_dev, pairs)),
            pltpu.SemaphoreType.DMA((2, exp_dev, max(pairs - 1, 1))),
            pltpu.SemaphoreType.DMA((2, exp_dev, max(pairs - 1, 1))),
            *gather_sems(2, lines, across),
        ],
        compiler_params=pltpu.CompilerParams(
            collective_id=1, has_side_effects=True, vmem_limit_bytes=(60 if spread_here else 62) << 20
        ),
        name="middle",
    )(
        attn,
        exact,
        hidden,
        grad,
        weights,
        w_in,
        w_out,
        own_g,
        small,
        slots,
        targets,
        lse_rows,
        routes,
        base,
        plan,
        qkv,
        lse,
    )


class Tiles:
    def __init__(self, plan_ref, blocks, keys):
        self.plan, self.blocks, self.half = plan_ref, blocks, blocks // 2
        self.start = plan_start(blocks)
        self.rows_from = self.start + 4 + (2 * (blocks + 1) if keys else 0)
        self.keys = keys
        self.count = blocks + 1

    def own(self, place):
        return self.plan[self.start + (1 - place if self.keys else place)]

    def row(self, step):
        return self.plan[self.rows_from + step]

    def place(self, step):
        if step <= self.half:
            return 1
        if step == self.half + 1:
            return 0
        return self.plan[self.start + 4 + self.blocks + 1 + step]

    def groups(self):
        found, step = [], 0
        while step <= self.half:
            size = 2 if step + 1 <= self.half else 1
            found.append((step, size))
            step += size
        return found + [(step, 1) for step in range(self.half + 1, self.count)]


def span(step, size=1):
    return slice(step * BLOCK, (step + size) * BLOCK)


def only(place, wanted, value):
    if isinstance(place, int):
        return value if place == wanted else jnp.zeros_like(value)
    return jnp.where(place == wanted, value, jnp.zeros_like(value))


def order_bias(bias, step, size, place, half):
    if step == 0:
        return bias[:, : size * BLOCK]
    if step == half + 1:
        return bias[:, :BLOCK]
    if step == half + 2:
        return jnp.where(place == 0, bias[:, BLOCK:], 0.0)
    return None


def forward_pair(tiles, load, bias, stacked, keys, scores, tops, totals, weights, values, others):
    half, count = tiles.half, tiles.count
    lowest = jnp.full((NEAR, BLOCK), MASKED, F32)
    for place in range(2):
        stacked[place] = stack_heads(load(0, None, tiles.own(place)))
    for step in range(count):
        row = tiles.row(step)
        keys[span(step), :] = load(1, row, None)
        tile, place = load(2, row, None), tiles.place(step)
        values[span(step), :] = only(place, 1, tile)
        if step > half:
            others[span(step - half - 1), :] = only(place, 0, tile)
    best = [lowest, lowest]
    for step, size in tiles.groups():
        place = tiles.place(step)
        part = dot(stacked[place], keys[span(step, size), :], 1, 1)
        extra = order_bias(bias, step, size, place, half)
        if extra is not None:
            part = part + extra
        scores[:, span(step, size)] = part
        part = fold_lanes(part, jnp.maximum) if size == 2 else part
        for wanted in range(2):
            if isinstance(place, int):
                if place == wanted:
                    best[wanted] = jnp.maximum(best[wanted], part)
            else:
                best[wanted] = jnp.maximum(best[wanted], jnp.where(place == wanted, part, MASKED))
    for wanted in range(2):
        top = jnp.max(best[wanted], axis=-1, keepdims=True)
        tops[wanted] = jnp.broadcast_to(top, (NEAR, BLOCK))
    total = [jnp.zeros((NEAR, BLOCK), F32)] * 2
    for step in range(count):
        place = tiles.place(step)
        part = jnp.exp(scores[:, span(step)] - tops[place])
        high = part.astype(BF16)
        weights[:NEAR, span(step)] = high
        weights[NEAR:, span(step)] = (part - high.astype(F32)).astype(BF16)
        for wanted in range(2):
            if not isinstance(place, int) or place == wanted:
                total[wanted] = total[wanted] + only(place, wanted, part)
    results = []
    for wanted in range(2):
        whole = jnp.sum(total[wanted], axis=-1, keepdims=True)
        if wanted:
            summed = dot(weights[...], values[...])
        else:
            summed = dot(weights[:, span(half + 1, count - half - 1)], others[...])
        main = summed[:NEAR] / whole
        exact = main + summed[NEAR:] / whole
        totals[wanted] = tops[wanted] + jnp.log(jnp.broadcast_to(whole, (NEAR, BLOCK)))
        results.append((merge_heads(main).astype(BF16), merge_heads(exact)))
    return results


def in_order(tiles, pair):
    first = tiles.own(0) == 0
    return jnp.where(first, pair[0], pair[1]), jnp.where(first, pair[1], pair[0])


def forward_kernel(
    plan_ref, q_ref, k_ref, v_ref, base_ref, out_ref, exact_ref, lse_ref, row_ref, bias, *scratch
):
    blocks = q_ref.shape[0] // BLOCK
    tiles = Tiles(plan_ref, blocks, False)
    refs = (q_ref, k_ref, v_ref)
    me = lax.axis_index("ctx")
    near = near_bias(base_ref)
    bias[...] = jnp.concatenate([near[:, BLOCK:], near[:, :BLOCK]], axis=1)
    totals = scratch[4]

    def load(part, row, own):
        return refs[part][rows_at(2 * me + own if row is None else row), :]

    results = forward_pair(tiles, load, bias, *scratch)
    main = in_order(tiles, [result[0] for result in results])
    exact = in_order(tiles, [result[1] for result in results])
    lse = in_order(tiles, [totals[0], totals[1]])
    for own in range(2):
        rows = pl.ds(own * BLOCK, BLOCK)
        out_ref[rows, :] = main[own]
        exact_ref[rows, :] = exact[own]
        lse_ref[0, own] = lse[own]
        turned = jnp.transpose(lse[own])
        for head in range(2):
            row_ref[0, head : head + 1, own * BLOCK : (own + 1) * BLOCK] = turned[
                :1, head * BLOCK : (head + 1) * BLOCK
            ]
    row_ref[0, 2:8, :] = jnp.zeros((6, NEAR), F32)


def forward_scratch(blocks):
    count = blocks + 1
    rest = count - blocks // 2 - 1
    return [
        pltpu.VMEM((2, NEAR, BLOCK), BF16),
        pltpu.VMEM((count * BLOCK, BLOCK), BF16),
        pltpu.VMEM((NEAR, count * BLOCK), F32),
        pltpu.VMEM((2, NEAR, BLOCK), F32),
        pltpu.VMEM((2, NEAR, BLOCK), F32),
        pltpu.VMEM((2 * NEAR, count * BLOCK), BF16),
        pltpu.VMEM((count * BLOCK, BLOCK), BF16),
        pltpu.VMEM((rest * BLOCK, BLOCK), BF16),
    ]


def pair_specs(rows, width):
    pairs = width // BLOCK

    def column(offset):
        return pl.BlockSpec((rows, BLOCK), lambda pair, plan: (0, offset + pair))

    return [column(0), column(pairs), column(2 * pairs)]


def attend_forward(plan, qkv, base, width):
    rows = qkv.shape[0]
    own = pl.BlockSpec((NEAR, BLOCK), lambda pair, plan: (0, pair))
    return pl.pallas_call(
        forward_kernel,
        grid_spec=pltpu.PrefetchScalarGridSpec(
            num_scalar_prefetch=1,
            grid=(PAIRS,),
            in_specs=pair_specs(rows, width)
            + [pl.BlockSpec((1, 8, SPAN), lambda pair, plan: (pair, 0, 0))],
            out_specs=[
                own,
                own,
                pl.BlockSpec((1, 2, NEAR, BLOCK), lambda pair, plan: (pair, 0, 0, 0)),
                pl.BlockSpec((1, 8, NEAR), lambda pair, plan: (pair, 0, 0)),
            ],
            scratch_shapes=[pltpu.VMEM((NEAR, NEAR), F32), *forward_scratch(rows // BLOCK)],
        ),
        out_shape=[
            jax.ShapeDtypeStruct((NEAR, width), BF16),
            jax.ShapeDtypeStruct((NEAR, width), F32),
            jax.ShapeDtypeStruct((PAIRS, 2, NEAR, BLOCK), F32),
            jax.ShapeDtypeStruct((PAIRS, 8, NEAR), F32),
        ],
        compiler_params=pltpu.CompilerParams(vmem_limit_bytes=60 << 20),
        name="attend_forward",
    )(plan, qkv, qkv, qkv, base)


def put_sums(sums_ref, place, near_ref, far):
    row_ids = lax.broadcasted_iota(jnp.int32, (BLOCK, SPAN), 0)
    for head in range(2):
        part = near_ref[head * BLOCK : (head + 1) * BLOCK, :]
        part = jnp.concatenate([part, jnp.zeros((BLOCK, BLOCK), F32)], axis=1)
        for bit in range(BLOCK.bit_length() - 1):
            moved = pltpu.roll(part, SPAN - (1 << bit), 1)
            part = jnp.where((row_ids >> bit) & 1 == 1, moved, part)
        sums_ref[place, head : head + 1, :] = jnp.sum(part, axis=0, keepdims=True)
        far_part = jnp.sum(far[head * BLOCK : (head + 1) * BLOCK], axis=0, keepdims=True)
        sums_ref[place, 2 + head : 3 + head, :] = jnp.concatenate(
            [far_part, jnp.zeros((1, NEAR), F32)], axis=1
        )
    sums_ref[place, 4:8, :] = jnp.zeros((4, SPAN), F32)


def query_kernel(
    plan_ref, q_ref, k_ref, v_ref, base_ref, do_ref, exact_ref, lse_ref, dq_ref, sums_ref, bias_ref, near_ref
):
    bias_ref[...] = near_bias(base_ref)
    lanes = lane_ids(2 * BLOCK, NEAR)
    far = jnp.zeros((2 * BLOCK, BLOCK), F32)
    for own in range(2):
        block = plan_ref[own]
        rows = pl.ds(own * BLOCK, BLOCK)
        stacked = stack_heads(q_ref[rows_at(plan_ref[SOURCE + 1 + block]), :])
        grads = stack_heads(do_ref[rows, :])
        exact = exact_ref[rows, :]
        product = grads.astype(F32) * jnp.concatenate([exact, exact], axis=0)
        delta = jnp.sum(product, axis=-1, keepdims=True)
        lse = lse_ref[0, own][:, :1]

        def grad_scores(scores, start):
            weights = jnp.exp(scores - lse)
            return weights * (dot(grads, two_tiles(v_ref, plan_ref, start), 1, 1) - delta)

        scores = dot(stacked, two_tiles(k_ref, plan_ref, block), 1, 1) + bias_ref[...]
        scores = jnp.where(lanes + block * BLOCK < BLOCK, MASKED, scores)
        near = grad_scores(scores, block)
        if own == 0:
            near_ref[...] = near
        else:
            near_ref[...] += near

        def step(chunk, carry):
            grad_q, far = carry
            start = block - 2 * chunk
            keys = two_tiles(k_ref, plan_ref, start)
            part = dot(stacked, keys, 1, 1)
            part = jnp.where(lanes + start * BLOCK < BLOCK, MASKED, part)
            grad_s = grad_scores(part, start)
            return (grad_q + dot(grad_s.astype(BF16), keys), far + fold_lanes(grad_s, jnp.add))

        grad_q, far = lax.fori_loop(
            1,
            jnp.maximum(block, 1) // 2 + 1,
            step,
            (dot(near.astype(BF16), two_tiles(k_ref, plan_ref, block)), far),
        )
        dq_ref[rows, :] = merge_heads(grad_q).astype(BF16)
    put_sums(sums_ref, 0, near_ref, far)


def attend_queries(plan, qkv, base, grad_out, exact, lse):
    rows, width = qkv.shape[0], grad_out.shape[1]
    own = pl.BlockSpec((NEAR, BLOCK), lambda pair, plan: (0, pair))
    row_spec = pl.BlockSpec((1, 8, SPAN), lambda pair, plan: (pair, 0, 0))
    return pl.pallas_call(
        query_kernel,
        grid_spec=pltpu.PrefetchScalarGridSpec(
            num_scalar_prefetch=1,
            grid=(PAIRS,),
            in_specs=pair_specs(rows, width)
            + [
                row_spec,
                own,
                own,
                pl.BlockSpec((1, 2, NEAR, BLOCK), lambda pair, plan: (pair, 0, 0, 0)),
            ],
            out_specs=[own, row_spec],
            scratch_shapes=[pltpu.VMEM((NEAR, NEAR), F32), pltpu.VMEM((NEAR, NEAR), F32)],
        ),
        out_shape=[
            jax.ShapeDtypeStruct((NEAR, width), BF16),
            jax.ShapeDtypeStruct((PAIRS, 8, SPAN), F32),
        ],
        compiler_params=pltpu.CompilerParams(vmem_limit_bytes=60 << 20),
        name="attend_queries",
    )(plan, qkv, qkv, qkv, base, grad_out, exact, lse)


def key_pair(tiles, load, stat, bias, mine, queries, grads, rest_q, rest_g, stats, grad_s, weights):
    half, count = tiles.half, tiles.count
    for place in range(2):
        for part in range(2):
            mine[part, place] = stack_heads(load(1 + part, None, tiles.own(place)))
    for step in range(count):
        row, place = tiles.row(step), tiles.place(step)
        for part, whole, rest in ((0, queries, rest_q), (3, grads, rest_g)):
            tile = load(part, row, None)
            whole[0, span(step), :] = tile
            whole[1, span(step), :] = only(place, 1, tile)
            if step > half:
                rest[span(step - half - 1), :] = only(place, 0, tile)
        stats[:, span(step)] = stat(row)
    for step, size in tiles.groups():
        place = tiles.place(step)
        scores = dot(mine[0, place], queries[0, span(step, size), :], 1, 1)
        extra = order_bias(bias, step, size, place, half)
        if extra is not None:
            scores = scores + extra
        push = dot(mine[1, place], grads[0, span(step, size), :], 1, 1)
        for head in range(2):
            rows = slice(head * BLOCK, (head + 1) * BLOCK)
            part = jnp.exp(scores[rows] - stats[head : head + 1, span(step, size)])
            weights[rows, span(step, size)] = part.astype(BF16)
            part = part * (push[rows] - stats[2 + head : 3 + head, span(step, size)])
            grad_s[rows, span(step, size)] = part.astype(BF16)
    tail = span(half + 1, count - half - 1)
    grad_k = (dot(grad_s[:, tail], rest_q[...]), dot(grad_s[...], queries[1]))
    grad_v = (dot(weights[:, tail], rest_g[...]), dot(weights[...], grads[1]))
    return [
        [merge_heads(part).astype(BF16) for part in grad] for grad in (grad_k, grad_v)
    ]


def key_kernel(plan_ref, q_ref, k_ref, v_ref, base_ref, do_ref, stats_ref, *refs):
    passed = (len(refs) - 11) // 2
    passed_in, outs, passed_out = (
        refs[:passed],
        refs[passed : passed + 2],
        refs[passed + 2 : 2 * passed + 2],
    )
    bias, *scratch = refs[2 * passed + 2 :]
    for src, dst in zip(passed_in, passed_out):
        dst[...] = src[...]
    blocks = q_ref.shape[0] // BLOCK
    tiles = Tiles(plan_ref, blocks, True)
    tile_refs = (q_ref, k_ref, v_ref, do_ref)
    me = lax.axis_index("ctx")
    bias[...] = near_bias(base_ref)

    def load(part, row, own):
        return tile_refs[part][rows_at(2 * me + own if row is None else row), :]

    def stat(row):
        return stats_ref[row // 2, 0, :, rows_at(row % 2)]

    for out, grad in zip(outs, key_pair(tiles, load, stat, bias, *scratch)):
        for own, part in enumerate(in_order(tiles, grad)):
            out[own * BLOCK : (own + 1) * BLOCK, :] = part


def key_scratch(blocks):
    count = blocks + 1
    rest = count - blocks // 2 - 1
    return [
        pltpu.VMEM((2, 2, NEAR, BLOCK), BF16),
        pltpu.VMEM((2, count * BLOCK, BLOCK), BF16),
        pltpu.VMEM((2, count * BLOCK, BLOCK), BF16),
        pltpu.VMEM((rest * BLOCK, BLOCK), BF16),
        pltpu.VMEM((rest * BLOCK, BLOCK), BF16),
        pltpu.VMEM((8, count * BLOCK), F32),
        pltpu.VMEM((NEAR, count * BLOCK), BF16),
        pltpu.VMEM((NEAR, count * BLOCK), BF16),
    ]


def attend_keys(plan, qkv, base, grad_out, stats, passed):
    rows, width = grad_out.shape
    own = pl.BlockSpec((NEAR, BLOCK), lambda pair, plan: (0, pair))
    pieces = [own] + [
        pl.BlockSpec(
            (array.shape[0], array.shape[1] // PAIRS, array.shape[2]), lambda pair, plan: (0, pair, 0)
        )
        for array in passed[1:]
    ]
    return pl.pallas_call(
        key_kernel,
        grid_spec=pltpu.PrefetchScalarGridSpec(
            num_scalar_prefetch=1,
            grid=(PAIRS,),
            in_specs=pair_specs(rows, width)
            + [
                pl.BlockSpec((1, 8, SPAN), lambda pair, plan: (pair, 0, 0)),
                pl.BlockSpec((rows, BLOCK), lambda pair, plan: (0, pair)),
                pl.BlockSpec(
                    (rows // NEAR, 1, 8, NEAR), lambda pair, plan: (0, pair, 0, 0)
                ),
            ]
            + pieces,
            out_specs=[own, own] + pieces,
            scratch_shapes=[pltpu.VMEM((NEAR, NEAR), F32), *key_scratch(rows // BLOCK)],
        ),
        out_shape=[jax.ShapeDtypeStruct((NEAR, width), BF16)] * 2
        + [jax.ShapeDtypeStruct(array.shape, array.dtype) for array in passed],
        compiler_params=pltpu.CompilerParams(vmem_limit_bytes=60 << 20),
        name="attend_keys",
    )(plan, qkv, qkv, qkv, base, grad_out, stats, *passed)


BITS = {"core": ("wsh", 1), "x": ("wsh", 2), "y": ("ctx", 1), "near": ("ctx", 2), "far": ("ctx", 4)}
ORDERS = (
    ("core", "x", "near", "y", "far"),
    ("core", "x", "y", "near", "far"),
    ("core", "y", "near", "x", "far"),
    ("core", "near", "y", "x", "far"),
)


def halved_shapes(order, share, width):
    shapes, blocks, rows, columns = [], 4, share, width
    for name in order:
        if name in ("core", "x"):
            blocks //= 2
        elif name == "y":
            columns //= 2
        else:
            rows //= 2
        shapes.append((blocks, rows, columns))
    return shapes


def partner(name):
    axis, bit = BITS[name]
    me = lax.axis_index(axis)
    side = (me // bit) % 2
    return axis, me + bit * (1 - 2 * side), side


def tail_kernel(
    experts,
    dq_ref,
    dk_ref,
    dv_ref,
    hidden_ref,
    grad_mid_ref,
    weights_ref,
    grad_wo_ref,
    small_ref,
    router_ref,
    gain_ref,
    sums_ref,
    hot_ref,
    input_grad_out,
    shares_out,
    router_out,
    gains_out,
    table_out,
    weights,
    hidden,
    grad_mid,
    grad_wo,
    total,
    gathered,
    pack,
    pack_recv,
    *rest,
):
    steps = len(BITS)
    sends = [rest[matrix * steps : (matrix + 1) * steps] for matrix in range(4)]
    rest = rest[4 * steps :]
    recvs = [rest[matrix * steps : (matrix + 1) * steps] for matrix in range(4)]
    fetch_sems, half_send, half_recv, whole_send, whole_recv, pack_send, pack_sem = rest[4 * steps :]
    tokens, width = dq_ref.shape
    share = total.shape[2]
    sources = (
        (hidden_ref, hidden),
        (grad_wo_ref, grad_wo),
        (weights_ref.at[pl.ds(0, 3)], weights),
        (grad_mid_ref, grad_mid),
    )
    fetches = [
        pltpu.make_async_copy(src, dst, fetch_sems.at[place])
        for place, (src, dst) in enumerate(sources)
    ]
    for fetch in fetches:
        fetch.start()
    barrier = pltpu.get_barrier_semaphore()
    for name in BITS:
        axis, peer, side = partner(name)
        pl.semaphore_signal(
            barrier, inc=1, device_id={axis: peer}, device_id_type=pl.DeviceIdType.MESH
        )
    pl.semaphore_wait(barrier, steps)

    def remote(source, target, send, recv, name):
        axis, peer, side = partner(name)
        return pltpu.make_async_remote_copy(
            src_ref=source,
            dst_ref=target,
            send_sem=send,
            recv_sem=recv,
            device_id={axis: peer},
            device_id_type=pl.DeviceIdType.MESH,
        )

    regions = []
    for order in ORDERS:
        blocks, row, column, kept = [0, 1, 2, 3], 0, 0, []
        rows, columns = share, width
        for name in order:
            side = partner(name)[2]
            if name == "core":
                pair = [(line * 2 + side, line * 2 + 1 - side) for line in range(2)]
                keep = ([a for a, b in pair], row, column)
                sent = ([b for a, b in pair], row, column)
            elif name == "x":
                core = partner("core")[2]
                keep = ([side * 2 + core], row, column)
                sent = ([(1 - side) * 2 + core], row, column)
            elif name == "y":
                columns //= 2
                keep = (blocks, row, column + side * columns)
                sent = (blocks, row, column + (1 - side) * columns)
            else:
                rows //= 2
                keep = (blocks, row + side * rows, column)
                sent = (blocks, row + (1 - side) * rows, column)
            blocks, row, column = keep
            kept.append((keep, sent))
        regions.append(kept)

    def spans(matrix, step, region):
        shape = sends[matrix][step].shape
        blocks, row, column = region
        row_part = pl.ds(row if isinstance(row, int) else pl.multiple_of(row, 16), shape[1])
        column_part = pl.ds(
            column if isinstance(column, int) else pl.multiple_of(column, BLOCK), shape[2]
        )
        return blocks, row_part, column_part

    def half_copy(matrix, step):
        return remote(
            sends[matrix][step],
            recvs[matrix][step],
            half_send.at[matrix, step],
            half_recv.at[matrix, step],
            ORDERS[matrix][step],
        )

    def give(matrix, step):
        blocks, row_part, column_part = spans(matrix, step, regions[matrix][step][1])
        for place, block in enumerate(blocks):
            sends[matrix][step][place] = total[matrix, block, row_part, column_part].astype(BF16)
        half_copy(matrix, step).start()

    def take(matrix, step):
        half_copy(matrix, step).wait_recv()
        blocks, row_part, column_part = spans(matrix, step, regions[matrix][step][0])
        for place, block in enumerate(blocks):
            total[matrix, block, row_part, column_part] += recvs[matrix][step][place].astype(F32)

    def whole_view(matrix, step):
        keep = regions[matrix][step][0]
        blocks, row_part, column_part = spans(matrix, step, keep)
        return gathered.at[matrix, row_part, column_part]

    wholes = [[name for name in order if BITS[name][0] == "ctx"] for order in ORDERS]

    def whole_copy(matrix, back):
        name = wholes[matrix][2 - back]
        step = ORDERS[matrix].index(name)
        blocks, row, column = regions[matrix][step][0]
        shape = sends[matrix][step].shape
        row_part = pl.ds(row if isinstance(row, int) else pl.multiple_of(row, 16), shape[1])
        column_part = pl.ds(
            column if isinstance(column, int) else pl.multiple_of(column, BLOCK), shape[2]
        )
        view = gathered.at[matrix, row_part, column_part]
        return remote(view, view, whole_send.at[matrix, back], whole_recv.at[matrix, back], name)

    fetches[0].wait()
    resid = hidden[...].astype(F32)
    inv = lax.rsqrt(jnp.mean(resid * resid, axis=-1, keepdims=True) + epsilon)
    gain = jnp.transpose(small_ref[...].astype(F32))[experts : experts + 1, :]
    normed = (resid * inv * gain).astype(BF16)
    for matrix, ref in ((1, dq_ref), (2, dk_ref), (3, dv_ref)):
        part = dot(normed, ref[...], 0, 0)
        for block in range(4):
            total[matrix, block] = part[block * share : (block + 1) * share]
        give(matrix, 0)
    fetches[1].wait()
    for block in range(4):
        total[0, block] = grad_wo[block * share : (block + 1) * share, :].astype(F32)
    give(0, 0)
    fetches[2].wait()
    grad_normed = dot(dq_ref[...], weights[0], 1, 1)
    grad_normed = grad_normed + dot(dk_ref[...], weights[1], 1, 1)
    grad_normed = grad_normed + dot(dv_ref[...], weights[2], 1, 1)
    pack[...] = jnp.zeros_like(pack)
    pack[:experts, :] = router_ref[...]
    pack[experts : experts + 1, :] = jnp.sum(grad_normed * resid * inv, axis=0, keepdims=True)
    pack[experts + 1 : experts + 2, :] = gain_ref[0:1, :]
    last = lane_ids(2, BLOCK) == hot_ref.shape[1] - 1
    for pair in range(PAIRS):
        near = lax.dot_general(
            sums_ref[pair, 0:2, :],
            hot_ref[...],
            (((1,), (0,)), ((), ())),
            precision=HIGH,
            preferred_element_type=F32,
        )
        near = jnp.concatenate([near, jnp.zeros((2, BLOCK - near.shape[1]), F32)], axis=1)
        distant = jnp.sum(sums_ref[pair, 2:4, :], axis=1, keepdims=True)
        place = experts + 8 + 2 * pair
        pack[place : place + 2, :BLOCK] = near + jnp.where(last, distant, 0.0)

    def pack_copy(step):
        return remote(
            pack_recv.at[0, step],
            pack_recv.at[1, step],
            pack_send.at[step],
            pack_sem.at[step],
            list(BITS)[step],
        )

    for step in range(steps):
        pack_recv[0, step] = pack[...]
        pack_copy(step).start()
        for matrix in (1, 2, 3, 0):
            take(matrix, step)
            if step + 1 < steps:
                give(matrix, step + 1)
        if step == 0:
            fetches[3].wait()
            scaled = grad_normed * gain
            mean = jnp.mean(scaled * resid, axis=-1, keepdims=True)
            grad_in = grad_mid[...] + inv * scaled - resid * inv * inv * inv * mean
            input_grad_out[...] = grad_in.astype(BF16)
        pack_copy(step).wait_recv()
        pack[...] += pack_recv[1, step]

    mine = lax.axis_index("wsh")
    for matrix in range(4):
        keep = regions[matrix][steps - 1][0]
        blocks, row_part, column_part = spans(matrix, steps - 1, keep)
        gathered[matrix, row_part, column_part] = total[
            matrix, blocks[0], row_part, column_part
        ].astype(BF16)
        whole_copy(matrix, 0).start()
    for back in range(3):
        for matrix in range(4):
            whole_copy(matrix, back).wait_recv()
            if back < 2:
                whole_copy(matrix, back + 1).start()
            else:
                shares_out[matrix] = gathered[matrix]
        if back == 0:
            buckets = table_out.shape[0]
            for block in range(4):

                @pl.when(mine == block)
                def _():
                    rows = pack[: experts + 8, block * share : (block + 1) * share]
                    turned = jnp.transpose(rows)
                    router_out[...] = turned[:, :experts]
                    gains_out[...] = rows[experts : experts + 8]
                    table = jnp.transpose(pack[experts + 8 :, :BLOCK])
                    table_out[...] = table[block * buckets : (block + 1) * buckets, :HEADS]

    for step in range(steps):
        pack_copy(step).wait_send()
        for matrix in range(4):
            half_copy(matrix, step).wait_send()
    for back in range(3):
        for matrix in range(4):
            whole_copy(matrix, back).wait_send()


def tail(experts, dq, dk, dv, hidden, grad_mid, weights, grad_wo, small, router, gains, sums, hot, share, buckets):
    tokens, width = dq.shape
    vmem = pl.BlockSpec(memory_space=pltpu.VMEM)
    anywhere = pl.BlockSpec(memory_space=pl.ANY)
    steps = len(BITS)
    pieces = [shape for order in ORDERS for shape in halved_shapes(order, share, width)]
    buffers = [pltpu.VMEM(shape, BF16) for shape in pieces]
    rows = experts + 8 + 16
    dma = pltpu.SemaphoreType.DMA
    return pl.pallas_call(
        functools.partial(tail_kernel, experts),
        in_specs=[vmem] * 3 + [anywhere] * 4 + [vmem] * 5,
        out_specs=[vmem] * 5,
        out_shape=[
            jax.ShapeDtypeStruct((tokens, width), BF16),
            jax.ShapeDtypeStruct((4, share, width), BF16),
            jax.ShapeDtypeStruct((share, experts), F32),
            jax.ShapeDtypeStruct((8, share), F32),
            jax.ShapeDtypeStruct((buckets, HEADS), F32),
        ],
        scratch_shapes=[
            pltpu.VMEM((3, width, width), BF16),
            pltpu.VMEM((tokens, width), BF16),
            pltpu.VMEM((tokens, width), F32),
            pltpu.VMEM((width, width), BF16),
            pltpu.VMEM((4, 4, share, width), F32),
            pltpu.VMEM((4, share, width), BF16),
            pltpu.VMEM((rows, width), F32),
            pltpu.VMEM((2, steps, rows, width), F32),
            *buffers,
            *buffers,
            dma((4,)),
            dma((4, steps)),
            dma((4, steps)),
            dma((4, 3)),
            dma((4, 3)),
            dma((steps,)),
            dma((steps,)),
        ],
        compiler_params=pltpu.CompilerParams(
            collective_id=2, has_side_effects=True, vmem_limit_bytes=60 << 20
        ),
        name="tail",
    )(dq, dk, dv, hidden, grad_mid, weights, grad_wo, small, router, gains, sums, hot)


def finish_kernel(
    input_ref, shares_ref, router_ref, gains_ref, table_ref, input_out, wq, wk, wv, wo, router, gain_a, gain_m, table
):
    input_out[...] = input_ref[...]
    for place, out in enumerate((wo, wq, wk, wv)):
        out[...] = shares_ref[place].astype(F32)
    router[...] = router_ref[...]
    gain_a[...] = gains_ref[0, :]
    gain_m[...] = gains_ref[1, :]
    table[...] = table_ref[...]


def finish(grad_input, shares, router, gains, table):
    share, width = shares.shape[1:]
    vmem = pl.BlockSpec(memory_space=pltpu.VMEM)
    return pl.pallas_call(
        finish_kernel,
        in_specs=[vmem] * 5,
        out_specs=[vmem] * 9,
        out_shape=[
            jax.ShapeDtypeStruct(grad_input.shape, BF16),
            *[jax.ShapeDtypeStruct((share, width), F32)] * 4,
            jax.ShapeDtypeStruct(router.shape, F32),
            jax.ShapeDtypeStruct((share,), F32),
            jax.ShapeDtypeStruct((share,), F32),
            jax.ShapeDtypeStruct(table.shape, F32),
        ],
        compiler_params=pltpu.CompilerParams(vmem_limit_bytes=60 << 20),
        name="finish",
    )(grad_input, shares, router, gains, table)


def rms_forward(values, gain_vec):
    inv_rms = lax.rsqrt(jnp.mean(values * values, axis=-1, keepdims=True) + epsilon)
    return (values * inv_rms * gain_vec, inv_rms)


def rms_backward(values, inv_rms, gain_vec, upstream):
    grad_gain = jnp.sum(upstream * values * inv_rms, axis=0)
    scaled = upstream * gain_vec
    grad_values = inv_rms * scaled - values * inv_rms**3 * jnp.mean(
        scaled * values, axis=-1, keepdims=True
    )
    return (grad_values, grad_gain)


def per_device(
    hidden_in,
    w_query,
    w_key,
    w_value,
    w_output,
    w_router,
    gain_attn,
    gain_moe,
    rel_bias,
    w_in,
    w_out,
    routes,
    block_pairs,
    cotangent,
):
    tokens, width = hidden_in.shape[1:]
    ctx_count, wsh_count = lax.axis_size("ctx"), lax.axis_size("wsh")
    ctx_rank, wsh_rank = lax.axis_index("ctx"), lax.axis_index("wsh")
    length = tokens * ctx_count
    blocks = length // BLOCK
    experts, exp_dev = w_router.shape[1], w_in.shape[0]
    slot_most = 2 * tokens // experts
    capacity = (9 * length // (8 * experts) + 7) // 8 * 8

    def over(axis, array, dim=0):
        return lax.all_gather(array, axis, axis=dim, tiled=True)

    share = width // wsh_count
    small = jnp.concatenate(
        [
            w_router,
            gain_attn[:, None],
            gain_moe[:, None],
            jnp.pad(rel_bias, ((0, share - rel_bias.shape[0]), (0, 0))),
        ],
        axis=1,
    )
    small = jnp.pad(small, ((0, 0), (0, BLOCK - small.shape[1])))
    lanes = wrapped_lanes()
    buckets = rel_bias.shape[0] * wsh_count
    query_hot = onehot_of(BLOCK - lanes, buckets)
    key_hot = onehot_of(lanes, buckets)

    def hot_rows(hot):
        spread = np.zeros((wsh_count, share, SPAN), np.float32)
        spread[:, : rel_bias.shape[0]] = hot.T.reshape(wsh_count, -1, SPAN)
        return jnp.asarray(spread.reshape(width, SPAN), BF16)

    qkv, weights, small, slot_rows, targets, own_g, plan, query_base, key_base = project(
        (ctx_count, wsh_count),
        capacity,
        experts,
        slot_most,
        hidden_in[0],
        (w_query, w_key, w_value, w_output),
        small,
        routes.reshape(1, tokens),
        block_pairs,
        hot_rows(query_hot),
        hot_rows(key_hot),
        cotangent[0],
    )
    attn_low, attn_exact, lse, lse_rows = attend_forward(plan, qkv, query_base, width)
    (
        output_rows,
        grad_mid,
        grad_heads,
        heads_all,
        stats,
        grad_wo,
        grad_router,
        grad_gain_m,
        grad_q,
        sums,
        grad_w_in,
        grad_w_out,
    ) = middle(
        (ctx_count, wsh_count),
        experts,
        attn_low,
        attn_exact,
        hidden_in[0],
        cotangent[0],
        weights,
        w_in,
        w_out,
        own_g,
        small,
        slot_rows,
        targets,
        lse_rows,
        routes.reshape(tokens, 1),
        query_base,
        plan,
        qkv.reshape(blocks, BLOCK, 3 * width),
        lse,
    )

    if heads_all.shape[0] == tokens:
        heads_all = dot(over("ctx", heads_all), weights[3], 1, 1).astype(BF16)
        stats = over("ctx", stats)
        grad_q, sums = attend_queries(
            plan, qkv, query_base, grad_heads, attn_exact, lse
        )
    grad_k, grad_v, output_rows, grad_w_in, grad_w_out = attend_keys(
        plan, qkv, key_base, heads_all, stats, (output_rows, grad_w_in, grad_w_out)
    )

    bucket_share = buckets // wsh_count
    if ctx_count == 8 and wsh_count == 4 and share % 64 == 0:
        results = tail(
            experts,
            grad_q,
            grad_k,
            grad_v,
            hidden_in[0],
            grad_mid,
            weights,
            grad_wo,
            small,
            grad_router,
            grad_gain_m,
            sums,
            jnp.asarray(query_hot),
            share,
            bucket_share,
        )
        grad_input, *shares = finish(*results)
        return (output_rows[None], grad_input[None], *shares, grad_w_in, grad_w_out)

    near_sums = sums[:, :2].reshape(HEADS, SPAN)
    far_sums = jnp.sum(sums[:, 2:4].reshape(HEADS, SPAN), axis=1)
    grad_table = jnp.dot(jnp.asarray(query_hot.T), near_sums.T, precision=HIGH)
    grad_table = grad_table.at[buckets - 1].add(far_sums)

    resid_in = hidden_in[0].astype(F32)
    full_query, full_key, full_value = (weights[place] for place in range(3))
    gain_one = small[:, experts].astype(F32)
    normed_one, inv_one = rms_forward(resid_in, gain_one)
    normed_one = normed_one.astype(BF16)
    grad_normed_one = dot(grad_q, full_query, 1, 1)
    grad_normed_one = grad_normed_one + dot(grad_k, full_key, 1, 1)
    grad_normed_one = grad_normed_one + dot(grad_v, full_value, 1, 1)
    grad_in_norm, grad_gain_a = rms_backward(resid_in, inv_one, gain_one, grad_normed_one)
    grad_input = (grad_mid + grad_in_norm).astype(BF16)

    def reduce_weight(grad):
        part = lax.psum_scatter(grad.astype(BF16), "wsh", scatter_dimension=0, tiled=True)
        return lax.psum(part, "ctx").astype(F32)

    grad_wq = dot(normed_one, grad_q, 0, 0)
    grad_wk = dot(normed_one, grad_k, 0, 0)
    grad_wv = dot(normed_one, grad_v, 0, 0)
    shares = [reduce_weight(grad) for grad in (grad_wq, grad_wk, grad_wv, grad_wo)]
    columns = jnp.concatenate(
        [grad_router.T, grad_gain_a[:, None], grad_gain_m[0][:, None]], axis=1
    )
    table = jnp.pad(grad_table, ((0, 0), (0, columns.shape[1] - HEADS)))
    summed = lax.psum(jnp.concatenate([columns, table], axis=0), ("ctx", "wsh"))
    own_columns = lax.dynamic_slice_in_dim(summed[:width], wsh_rank * share, share, 0)
    own_table = lax.dynamic_slice_in_dim(
        summed[width:, :HEADS], wsh_rank * bucket_share, bucket_share, 0
    )
    return (
        output_rows.astype(BF16)[None],
        grad_input[None],
        *shares,
        own_columns[:, :experts],
        own_columns[:, experts],
        own_columns[:, experts + 1],
        own_table,
        grad_w_in,
        grad_w_out,
    )


def solution(mesh):
    in_specs = (
        P("wsh", "ctx", None),
        P("wsh", None),
        P("wsh", None),
        P("wsh", None),
        P("wsh", None),
        P("wsh", None),
        P("wsh"),
        P("wsh"),
        P("wsh", None),
        P("ctx", None, "wsh"),
        P("ctx", "wsh", None),
        P("wsh", "ctx", None),
        P(),
        P("wsh", "ctx", None),
    )
    out_specs = (
        P("wsh", "ctx", None),
        P("wsh", "ctx", None),
        P("wsh", None),
        P("wsh", None),
        P("wsh", None),
        P("wsh", None),
        P("wsh", None),
        P("wsh"),
        P("wsh"),
        P("wsh", None),
        P("ctx", None, "wsh"),
        P("ctx", "wsh", None),
    )
    return jax.shard_map(
        per_device, mesh=mesh, in_specs=in_specs, out_specs=out_specs, check_vma=False
    )
```

```python
import functools
import math

import jax
import jax.numpy as jnp
import numpy as np
from jax import lax
from jax.experimental import pallas as pl
from jax.experimental.pallas import tpu as pltpu
from jax.sharding import PartitionSpec as P

HEADS = 12
HEAD_DIM = 64
BLOCK = 128
PAIRS = HEADS // 2
NEAR = 2 * BLOCK
SPAN = 3 * BLOCK
epsilon = 1e-06
MASKED = -1e30
bucket_edges = [math.ceil(16 * 8 ** (marker / 16)) for marker in range(1, 16)]
F32 = jnp.float32
BF16 = jnp.bfloat16
HIGH = lax.Precision.HIGHEST


def bucket_of(distance):
    gap = np.maximum(distance, 0)
    count = np.full(gap.shape, 16, np.int32)
    for edge in bucket_edges:
        count = count + (gap >= edge)
    return np.where(gap < 16, gap, count)


def wrapped_lanes():
    lanes = np.arange(SPAN)
    return np.where(lanes < NEAR, lanes, lanes - SPAN)


def onehot_of(distance, buckets):
    return (bucket_of(distance)[:, None] == np.arange(buckets)[None, :]).astype(np.float32)


def dot(left, right, left_dim=1, right_dim=0):
    return lax.dot_general(
        left, right, (((left_dim,), (right_dim,)), ((), ())), preferred_element_type=F32
    )


def lane_ids(rows, lanes):
    return lax.broadcasted_iota(jnp.int32, (rows, lanes), 1)


def stack_heads(rows):
    first = lane_ids(rows.shape[0], BLOCK) < HEAD_DIM
    zero = jnp.zeros_like(rows)
    return jnp.concatenate([jnp.where(first, rows, zero), jnp.where(first, zero, rows)], axis=0)


def merge_heads(stacked):
    half = stacked.shape[0] // 2
    first = lane_ids(half, BLOCK) < HEAD_DIM
    return jnp.where(first, stacked[:half], stacked[half:])


def fold_lanes(tile, combine):
    return combine(tile[:, :BLOCK], tile[:, BLOCK:])


def near_bias(base_ref, place=0):
    tiles = []
    for head in range(2):
        row = jnp.broadcast_to(base_ref[place, head : head + 1, :], (BLOCK, SPAN))
        tiles.append(pltpu.roll(row, 0, 1, stride=1, stride_axis=0)[:, :NEAR])
    return jnp.concatenate(tiles, axis=0)


def rows_at(block):
    return pl.ds(pl.multiple_of(block * BLOCK, BLOCK), BLOCK)


def two_tiles(ref, plan_ref, tile):
    tile = SOURCE + tile
    return jnp.concatenate(
        [ref[rows_at(plan_ref[tile]), :], ref[rows_at(plan_ref[tile + 1]), :]], axis=0
    )


class LineGather:
    def __init__(self, axis, lines, across, views, own, sems, crossing=None):
        self.axis, self.lines, self.across = axis, lines, across
        self.views, self.own, self.sems = views, own, sems
        self.crossing = crossing or ["all"] * len(views)
        self.me = lax.axis_index(axis)
        self.line, self.column = self.me // across, self.me % across

    def copy(self, part, block, peer, kind, place, own=False):
        send, recv = self.sems
        view = self.views[part](block)
        return pltpu.make_async_remote_copy(
            src_ref=self.own[part] if own else view,
            dst_ref=view,
            send_sem=send.at[part, kind, place],
            recv_sem=recv.at[part, kind, place],
            device_id={self.axis: peer},
            device_id_type=pl.DeviceIdType.MESH,
        )

    def line_send(self, part, way, step):
        place = self.line - way * step
        ahead = self.line + way
        there = (place >= 0) & (place < self.lines) & (ahead >= 0) & (ahead < self.lines)
        copy = self.copy(
            part,
            place * self.across + self.column,
            ahead * self.across + self.column,
            (1 - way) // 2,
            step,
            own=step == 0,
        )
        return there, copy

    def line_recv(self, part, way, step):
        place = self.line - way * (step + 1)
        there = (place >= 0) & (place < self.lines)
        block = place * self.across + self.column
        return there, block, self.copy(part, block, self.me, (1 - way) // 2, step)

    def cross_send(self, part, block, ahead, own=False):
        peer = self.line * self.across + (self.column + ahead) % self.across
        return self.copy(part, block, peer, 1 + ahead, block // self.across, own)

    def cross_recv(self, part, line, ahead):
        block = line * self.across + (self.column + self.across - ahead) % self.across
        return self.copy(part, block, self.me, 1 + ahead, line)

    def begin(self, part):
        for way in (1, -1):
            there, copy = self.line_send(part, way, 0)
            pl.when(there)(copy.start)
        if self.crossing[part] != "none":
            for ahead in range(1, self.across):
                self.cross_send(part, self.me, ahead, own=True).start()

    def advance(self, part, step):
        for way in (1, -1):
            there, block, arrived = self.line_recv(part, way, step)

            pl.when(there)(arrived.wait_recv)
            if step + 2 < self.lines:
                onward, copy = self.line_send(part, way, step + 1)
                pl.when(onward)(copy.start)
            if self.crossing[part] == "all":
                for ahead in range(1, self.across):
                    pl.when(there)(self.cross_send(part, block, ahead).start)

    def wait_cross(self, part):
        for ahead in range(1, self.across):
            for line in range(self.lines):
                self.cross_recv(part, line, ahead).wait_recv()

    def finish(self):
        for part in range(len(self.views)):
            for step in range(self.lines - 1):
                for way in (1, -1):
                    there, copy = self.line_send(part, way, step)
                    pl.when(there)(copy.wait_send)
            for ahead in range(1, self.across):
                if self.crossing[part] == "all":
                    for line in range(self.lines):
                        self.cross_send(part, line * self.across + self.column, ahead).wait_send()
                elif self.crossing[part] == "own":
                    self.cross_send(part, self.me, ahead).wait_send()


class RowGather:
    def __init__(self, counts, held, sems):
        lines, across = grid_of(counts[0])
        tokens = held.shape[1]
        self.across, self.lines = across, lines
        me = lax.axis_index("ctx")
        self.me = me
        self.balanced = across == 2 and tokens % 32 == 0
        bulk = tokens * 13 // 16 if self.balanced else tokens
        half = bulk // 32 * 16
        cuts = [(0, half), (half, bulk - half)]

        def view(start, rows, turn):
            def of(block):
                if turn:
                    block = block + 1 - 2 * (block % 2)
                return held.at[block, pl.ds(start, rows), :]

            return of

        views = [view(start, rows, False) for start, rows in cuts]
        crossing = ["all", "all"]
        if self.balanced:
            views += [view(bulk, tokens - bulk, turn) for turn in (False, True)]
            crossing += ["own", "none"]
        self.parts = len(views)
        self.gather = LineGather(
            "ctx", lines, across, views, [of(me) for of in views], sems, crossing
        )

    def begin(self):
        for part in range(min(self.parts, 3)):
            self.gather.begin(part)

    def advance(self, step):
        if self.balanced and step == 0:
            self.gather.cross_recv(2, self.gather.line, 1).wait_recv()
            self.gather.begin(3)
        for part in range(self.parts):
            self.gather.advance(part, step)

    def wait_cross(self, line, ahead):
        for part in range(2):
            self.gather.cross_recv(part, line, ahead).wait_recv()

    def finish(self):
        self.gather.finish()


def row_parts(ctx_count, tokens):
    return 4 if grid_of(ctx_count)[1] == 2 and tokens % 32 == 0 else 2


def gather_sems(parts, lines, across):
    return [pltpu.SemaphoreType.DMA((parts, 1 + across, lines))] * 2


def greet(counts):
    barrier = pltpu.get_barrier_semaphore()
    for axis, count in zip(("ctx", "wsh"), counts):
        me = lax.axis_index(axis)
        for ahead in range(1, count):
            pl.semaphore_signal(
                barrier,
                inc=1,
                device_id={axis: (me + ahead) % count},
                device_id_type=pl.DeviceIdType.MESH,
            )
    pl.semaphore_wait(barrier, sum(counts) - 2)


class Exchange:
    def __init__(self, count, experts, most, sems, source, target):
        self.count, self.experts, self.most = count, experts, most
        self.send, self.recv = sems
        self.source, self.target = source, target
        self.me = lax.axis_index("ctx")

    def rows(self, place):
        return pl.ds(pl.multiple_of(place * self.most, self.most), self.most)

    def copy(self, expert, ahead, outward):
        peer = (self.me + ahead) % self.count if outward else (self.me + self.count - ahead) % self.count
        return pltpu.make_async_remote_copy(
            src_ref=self.source(expert, peer),
            dst_ref=self.target(expert, self.me),
            send_sem=self.send.at[expert, ahead - 1],
            recv_sem=self.recv.at[expert, ahead - 1],
            device_id={"ctx": peer},
            device_id_type=pl.DeviceIdType.MESH,
        )

    def start(self, expert):
        for ahead in range(1, self.count):
            self.copy(expert, ahead, True).start()
        self.target(expert, self.me)[...] = self.source(expert, self.me)[...]

    def wait(self, expert):
        for ahead in range(1, self.count):
            peer = (self.me + self.count - ahead) % self.count
            pltpu.make_async_remote_copy(
                src_ref=self.source(expert, peer),
                dst_ref=self.target(expert, peer),
                send_sem=self.send.at[expert, ahead - 1],
                recv_sem=self.recv.at[expert, ahead - 1],
                device_id={"ctx": peer},
                device_id_type=pl.DeviceIdType.MESH,
            ).wait_recv()

    def finish(self, expert):
        for ahead in range(1, self.count):
            self.copy(expert, ahead, True).wait_send()


def exchange_sems(count, experts):
    return [pltpu.SemaphoreType.DMA((experts, count - 1))] * 2


def cap_map(target_ref, expert, capacity):
    slots = target_ref.shape[1]
    rows = lax.broadcasted_iota(jnp.int32, (capacity, slots), 0)
    return (rows == jnp.broadcast_to(target_ref[expert : expert + 1, :], rows.shape)).astype(F32).astype(BF16)


def placement_of(slot_ref, slots):
    rows = lax.broadcasted_iota(jnp.int32, (slots, slot_ref.shape[1]), 0)
    return (rows == jnp.broadcast_to(slot_ref[0:1, :], rows.shape)).astype(F32).astype(BF16)


def grid_of(count):
    lines = 4 if count % 4 == 0 else 1
    return lines, count // lines


def route_slots(routes_ref, chosen_ref, most):
    experts, tokens = chosen_ref.shape
    ids = lax.broadcasted_iota(jnp.int32, (experts, tokens), 0)
    routes = jnp.broadcast_to(routes_ref[0:1, :], ids.shape)
    chosen = (ids == routes).astype(F32)
    chosen_ref[...] = chosen
    earlier = lax.broadcasted_iota(jnp.int32, (tokens, tokens), 0) < lax.broadcasted_iota(
        jnp.int32, (tokens, tokens), 1
    )
    before = dot(chosen.astype(BF16), earlier.astype(F32).astype(BF16))
    rank = jnp.sum(chosen * before, axis=0, keepdims=True).astype(jnp.int32)
    return routes_ref[0:1, :] * most + rank, jnp.sum(chosen, axis=1, keepdims=True)


SOURCE = 2


def plan_start(blocks):
    return SOURCE + blocks + 2


def plan_size(blocks):
    return plan_start(blocks) + 4 + 3 * (blocks + 1)


def write_plan(pairs_ref, plan, me):
    blocks = 2 * pairs_ref.shape[0]
    half = blocks // 2
    own = [pairs_ref[me, side] for side in range(2)]
    plan[0], plan[1] = own[0], own[1]
    plan[SOURCE] = jnp.int32(0)
    plan[SOURCE + blocks + 1] = jnp.int32(0)

    def place(position, carry):
        found = jnp.int32(0)
        for row in range(blocks):
            found = found + jnp.where(pairs_ref[row // 2, row % 2] == position, row, 0)
        plan[SOURCE + 1 + position] = found
        return carry

    lax.fori_loop(0, blocks, place, 0)
    early, late = jnp.minimum(own[0], own[1]), jnp.maximum(own[0], own[1])
    first = jnp.where(own[0] < own[1], 0, 1).astype(jnp.int32)
    start = plan_start(blocks)
    plan[start], plan[start + 1] = first, 1 - first
    plan[start + 2], plan[start + 3] = early, late
    start = start + 4
    for step in range(blocks + 1):
        rest = step - (half + 2)
        if step <= half:
            tile, owner = late - step, jnp.int32(1)
        elif step == half + 1:
            tile, owner = early, jnp.int32(0)
        else:
            tile = jnp.where(rest < early, early - 1 - rest, late - half - 1 - (rest - early))
            owner = jnp.where(rest < early, 0, 1).astype(jnp.int32)
        tile = jnp.minimum(jnp.maximum(tile, 0), blocks - 1)
        plan[start + step] = plan[SOURCE + 1 + tile]
        plan[start + blocks + 1 + step] = owner
        plan[start + 2 * blocks + 2 + step] = plan[SOURCE + blocks - tile]


def project_kernel(
    counts,
    capacity,
    rows_ref,
    wq_ref,
    wk_ref,
    wv_ref,
    wo_ref,
    small_ref,
    routes_ref,
    pairs_ref,
    query_hot_ref,
    key_hot_ref,
    qkv_out,
    weights_out,
    small_out,
    slot_out,
    target_out,
    plan_out,
    query_base_out,
    key_base_out,
    held,
    weights,
    smalls,
    gain,
    ready,
    chosen,
    tallies,
    row_send,
    row_recv,
    weight_send,
    weight_recv,
    tally_send,
    tally_recv,
    out_sems,
    local_sems,
):
    ctx_count, wsh_count = counts
    experts = chosen.shape[0]
    exp_dev = experts // ctx_count
    lanes = experts
    tokens, width = rows_ref.shape
    share = wq_ref.shape[0]
    lines, across = grid_of(ctx_count)
    pairs = wsh_count // 2

    def shard(block):
        return pl.ds(pl.multiple_of(block * share, 16), share)

    def weight_view(place):
        return lambda block: weights.at[place, shard(block), :]

    rows = RowGather(counts, held, (row_send, row_recv))
    mats = LineGather(
        "wsh",
        pairs,
        2,
        [lambda block: smalls.at[shard(block), :]] + [weight_view(place) for place in range(4)],
        None,
        (weight_send, weight_recv),
    )
    mats.own = [view(mats.me) for view in mats.views]
    own_weights = (small_ref, wq_ref, wk_ref, wv_ref, wo_ref)
    own_copies = [
        pltpu.make_async_copy(ref, view, local_sems.at[2 + place])
        for place, (ref, view) in enumerate(
            [(rows_ref, held.at[rows.me])]
            + list(zip(own_weights, mats.own))
        )
    ]
    for copy in own_copies:
        copy.start()
    greet(counts)
    own_copies[0].wait()
    rows.begin()
    for part in range(5):
        own_copies[1 + part].wait()
        if part < 4:
            mats.begin(part)
    most = target_out.shape[1] // ctx_count
    slot, tally = route_slots(routes_ref, chosen, most)
    slot_out[...] = jnp.broadcast_to(slot, slot_out.shape)
    tallies[rows.me] = jnp.broadcast_to(tally, (experts, BLOCK))
    counted = Exchange(
        ctx_count,
        1,
        most,
        (tally_send, tally_recv),
        lambda expert, peer: tallies.at[rows.me],
        lambda expert, peer: tallies.at[peer],
    )
    for ahead in range(1, ctx_count):
        counted.copy(0, ahead, True).start()
    write_plan(pairs_ref, plan_out, rows.me)

    def place_targets():
        counted.wait(0)
        lane = lane_ids(1, ctx_count * most)
        for expert in range(exp_dev):
            offset = jnp.zeros((1, 1), F32)
            target = jnp.full((1, ctx_count * most), capacity, jnp.int32)
            for source in range(ctx_count):
                count = tallies[source, pl.ds(rows.me * exp_dev + expert, 1), 0:1]
                inside = (lane >= source * most) & (
                    lane < source * most + jnp.broadcast_to(count.astype(jnp.int32), lane.shape)
                )
                place = lane - source * most + jnp.broadcast_to(offset.astype(jnp.int32), lane.shape)
                target = jnp.where(inside, place, target)
                offset = offset + count
            target_out[expert : expert + 1, :] = target
        target_out[exp_dev:, :] = jnp.zeros_like(target_out[exp_dev:, :])

    for step in range(lines - 2):
        rows.advance(step)
        if step == 0:
            place_targets()
    for step in range(pairs - 1):
        for part in range(4):
            mats.advance(part, step)
    mats.begin(4)
    for part in range(4):
        mats.wait_cross(part)
    small_copy = pltpu.make_async_copy(smalls, small_out, local_sems.at[1])
    small_copy.start()
    turned = jnp.transpose(smalls[...].astype(F32))
    gain[...] = turned[lanes : lanes + 8, :]
    for hot_ref, base_out, sign in (
        (query_hot_ref, query_base_out, -1),
        (key_hot_ref, key_base_out, 1),
    ):
        table = dot(turned.astype(BF16), hot_ref[...])
        lane = lane_ids(BLOCK, SPAN)
        lane = jnp.where(lane < NEAR, lane, lane - SPAN)
        gap = lane if sign > 0 else BLOCK - lane
        last = jnp.max(jnp.where(gap == NEAR - 1, table, -jnp.inf), axis=1, keepdims=True)
        table = jnp.where(gap >= 0, table - last, MASKED)
        for pair in range(PAIRS):
            start = experts + 2 + 2 * pair
            base_out[pair] = jnp.zeros((8, SPAN), F32)
            base_out[pair, 0:2, :] = table[start : start + 2]
    rows.advance(lines - 2)
    column = rows.me % across
    upper = rows.me // across // max(lines // 2, 1)

    def put(slot, block):
        place = pl.ds(pl.multiple_of(block * tokens, tokens), tokens)
        return pltpu.make_async_copy(ready.at[slot], qkv_out.at[place, :], out_sems.at[slot])

    def order(step):
        ahead, line = step // lines, step % lines
        line = line + upper * (lines - 1 - 2 * line)
        return line, ahead, line * across + (column + across - ahead) % across

    def step_body(step, carry):
        line, ahead, block = order(step)
        slot = step % 2
        for skip in range(1, across):

            @pl.when(ahead == skip)
            def _():
                rows.wait_cross(line, skip)

        @pl.when(step >= 2)
        def _():
            put(slot, order(step - 2)[2]).wait()

        values = held[block].astype(F32)
        inv = lax.rsqrt(jnp.mean(values * values, axis=-1, keepdims=True) + epsilon)
        normed = (values * inv * gain[0:1, :]).astype(BF16)
        for place in range(3):
            ready[slot, :, place * width : (place + 1) * width] = dot(
                normed, weights[place]
            ).astype(BF16)
        put(slot, block).start()
        return carry

    lax.fori_loop(0, ctx_count // 2, step_body, 0)
    for step in range(pairs - 1):
        mats.advance(4, step)
    lax.fori_loop(ctx_count // 2, ctx_count, step_body, 0)
    mats.wait_cross(4)
    weights_copy = pltpu.make_async_copy(weights, weights_out, local_sems.at[0])
    weights_copy.start()
    for step in (ctx_count - 2, ctx_count - 1):
        put(step % 2, order(step)[2]).wait()
    weights_copy.wait()
    small_copy.wait()
    counted.finish(0)
    rows.finish()
    mats.finish()


def project(
    counts, capacity, experts, most, rows, weights, small, routes, pairs, query_hot, key_hot
):
    tokens, width = rows.shape
    ctx_count, wsh_count = counts
    length = tokens * ctx_count
    lines, across = grid_of(ctx_count)
    vmem = pl.BlockSpec(memory_space=pltpu.VMEM)
    anywhere = pl.BlockSpec(memory_space=pl.ANY)
    smem = pl.BlockSpec(memory_space=pltpu.SMEM)
    return pl.pallas_call(
        functools.partial(project_kernel, counts, capacity),
        in_specs=[anywhere] * 6 + [vmem, smem, vmem, vmem],
        out_specs=[anywhere] * 3 + [vmem] * 2 + [smem] + [vmem] * 2,
        out_shape=[
            jax.ShapeDtypeStruct((length, 3 * width), BF16),
            jax.ShapeDtypeStruct((4, width, width), BF16),
            jax.ShapeDtypeStruct((width, small.shape[1]), BF16),
            jax.ShapeDtypeStruct((8, tokens), jnp.int32),
            jax.ShapeDtypeStruct((8, ctx_count * most), jnp.int32),
            jax.ShapeDtypeStruct((plan_size(2 * ctx_count),), jnp.int32),
            jax.ShapeDtypeStruct((PAIRS, 8, SPAN), F32),
            jax.ShapeDtypeStruct((PAIRS, 8, SPAN), F32),
        ],
        scratch_shapes=[
            pltpu.VMEM((ctx_count, tokens, width), BF16),
            pltpu.VMEM((4, width, width), BF16),
            pltpu.VMEM((width, small.shape[1]), BF16),
            pltpu.VMEM((8, width), F32),
            pltpu.VMEM((2, tokens, 3 * width), BF16),
            pltpu.VMEM((experts, tokens), F32),
            pltpu.VMEM((ctx_count, experts, BLOCK), F32),
            *gather_sems(row_parts(ctx_count, tokens), lines, across),
            *gather_sems(5, wsh_count // 2, 2),
            *exchange_sems(ctx_count, 1),
            pltpu.SemaphoreType.DMA((2,)),
            pltpu.SemaphoreType.DMA((8,)),
        ],
        compiler_params=pltpu.CompilerParams(
            collective_id=0, has_side_effects=True, vmem_limit_bytes=60 << 20
        ),
        name="project",
    )(rows, *weights, small, routes, pairs, query_hot, key_hot)


def gelu_parts(values):
    slope, cubic = math.sqrt(2 / math.pi), 0.044715
    square = values * values
    bent = jnp.tanh(slope * (values + cubic * values * square))
    outer = 0.5 * (1.0 + bent)
    derivative = outer + 0.5 * values * (1.0 - bent * bent) * slope * (1.0 + 3 * cubic * square)
    return values * outer, derivative


def choose(rows, router, experts, expert):
    logits = dot(rows, router)
    lanes = lane_ids(rows.shape[0], router.shape[1])
    logits = jnp.where(lanes < experts, logits, MASKED)
    weights = jnp.exp(logits - jnp.max(logits, axis=-1, keepdims=True))
    probs = weights / jnp.sum(weights, axis=-1, keepdims=True)
    hot = (lanes == expert).astype(F32)
    return probs, hot, jnp.sum(probs * hot, axis=-1, keepdims=True)


def middle_kernel(
    counts,
    experts,
    spread_here,
    attn_ref,
    exact_ref,
    hidden_ref,
    grad_ref,
    weights_ref,
    w_in_ref,
    w_out_ref,
    small_ref,
    slot_ref,
    target_ref,
    lse_ref,
    routes_ref,
    base_ref,
    plan_ref,
    qkv_ref,
    output_out,
    grad_mid_out,
    grad_heads_out,
    heads_all_out,
    stats_out,
    grad_wo_out,
    grad_router_out,
    grad_gain_out,
    dq_out,
    sums_out,
    grad_in_out,
    grad_out_out,
    qkv,
    lse_all,
    stacked_q,
    stacked_g,
    delta_rep,
    bias,
    near,
    tile_keys,
    scores,
    tops,
    tile_weights,
    tile_values,
    other_values,
    lse_rows,
    own_g,
    early_in,
    attn,
    heads,
    exact_blocks,
    hidden,
    grad,
    wo,
    w_in,
    w_out,
    resid,
    incoming,
    own_x,
    all_x,
    all_g,
    hid,
    du,
    parts,
    from_mate,
    from_far,
    shares,
    mate_shares,
    far_shares,
    returning,
    home,
    branch,
    stats,
    stage_in,
    stage_out,
    heads_stage,
    fetch_sems,
    out_sems,
    heads_sems,
    x_send,
    x_recv,
    g_send,
    g_recv,
    early_send,
    early_recv,
    go_send,
    go_recv,
    back_send,
    back_recv,
    mate_send,
    mate_recv,
    far_send,
    far_recv,
    branch_send,
    branch_recv,
    stat_send,
    stat_recv,
):
    ctx_count, wsh_count = counts
    tokens, width = hidden.shape
    exp_dev, capacity = own_x.shape[:2]
    most = incoming.shape[1] // ctx_count
    lines, across = grid_of(ctx_count)
    pairs = wsh_count // 2
    me = lax.axis_index("ctx")
    home_row = me if spread_here else 0
    sources = [
        (grad_ref, grad),
        (weights_ref.at[3], wo),
        (hidden_ref, hidden),
        (w_in_ref, w_in),
        (w_out_ref, w_out),
    ]
    if spread_here:
        sources.insert(1, (qkv_ref, qkv))
    else:
        sources += [(attn_ref, attn), (exact_ref, exact_blocks)]
    fetches = [
        pltpu.make_async_copy(src, dst, fetch_sems.at[place])
        for place, (src, dst) in enumerate(sources)
    ]
    for fetch in fetches:
        fetch.start()
    views = [
        (lambda buffer, expert: lambda block: buffer.at[expert, block])(buffer, expert)
        for buffer in (all_g, all_x)
        for expert in range(exp_dev)
    ]
    gather_g = LineGather(
        "wsh",
        pairs,
        2,
        views[:exp_dev],
        [own_g.at[expert] for expert in range(exp_dev)],
        (g_send, g_recv),
    )
    gather_x = LineGather(
        "wsh",
        pairs,
        2,
        views[exp_dev:],
        [own_x.at[expert] for expert in range(exp_dev)],
        (x_send, x_recv),
    )
    wsh_me, my_line, my_core = gather_x.me, gather_x.line, gather_x.column
    greet(counts)
    fetches[0].wait()
    returning[1] = dot(placement_of(slot_ref, experts * most), grad[...]).astype(BF16)
    early = Exchange(
        ctx_count,
        exp_dev,
        most,
        (early_send, early_recv),
        lambda expert, peer: returning.at[1, early.rows(peer * exp_dev + expert), :],
        lambda expert, peer: early_in.at[expert, early.rows(peer), :],
    )
    for expert in range(exp_dev):
        early.start(expert)

    def pass_on():
        for expert in range(exp_dev):
            early.wait(expert)
            own_g[expert] = dot(cap_map(target_ref, expert, capacity), early_in[expert]).astype(BF16)
            gather_g.begin(expert)
            all_g[expert, wsh_me] = own_g[expert]

    if spread_here:
        tiles = Tiles(plan_ref, 2 * ctx_count, False)
        fetches[1].wait()

        def attend(pair, carry):
            pair_lanes = pl.ds(pl.multiple_of(pair * BLOCK, BLOCK), BLOCK)

            def load(part, row):
                lanes = pl.ds(pl.multiple_of(part * width + pair * BLOCK, BLOCK), BLOCK)
                return qkv[row, :, lanes]

            near_tiles = near_bias(base_ref, pair)
            bias[...] = jnp.concatenate(
                [near_tiles[:, BLOCK:], near_tiles[:, :BLOCK]], axis=1
            )
            totals = lse_all.at[pair]
            results = forward_pair(
                tiles,
                load,
                bias,
                stacked_q,
                tile_keys,
                scores,
                tops,
                totals,
                tile_weights,
                tile_values,
                other_values,
            )
            main = in_order(tiles, [result[0] for result in results])
            whole = in_order(tiles, [result[1] for result in results])
            lse = in_order(tiles, [totals[0], totals[1]])
            for own in range(2):
                rows = pl.ds(own * BLOCK, BLOCK)
                attn[rows, pair_lanes] = main[own]
                exact_blocks[own, :, pair_lanes] = whole[own]
                turned = jnp.transpose(lse[own])
                for head in range(2):
                    lse_rows[pair, head : head + 1, own * BLOCK : (own + 1) * BLOCK] = turned[
                        :1, head * BLOCK : (head + 1) * BLOCK
                    ]
            lse_rows[pair, 2:8, :] = jnp.zeros((6, 2 * BLOCK), F32)
            return carry

        lax.fori_loop(0, PAIRS - 1, attend, 0)
        pass_on()
        lax.fori_loop(PAIRS - 1, PAIRS, attend, 0)
    else:
        lse_rows[...] = lse_ref[...]
        pass_on()

    small_t = jnp.transpose(small_ref[...].astype(F32))[experts : experts + 8, :]
    gain_two = small_t[1:2, :]
    router = jnp.where(
        lane_ids(width, small_ref.shape[1]) < experts, small_ref[...], jnp.zeros_like(small_ref)
    )
    for fetch in fetches[2 if spread_here else 1 :]:
        fetch.wait()
    resid[...] = hidden[...].astype(F32) + dot(attn[...], wo[...])
    inv_two = lax.rsqrt(jnp.mean(resid[...] * resid[...], axis=-1, keepdims=True) + epsilon)
    normed_two = (resid[...] * inv_two * gain_two).astype(BF16)
    units = w_in.shape[2]
    placement = placement_of(slot_ref, experts * most)
    returning[0] = dot(placement, normed_two).astype(BF16)
    forth = Exchange(
        ctx_count,
        exp_dev,
        most,
        (go_send, go_recv),
        lambda expert, peer: returning.at[0, forth.rows(peer * exp_dev + expert), :],
        lambda expert, peer: incoming.at[expert, forth.rows(peer), :],
    )
    forth.start(0)
    gate = choose(normed_two, router, experts, routes_ref[...])[2]
    for expert in range(exp_dev):
        for step in range(pairs - 1):
            gather_g.advance(expert, step)
    gather_g.finish()

    summed = (parts.at[0], parts.at[1], shares)
    mate_parts = (from_mate.at[0], from_mate.at[1], mate_shares)
    far_parts = (from_far.at[0], from_far.at[1], far_shares)

    def mate_copy(array, expert, line):
        mine = line * 2 + 1 - my_core
        return pltpu.make_async_remote_copy(
            src_ref=summed[array].at[expert, mine],
            dst_ref=mate_parts[array].at[expert, line],
            send_sem=mate_send.at[array, expert, line],
            recv_sem=mate_recv.at[array, expert, line],
            device_id={"wsh": my_line * 2 + 1 - my_core},
            device_id_type=pl.DeviceIdType.MESH,
        )

    def far_copy(array, expert, ahead):
        line = (my_line + ahead) % pairs
        return pltpu.make_async_remote_copy(
            src_ref=summed[array].at[expert, line * 2 + my_core],
            dst_ref=far_parts[array].at[expert, ahead - 1],
            send_sem=far_send.at[array, expert, ahead - 1],
            recv_sem=far_recv.at[array, expert, ahead - 1],
            device_id={"wsh": line * 2 + my_core},
            device_id_type=pl.DeviceIdType.MESH,
        )

    def work(expert, ahead):
        line = (my_line + ahead) % pairs
        both = pl.ds(line * 2, 2)
        gather_x.cross_recv(expert, line, 1).wait_recv()
        gather_g.cross_recv(expert, line, 1).wait_recv()
        rows = all_x[expert, both].reshape(2 * capacity, width)
        active, slope = gelu_parts(dot(rows, w_in[expert]))
        active = active.astype(BF16)
        hid[expert, both] = active.reshape(2, capacity, units)
        share = choose(rows, router, experts, exp_dev * me + expert)[2]
        grads = all_g[expert, both].reshape(2 * capacity, width).astype(F32)
        grads = (share * grads).astype(BF16)
        all_g[expert, both] = grads.reshape(2, capacity, width)
        push = dot(grads, w_out[expert], 1, 1)
        product = jnp.sum(push * active.astype(F32), axis=-1, keepdims=True)
        product = jnp.transpose(jnp.broadcast_to(product, (2 * capacity, BLOCK)))
        for core in range(2):
            shares[expert, line * 2 + core] = product[:8, core * capacity : (core + 1) * capacity]
        mate_copy(2, expert, line).start()
        grad_u = (push * slope).astype(BF16)
        du[expert, both] = grad_u.reshape(2, capacity, units)
        part = dot(grad_u, w_in[expert], 1, 1).astype(BF16)
        parts[1, expert, both] = part.reshape(2, capacity, width)
        mate_copy(1, expert, line).start()
        part = dot(active, w_out[expert]).astype(BF16)
        parts[0, expert, both] = part.reshape(2, capacity, width)
        mate_copy(0, expert, line).start()

    def fold(array, expert, ahead):
        line = (my_line + ahead) % pairs
        mate_copy(array, expert, line).wait_recv()
        both = summed[array][expert, line * 2 + my_core].astype(F32) + mate_parts[array][
            expert, line
        ].astype(F32)
        summed[array][expert, line * 2 + my_core] = both.astype(summed[array].dtype)
        far_copy(array, expert, ahead).start()

    def whole(array, expert):
        mate_copy(array, expert, my_line).wait_recv()
        total = summed[array][expert, my_line * 2 + my_core].astype(F32) + mate_parts[array][
            expert, my_line
        ].astype(F32)
        for ahead in range(1, pairs):
            far_copy(array, expert, ahead).wait_recv()
            total = total + far_parts[array][expert, ahead - 1].astype(F32)
        return total

    back = [
        Exchange(
            ctx_count,
            exp_dev,
            most,
            (back_send.at[array], back_recv.at[array]),
            (
                lambda array: lambda expert, peer: returning.at[
                    array, forth.rows(expert * ctx_count + peer), :
                ]
            )(array),
            (
                lambda array: lambda expert, peer: home.at[
                    array, forth.rows(peer * exp_dev + expert), :
                ]
            )(array),
        )
        for array in range(2)
    ]

    def settle(expert):
        expert_rows = pl.ds(expert * ctx_count * most, ctx_count * most)
        rows = own_x[expert]
        probs, hot, share = choose(rows, router, experts, exp_dev * me + expert)
        product = jnp.transpose(whole(2, expert))[:, :1]
        grad_logits = (product * (hot - probs)).astype(BF16)
        grad_rows = whole(1, expert).astype(BF16).astype(F32) + dot(grad_logits, router, 1, 1)
        spread = cap_map(target_ref, expert, capacity)
        returning[1, expert_rows] = dot(spread, grad_rows.astype(BF16), 0, 0).astype(BF16)
        back[1].start(expert)
        router_part = dot(grad_logits, rows, 0, 0)[:experts]
        if expert == 0:
            grad_router_out[...] = router_part
        else:
            grad_router_out[...] += router_part

    for expert in range(exp_dev):
        early.finish(expert)
    for expert in range(exp_dev):
        forth.wait(expert)
        if expert + 1 < exp_dev:
            forth.start(expert + 1)
        own_x[expert] = dot(cap_map(target_ref, expert, capacity), incoming[expert]).astype(BF16)
        gather_x.begin(expert)
        all_x[expert, wsh_me] = own_x[expert]
        work(expert, 0)
        if expert:
            settle(expert - 1)
        for step in range(pairs - 1):
            gather_x.advance(expert, step)

        def others(ahead, carry):
            work(expert, ahead)
            return carry

        if pairs == 2:
            work(expert, 1)
        else:
            lax.fori_loop(1, pairs, others, 0)
        for ahead in range(1, pairs):
            fold(2, expert, ahead)
            fold(1, expert, ahead)
    settle(exp_dev - 1)
    for expert in range(exp_dev):
        forth.finish(expert)
        for ahead in range(1, pairs):
            fold(0, expert, ahead)

    def in_copy(expert):
        return pltpu.make_async_copy(stage_in, grad_in_out.at[expert], out_sems.at[1])

    one_stage = units == width
    out_stage = stage_in if one_stage else stage_out

    def out_copy(expert):
        return pltpu.make_async_copy(out_stage, grad_out_out.at[expert], out_sems.at[0])

    group = min(wsh_count, 4)

    def slot_sum(stage, left, right, expert):
        def part(turn):
            blocks = pl.ds(turn * group, group)
            return dot(
                left[expert, blocks].reshape(group * capacity, left.shape[3]),
                right[expert, blocks].reshape(group * capacity, right.shape[3]),
                0,
                0,
            )

        stage[...] = part(0)
        if wsh_count > group:

            def add(turn, carry):
                stage[...] += part(turn)
                return carry

            lax.fori_loop(1, wsh_count // group, add, 0)

    def grads_of(expert):
        if expert:
            (in_copy if one_stage else out_copy)(expert - 1).wait()
        slot_sum(out_stage, hid, all_g, expert)
        out_copy(expert).start()
        if one_stage:
            out_copy(expert).wait()
        elif expert:
            in_copy(expert - 1).wait()
        slot_sum(stage_in, all_x, du, expert)
        in_copy(expert).start()

    for expert in range(exp_dev):
        grads_of(expert)
        expert_rows = pl.ds(expert * ctx_count * most, ctx_count * most)
        spread = cap_map(target_ref, expert, capacity)
        out_rows = whole(0, expert).astype(BF16)
        returning[0, expert_rows] = dot(spread, out_rows, 0, 0).astype(BF16)
    grad_up = grad[...].astype(F32)
    for expert in range(exp_dev):
        back[1].wait(expert)
    grad_normed = dot(placement_of(slot_ref, experts * most), home[1], 0, 0)
    scaled = grad_normed * gain_two
    mean = jnp.mean(scaled * resid[...], axis=-1, keepdims=True)
    gain_part = jnp.sum(grad_normed * resid[...] * inv_two, axis=0, keepdims=True)
    grad_gain_out[...] = jnp.broadcast_to(gain_part, grad_gain_out.shape)
    grad_mid = grad_up + inv_two * scaled - resid[...] * inv_two * inv_two * inv_two * mean
    grad_mid_out[...] = grad_mid
    branch[home_row] = grad_mid.astype(BF16)

    if spread_here:
        gather_d = RowGather(counts, branch, (branch_send, branch_recv))
        gather_s = LineGather(
            "ctx",
            lines,
            across,
            [lambda block: stats.at[block]],
            [stats.at[me]],
            (stat_send, stat_recv),
        )
        gather_d.begin()
    for expert in range(exp_dev):
        back[0].start(expert)
    grad_heads = dot(branch[home_row], wo[...], 1, 1).astype(BF16)
    grad_heads_out[...] = grad_heads
    if spread_here:
        for own in range(2):
            heads[own] = grad_heads[own * BLOCK : (own + 1) * BLOCK]
    product = grad_heads.astype(F32) * exact_blocks[...].reshape(tokens, width)
    head_of = lax.broadcasted_iota(jnp.int32, (width, BLOCK), 0) // HEAD_DIM
    head_hot = (head_of == lane_ids(width, BLOCK)).astype(F32)
    delta = jnp.transpose(
        lax.dot_general(
            product, head_hot, (((1,), (0,)), ((), ())), precision=HIGH, preferred_element_type=F32
        )
    )
    for pair in range(PAIRS):
        stats[home_row, pair] = lse_rows[pair]
        stats[home_row, pair, 2:4, :] = delta[2 * pair : 2 * pair + 2, :]
    if spread_here:
        gather_s.begin(0)

    grad_wo_out[...] = dot(attn[...], branch[home_row], 0, 0).astype(BF16)

    plan_from = plan_start(2 * ctx_count)
    half = ctx_count

    def query_pair(pair, carry):
        pair_lanes = pl.ds(pl.multiple_of(pair * BLOCK, BLOCK), BLOCK)

        def tile(part, step):
            lanes = pl.ds(pl.multiple_of(part * width + pair * BLOCK, BLOCK), BLOCK)
            return qkv[plan_ref[plan_from + 4 + step], :, lanes]

        bias[...] = near_bias(base_ref, pair)
        for place in range(2):
            own = plan_ref[plan_from + place]
            stacked_q[place] = stack_heads(tile(0, 0 if place else half + 1))
            grads = stack_heads(heads[own, :, pair_lanes])
            stacked_g[place] = grads
            own_exact = exact_blocks[own, :, pair_lanes]
            product = grads.astype(F32) * jnp.concatenate([own_exact, own_exact], axis=0)
            delta_rep[place] = jnp.broadcast_to(
                jnp.sum(product, axis=-1, keepdims=True), (2 * BLOCK, BLOCK)
            )

        def score_grads(place, step, extra):
            keys = tile(1, step)
            part = dot(stacked_q[place], keys, 1, 1)
            if extra is not None:
                part = part + extra
            weights = jnp.exp(part - lse_all[pair, place])
            grad_s = weights * (dot(stacked_g[place], tile(2, step), 1, 1) - delta_rep[place])
            return grad_s, dot(grad_s.astype(BF16), keys)

        diagonal, big = score_grads(1, 0, bias[:, BLOCK:])
        beside, more = score_grads(1, 1, bias[:, :BLOCK])
        big = big + more
        far = jnp.zeros((2 * BLOCK, BLOCK), F32)
        for step in range(2, half + 1):
            grad_s, more = score_grads(1, step, None)
            far, big = far + grad_s, big + more
        grad_s, small_part = score_grads(0, half + 1, bias[:, BLOCK:])
        near[:, BLOCK:] = diagonal + grad_s
        for step in range(half + 2, 2 * half + 1):
            place = plan_ref[plan_from + 4 + 2 * half + 1 + step]
            later = place.astype(F32)
            sooner = 1.0 - later
            extra = None
            if step == half + 2:
                extra = bias[:, :BLOCK] * sooner
            grad_s, more = score_grads(place, step, extra)
            if step == half + 2:
                near[:, :BLOCK] = beside + grad_s * sooner
                far = far + grad_s * later
            else:
                far = far + grad_s
            big = big + more * later
            small_part = small_part + more * sooner
        second = plan_ref[plan_from].astype(F32)
        small_part, big = merge_heads(small_part), merge_heads(big)
        first = 1.0 - second
        dq_out[:BLOCK, pair_lanes] = (small_part * first + big * second).astype(BF16)
        dq_out[BLOCK:, pair_lanes] = (big * first + small_part * second).astype(BF16)
        put_sums(sums_out, pair, near, far)
        return carry

    def query_pairs(turn):
        share = PAIRS // (lines - 1)
        lax.fori_loop(turn * share, (turn + 1) * share, query_pair, 0)

    if spread_here:
        for step in range(lines - 1):
            query_pairs(step)
            gather_d.advance(step)
            gather_s.advance(0, step)
    for expert in range(exp_dev):
        back[0].wait(expert)
    token_out = dot(placement_of(slot_ref, experts * most), home[0], 0, 0)
    output_out[...] = (resid[...] + gate * token_out).astype(BF16)
    column = me % across
    upper = me // across // max(lines // 2, 1)

    def order(step):
        ahead, line = step // lines, step % lines
        line = line + upper * (lines - 1 - 2 * line)
        return line, ahead, line * across + (column + across - ahead) % across

    def put(slot, block):
        place = pl.ds(pl.multiple_of(block * tokens, tokens), tokens)
        return pltpu.make_async_copy(
            heads_stage.at[slot], heads_all_out.at[place, :], heads_sems.at[slot]
        )

    def heads_step(step, carry):
        line, ahead, block = order(step)
        slot = step % 2
        for skip in range(1, across):

            @pl.when(ahead == skip)
            def _():
                gather_d.wait_cross(line, skip)
                gather_s.cross_recv(0, line, skip).wait_recv()

        @pl.when(step >= 2)
        def _():
            put(slot, order(step - 2)[2]).wait()

        heads_stage[slot] = dot(branch[block], wo[...], 1, 1).astype(BF16)
        put(slot, block).start()
        return carry

    if spread_here:
        lax.fori_loop(0, ctx_count, heads_step, 0)
    stats_copy = pltpu.make_async_copy(stats, stats_out, fetch_sems.at[0])
    stats_copy.start()
    if spread_here:
        for step in (ctx_count - 2, ctx_count - 1):
            put(step % 2, order(step)[2]).wait()
    else:
        heads_stage[0] = branch[0]
        own_branch = pltpu.make_async_copy(heads_stage.at[0], heads_all_out, heads_sems.at[0])
        own_branch.start()
        own_branch.wait()
    if not one_stage:
        out_copy(exp_dev - 1).wait()
    in_copy(exp_dev - 1).wait()
    stats_copy.wait()
    for expert in range(exp_dev):
        for array in range(2):
            back[array].finish(expert)
        for array in range(3):
            for line in range(pairs):
                mate_copy(array, expert, line).wait_send()
            for ahead in range(1, pairs):
                far_copy(array, expert, ahead).wait_send()
    gather_x.finish()
    if spread_here:
        gather_d.finish()
        gather_s.finish()


def middle(
    counts,
    experts,
    attn,
    exact,
    hidden,
    grad,
    weights,
    w_in,
    w_out,
    small,
    slots,
    targets,
    lse_rows,
    routes,
    base,
    plan,
    qkv,
    capacity,
):
    ctx_count, wsh_count = counts
    tokens, width = hidden.shape
    exp_dev = w_in.shape[0]
    units = w_in.shape[2]
    slot_count = targets.shape[1]
    all_slots = experts * (slot_count // ctx_count)
    lines, across = grid_of(ctx_count)
    pairs = wsh_count // 2
    vmem = pl.BlockSpec(memory_space=pltpu.VMEM)
    anywhere = pl.BlockSpec(memory_space=pl.ANY)
    slot_rows = (exp_dev, wsh_count, capacity)
    spread_here = wsh_count <= 4
    held = ctx_count if spread_here else 1
    score_rows = NEAR if spread_here else 16
    forward = forward_scratch(2 * ctx_count) if spread_here else [pltpu.VMEM((8, BLOCK), F32)] * 8
    return pl.pallas_call(
        functools.partial(middle_kernel, counts, experts, spread_here),
        in_specs=[anywhere] * 7
        + [vmem] * 6
        + [pl.BlockSpec(memory_space=pltpu.SMEM), anywhere],
        out_specs=[vmem] * 3 + [anywhere] * 2 + [vmem] * 5 + [anywhere] * 2,
        out_shape=[
            jax.ShapeDtypeStruct((tokens, width), BF16),
            jax.ShapeDtypeStruct((tokens, width), F32),
            jax.ShapeDtypeStruct((tokens, width), BF16),
            jax.ShapeDtypeStruct((tokens * held, width), BF16),
            jax.ShapeDtypeStruct((held, PAIRS, 8, tokens), F32),
            jax.ShapeDtypeStruct((width, width), BF16),
            jax.ShapeDtypeStruct((experts, width), F32),
            jax.ShapeDtypeStruct((8, width), F32),
            jax.ShapeDtypeStruct((tokens if spread_here else 16, width), BF16),
            jax.ShapeDtypeStruct((PAIRS, 8, SPAN), F32),
            jax.ShapeDtypeStruct((exp_dev, width, units), F32),
            jax.ShapeDtypeStruct((exp_dev, units, width), F32),
        ],
        scratch_shapes=[
            pltpu.VMEM(qkv.shape if spread_here else (1, 16, BLOCK), BF16),
            pltpu.VMEM((PAIRS, 2, NEAR, BLOCK) if spread_here else (1, 2, 8, BLOCK), F32),
            pltpu.VMEM((2, score_rows, BLOCK), BF16),
            pltpu.VMEM((2, score_rows, BLOCK), BF16),
            pltpu.VMEM((2, score_rows, BLOCK), F32),
            pltpu.VMEM((score_rows, NEAR), F32),
            pltpu.VMEM((score_rows, NEAR), F32),
            *forward[1:4],
            *forward[5:],
            pltpu.VMEM((PAIRS, 8, tokens), F32),
            pltpu.VMEM((exp_dev, capacity, width), BF16),
            pltpu.VMEM((exp_dev, slot_count, width), BF16),
            pltpu.VMEM((tokens, width), BF16),
            pltpu.VMEM((2, BLOCK if spread_here else 16, width), BF16),
            pltpu.VMEM((2, BLOCK, width), F32),
            pltpu.VMEM((tokens, width), BF16),
            pltpu.VMEM((tokens, width), BF16),
            pltpu.VMEM((width, width), BF16),
            pltpu.VMEM(w_in.shape, BF16),
            pltpu.VMEM(w_out.shape, BF16),
            pltpu.VMEM((tokens, width), F32),
            pltpu.VMEM((exp_dev, slot_count, width), BF16),
            pltpu.VMEM((exp_dev, capacity, width), BF16),
            pltpu.VMEM((*slot_rows, width), BF16),
            pltpu.VMEM((*slot_rows, width), BF16),
            pltpu.VMEM((*slot_rows, units), BF16),
            pltpu.VMEM((*slot_rows, units), BF16),
            pltpu.VMEM((2, *slot_rows, width), BF16),
            pltpu.VMEM((2, exp_dev, pairs, capacity, width), BF16),
            pltpu.VMEM((2, exp_dev, max(pairs - 1, 1), capacity, width), BF16),
            pltpu.VMEM((exp_dev, wsh_count, 8, capacity), F32),
            pltpu.VMEM((exp_dev, pairs, 8, capacity), F32),
            pltpu.VMEM((exp_dev, max(pairs - 1, 1), 8, capacity), F32),
            pltpu.VMEM((2, all_slots, width), BF16),
            pltpu.VMEM((2, all_slots, width), BF16),
            pltpu.VMEM((held, tokens, width), BF16),
            pltpu.VMEM((held, PAIRS, 8, tokens), F32),
            pltpu.VMEM((width, units), F32),
            pltpu.VMEM((8, BLOCK) if units == width else (units, width), F32),
            pltpu.VMEM((2, tokens, width), BF16),
            pltpu.SemaphoreType.DMA((9,)),
            pltpu.SemaphoreType.DMA((2,)),
            pltpu.SemaphoreType.DMA((2,)),
            *gather_sems(exp_dev, pairs, 2),
            *gather_sems(exp_dev, pairs, 2),
            *exchange_sems(ctx_count, exp_dev),
            *exchange_sems(ctx_count, exp_dev),
            pltpu.SemaphoreType.DMA((2, exp_dev, ctx_count - 1)),
            pltpu.SemaphoreType.DMA((2, exp_dev, ctx_count - 1)),
            pltpu.SemaphoreType.DMA((3, exp_dev, pairs)),
            pltpu.SemaphoreType.DMA((3, exp_dev, pairs)),
            pltpu.SemaphoreType.DMA((3, exp_dev, max(pairs - 1, 1))),
            pltpu.SemaphoreType.DMA((3, exp_dev, max(pairs - 1, 1))),
            *gather_sems(row_parts(ctx_count, tokens), lines, across),
            *gather_sems(1, lines, across),
        ],
        compiler_params=pltpu.CompilerParams(
            collective_id=1, has_side_effects=True, vmem_limit_bytes=(62 if spread_here else 63) << 20
        ),
        name="middle",
    )(
        attn,
        exact,
        hidden,
        grad,
        weights,
        w_in,
        w_out,
        small,
        slots,
        targets,
        lse_rows,
        routes,
        base,
        plan,
        qkv,
    )


class Tiles:
    def __init__(self, plan_ref, blocks, keys):
        self.plan, self.blocks, self.half = plan_ref, blocks, blocks // 2
        self.start = plan_start(blocks)
        self.rows_from = self.start + 4 + (2 * (blocks + 1) if keys else 0)
        self.keys = keys
        self.count = blocks + 1

    def own(self, place):
        return self.plan[self.start + (1 - place if self.keys else place)]

    def own_step(self, place):
        return 0 if place else self.half + 1

    def row(self, step):
        return self.plan[self.rows_from + step]

    def place(self, step):
        if step <= self.half:
            return 1
        if step == self.half + 1:
            return 0
        return self.plan[self.start + 4 + self.blocks + 1 + step]

    def groups(self):
        found, step = [], 0
        while step <= self.half:
            size = 2 if step + 1 <= self.half else 1
            found.append((step, size))
            step += size
        return found + [(step, 1) for step in range(self.half + 1, self.count)]


def span(step, size=1):
    return slice(step * BLOCK, (step + size) * BLOCK)


def share_of(place, wanted):
    return place.astype(F32) if wanted else 1.0 - place.astype(F32)


def only(place, wanted, value):
    if isinstance(place, int):
        return value if place == wanted else jnp.zeros_like(value)
    return value * share_of(place, wanted).astype(value.dtype)


def order_bias(bias, step, size, place, half):
    if step == 0:
        return bias[:, : size * BLOCK]
    if step == half + 1:
        return bias[:, :BLOCK]
    if step == half + 2:
        return bias[:, BLOCK:] * share_of(place, 0)
    return None


def forward_pair(tiles, load, bias, stacked, keys, scores, tops, totals, weights, values, others):
    half, count = tiles.half, tiles.count
    lowest = jnp.full((NEAR, BLOCK), MASKED, F32)
    for place in range(2):
        stacked[place] = stack_heads(load(0, tiles.row(tiles.own_step(place))))
    for step in range(count):
        row = tiles.row(step)
        keys[span(step), :] = load(1, row)
        tile, place = load(2, row), tiles.place(step)
        values[span(step), :] = only(place, 1, tile)
        if step > half:
            others[span(step - half - 1), :] = only(place, 0, tile)
    best = [lowest, lowest]
    for step, size in tiles.groups():
        place = tiles.place(step)
        part = dot(stacked[place], keys[span(step, size), :], 1, 1)
        extra = order_bias(bias, step, size, place, half)
        if extra is not None:
            part = part + extra
        scores[:, span(step, size)] = part
        part = fold_lanes(part, jnp.maximum) if size == 2 else part
        for wanted in range(2):
            if isinstance(place, int):
                if place == wanted:
                    best[wanted] = jnp.maximum(best[wanted], part)
            else:
                share = share_of(place, wanted)
                best[wanted] = jnp.maximum(best[wanted], part * share + MASKED * (1.0 - share))
    for wanted in range(2):
        top = jnp.max(best[wanted], axis=-1, keepdims=True)
        tops[wanted] = jnp.broadcast_to(top, (NEAR, BLOCK))
    total = [jnp.zeros((NEAR, BLOCK), F32)] * 2
    for step in range(count):
        place = tiles.place(step)
        part = jnp.exp(scores[:, span(step)] - tops[place])
        high = part.astype(BF16)
        weights[:NEAR, span(step)] = high
        weights[NEAR:, span(step)] = (part - high.astype(F32)).astype(BF16)
        for wanted in range(2):
            if not isinstance(place, int) or place == wanted:
                total[wanted] = total[wanted] + only(place, wanted, part)
    results = []
    for wanted in range(2):
        whole = jnp.sum(total[wanted], axis=-1, keepdims=True)
        if wanted:
            summed = dot(weights[...], values[...])
        else:
            summed = dot(weights[:, span(half + 1, count - half - 1)], others[...])
        main = summed[:NEAR] / whole
        exact = main + summed[NEAR:] / whole
        totals[wanted] = tops[wanted] + jnp.log(jnp.broadcast_to(whole, (NEAR, BLOCK)))
        results.append((merge_heads(main).astype(BF16), merge_heads(exact)))
    return results


def in_order(tiles, pair):
    kind = pair[0].dtype
    second = tiles.own(0).astype(F32)
    first, second = (1.0 - second).astype(kind), second.astype(kind)
    return pair[0] * first + pair[1] * second, pair[1] * first + pair[0] * second


def forward_kernel(
    plan_ref, q_ref, k_ref, v_ref, base_ref, out_ref, exact_ref, lse_ref, row_ref, bias, *scratch
):
    blocks = q_ref.shape[0] // BLOCK
    tiles = Tiles(plan_ref, blocks, False)
    refs = (q_ref, k_ref, v_ref)
    near = near_bias(base_ref)
    bias[...] = jnp.concatenate([near[:, BLOCK:], near[:, :BLOCK]], axis=1)
    totals = scratch[4]

    def load(part, row):
        return refs[part][rows_at(row), :]

    results = forward_pair(tiles, load, bias, *scratch)
    main = in_order(tiles, [result[0] for result in results])
    exact = in_order(tiles, [result[1] for result in results])
    lse = in_order(tiles, [totals[0], totals[1]])
    for own in range(2):
        rows = pl.ds(own * BLOCK, BLOCK)
        out_ref[rows, :] = main[own]
        exact_ref[rows, :] = exact[own]
        lse_ref[0, own] = lse[own]
        turned = jnp.transpose(lse[own])
        for head in range(2):
            row_ref[0, head : head + 1, own * BLOCK : (own + 1) * BLOCK] = turned[
                :1, head * BLOCK : (head + 1) * BLOCK
            ]
    row_ref[0, 2:8, :] = jnp.zeros((6, NEAR), F32)


def forward_scratch(blocks):
    count = blocks + 1
    rest = count - blocks // 2 - 1
    return [
        pltpu.VMEM((2, NEAR, BLOCK), BF16),
        pltpu.VMEM((count * BLOCK, BLOCK), BF16),
        pltpu.VMEM((NEAR, count * BLOCK), F32),
        pltpu.VMEM((2, NEAR, BLOCK), F32),
        pltpu.VMEM((2, NEAR, BLOCK), F32),
        pltpu.VMEM((2 * NEAR, count * BLOCK), BF16),
        pltpu.VMEM((count * BLOCK, BLOCK), BF16),
        pltpu.VMEM((rest * BLOCK, BLOCK), BF16),
    ]


def pair_specs(rows, width):
    pairs = width // BLOCK

    def column(offset):
        return pl.BlockSpec((rows, BLOCK), lambda pair, plan: (0, offset + pair))

    return [column(0), column(pairs), column(2 * pairs)]


def attend_forward(plan, qkv, base, width):
    rows = qkv.shape[0]
    own = pl.BlockSpec((NEAR, BLOCK), lambda pair, plan: (0, pair))
    return pl.pallas_call(
        forward_kernel,
        grid_spec=pltpu.PrefetchScalarGridSpec(
            num_scalar_prefetch=1,
            grid=(PAIRS,),
            in_specs=pair_specs(rows, width)
            + [pl.BlockSpec((1, 8, SPAN), lambda pair, plan: (pair, 0, 0))],
            out_specs=[
                own,
                own,
                pl.BlockSpec((1, 2, NEAR, BLOCK), lambda pair, plan: (pair, 0, 0, 0)),
                pl.BlockSpec((1, 8, NEAR), lambda pair, plan: (pair, 0, 0)),
            ],
            scratch_shapes=[pltpu.VMEM((NEAR, NEAR), F32), *forward_scratch(rows // BLOCK)],
        ),
        out_shape=[
            jax.ShapeDtypeStruct((NEAR, width), BF16),
            jax.ShapeDtypeStruct((NEAR, width), F32),
            jax.ShapeDtypeStruct((PAIRS, 2, NEAR, BLOCK), F32),
            jax.ShapeDtypeStruct((PAIRS, 8, NEAR), F32),
        ],
        compiler_params=pltpu.CompilerParams(vmem_limit_bytes=60 << 20),
        name="attend_forward",
    )(plan, qkv, qkv, qkv, base)


def put_sums(sums_ref, place, near_ref, far):
    row_ids = lax.broadcasted_iota(jnp.int32, (BLOCK, SPAN), 0)
    for head in range(2):
        part = near_ref[head * BLOCK : (head + 1) * BLOCK, :]
        part = jnp.concatenate([part, jnp.zeros((BLOCK, BLOCK), F32)], axis=1)
        for bit in range(BLOCK.bit_length() - 1):
            moved = pltpu.roll(part, SPAN - (1 << bit), 1)
            part = jnp.where((row_ids >> bit) & 1 == 1, moved, part)
        sums_ref[place, head : head + 1, :] = jnp.sum(part, axis=0, keepdims=True)
        far_part = jnp.sum(far[head * BLOCK : (head + 1) * BLOCK], axis=0, keepdims=True)
        sums_ref[place, 2 + head : 3 + head, :] = jnp.concatenate(
            [far_part, jnp.zeros((1, NEAR), F32)], axis=1
        )
    sums_ref[place, 4:8, :] = jnp.zeros((4, SPAN), F32)


def query_kernel(
    plan_ref, q_ref, k_ref, v_ref, base_ref, do_ref, exact_ref, lse_ref, dq_ref, sums_ref, bias_ref, near_ref
):
    bias_ref[...] = near_bias(base_ref)
    lanes = lane_ids(2 * BLOCK, NEAR)
    far = jnp.zeros((2 * BLOCK, BLOCK), F32)
    for own in range(2):
        block = plan_ref[own]
        rows = pl.ds(own * BLOCK, BLOCK)
        stacked = stack_heads(q_ref[rows_at(plan_ref[SOURCE + 1 + block]), :])
        grads = stack_heads(do_ref[rows, :])
        exact = exact_ref[rows, :]
        product = grads.astype(F32) * jnp.concatenate([exact, exact], axis=0)
        delta = jnp.sum(product, axis=-1, keepdims=True)
        lse = lse_ref[0, own][:, :1]

        def grad_scores(scores, start):
            weights = jnp.exp(scores - lse)
            return weights * (dot(grads, two_tiles(v_ref, plan_ref, start), 1, 1) - delta)

        scores = dot(stacked, two_tiles(k_ref, plan_ref, block), 1, 1) + bias_ref[...]
        scores = jnp.where(lanes + block * BLOCK < BLOCK, MASKED, scores)
        near = grad_scores(scores, block)
        if own == 0:
            near_ref[...] = near
        else:
            near_ref[...] += near

        def step(chunk, carry):
            grad_q, far = carry
            start = block - 2 * chunk
            keys = two_tiles(k_ref, plan_ref, start)
            part = dot(stacked, keys, 1, 1)
            part = jnp.where(lanes + start * BLOCK < BLOCK, MASKED, part)
            grad_s = grad_scores(part, start)
            return (grad_q + dot(grad_s.astype(BF16), keys), far + fold_lanes(grad_s, jnp.add))

        grad_q, far = lax.fori_loop(
            1,
            jnp.maximum(block, 1) // 2 + 1,
            step,
            (dot(near.astype(BF16), two_tiles(k_ref, plan_ref, block)), far),
        )
        dq_ref[rows, :] = merge_heads(grad_q).astype(BF16)
    put_sums(sums_ref, 0, near_ref, far)


def attend_queries(plan, qkv, base, grad_out, exact, lse):
    rows, width = qkv.shape[0], grad_out.shape[1]
    own = pl.BlockSpec((NEAR, BLOCK), lambda pair, plan: (0, pair))
    row_spec = pl.BlockSpec((1, 8, SPAN), lambda pair, plan: (pair, 0, 0))
    return pl.pallas_call(
        query_kernel,
        grid_spec=pltpu.PrefetchScalarGridSpec(
            num_scalar_prefetch=1,
            grid=(PAIRS,),
            in_specs=pair_specs(rows, width)
            + [
                row_spec,
                own,
                own,
                pl.BlockSpec((1, 2, NEAR, BLOCK), lambda pair, plan: (pair, 0, 0, 0)),
            ],
            out_specs=[own, row_spec],
            scratch_shapes=[pltpu.VMEM((NEAR, NEAR), F32), pltpu.VMEM((NEAR, NEAR), F32)],
        ),
        out_shape=[
            jax.ShapeDtypeStruct((NEAR, width), BF16),
            jax.ShapeDtypeStruct((PAIRS, 8, SPAN), F32),
        ],
        compiler_params=pltpu.CompilerParams(vmem_limit_bytes=60 << 20),
        name="attend_queries",
    )(plan, qkv, qkv, qkv, base, grad_out, exact, lse)


def key_pair(tiles, load, stat, bias, mine, queries, grads, rest_q, rest_g, stats, grad_s, weights):
    half, count = tiles.half, tiles.count
    for place in range(2):
        for part in range(2):
            mine[part, place] = stack_heads(load(1 + part, tiles.row(tiles.own_step(place))))
    for step in range(count):
        row, place = tiles.row(step), tiles.place(step)
        for part, whole, rest in ((0, queries, rest_q), (3, grads, rest_g)):
            tile = load(part, row)
            whole[0, span(step), :] = tile
            whole[1, span(step), :] = only(place, 1, tile)
            if step > half:
                rest[span(step - half - 1), :] = only(place, 0, tile)
        stats[:, span(step)] = stat(row)
    for step, size in tiles.groups():
        place = tiles.place(step)
        scores = dot(mine[0, place], queries[0, span(step, size), :], 1, 1)
        extra = order_bias(bias, step, size, place, half)
        if extra is not None:
            scores = scores + extra
        push = dot(mine[1, place], grads[0, span(step, size), :], 1, 1)
        for head in range(2):
            rows = slice(head * BLOCK, (head + 1) * BLOCK)
            part = jnp.exp(scores[rows] - stats[head : head + 1, span(step, size)])
            weights[rows, span(step, size)] = part.astype(BF16)
            part = part * (push[rows] - stats[2 + head : 3 + head, span(step, size)])
            grad_s[rows, span(step, size)] = part.astype(BF16)
    tail = span(half + 1, count - half - 1)
    grad_k = (dot(grad_s[:, tail], rest_q[...]), dot(grad_s[...], queries[1]))
    grad_v = (dot(weights[:, tail], rest_g[...]), dot(weights[...], grads[1]))
    return [
        [merge_heads(part).astype(BF16) for part in grad] for grad in (grad_k, grad_v)
    ]


def key_kernel(plan_ref, q_ref, k_ref, v_ref, base_ref, do_ref, stats_ref, *refs):
    passed = (len(refs) - 11) // 2
    passed_in, outs, passed_out = (
        refs[:passed],
        refs[passed : passed + 2],
        refs[passed + 2 : 2 * passed + 2],
    )
    bias, *scratch = refs[2 * passed + 2 :]
    for src, dst in zip(passed_in, passed_out):
        dst[...] = src[...]
    blocks = q_ref.shape[0] // BLOCK
    tiles = Tiles(plan_ref, blocks, True)
    tile_refs = (q_ref, k_ref, v_ref, do_ref)
    bias[...] = near_bias(base_ref)

    def load(part, row):
        return tile_refs[part][rows_at(row), :]

    def stat(row):
        return stats_ref[row // 2, 0, :, rows_at(row % 2)]

    for out, grad in zip(outs, key_pair(tiles, load, stat, bias, *scratch)):
        for own, part in enumerate(in_order(tiles, grad)):
            out[own * BLOCK : (own + 1) * BLOCK, :] = part


def key_scratch(blocks):
    count = blocks + 1
    rest = count - blocks // 2 - 1
    return [
        pltpu.VMEM((2, 2, NEAR, BLOCK), BF16),
        pltpu.VMEM((2, count * BLOCK, BLOCK), BF16),
        pltpu.VMEM((2, count * BLOCK, BLOCK), BF16),
        pltpu.VMEM((rest * BLOCK, BLOCK), BF16),
        pltpu.VMEM((rest * BLOCK, BLOCK), BF16),
        pltpu.VMEM((8, count * BLOCK), F32),
        pltpu.VMEM((NEAR, count * BLOCK), BF16),
        pltpu.VMEM((NEAR, count * BLOCK), BF16),
    ]


def attend_keys(plan, qkv, base, grad_out, stats, passed):
    rows, width = grad_out.shape
    own = pl.BlockSpec((NEAR, BLOCK), lambda pair, plan: (0, pair))
    pieces = [own] + [
        pl.BlockSpec(
            (array.shape[0], array.shape[1] // PAIRS, array.shape[2]), lambda pair, plan: (0, pair, 0)
        )
        for array in passed[1:]
    ]
    return pl.pallas_call(
        key_kernel,
        grid_spec=pltpu.PrefetchScalarGridSpec(
            num_scalar_prefetch=1,
            grid=(PAIRS,),
            in_specs=pair_specs(rows, width)
            + [
                pl.BlockSpec((1, 8, SPAN), lambda pair, plan: (pair, 0, 0)),
                pl.BlockSpec((rows, BLOCK), lambda pair, plan: (0, pair)),
                pl.BlockSpec(
                    (rows // NEAR, 1, 8, NEAR), lambda pair, plan: (0, pair, 0, 0)
                ),
            ]
            + pieces,
            out_specs=[own, own] + pieces,
            scratch_shapes=[pltpu.VMEM((NEAR, NEAR), F32), *key_scratch(rows // BLOCK)],
        ),
        out_shape=[jax.ShapeDtypeStruct((NEAR, width), BF16)] * 2
        + [jax.ShapeDtypeStruct(array.shape, array.dtype) for array in passed],
        compiler_params=pltpu.CompilerParams(vmem_limit_bytes=60 << 20),
        name="attend_keys",
    )(plan, qkv, qkv, qkv, base, grad_out, stats, *passed)


BITS = {"core": ("wsh", 1), "x": ("wsh", 2), "y": ("ctx", 1), "near": ("ctx", 2), "far": ("ctx", 4)}
ORDERS = (
    ("core", "x", "near", "y", "far"),
    ("core", "x", "y", "near", "far"),
    ("core", "y", "near", "x", "far"),
    ("core", "near", "y", "x", "far"),
)


def halved_shapes(order, share, width):
    shapes, blocks, rows, columns = [], 4, share, width
    for name in order:
        if name in ("core", "x"):
            blocks //= 2
        elif name == "y":
            columns //= 2
        else:
            rows //= 2
        shapes.append((blocks, rows, columns))
    return shapes


def partner(name):
    axis, bit = BITS[name]
    me = lax.axis_index(axis)
    side = (me // bit) % 2
    return axis, me + bit * (1 - 2 * side), side


def tail_kernel(
    experts,
    dq_ref,
    dk_ref,
    dv_ref,
    hidden_ref,
    grad_mid_ref,
    weights_ref,
    grad_wo_ref,
    small_ref,
    router_ref,
    gain_ref,
    sums_ref,
    hot_ref,
    input_grad_out,
    shares_out,
    router_out,
    gains_out,
    table_out,
    weights,
    hidden,
    grad_mid,
    grad_wo,
    total,
    gathered,
    pack,
    pack_recv,
    *rest,
):
    steps = len(BITS)
    sends = [rest[matrix * steps : (matrix + 1) * steps] for matrix in range(4)]
    rest = rest[4 * steps :]
    recvs = [rest[matrix * steps : (matrix + 1) * steps] for matrix in range(4)]
    fetch_sems, half_send, half_recv, whole_send, whole_recv, pack_send, pack_sem = rest[4 * steps :]
    tokens, width = dq_ref.shape
    share = total.shape[2]
    sources = (
        (hidden_ref, hidden),
        (grad_wo_ref, grad_wo),
        (weights_ref.at[pl.ds(0, 3)], weights),
        (grad_mid_ref, grad_mid),
    )
    fetches = [
        pltpu.make_async_copy(src, dst, fetch_sems.at[place])
        for place, (src, dst) in enumerate(sources)
    ]
    for fetch in fetches:
        fetch.start()
    barrier = pltpu.get_barrier_semaphore()
    for name in BITS:
        axis, peer, side = partner(name)
        pl.semaphore_signal(
            barrier, inc=1, device_id={axis: peer}, device_id_type=pl.DeviceIdType.MESH
        )
    pl.semaphore_wait(barrier, steps)

    def remote(source, target, send, recv, name):
        axis, peer, side = partner(name)
        return pltpu.make_async_remote_copy(
            src_ref=source,
            dst_ref=target,
            send_sem=send,
            recv_sem=recv,
            device_id={axis: peer},
            device_id_type=pl.DeviceIdType.MESH,
        )

    regions = []
    for order in ORDERS:
        blocks, row, column, kept = [0, 1, 2, 3], 0, 0, []
        rows, columns = share, width
        for name in order:
            side = partner(name)[2]
            if name == "core":
                pair = [(line * 2 + side, line * 2 + 1 - side) for line in range(2)]
                keep = ([a for a, b in pair], row, column)
                sent = ([b for a, b in pair], row, column)
            elif name == "x":
                core = partner("core")[2]
                keep = ([side * 2 + core], row, column)
                sent = ([(1 - side) * 2 + core], row, column)
            elif name == "y":
                columns //= 2
                keep = (blocks, row, column + side * columns)
                sent = (blocks, row, column + (1 - side) * columns)
            else:
                rows //= 2
                keep = (blocks, row + side * rows, column)
                sent = (blocks, row + (1 - side) * rows, column)
            blocks, row, column = keep
            kept.append((keep, sent))
        regions.append(kept)

    def spans(matrix, step, region):
        shape = sends[matrix][step].shape
        blocks, row, column = region
        row_part = pl.ds(row if isinstance(row, int) else pl.multiple_of(row, 16), shape[1])
        column_part = pl.ds(
            column if isinstance(column, int) else pl.multiple_of(column, BLOCK), shape[2]
        )
        return blocks, row_part, column_part

    def half_copy(matrix, step):
        return remote(
            sends[matrix][step],
            recvs[matrix][step],
            half_send.at[matrix, step],
            half_recv.at[matrix, step],
            ORDERS[matrix][step],
        )

    def give(matrix, step):
        blocks, row_part, column_part = spans(matrix, step, regions[matrix][step][1])
        for place, block in enumerate(blocks):
            sends[matrix][step][place] = total[matrix, block, row_part, column_part].astype(BF16)
        half_copy(matrix, step).start()

    def take(matrix, step):
        half_copy(matrix, step).wait_recv()
        blocks, row_part, column_part = spans(matrix, step, regions[matrix][step][0])
        for place, block in enumerate(blocks):
            total[matrix, block, row_part, column_part] += recvs[matrix][step][place].astype(F32)

    def whole_view(matrix, step):
        keep = regions[matrix][step][0]
        blocks, row_part, column_part = spans(matrix, step, keep)
        return gathered.at[matrix, row_part, column_part]

    wholes = [[name for name in order if BITS[name][0] == "ctx"] for order in ORDERS]

    def whole_copy(matrix, back):
        name = wholes[matrix][2 - back]
        step = ORDERS[matrix].index(name)
        blocks, row, column = regions[matrix][step][0]
        shape = sends[matrix][step].shape
        row_part = pl.ds(row if isinstance(row, int) else pl.multiple_of(row, 16), shape[1])
        column_part = pl.ds(
            column if isinstance(column, int) else pl.multiple_of(column, BLOCK), shape[2]
        )
        view = gathered.at[matrix, row_part, column_part]
        return remote(view, view, whole_send.at[matrix, back], whole_recv.at[matrix, back], name)

    fetches[0].wait()
    resid = hidden[...].astype(F32)
    inv = lax.rsqrt(jnp.mean(resid * resid, axis=-1, keepdims=True) + epsilon)
    gain = jnp.transpose(small_ref[...].astype(F32))[experts : experts + 1, :]
    normed = (resid * inv * gain).astype(BF16)
    for matrix, ref in ((1, dq_ref), (2, dk_ref), (3, dv_ref)):
        part = dot(normed, ref[...], 0, 0)
        for block in range(4):
            total[matrix, block] = part[block * share : (block + 1) * share]
        give(matrix, 0)
    fetches[1].wait()
    for block in range(4):
        total[0, block] = grad_wo[block * share : (block + 1) * share, :].astype(F32)
    give(0, 0)
    fetches[2].wait()
    grad_normed = dot(dq_ref[...], weights[0], 1, 1)
    grad_normed = grad_normed + dot(dk_ref[...], weights[1], 1, 1)
    grad_normed = grad_normed + dot(dv_ref[...], weights[2], 1, 1)
    pack[...] = jnp.zeros_like(pack)
    pack[:experts, :] = router_ref[...]
    pack[experts : experts + 1, :] = jnp.sum(grad_normed * resid * inv, axis=0, keepdims=True)
    pack[experts + 1 : experts + 2, :] = gain_ref[0:1, :]
    last = lane_ids(2, BLOCK) == hot_ref.shape[1] - 1
    for pair in range(PAIRS):
        near = lax.dot_general(
            sums_ref[pair, 0:2, :],
            hot_ref[...],
            (((1,), (0,)), ((), ())),
            precision=HIGH,
            preferred_element_type=F32,
        )
        near = jnp.concatenate([near, jnp.zeros((2, BLOCK - near.shape[1]), F32)], axis=1)
        distant = jnp.sum(sums_ref[pair, 2:4, :], axis=1, keepdims=True)
        place = experts + 8 + 2 * pair
        pack[place : place + 2, :BLOCK] = near + jnp.where(last, distant, 0.0)

    def pack_copy(step):
        return remote(
            pack_recv.at[0, step],
            pack_recv.at[1, step],
            pack_send.at[step],
            pack_sem.at[step],
            list(BITS)[step],
        )

    for step in range(steps):
        pack_recv[0, step] = pack[...]
        pack_copy(step).start()
        for matrix in (1, 2, 3, 0):
            take(matrix, step)
            if step + 1 < steps:
                give(matrix, step + 1)
        if step == 0:
            fetches[3].wait()
            scaled = grad_normed * gain
            mean = jnp.mean(scaled * resid, axis=-1, keepdims=True)
            grad_in = grad_mid[...] + inv * scaled - resid * inv * inv * inv * mean
            input_grad_out[...] = grad_in.astype(BF16)
        pack_copy(step).wait_recv()
        pack[...] += pack_recv[1, step]

    mine = lax.axis_index("wsh")
    for matrix in range(4):
        keep = regions[matrix][steps - 1][0]
        blocks, row_part, column_part = spans(matrix, steps - 1, keep)
        gathered[matrix, row_part, column_part] = total[
            matrix, blocks[0], row_part, column_part
        ].astype(BF16)
        whole_copy(matrix, 0).start()
    for back in range(3):
        for matrix in range(4):
            whole_copy(matrix, back).wait_recv()
            if back < 2:
                whole_copy(matrix, back + 1).start()
            else:
                shares_out[matrix] = gathered[matrix]
        if back == 0:
            buckets = table_out.shape[0]
            for block in range(4):

                @pl.when(mine == block)
                def _():
                    rows = pack[: experts + 8, block * share : (block + 1) * share]
                    turned = jnp.transpose(rows)
                    router_out[...] = turned[:, :experts]
                    gains_out[...] = rows[experts : experts + 8]
                    table = jnp.transpose(pack[experts + 8 :, :BLOCK])
                    table_out[...] = table[block * buckets : (block + 1) * buckets, :HEADS]

    for step in range(steps):
        pack_copy(step).wait_send()
        for matrix in range(4):
            half_copy(matrix, step).wait_send()
    for back in range(3):
        for matrix in range(4):
            whole_copy(matrix, back).wait_send()


def tail(experts, dq, dk, dv, hidden, grad_mid, weights, grad_wo, small, router, gains, sums, hot, share, buckets):
    tokens, width = dq.shape
    vmem = pl.BlockSpec(memory_space=pltpu.VMEM)
    anywhere = pl.BlockSpec(memory_space=pl.ANY)
    steps = len(BITS)
    pieces = [shape for order in ORDERS for shape in halved_shapes(order, share, width)]
    buffers = [pltpu.VMEM(shape, BF16) for shape in pieces]
    rows = experts + 8 + 16
    dma = pltpu.SemaphoreType.DMA
    return pl.pallas_call(
        functools.partial(tail_kernel, experts),
        in_specs=[vmem] * 3 + [anywhere] * 4 + [vmem] * 5,
        out_specs=[vmem] * 5,
        out_shape=[
            jax.ShapeDtypeStruct((tokens, width), BF16),
            jax.ShapeDtypeStruct((4, share, width), BF16),
            jax.ShapeDtypeStruct((share, experts), F32),
            jax.ShapeDtypeStruct((8, share), F32),
            jax.ShapeDtypeStruct((buckets, HEADS), F32),
        ],
        scratch_shapes=[
            pltpu.VMEM((3, width, width), BF16),
            pltpu.VMEM((tokens, width), BF16),
            pltpu.VMEM((tokens, width), F32),
            pltpu.VMEM((width, width), BF16),
            pltpu.VMEM((4, 4, share, width), F32),
            pltpu.VMEM((4, share, width), BF16),
            pltpu.VMEM((rows, width), F32),
            pltpu.VMEM((2, steps, rows, width), F32),
            *buffers,
            *buffers,
            dma((4,)),
            dma((4, steps)),
            dma((4, steps)),
            dma((4, 3)),
            dma((4, 3)),
            dma((steps,)),
            dma((steps,)),
        ],
        compiler_params=pltpu.CompilerParams(
            collective_id=2, has_side_effects=True, vmem_limit_bytes=60 << 20
        ),
        name="tail",
    )(dq, dk, dv, hidden, grad_mid, weights, grad_wo, small, router, gains, sums, hot)


def finish_kernel(
    input_ref, shares_ref, router_ref, gains_ref, table_ref, input_out, wq, wk, wv, wo, router, gain_a, gain_m, table
):
    input_out[...] = input_ref[...]
    for place, out in enumerate((wo, wq, wk, wv)):
        out[...] = shares_ref[place].astype(F32)
    router[...] = router_ref[...]
    gain_a[...] = gains_ref[0, :]
    gain_m[...] = gains_ref[1, :]
    table[...] = table_ref[...]


def finish(grad_input, shares, router, gains, table):
    share, width = shares.shape[1:]
    vmem = pl.BlockSpec(memory_space=pltpu.VMEM)
    return pl.pallas_call(
        finish_kernel,
        in_specs=[vmem] * 5,
        out_specs=[vmem] * 9,
        out_shape=[
            jax.ShapeDtypeStruct(grad_input.shape, BF16),
            *[jax.ShapeDtypeStruct((share, width), F32)] * 4,
            jax.ShapeDtypeStruct(router.shape, F32),
            jax.ShapeDtypeStruct((share,), F32),
            jax.ShapeDtypeStruct((share,), F32),
            jax.ShapeDtypeStruct(table.shape, F32),
        ],
        compiler_params=pltpu.CompilerParams(vmem_limit_bytes=60 << 20),
        name="finish",
    )(grad_input, shares, router, gains, table)


def rms_forward(values, gain_vec):
    inv_rms = lax.rsqrt(jnp.mean(values * values, axis=-1, keepdims=True) + epsilon)
    return (values * inv_rms * gain_vec, inv_rms)


def rms_backward(values, inv_rms, gain_vec, upstream):
    grad_gain = jnp.sum(upstream * values * inv_rms, axis=0)
    scaled = upstream * gain_vec
    grad_values = inv_rms * scaled - values * inv_rms**3 * jnp.mean(
        scaled * values, axis=-1, keepdims=True
    )
    return (grad_values, grad_gain)


def per_device(
    hidden_in,
    w_query,
    w_key,
    w_value,
    w_output,
    w_router,
    gain_attn,
    gain_moe,
    rel_bias,
    w_in,
    w_out,
    routes,
    block_pairs,
    cotangent,
):
    tokens, width = hidden_in.shape[1:]
    ctx_count, wsh_count = lax.axis_size("ctx"), lax.axis_size("wsh")
    ctx_rank, wsh_rank = lax.axis_index("ctx"), lax.axis_index("wsh")
    length = tokens * ctx_count
    blocks = length // BLOCK
    experts, exp_dev = w_router.shape[1], w_in.shape[0]
    slot_most = 2 * tokens // experts
    capacity = (9 * length // (8 * experts) + 7) // 8 * 8

    def over(axis, array, dim=0):
        return lax.all_gather(array, axis, axis=dim, tiled=True)

    share = width // wsh_count
    small = jnp.concatenate(
        [
            w_router,
            gain_attn[:, None],
            gain_moe[:, None],
            jnp.pad(rel_bias, ((0, share - rel_bias.shape[0]), (0, 0))),
        ],
        axis=1,
    )
    small = jnp.pad(small, ((0, 0), (0, BLOCK - small.shape[1])))
    lanes = wrapped_lanes()
    buckets = rel_bias.shape[0] * wsh_count
    query_hot = onehot_of(BLOCK - lanes, buckets)
    key_hot = onehot_of(lanes, buckets)

    def hot_rows(hot):
        spread = np.zeros((wsh_count, share, SPAN), np.float32)
        spread[:, : rel_bias.shape[0]] = hot.T.reshape(wsh_count, -1, SPAN)
        return jnp.asarray(spread.reshape(width, SPAN), BF16)

    qkv, weights, small, slot_rows, targets, plan, query_base, key_base = project(
        (ctx_count, wsh_count),
        capacity,
        experts,
        slot_most,
        hidden_in[0],
        (w_query, w_key, w_value, w_output),
        small,
        routes.reshape(1, tokens),
        block_pairs,
        hot_rows(query_hot),
        hot_rows(key_hot),
    )
    if wsh_count > 4:
        attn_low, attn_exact, lse, lse_rows = attend_forward(plan, qkv, query_base, width)
    else:
        attn_low = attn_exact = hidden_in[0]
        lse_rows = query_base
    (
        output_rows,
        grad_mid,
        grad_heads,
        heads_all,
        stats,
        grad_wo,
        grad_router,
        grad_gain_m,
        grad_q,
        sums,
        grad_w_in,
        grad_w_out,
    ) = middle(
        (ctx_count, wsh_count),
        experts,
        attn_low,
        attn_exact.reshape(2, BLOCK, width),
        hidden_in[0],
        cotangent[0],
        weights,
        w_in,
        w_out,
        small,
        slot_rows,
        targets,
        lse_rows,
        routes.reshape(tokens, 1),
        query_base,
        plan,
        qkv.reshape(blocks, BLOCK, 3 * width),
        capacity,
    )

    if heads_all.shape[0] == tokens:
        heads_all = dot(over("ctx", heads_all), weights[3], 1, 1).astype(BF16)
        stats = over("ctx", stats)
        grad_q, sums = attend_queries(
            plan, qkv, query_base, grad_heads, attn_exact, lse
        )
    grad_k, grad_v, output_rows, grad_w_in, grad_w_out = attend_keys(
        plan, qkv, key_base, heads_all, stats, (output_rows, grad_w_in, grad_w_out)
    )

    bucket_share = buckets // wsh_count
    if ctx_count == 8 and wsh_count == 4 and share % 64 == 0:
        results = tail(
            experts,
            grad_q,
            grad_k,
            grad_v,
            hidden_in[0],
            grad_mid,
            weights,
            grad_wo,
            small,
            grad_router,
            grad_gain_m,
            sums,
            jnp.asarray(query_hot),
            share,
            bucket_share,
        )
        grad_input, *shares = finish(*results)
        return (output_rows[None], grad_input[None], *shares, grad_w_in, grad_w_out)

    near_sums = sums[:, :2].reshape(HEADS, SPAN)
    far_sums = jnp.sum(sums[:, 2:4].reshape(HEADS, SPAN), axis=1)
    grad_table = jnp.dot(jnp.asarray(query_hot.T), near_sums.T, precision=HIGH)
    grad_table = grad_table.at[buckets - 1].add(far_sums)

    resid_in = hidden_in[0].astype(F32)
    full_query, full_key, full_value = (weights[place] for place in range(3))
    gain_one = small[:, experts].astype(F32)
    normed_one, inv_one = rms_forward(resid_in, gain_one)
    normed_one = normed_one.astype(BF16)
    grad_normed_one = dot(grad_q, full_query, 1, 1)
    grad_normed_one = grad_normed_one + dot(grad_k, full_key, 1, 1)
    grad_normed_one = grad_normed_one + dot(grad_v, full_value, 1, 1)
    grad_in_norm, grad_gain_a = rms_backward(resid_in, inv_one, gain_one, grad_normed_one)
    grad_input = (grad_mid + grad_in_norm).astype(BF16)

    def reduce_weight(grad):
        part = lax.psum_scatter(grad.astype(BF16), "wsh", scatter_dimension=0, tiled=True)
        return lax.psum(part, "ctx").astype(F32)

    grad_wq = dot(normed_one, grad_q, 0, 0)
    grad_wk = dot(normed_one, grad_k, 0, 0)
    grad_wv = dot(normed_one, grad_v, 0, 0)
    shares = [reduce_weight(grad) for grad in (grad_wq, grad_wk, grad_wv, grad_wo)]
    columns = jnp.concatenate(
        [grad_router.T, grad_gain_a[:, None], grad_gain_m[0][:, None]], axis=1
    )
    table = jnp.pad(grad_table, ((0, 0), (0, columns.shape[1] - HEADS)))
    summed = lax.psum(jnp.concatenate([columns, table], axis=0), ("ctx", "wsh"))
    own_columns = lax.dynamic_slice_in_dim(summed[:width], wsh_rank * share, share, 0)
    own_table = lax.dynamic_slice_in_dim(
        summed[width:, :HEADS], wsh_rank * bucket_share, bucket_share, 0
    )
    return (
        output_rows.astype(BF16)[None],
        grad_input[None],
        *shares,
        own_columns[:, :experts],
        own_columns[:, experts],
        own_columns[:, experts + 1],
        own_table,
        grad_w_in,
        grad_w_out,
    )


def solution(mesh):
    in_specs = (
        P("wsh", "ctx", None),
        P("wsh", None),
        P("wsh", None),
        P("wsh", None),
        P("wsh", None),
        P("wsh", None),
        P("wsh"),
        P("wsh"),
        P("wsh", None),
        P("ctx", None, "wsh"),
        P("ctx", "wsh", None),
        P("wsh", "ctx", None),
        P(),
        P("wsh", "ctx", None),
    )
    out_specs = (
        P("wsh", "ctx", None),
        P("wsh", "ctx", None),
        P("wsh", None),
        P("wsh", None),
        P("wsh", None),
        P("wsh", None),
        P("wsh", None),
        P("wsh"),
        P("wsh"),
        P("wsh", None),
        P("ctx", None, "wsh"),
        P("ctx", "wsh", None),
    )
    return jax.shard_map(
        per_device, mesh=mesh, in_specs=in_specs, out_specs=out_specs, check_vma=False
    )
```

```python
import functools
import math

import jax
import jax.numpy as jnp
import numpy as np
from jax import lax
from jax.experimental import pallas as pl
from jax.experimental.pallas import tpu as pltpu
from jax.sharding import PartitionSpec as P

HEADS = 12
HEAD_DIM = 64
BLOCK = 128
PAIRS = HEADS // 2
NEAR = 2 * BLOCK
SPAN = 3 * BLOCK
epsilon = 1e-06
MASKED = -1e30
bucket_edges = [math.ceil(16 * 8 ** (marker / 16)) for marker in range(1, 16)]
F32 = jnp.float32
BF16 = jnp.bfloat16
HIGH = lax.Precision.HIGHEST


def bucket_of(distance):
    gap = np.maximum(distance, 0)
    count = np.full(gap.shape, 16, np.int32)
    for edge in bucket_edges:
        count = count + (gap >= edge)
    return np.where(gap < 16, gap, count)


def wrapped_lanes():
    lanes = np.arange(SPAN)
    return np.where(lanes < NEAR, lanes, lanes - SPAN)


def onehot_of(distance, buckets):
    return (bucket_of(distance)[:, None] == np.arange(buckets)[None, :]).astype(np.float32)


def dot(left, right, left_dim=1, right_dim=0):
    return lax.dot_general(
        left, right, (((left_dim,), (right_dim,)), ((), ())), preferred_element_type=F32
    )


def lane_ids(rows, lanes):
    return lax.broadcasted_iota(jnp.int32, (rows, lanes), 1)


def stack_heads(rows):
    first = lane_ids(rows.shape[0], BLOCK) < HEAD_DIM
    zero = jnp.zeros_like(rows)
    return jnp.concatenate([jnp.where(first, rows, zero), jnp.where(first, zero, rows)], axis=0)


def merge_heads(stacked):
    half = stacked.shape[0] // 2
    first = lane_ids(half, BLOCK) < HEAD_DIM
    return jnp.where(first, stacked[:half], stacked[half:])


def fold_lanes(tile, combine):
    return combine(tile[:, :BLOCK], tile[:, BLOCK:])


def near_bias(base_ref, place=0):
    tiles = []
    for head in range(2):
        row = jnp.broadcast_to(base_ref[place, head : head + 1, :], (BLOCK, SPAN))
        tiles.append(pltpu.roll(row, 0, 1, stride=1, stride_axis=0)[:, :NEAR])
    return jnp.concatenate(tiles, axis=0)


def rows_at(block):
    return pl.ds(pl.multiple_of(block * BLOCK, BLOCK), BLOCK)


def two_tiles(ref, plan_ref, tile):
    tile = SOURCE + tile
    return jnp.concatenate(
        [ref[rows_at(plan_ref[tile]), :], ref[rows_at(plan_ref[tile + 1]), :]], axis=0
    )


class LineGather:
    def __init__(self, axis, lines, across, views, own, sems, crossing=None):
        self.axis, self.lines, self.across = axis, lines, across
        self.views, self.own, self.sems = views, own, sems
        self.crossing = crossing or ["all"] * len(views)
        self.me = lax.axis_index(axis)
        self.line, self.column = self.me // across, self.me % across

    def copy(self, part, block, peer, kind, place, own=False):
        send, recv = self.sems
        view = self.views[part](block)
        return pltpu.make_async_remote_copy(
            src_ref=self.own[part] if own else view,
            dst_ref=view,
            send_sem=send.at[part, kind, place],
            recv_sem=recv.at[part, kind, place],
            device_id={self.axis: peer},
            device_id_type=pl.DeviceIdType.MESH,
        )

    def line_send(self, part, way, step):
        place = self.line - way * step
        ahead = self.line + way
        there = (place >= 0) & (place < self.lines) & (ahead >= 0) & (ahead < self.lines)
        copy = self.copy(
            part,
            place * self.across + self.column,
            ahead * self.across + self.column,
            (1 - way) // 2,
            step,
            own=step == 0,
        )
        return there, copy

    def line_recv(self, part, way, step):
        place = self.line - way * (step + 1)
        there = (place >= 0) & (place < self.lines)
        block = place * self.across + self.column
        return there, block, self.copy(part, block, self.me, (1 - way) // 2, step)

    def cross_send(self, part, block, ahead, own=False):
        peer = self.line * self.across + (self.column + ahead) % self.across
        return self.copy(part, block, peer, 1 + ahead, block // self.across, own)

    def cross_recv(self, part, line, ahead):
        block = line * self.across + (self.column + self.across - ahead) % self.across
        return self.copy(part, block, self.me, 1 + ahead, line)

    def begin(self, part):
        for way in (1, -1):
            there, copy = self.line_send(part, way, 0)
            pl.when(there)(copy.start)
        if self.crossing[part] != "none":
            for ahead in range(1, self.across):
                self.cross_send(part, self.me, ahead, own=True).start()

    def advance(self, part, step):
        for way in (1, -1):
            there, block, arrived = self.line_recv(part, way, step)

            pl.when(there)(arrived.wait_recv)
            if step + 2 < self.lines:
                onward, copy = self.line_send(part, way, step + 1)
                pl.when(onward)(copy.start)
            if self.crossing[part] == "all":
                for ahead in range(1, self.across):
                    pl.when(there)(self.cross_send(part, block, ahead).start)

    def wait_cross(self, part):
        for ahead in range(1, self.across):
            for line in range(self.lines):
                self.cross_recv(part, line, ahead).wait_recv()

    def finish(self):
        for part in range(len(self.views)):
            for step in range(self.lines - 1):
                for way in (1, -1):
                    there, copy = self.line_send(part, way, step)
                    pl.when(there)(copy.wait_send)
            for ahead in range(1, self.across):
                if self.crossing[part] == "all":
                    for line in range(self.lines):
                        self.cross_send(part, line * self.across + self.column, ahead).wait_send()
                elif self.crossing[part] == "own":
                    self.cross_send(part, self.me, ahead).wait_send()


class RowGather:
    def __init__(self, counts, held, sems):
        lines, across = grid_of(counts[0])
        tokens = held.shape[1]
        self.across, self.lines = across, lines
        me = lax.axis_index("ctx")
        self.me = me
        self.balanced = across == 2 and tokens % 32 == 0
        bulk = tokens * 14 // 16 if self.balanced else tokens
        half = bulk // 32 * 16
        cuts = [(0, half), (half, bulk - half)]

        def view(start, rows, turn):
            def of(block):
                if turn:
                    block = block + 1 - 2 * (block % 2)
                return held.at[block, pl.ds(start, rows), :]

            return of

        views = [view(start, rows, False) for start, rows in cuts]
        crossing = ["all", "all"]
        if self.balanced:
            views += [view(bulk, tokens - bulk, turn) for turn in (False, True)]
            crossing += ["own", "none"]
        self.parts = len(views)
        self.gather = LineGather(
            "ctx", lines, across, views, [of(me) for of in views], sems, crossing
        )

    def begin(self):
        for part in range(min(self.parts, 3)):
            self.gather.begin(part)

    def advance(self, step):
        if self.balanced and step == 0:
            self.gather.cross_recv(2, self.gather.line, 1).wait_recv()
            self.gather.begin(3)
        for part in range(self.parts):
            self.gather.advance(part, step)

    def wait_cross(self, line, ahead):
        for part in range(2):
            self.gather.cross_recv(part, line, ahead).wait_recv()

    def finish(self):
        self.gather.finish()


def row_parts(ctx_count, tokens):
    return 4 if grid_of(ctx_count)[1] == 2 and tokens % 32 == 0 else 2


def gather_sems(parts, lines, across):
    return [pltpu.SemaphoreType.DMA((parts, 1 + across, lines))] * 2


def greet(counts):
    barrier = pltpu.get_barrier_semaphore()
    for axis, count in zip(("ctx", "wsh"), counts):
        me = lax.axis_index(axis)
        for ahead in range(1, count):
            pl.semaphore_signal(
                barrier,
                inc=1,
                device_id={axis: (me + ahead) % count},
                device_id_type=pl.DeviceIdType.MESH,
            )
    pl.semaphore_wait(barrier, sum(counts) - 2)


class Exchange:
    def __init__(self, count, experts, most, sems, source, target):
        self.count, self.experts, self.most = count, experts, most
        self.send, self.recv = sems
        self.source, self.target = source, target
        self.me = lax.axis_index("ctx")

    def rows(self, place):
        return pl.ds(pl.multiple_of(place * self.most, self.most), self.most)

    def copy(self, expert, ahead, outward):
        peer = (self.me + ahead) % self.count if outward else (self.me + self.count - ahead) % self.count
        return pltpu.make_async_remote_copy(
            src_ref=self.source(expert, peer),
            dst_ref=self.target(expert, self.me),
            send_sem=self.send.at[expert, ahead - 1],
            recv_sem=self.recv.at[expert, ahead - 1],
            device_id={"ctx": peer},
            device_id_type=pl.DeviceIdType.MESH,
        )

    def start(self, expert):
        for ahead in range(1, self.count):
            self.copy(expert, ahead, True).start()
        self.target(expert, self.me)[...] = self.source(expert, self.me)[...]

    def wait(self, expert):
        for ahead in range(1, self.count):
            peer = (self.me + self.count - ahead) % self.count
            pltpu.make_async_remote_copy(
                src_ref=self.source(expert, peer),
                dst_ref=self.target(expert, peer),
                send_sem=self.send.at[expert, ahead - 1],
                recv_sem=self.recv.at[expert, ahead - 1],
                device_id={"ctx": peer},
                device_id_type=pl.DeviceIdType.MESH,
            ).wait_recv()

    def finish(self, expert):
        for ahead in range(1, self.count):
            self.copy(expert, ahead, True).wait_send()


def exchange_sems(count, experts):
    return [pltpu.SemaphoreType.DMA((experts, count - 1))] * 2


def cap_map(target_ref, expert, capacity):
    slots = target_ref.shape[1]
    rows = lax.broadcasted_iota(jnp.int32, (capacity, slots), 0)
    return (rows == jnp.broadcast_to(target_ref[expert : expert + 1, :], rows.shape)).astype(F32).astype(BF16)


def placement_of(slot_ref, slots):
    rows = lax.broadcasted_iota(jnp.int32, (slots, slot_ref.shape[1]), 0)
    return (rows == jnp.broadcast_to(slot_ref[0:1, :], rows.shape)).astype(F32).astype(BF16)


def grid_of(count):
    lines = 4 if count % 4 == 0 else 1
    return lines, count // lines


def route_slots(routes_ref, chosen_ref, most):
    experts, tokens = chosen_ref.shape
    ids = lax.broadcasted_iota(jnp.int32, (experts, tokens), 0)
    routes = jnp.broadcast_to(routes_ref[0:1, :], ids.shape)
    chosen = (ids == routes).astype(F32)
    chosen_ref[...] = chosen
    earlier = lax.broadcasted_iota(jnp.int32, (tokens, tokens), 0) < lax.broadcasted_iota(
        jnp.int32, (tokens, tokens), 1
    )
    before = dot(chosen.astype(BF16), earlier.astype(F32).astype(BF16))
    rank = jnp.sum(chosen * before, axis=0, keepdims=True).astype(jnp.int32)
    return routes_ref[0:1, :] * most + rank, jnp.sum(chosen, axis=1, keepdims=True)


SOURCE = 2


def plan_start(blocks):
    return SOURCE + blocks + 2


def plan_size(blocks):
    return plan_start(blocks) + 4 + 3 * (blocks + 1)


def write_plan(pairs_ref, plan, me):
    blocks = 2 * pairs_ref.shape[1]
    half = blocks // 2
    own = [pairs_ref[side, me] for side in range(2)]
    plan[0], plan[1] = own[0], own[1]
    plan[SOURCE] = jnp.int32(0)
    plan[SOURCE + blocks + 1] = jnp.int32(0)

    def place(position, carry):
        found = jnp.int32(0)
        for row in range(blocks):
            found = found + jnp.where(pairs_ref[row % 2, row // 2] == position, row, 0)
        plan[SOURCE + 1 + position] = found
        return carry

    lax.fori_loop(0, blocks, place, 0)
    early, late = jnp.minimum(own[0], own[1]), jnp.maximum(own[0], own[1])
    first = jnp.where(own[0] < own[1], 0, 1).astype(jnp.int32)
    start = plan_start(blocks)
    plan[start], plan[start + 1] = first, 1 - first
    plan[start + 2], plan[start + 3] = early, late
    start = start + 4
    for step in range(blocks + 1):
        rest = step - (half + 2)
        if step <= half:
            tile, owner = late - step, jnp.int32(1)
        elif step == half + 1:
            tile, owner = early, jnp.int32(0)
        else:
            tile = jnp.where(rest < early, early - 1 - rest, late - half - 1 - (rest - early))
            owner = jnp.where(rest < early, 0, 1).astype(jnp.int32)
        tile = jnp.minimum(jnp.maximum(tile, 0), blocks - 1)
        plan[start + step] = plan[SOURCE + 1 + tile]
        plan[start + blocks + 1 + step] = owner
        plan[start + 2 * blocks + 2 + step] = plan[SOURCE + blocks - tile]


def project_kernel(
    counts,
    capacity,
    rows_ref,
    wq_ref,
    wk_ref,
    wv_ref,
    wo_ref,
    router_ref,
    gain_a_ref,
    gain_m_ref,
    bias_ref,
    routes_ref,
    pairs_in_ref,
    query_hot_ref,
    key_hot_ref,
    qkv_out,
    weights_out,
    small_out,
    slot_out,
    target_out,
    plan_out,
    query_base_out,
    key_base_out,
    held,
    weights,
    own_small,
    smalls,
    gain,
    pairs_ref,
    ready,
    chosen,
    tallies,
    row_send,
    row_recv,
    weight_send,
    weight_recv,
    tally_send,
    tally_recv,
    out_sems,
    local_sems,
):
    ctx_count, wsh_count = counts
    experts = chosen.shape[0]
    exp_dev = experts // ctx_count
    lanes = experts
    tokens, width = rows_ref.shape
    share = wq_ref.shape[0]
    lines, across = grid_of(ctx_count)
    pairs = wsh_count // 2

    def shard(block):
        return pl.ds(pl.multiple_of(block * share, 16), share)

    def weight_view(place):
        return lambda block: weights.at[place, shard(block), :]

    rows = RowGather(counts, held, (row_send, row_recv))
    mats = LineGather(
        "wsh",
        pairs,
        2,
        [lambda block: smalls.at[block]] + [weight_view(place) for place in range(4)],
        None,
        (weight_send, weight_recv),
    )
    mats.own = [view(mats.me) for view in mats.views]
    own_weights = (wq_ref, wk_ref, wv_ref, wo_ref)
    own_copies = [
        pltpu.make_async_copy(ref, view, local_sems.at[2 + place])
        for place, (ref, view) in enumerate(
            [(rows_ref, held.at[rows.me])]
            + list(zip(own_weights, mats.own[1:]))
        )
    ]
    for copy in own_copies:
        copy.start()
    pairs_copy = pltpu.make_async_copy(pairs_in_ref, pairs_ref, local_sems.at[7])
    pairs_copy.start()
    buckets = bias_ref.shape[0]
    own_small[...] = jnp.zeros_like(own_small)
    own_small[:experts, :share] = router_ref[...].astype(F32)
    own_small[experts : experts + 1, :share] = gain_a_ref[...].astype(F32).reshape(1, share)
    own_small[experts + 1 : experts + 2, :share] = gain_m_ref[...].astype(F32).reshape(1, share)
    own_small[experts + 8 : experts + 8 + buckets, :HEADS] = bias_ref[...].astype(F32)
    smalls[mats.me] = own_small[...].astype(BF16)
    greet(counts)
    own_copies[0].wait()
    rows.begin()
    mats.begin(0)
    for part in range(1, 5):
        own_copies[part].wait()
        if part < 4:
            mats.begin(part)
    most = target_out.shape[1] // ctx_count
    slot, tally = route_slots(routes_ref, chosen, most)
    slot_out[...] = jnp.broadcast_to(slot, slot_out.shape)
    tallies[rows.me] = jnp.broadcast_to(tally, (experts, BLOCK))
    counted = Exchange(
        ctx_count,
        1,
        most,
        (tally_send, tally_recv),
        lambda expert, peer: tallies.at[rows.me],
        lambda expert, peer: tallies.at[peer],
    )
    for ahead in range(1, ctx_count):
        counted.copy(0, ahead, True).start()
    pairs_copy.wait()
    write_plan(pairs_ref, plan_out, rows.me)

    def place_targets():
        counted.wait(0)
        lane = lane_ids(1, ctx_count * most)
        for expert in range(exp_dev):
            offset = jnp.zeros((1, 1), F32)
            target = jnp.full((1, ctx_count * most), capacity, jnp.int32)
            for source in range(ctx_count):
                count = tallies[source, pl.ds(rows.me * exp_dev + expert, 1), 0:1]
                inside = (lane >= source * most) & (
                    lane < source * most + jnp.broadcast_to(count.astype(jnp.int32), lane.shape)
                )
                place = lane - source * most + jnp.broadcast_to(offset.astype(jnp.int32), lane.shape)
                target = jnp.where(inside, place, target)
                offset = offset + count
            target_out[expert : expert + 1, :] = target
        target_out[exp_dev:, :] = jnp.zeros_like(target_out[exp_dev:, :])

    for step in range(lines - 2):
        rows.advance(step)
        if step == 0:
            place_targets()
    for step in range(pairs - 1):
        for part in range(4):
            mats.advance(part, step)
    mats.begin(4)
    for part in range(4):
        mats.wait_cross(part)
    parts = [smalls[block].astype(F32) for block in range(wsh_count)]
    bias_rows = [part[experts + 8 : experts + 8 + buckets, :BLOCK] for part in parts]
    bias_rows = jnp.concatenate(bias_rows, axis=0).astype(BF16)
    turned = jnp.concatenate([part[: experts + 8, :share] for part in parts], axis=1)
    spare = jnp.zeros((BLOCK - turned.shape[0], width), F32)
    turned = jnp.concatenate([turned, spare], axis=0)
    small_out[...] = turned.astype(BF16)
    gain[...] = turned[lanes : lanes + 8, :]
    for hot_ref, base_out, sign in (
        (query_hot_ref, query_base_out, -1),
        (key_hot_ref, key_base_out, 1),
    ):
        table = dot(bias_rows, hot_ref[...], 0, 0)
        lane = lane_ids(BLOCK, SPAN)
        lane = jnp.where(lane < NEAR, lane, lane - SPAN)
        gap = lane if sign > 0 else BLOCK - lane
        last = jnp.max(jnp.where(gap == NEAR - 1, table, -jnp.inf), axis=1, keepdims=True)
        table = jnp.where(gap >= 0, table - last, MASKED)
        for pair in range(PAIRS):
            base_out[pair] = jnp.zeros((8, SPAN), F32)
            base_out[pair, 0:2, :] = table[2 * pair : 2 * pair + 2]
    ahead_of_last = 5 if lines == 4 and across == 2 else 0
    if not ahead_of_last:
        rows.advance(lines - 2)
    column = rows.me % across
    upper = rows.me // across // max(lines // 2, 1)

    def put(slot, block):
        place = pl.ds(pl.multiple_of(block * tokens, tokens), tokens)
        return pltpu.make_async_copy(ready.at[slot], qkv_out.at[place, :], out_sems.at[slot])

    def order(step):
        if ahead_of_last:
            step = jnp.asarray(step)
            step = jnp.where(
                step < 3, step, jnp.where(step < 5, step + 1, jnp.where(step == 5, 3, step))
            )
        ahead, line = step // lines, step % lines
        line = line + upper * (lines - 1 - 2 * line)
        return line, ahead, line * across + (column + across - ahead) % across

    def step_body(step, carry):
        line, ahead, block = order(step)
        slot = step % 2
        for skip in range(1, across):

            @pl.when(ahead == skip)
            def _():
                rows.wait_cross(line, skip)

        @pl.when(step >= 2)
        def _():
            put(slot, order(step - 2)[2]).wait()

        values = held[block].astype(F32)
        inv = lax.rsqrt(jnp.mean(values * values, axis=-1, keepdims=True) + epsilon)
        normed = (values * inv * gain[0:1, :]).astype(BF16)
        for place in range(3):
            ready[slot, :, place * width : (place + 1) * width] = dot(
                normed, weights[place]
            ).astype(BF16)
        put(slot, block).start()
        return carry

    first = ahead_of_last or ctx_count // 2
    lax.fori_loop(0, first, step_body, 0)
    if ahead_of_last:
        rows.advance(lines - 2)
    for step in range(pairs - 1):
        mats.advance(4, step)
    lax.fori_loop(first, ctx_count, step_body, 0)
    mats.wait_cross(4)
    weights_copy = pltpu.make_async_copy(weights, weights_out, local_sems.at[0])
    weights_copy.start()
    for step in (ctx_count - 2, ctx_count - 1):
        put(step % 2, order(step)[2]).wait()
    weights_copy.wait()
    counted.finish(0)
    rows.finish()
    mats.finish()


def project(
    counts, capacity, experts, most, rows, weights, small, routes, pairs, query_hot, key_hot
):
    tokens, width = rows.shape
    ctx_count, wsh_count = counts
    length = tokens * ctx_count
    lines, across = grid_of(ctx_count)
    small_rows = -(-(experts + 8 + small[3].shape[0]) // 16) * 16
    small_lanes = -(-(width // wsh_count) // BLOCK) * BLOCK
    vmem = pl.BlockSpec(memory_space=pltpu.VMEM)
    anywhere = pl.BlockSpec(memory_space=pl.ANY)
    smem = pl.BlockSpec(memory_space=pltpu.SMEM)
    return pl.pallas_call(
        functools.partial(project_kernel, counts, capacity),
        in_specs=[anywhere] * 5 + [vmem] * 5 + [anywhere, vmem, vmem],
        out_specs=[anywhere] * 2 + [vmem] * 3 + [smem] + [vmem] * 2,
        out_shape=[
            jax.ShapeDtypeStruct((length, 3 * width), BF16),
            jax.ShapeDtypeStruct((4, width, width), BF16),
            jax.ShapeDtypeStruct((BLOCK, width), BF16),
            jax.ShapeDtypeStruct((8, tokens), jnp.int32),
            jax.ShapeDtypeStruct((8, ctx_count * most), jnp.int32),
            jax.ShapeDtypeStruct((plan_size(2 * ctx_count),), jnp.int32),
            jax.ShapeDtypeStruct((PAIRS, 8, SPAN), F32),
            jax.ShapeDtypeStruct((PAIRS, 8, SPAN), F32),
        ],
        scratch_shapes=[
            pltpu.VMEM((ctx_count, tokens, width), BF16),
            pltpu.VMEM((4, width, width), BF16),
            pltpu.VMEM((small_rows, small_lanes), F32),
            pltpu.VMEM((wsh_count, small_rows, small_lanes), BF16),
            pltpu.VMEM((8, width), F32),
            pltpu.SMEM(pairs.shape, jnp.int32),
            pltpu.VMEM((2, tokens, 3 * width), BF16),
            pltpu.VMEM((experts, tokens), F32),
            pltpu.VMEM((ctx_count, experts, BLOCK), F32),
            *gather_sems(row_parts(ctx_count, tokens), lines, across),
            *gather_sems(5, wsh_count // 2, 2),
            *exchange_sems(ctx_count, 1),
            pltpu.SemaphoreType.DMA((2,)),
            pltpu.SemaphoreType.DMA((8,)),
        ],
        compiler_params=pltpu.CompilerParams(
            collective_id=0, has_side_effects=True, vmem_limit_bytes=60 << 20
        ),
        name="project",
    )(rows, *weights, *small, routes, pairs, query_hot, key_hot)


def gelu_parts(values):
    slope, cubic = math.sqrt(2 / math.pi), 0.044715
    square = values * values
    bent = jnp.tanh(slope * (values + cubic * values * square))
    outer = 0.5 * (1.0 + bent)
    derivative = outer + 0.5 * values * (1.0 - bent * bent) * slope * (1.0 + 3 * cubic * square)
    return values * outer, derivative


def choose(rows, router, experts, expert):
    logits = dot(rows, router, 1, 1)
    lanes = lane_ids(rows.shape[0], router.shape[0])
    logits = jnp.where(lanes < experts, logits, MASKED)
    weights = jnp.exp(logits - jnp.max(logits, axis=-1, keepdims=True))
    probs = weights / jnp.sum(weights, axis=-1, keepdims=True)
    hot = (lanes == expert).astype(F32)
    return probs, hot, jnp.sum(probs * hot, axis=-1, keepdims=True)


def middle_kernel(
    counts,
    experts,
    spread_here,
    attn_ref,
    exact_ref,
    hidden_ref,
    grad_ref,
    weights_ref,
    w_in_ref,
    w_out_ref,
    small_ref,
    slot_ref,
    target_ref,
    lse_ref,
    routes_ref,
    base_ref,
    plan_ref,
    qkv_ref,
    output_out,
    returned_out,
    resid_out,
    gate_out,
    grad_mid_out,
    grad_heads_out,
    heads_all_out,
    stats_out,
    grad_wo_out,
    grad_router_out,
    grad_gain_out,
    dq_out,
    sums_out,
    grad_in_out,
    grad_out_out,
    qkv,
    lse_all,
    stacked_q,
    stacked_g,
    delta_rep,
    bias,
    near,
    tile_keys,
    scores,
    tops,
    tile_weights,
    tile_values,
    other_values,
    lse_rows,
    own_g,
    early_in,
    attn,
    heads,
    exact_blocks,
    hidden,
    grad,
    wo,
    w_in,
    w_out,
    resid,
    incoming,
    own_x,
    all_x,
    all_g,
    hid,
    du,
    parts,
    from_mate,
    from_far,
    shares,
    mate_shares,
    far_shares,
    returning,
    home,
    branch,
    stats,
    stage_in,
    stage_out,
    heads_stage,
    fetch_sems,
    out_sems,
    heads_sems,
    x_send,
    x_recv,
    g_send,
    g_recv,
    early_send,
    early_recv,
    go_send,
    go_recv,
    back_send,
    back_recv,
    mate_send,
    mate_recv,
    far_send,
    far_recv,
    branch_send,
    branch_recv,
    stat_send,
    stat_recv,
):
    ctx_count, wsh_count = counts
    tokens, width = hidden.shape
    exp_dev, capacity = own_x.shape[:2]
    most = incoming.shape[1] // ctx_count
    lines, across = grid_of(ctx_count)
    pairs = wsh_count // 2
    me = lax.axis_index("ctx")
    home_row = me if spread_here else 0
    sources = [
        (grad_ref, grad),
        (weights_ref.at[3], wo),
        (hidden_ref, hidden),
        (w_in_ref, w_in),
        (w_out_ref, w_out),
    ]
    if spread_here:
        sources.insert(1, (qkv_ref, qkv))
    else:
        sources += [(attn_ref, attn), (exact_ref, exact_blocks)]
    fetches = [
        pltpu.make_async_copy(src, dst, fetch_sems.at[place])
        for place, (src, dst) in enumerate(sources)
    ]
    for fetch in fetches:
        fetch.start()
    views = [
        (lambda buffer, expert: lambda block: buffer.at[expert, block])(buffer, expert)
        for buffer in (all_g, all_x)
        for expert in range(exp_dev)
    ]
    gather_g = LineGather(
        "wsh",
        pairs,
        2,
        views[:exp_dev],
        [own_g.at[expert] for expert in range(exp_dev)],
        (g_send, g_recv),
    )
    gather_x = LineGather(
        "wsh",
        pairs,
        2,
        views[exp_dev:],
        [own_x.at[expert] for expert in range(exp_dev)],
        (x_send, x_recv),
    )
    wsh_me, my_line, my_core = gather_x.me, gather_x.line, gather_x.column
    greet(counts)
    fetches[0].wait()
    returning[1] = dot(placement_of(slot_ref, experts * most), grad[...]).astype(BF16)
    early = Exchange(
        ctx_count,
        exp_dev,
        most,
        (early_send, early_recv),
        lambda expert, peer: returning.at[1, early.rows(peer * exp_dev + expert), :],
        lambda expert, peer: early_in.at[expert, early.rows(peer), :],
    )
    for expert in range(exp_dev):
        early.start(expert)

    def pass_on():
        for expert in range(exp_dev):
            early.wait(expert)
            own_g[expert] = dot(cap_map(target_ref, expert, capacity), early_in[expert]).astype(BF16)
            gather_g.begin(expert)
            all_g[expert, wsh_me] = own_g[expert]

    if spread_here:
        tiles = Tiles(plan_ref, 2 * ctx_count, False)
        fetches[1].wait()

        def attend(pair, carry):
            pair_lanes = pl.ds(pl.multiple_of(pair * BLOCK, BLOCK), BLOCK)

            def load(part, row):
                lanes = pl.ds(pl.multiple_of(part * width + pair * BLOCK, BLOCK), BLOCK)
                return qkv[row, :, lanes]

            near_tiles = near_bias(base_ref, pair)
            bias[...] = jnp.concatenate(
                [near_tiles[:, BLOCK:], near_tiles[:, :BLOCK]], axis=1
            )
            totals = lse_all.at[pair]
            results = forward_pair(
                tiles,
                load,
                bias,
                stacked_q,
                tile_keys,
                scores,
                tops,
                totals,
                tile_weights,
                tile_values,
                other_values,
            )
            main = in_order(tiles, [result[0] for result in results])
            whole = in_order(tiles, [result[1] for result in results])
            lse = in_order(tiles, [totals[0], totals[1]])
            for own in range(2):
                rows = pl.ds(own * BLOCK, BLOCK)
                attn[rows, pair_lanes] = main[own]
                exact_blocks[own, :, pair_lanes] = whole[own]
                turned = jnp.transpose(lse[own])
                for head in range(2):
                    lse_rows[own, pair, head : head + 1, :] = turned[
                        :1, head * BLOCK : (head + 1) * BLOCK
                    ]
                lse_rows[own, pair, 2:8, :] = jnp.zeros((6, BLOCK), F32)
            return carry

        lax.fori_loop(0, PAIRS - 1, attend, 0)
        pass_on()
        lax.fori_loop(PAIRS - 1, PAIRS, attend, 0)
    else:
        lse_rows[...] = lse_ref[...]
        pass_on()

    gain_two = small_ref[...].astype(F32)[experts + 1 : experts + 2, :]
    row_ids = lax.broadcasted_iota(jnp.int32, (BLOCK, width), 0)
    router = jnp.where(row_ids < experts, small_ref[...], jnp.zeros((BLOCK, width), BF16))
    for fetch in fetches[2 if spread_here else 1 :]:
        fetch.wait()
    resid[...] = hidden[...].astype(F32) + dot(attn[...], wo[...])
    inv_two = lax.rsqrt(jnp.mean(resid[...] * resid[...], axis=-1, keepdims=True) + epsilon)
    normed_two = (resid[...] * inv_two * gain_two).astype(BF16)
    units = w_in.shape[2]
    placement = placement_of(slot_ref, experts * most)
    returning[0] = dot(placement, normed_two).astype(BF16)
    forth = Exchange(
        ctx_count,
        exp_dev,
        most,
        (go_send, go_recv),
        lambda expert, peer: returning.at[0, forth.rows(peer * exp_dev + expert), :],
        lambda expert, peer: incoming.at[expert, forth.rows(peer), :],
    )
    forth.start(0)
    routed = jnp.broadcast_to(routes_ref[...].astype(F32), (BLOCK, tokens))
    routed = jnp.transpose(routed)[:, :1].astype(jnp.int32)
    gate = choose(normed_two, router, experts, routed)[2]
    for expert in range(exp_dev):
        for step in range(pairs - 1):
            gather_g.advance(expert, step)
    gather_g.finish()

    summed = (parts.at[0], parts.at[1], shares)
    mate_parts = (from_mate.at[0], from_mate.at[1], mate_shares)
    far_parts = (from_far.at[0], from_far.at[1], far_shares)

    def mate_copy(array, expert, line):
        mine = line * 2 + 1 - my_core
        return pltpu.make_async_remote_copy(
            src_ref=summed[array].at[expert, mine],
            dst_ref=mate_parts[array].at[expert, line],
            send_sem=mate_send.at[array, expert, line],
            recv_sem=mate_recv.at[array, expert, line],
            device_id={"wsh": my_line * 2 + 1 - my_core},
            device_id_type=pl.DeviceIdType.MESH,
        )

    def far_copy(array, expert, ahead):
        line = (my_line + ahead) % pairs
        return pltpu.make_async_remote_copy(
            src_ref=summed[array].at[expert, line * 2 + my_core],
            dst_ref=far_parts[array].at[expert, ahead - 1],
            send_sem=far_send.at[array, expert, ahead - 1],
            recv_sem=far_recv.at[array, expert, ahead - 1],
            device_id={"wsh": line * 2 + my_core},
            device_id_type=pl.DeviceIdType.MESH,
        )

    def work(expert, ahead):
        line = (my_line + ahead) % pairs
        both = pl.ds(line * 2, 2)
        gather_x.cross_recv(expert, line, 1).wait_recv()
        gather_g.cross_recv(expert, line, 1).wait_recv()
        rows = all_x[expert, both].reshape(2 * capacity, width)
        active, slope = gelu_parts(dot(rows, w_in[expert]))
        active = active.astype(BF16)
        hid[expert, both] = active.reshape(2, capacity, units)
        share = choose(rows, router, experts, exp_dev * me + expert)[2]
        grads = all_g[expert, both].reshape(2 * capacity, width).astype(F32)
        grads = (share * grads).astype(BF16)
        all_g[expert, both] = grads.reshape(2, capacity, width)
        push = dot(grads, w_out[expert], 1, 1)
        product = jnp.sum(push * active.astype(F32), axis=-1, keepdims=True)
        product = jnp.transpose(jnp.broadcast_to(product, (2 * capacity, BLOCK)))
        for core in range(2):
            shares[expert, line * 2 + core] = product[:8, core * capacity : (core + 1) * capacity]
        mate_copy(2, expert, line).start()
        grad_u = (push * slope).astype(BF16)
        du[expert, both] = grad_u.reshape(2, capacity, units)
        part = dot(grad_u, w_in[expert], 1, 1).astype(BF16)
        parts[1, expert, both] = part.reshape(2, capacity, width)
        mate_copy(1, expert, line).start()
        part = dot(active, w_out[expert]).astype(BF16)
        parts[0, expert, both] = part.reshape(2, capacity, width)
        mate_copy(0, expert, line).start()

    def fold(array, expert, ahead):
        line = (my_line + ahead) % pairs
        mate_copy(array, expert, line).wait_recv()
        both = summed[array][expert, line * 2 + my_core].astype(F32) + mate_parts[array][
            expert, line
        ].astype(F32)
        summed[array][expert, line * 2 + my_core] = both.astype(summed[array].dtype)
        far_copy(array, expert, ahead).start()

    def whole(array, expert):
        mate_copy(array, expert, my_line).wait_recv()
        total = summed[array][expert, my_line * 2 + my_core].astype(F32) + mate_parts[array][
            expert, my_line
        ].astype(F32)
        for ahead in range(1, pairs):
            far_copy(array, expert, ahead).wait_recv()
            total = total + far_parts[array][expert, ahead - 1].astype(F32)
        return total

    back = [
        Exchange(
            ctx_count,
            exp_dev,
            most,
            (back_send.at[array], back_recv.at[array]),
            (
                lambda array: lambda expert, peer: returning.at[
                    array, forth.rows(expert * ctx_count + peer), :
                ]
            )(array),
            (
                lambda array: lambda expert, peer: home.at[
                    array, forth.rows(peer * exp_dev + expert), :
                ]
            )(array),
        )
        for array in range(2)
    ]

    def settle(expert):
        expert_rows = pl.ds(expert * ctx_count * most, ctx_count * most)
        rows = own_x[expert]
        probs, hot, share = choose(rows, router, experts, exp_dev * me + expert)
        product = jnp.transpose(whole(2, expert))[:, :1]
        grad_logits = (product * (hot - probs)).astype(BF16)
        grad_rows = whole(1, expert).astype(BF16).astype(F32) + dot(grad_logits, router)
        spread = cap_map(target_ref, expert, capacity)
        returning[1, expert_rows] = dot(spread, grad_rows.astype(BF16), 0, 0).astype(BF16)
        back[1].start(expert)
        router_part = dot(grad_logits, rows, 0, 0)[:experts]
        if expert == 0:
            grad_router_out[...] = router_part
        else:
            grad_router_out[...] += router_part

    for expert in range(exp_dev):
        early.finish(expert)
    for expert in range(exp_dev):
        forth.wait(expert)
        if expert + 1 < exp_dev:
            forth.start(expert + 1)
        own_x[expert] = dot(cap_map(target_ref, expert, capacity), incoming[expert]).astype(BF16)
        gather_x.begin(expert)
        all_x[expert, wsh_me] = own_x[expert]
        work(expert, 0)
        if expert:
            settle(expert - 1)
        for step in range(pairs - 1):
            gather_x.advance(expert, step)

        def others(ahead, carry):
            work(expert, ahead)
            return carry

        if pairs == 2:
            work(expert, 1)
        else:
            lax.fori_loop(1, pairs, others, 0)
        for ahead in range(1, pairs):
            fold(2, expert, ahead)
            fold(1, expert, ahead)
    settle(exp_dev - 1)
    for expert in range(exp_dev):
        forth.finish(expert)
        for ahead in range(1, pairs):
            fold(0, expert, ahead)

    def in_copy(expert):
        return pltpu.make_async_copy(stage_in, grad_in_out.at[expert], out_sems.at[1])

    one_stage = units == width
    out_stage = stage_in if one_stage else stage_out

    def out_copy(expert):
        return pltpu.make_async_copy(out_stage, grad_out_out.at[expert], out_sems.at[0])

    group = min(wsh_count, 4)

    def slot_sum(stage, left, right, expert):
        def part(turn):
            blocks = pl.ds(turn * group, group)
            return dot(
                left[expert, blocks].reshape(group * capacity, left.shape[3]),
                right[expert, blocks].reshape(group * capacity, right.shape[3]),
                0,
                0,
            )

        stage[...] = part(0).astype(stage.dtype)
        if wsh_count > group:

            def add(turn, carry):
                stage[...] += part(turn)
                return carry

            lax.fori_loop(1, wsh_count // group, add, 0)

    def grads_of(expert):
        if expert:
            (in_copy if one_stage else out_copy)(expert - 1).wait()
        slot_sum(out_stage, hid, all_g, expert)
        out_copy(expert).start()
        if one_stage:
            out_copy(expert).wait()
        elif expert:
            in_copy(expert - 1).wait()
        slot_sum(stage_in, all_x, du, expert)
        in_copy(expert).start()

    for expert in range(exp_dev):
        grads_of(expert)
        expert_rows = pl.ds(expert * ctx_count * most, ctx_count * most)
        spread = cap_map(target_ref, expert, capacity)
        out_rows = whole(0, expert).astype(BF16)
        returning[0, expert_rows] = dot(spread, out_rows, 0, 0).astype(BF16)
    grad_up = grad[...].astype(F32)
    for expert in range(exp_dev):
        back[1].wait(expert)
    grad_normed = dot(placement_of(slot_ref, experts * most), home[1], 0, 0)
    scaled = grad_normed * gain_two
    mean = jnp.mean(scaled * resid[...], axis=-1, keepdims=True)
    gain_part = jnp.sum(grad_normed * resid[...] * inv_two, axis=0, keepdims=True)
    grad_gain_out[...] = jnp.broadcast_to(gain_part, grad_gain_out.shape)
    grad_mid = grad_up + inv_two * scaled - resid[...] * inv_two * inv_two * inv_two * mean
    grad_mid_out[...] = grad_mid
    branch[home_row] = grad_mid.astype(BF16)

    if spread_here:
        gather_d = RowGather(counts, branch, (branch_send, branch_recv))
        gather_s = LineGather(
            "ctx",
            lines,
            across,
            [lambda block: stats.at[block]],
            [stats.at[me]],
            (stat_send, stat_recv),
        )
        gather_d.begin()
    if spread_here:
        returned_out[...] = returning[0]
        resid_out[...] = resid[...]
        gate_out[...] = jnp.broadcast_to(gate, gate_out.shape)
    else:
        for expert in range(exp_dev):
            back[0].start(expert)
    grad_heads = dot(branch[home_row], wo[...], 1, 1).astype(BF16)
    grad_heads_out[...] = grad_heads
    if spread_here:
        for own in range(2):
            heads[own] = grad_heads[own * BLOCK : (own + 1) * BLOCK]
    product = grad_heads.astype(F32) * exact_blocks[...].reshape(tokens, width)
    head_of = lax.broadcasted_iota(jnp.int32, (width, BLOCK), 0) // HEAD_DIM
    head_hot = (head_of == lane_ids(width, BLOCK)).astype(F32)
    delta = jnp.transpose(
        lax.dot_general(
            product, head_hot, (((1,), (0,)), ((), ())), precision=HIGH, preferred_element_type=F32
        )
    )
    for pair in range(PAIRS):
        for own in range(2):
            stats[home_row, own, pair] = lse_rows[own, pair]
            stats[home_row, own, pair, 2:4, :] = delta[
                2 * pair : 2 * pair + 2, own * BLOCK : (own + 1) * BLOCK
            ]
    if spread_here:
        gather_s.begin(0)

    grad_wo_out[...] = dot(attn[...], branch[home_row], 0, 0).astype(BF16)

    plan_from = plan_start(2 * ctx_count)
    half = ctx_count

    def query_pair(pair, carry):
        pair_lanes = pl.ds(pl.multiple_of(pair * BLOCK, BLOCK), BLOCK)

        def tile(part, step):
            lanes = pl.ds(pl.multiple_of(part * width + pair * BLOCK, BLOCK), BLOCK)
            return qkv[plan_ref[plan_from + 4 + step], :, lanes]

        bias[...] = near_bias(base_ref, pair)
        for place in range(2):
            own = plan_ref[plan_from + place]
            stacked_q[place] = stack_heads(tile(0, 0 if place else half + 1))
            grads = stack_heads(heads[own, :, pair_lanes])
            stacked_g[place] = grads
            own_exact = exact_blocks[own, :, pair_lanes]
            product = grads.astype(F32) * jnp.concatenate([own_exact, own_exact], axis=0)
            delta_rep[place] = jnp.broadcast_to(
                jnp.sum(product, axis=-1, keepdims=True), (2 * BLOCK, BLOCK)
            )

        def score_grads(place, step, extra):
            keys = tile(1, step)
            part = dot(stacked_q[place], keys, 1, 1)
            if extra is not None:
                part = part + extra
            weights = jnp.exp(part - lse_all[pair, place])
            grad_s = weights * (dot(stacked_g[place], tile(2, step), 1, 1) - delta_rep[place])
            return grad_s, dot(grad_s.astype(BF16), keys)

        diagonal, big = score_grads(1, 0, bias[:, BLOCK:])
        beside, more = score_grads(1, 1, bias[:, :BLOCK])
        big = big + more
        far = jnp.zeros((2 * BLOCK, BLOCK), F32)
        for step in range(2, half + 1):
            grad_s, more = score_grads(1, step, None)
            far, big = far + grad_s, big + more
        grad_s, small_part = score_grads(0, half + 1, bias[:, BLOCK:])
        near[:, BLOCK:] = diagonal + grad_s
        for step in range(half + 2, 2 * half + 1):
            place = plan_ref[plan_from + 4 + 2 * half + 1 + step]
            later = place.astype(F32)
            sooner = 1.0 - later
            extra = None
            if step == half + 2:
                extra = bias[:, :BLOCK] * sooner
            grad_s, more = score_grads(place, step, extra)
            if step == half + 2:
                near[:, :BLOCK] = beside + grad_s * sooner
                far = far + grad_s * later
            else:
                far = far + grad_s
            big = big + more * later
            small_part = small_part + more * sooner
        second = plan_ref[plan_from].astype(F32)
        small_part, big = merge_heads(small_part), merge_heads(big)
        first = 1.0 - second
        dq_out[:BLOCK, pair_lanes] = (small_part * first + big * second).astype(BF16)
        dq_out[BLOCK:, pair_lanes] = (big * first + small_part * second).astype(BF16)
        put_sums(sums_out, pair, near, far)
        return carry

    def query_pairs(turn):
        share = PAIRS // (lines - 1)
        lax.fori_loop(turn * share, (turn + 1) * share, query_pair, 0)

    if spread_here:
        for step in range(lines - 1):
            query_pairs(step)
            gather_d.advance(step)
            gather_s.advance(0, step)
    if not spread_here:
        for expert in range(exp_dev):
            back[0].wait(expert)
        token_out = dot(placement_of(slot_ref, experts * most), home[0], 0, 0)
        output_out[...] = (resid[...] + gate * token_out).astype(BF16)
    column = me % across
    upper = me // across // max(lines // 2, 1)

    def order(step):
        ahead, line = step // lines, step % lines
        line = line + upper * (lines - 1 - 2 * line)
        return line, ahead, line * across + (column + across - ahead) % across

    def put(slot, block):
        place = pl.ds(pl.multiple_of(block * tokens, tokens), tokens)
        return pltpu.make_async_copy(
            heads_stage.at[slot], heads_all_out.at[place, :], heads_sems.at[slot]
        )

    def heads_step(step, carry):
        line, ahead, block = order(step)
        slot = step % 2
        for skip in range(1, across):

            @pl.when(ahead == skip)
            def _():
                gather_d.wait_cross(line, skip)
                gather_s.cross_recv(0, line, skip).wait_recv()

        @pl.when(step >= 2)
        def _():
            put(slot, order(step - 2)[2]).wait()

        heads_stage[slot] = dot(branch[block], wo[...], 1, 1).astype(BF16)
        put(slot, block).start()
        return carry

    if spread_here:
        lax.fori_loop(0, ctx_count, heads_step, 0)
    stats_copy = pltpu.make_async_copy(stats, stats_out, fetch_sems.at[0])
    stats_copy.start()
    if spread_here:
        for step in (ctx_count - 2, ctx_count - 1):
            put(step % 2, order(step)[2]).wait()
    else:
        heads_stage[0] = branch[0]
        own_branch = pltpu.make_async_copy(heads_stage.at[0], heads_all_out, heads_sems.at[0])
        own_branch.start()
        own_branch.wait()
    if not one_stage:
        out_copy(exp_dev - 1).wait()
    in_copy(exp_dev - 1).wait()
    stats_copy.wait()
    for expert in range(exp_dev):
        for array in range(1 if spread_here else 0, 2):
            back[array].finish(expert)
        for array in range(3):
            for line in range(pairs):
                mate_copy(array, expert, line).wait_send()
            for ahead in range(1, pairs):
                far_copy(array, expert, ahead).wait_send()
    gather_x.finish()
    if spread_here:
        gather_d.finish()
        gather_s.finish()


def middle(
    counts,
    experts,
    attn,
    exact,
    hidden,
    grad,
    weights,
    w_in,
    w_out,
    small,
    slots,
    targets,
    lse_rows,
    routes,
    base,
    plan,
    qkv,
    capacity,
):
    ctx_count, wsh_count = counts
    tokens, width = hidden.shape
    exp_dev = w_in.shape[0]
    units = w_in.shape[2]
    slot_count = targets.shape[1]
    all_slots = experts * (slot_count // ctx_count)
    lines, across = grid_of(ctx_count)
    pairs = wsh_count // 2
    vmem = pl.BlockSpec(memory_space=pltpu.VMEM)
    anywhere = pl.BlockSpec(memory_space=pl.ANY)
    slot_rows = (exp_dev, wsh_count, capacity)
    spread_here = wsh_count <= 4
    held = ctx_count if spread_here else 1
    kept = BF16 if spread_here else F32
    score_rows = NEAR if spread_here else 16
    forward = forward_scratch(2 * ctx_count) if spread_here else [pltpu.VMEM((8, BLOCK), F32)] * 8
    return pl.pallas_call(
        functools.partial(middle_kernel, counts, experts, spread_here),
        in_specs=[anywhere] * 7
        + [vmem] * 6
        + [pl.BlockSpec(memory_space=pltpu.SMEM), anywhere],
        out_specs=[vmem] * 6 + [anywhere] * 2 + [vmem] * 5 + [anywhere] * 2,
        out_shape=[
            jax.ShapeDtypeStruct((16 if spread_here else tokens, width), BF16),
            jax.ShapeDtypeStruct((all_slots if spread_here else 16, width), BF16),
            jax.ShapeDtypeStruct((tokens if spread_here else 8, width), F32),
            jax.ShapeDtypeStruct((tokens, BLOCK), F32),
            jax.ShapeDtypeStruct((tokens, width), F32),
            jax.ShapeDtypeStruct((tokens, width), BF16),
            jax.ShapeDtypeStruct((tokens * held, width), BF16),
            jax.ShapeDtypeStruct((held, 2, PAIRS, 8, BLOCK), F32),
            jax.ShapeDtypeStruct((width, width), BF16),
            jax.ShapeDtypeStruct((experts, width), F32),
            jax.ShapeDtypeStruct((8, width), F32),
            jax.ShapeDtypeStruct((tokens if spread_here else 16, width), BF16),
            jax.ShapeDtypeStruct((PAIRS, 8, SPAN), F32),
            jax.ShapeDtypeStruct((exp_dev, width, units), kept),
            jax.ShapeDtypeStruct((exp_dev, units, width), kept),
        ],
        scratch_shapes=[
            pltpu.VMEM(qkv.shape if spread_here else (1, 16, BLOCK), BF16),
            pltpu.VMEM((PAIRS, 2, NEAR, BLOCK) if spread_here else (1, 2, 8, BLOCK), F32),
            pltpu.VMEM((2, score_rows, BLOCK), BF16),
            pltpu.VMEM((2, score_rows, BLOCK), BF16),
            pltpu.VMEM((2, score_rows, BLOCK), F32),
            pltpu.VMEM((score_rows, NEAR), F32),
            pltpu.VMEM((score_rows, NEAR), F32),
            *forward[1:4],
            *forward[5:],
            pltpu.VMEM((2, PAIRS, 8, BLOCK), F32),
            pltpu.VMEM((exp_dev, capacity, width), BF16),
            pltpu.VMEM((exp_dev, slot_count, width), BF16),
            pltpu.VMEM((tokens, width), BF16),
            pltpu.VMEM((2, BLOCK if spread_here else 16, width), BF16),
            pltpu.VMEM((2, BLOCK, width), F32),
            pltpu.VMEM((tokens, width), BF16),
            pltpu.VMEM((tokens, width), BF16),
            pltpu.VMEM((width, width), BF16),
            pltpu.VMEM(w_in.shape, BF16),
            pltpu.VMEM(w_out.shape, BF16),
            pltpu.VMEM((tokens, width), F32),
            pltpu.VMEM((exp_dev, slot_count, width), BF16),
            pltpu.VMEM((exp_dev, capacity, width), BF16),
            pltpu.VMEM((*slot_rows, width), BF16),
            pltpu.VMEM((*slot_rows, width), BF16),
            pltpu.VMEM((*slot_rows, units), BF16),
            pltpu.VMEM((*slot_rows, units), BF16),
            pltpu.VMEM((2, *slot_rows, width), BF16),
            pltpu.VMEM((2, exp_dev, pairs, capacity, width), BF16),
            pltpu.VMEM((2, exp_dev, max(pairs - 1, 1), capacity, width), BF16),
            pltpu.VMEM((exp_dev, wsh_count, 8, capacity), F32),
            pltpu.VMEM((exp_dev, pairs, 8, capacity), F32),
            pltpu.VMEM((exp_dev, max(pairs - 1, 1), 8, capacity), F32),
            pltpu.VMEM((2, all_slots, width), BF16),
            pltpu.VMEM((2, all_slots, width), BF16),
            pltpu.VMEM((held, tokens, width), BF16),
            pltpu.VMEM((held, 2, PAIRS, 8, BLOCK), F32),
            pltpu.VMEM((width, units), kept),
            pltpu.VMEM((16, BLOCK) if units == width else (units, width), kept),
            pltpu.VMEM((2, tokens, width), BF16),
            pltpu.SemaphoreType.DMA((9,)),
            pltpu.SemaphoreType.DMA((2,)),
            pltpu.SemaphoreType.DMA((2,)),
            *gather_sems(exp_dev, pairs, 2),
            *gather_sems(exp_dev, pairs, 2),
            *exchange_sems(ctx_count, exp_dev),
            *exchange_sems(ctx_count, exp_dev),
            pltpu.SemaphoreType.DMA((2, exp_dev, ctx_count - 1)),
            pltpu.SemaphoreType.DMA((2, exp_dev, ctx_count - 1)),
            pltpu.SemaphoreType.DMA((3, exp_dev, pairs)),
            pltpu.SemaphoreType.DMA((3, exp_dev, pairs)),
            pltpu.SemaphoreType.DMA((3, exp_dev, max(pairs - 1, 1))),
            pltpu.SemaphoreType.DMA((3, exp_dev, max(pairs - 1, 1))),
            *gather_sems(row_parts(ctx_count, tokens), lines, across),
            *gather_sems(1, lines, across),
        ],
        compiler_params=pltpu.CompilerParams(
            collective_id=1, has_side_effects=True, vmem_limit_bytes=(62 if spread_here else 63) << 20
        ),
        name="middle",
    )(
        attn,
        exact,
        hidden,
        grad,
        weights,
        w_in,
        w_out,
        small,
        slots,
        targets,
        lse_rows,
        routes,
        base,
        plan,
        qkv,
    )


class Tiles:
    def __init__(self, plan_ref, blocks, keys):
        self.plan, self.blocks, self.half = plan_ref, blocks, blocks // 2
        self.start = plan_start(blocks)
        self.rows_from = self.start + 4 + (2 * (blocks + 1) if keys else 0)
        self.keys = keys
        self.count = blocks + 1

    def own(self, place):
        return self.plan[self.start + (1 - place if self.keys else place)]

    def own_step(self, place):
        return 0 if place else self.half + 1

    def row(self, step):
        return self.plan[self.rows_from + step]

    def place(self, step):
        if step <= self.half:
            return 1
        if step == self.half + 1:
            return 0
        return self.plan[self.start + 4 + self.blocks + 1 + step]

    def groups(self):
        found, step = [], 0
        while step <= self.half:
            size = 2 if step + 1 <= self.half else 1
            found.append((step, size))
            step += size
        return found + [(step, 1) for step in range(self.half + 1, self.count)]


def span(step, size=1):
    return slice(step * BLOCK, (step + size) * BLOCK)


def share_of(place, wanted):
    return place.astype(F32) if wanted else 1.0 - place.astype(F32)


def only(place, wanted, value):
    if isinstance(place, int):
        return value if place == wanted else jnp.zeros_like(value)
    return value * share_of(place, wanted).astype(value.dtype)


def order_bias(bias, step, size, place, half):
    if step == 0:
        return bias[:, : size * BLOCK]
    if step == half + 1:
        return bias[:, :BLOCK]
    if step == half + 2:
        return bias[:, BLOCK:] * share_of(place, 0)
    return None


def forward_pair(tiles, load, bias, stacked, keys, scores, tops, totals, weights, values, others):
    half, count = tiles.half, tiles.count
    lowest = jnp.full((NEAR, BLOCK), MASKED, F32)
    for place in range(2):
        stacked[place] = stack_heads(load(0, tiles.row(tiles.own_step(place))))
    for step in range(count):
        row = tiles.row(step)
        keys[span(step), :] = load(1, row)
        tile, place = load(2, row), tiles.place(step)
        values[span(step), :] = only(place, 1, tile)
        if step > half:
            others[span(step - half - 1), :] = only(place, 0, tile)
    best = [lowest, lowest]
    for step, size in tiles.groups():
        place = tiles.place(step)
        part = dot(stacked[place], keys[span(step, size), :], 1, 1)
        extra = order_bias(bias, step, size, place, half)
        if extra is not None:
            part = part + extra
        scores[:, span(step, size)] = part
        part = fold_lanes(part, jnp.maximum) if size == 2 else part
        for wanted in range(2):
            if isinstance(place, int):
                if place == wanted:
                    best[wanted] = jnp.maximum(best[wanted], part)
            else:
                share = share_of(place, wanted)
                best[wanted] = jnp.maximum(best[wanted], part * share + MASKED * (1.0 - share))
    for wanted in range(2):
        top = jnp.max(best[wanted], axis=-1, keepdims=True)
        tops[wanted] = jnp.broadcast_to(top, (NEAR, BLOCK))
    total = [jnp.zeros((NEAR, BLOCK), F32)] * 2
    for step in range(count):
        place = tiles.place(step)
        part = jnp.exp(scores[:, span(step)] - tops[place])
        high = part.astype(BF16)
        weights[:NEAR, span(step)] = high
        weights[NEAR:, span(step)] = (part - high.astype(F32)).astype(BF16)
        for wanted in range(2):
            if not isinstance(place, int) or place == wanted:
                total[wanted] = total[wanted] + only(place, wanted, part)
    results = []
    for wanted in range(2):
        whole = jnp.sum(total[wanted], axis=-1, keepdims=True)
        if wanted:
            summed = dot(weights[...], values[...])
        else:
            summed = dot(weights[:, span(half + 1, count - half - 1)], others[...])
        main = summed[:NEAR] / whole
        exact = main + summed[NEAR:] / whole
        totals[wanted] = tops[wanted] + jnp.log(jnp.broadcast_to(whole, (NEAR, BLOCK)))
        results.append((merge_heads(main).astype(BF16), merge_heads(exact)))
    return results


def in_order(tiles, pair):
    kind = pair[0].dtype
    second = tiles.own(0).astype(F32)
    first, second = (1.0 - second).astype(kind), second.astype(kind)
    return pair[0] * first + pair[1] * second, pair[1] * first + pair[0] * second


def forward_kernel(
    plan_ref, q_ref, k_ref, v_ref, base_ref, out_ref, exact_ref, lse_ref, row_ref, bias, *scratch
):
    blocks = q_ref.shape[0] // BLOCK
    tiles = Tiles(plan_ref, blocks, False)
    refs = (q_ref, k_ref, v_ref)
    near = near_bias(base_ref)
    bias[...] = jnp.concatenate([near[:, BLOCK:], near[:, :BLOCK]], axis=1)
    totals = scratch[4]

    def load(part, row):
        return refs[part][rows_at(row), :]

    results = forward_pair(tiles, load, bias, *scratch)
    main = in_order(tiles, [result[0] for result in results])
    exact = in_order(tiles, [result[1] for result in results])
    lse = in_order(tiles, [totals[0], totals[1]])
    for own in range(2):
        rows = pl.ds(own * BLOCK, BLOCK)
        out_ref[rows, :] = main[own]
        exact_ref[rows, :] = exact[own]
        lse_ref[0, own] = lse[own]
        turned = jnp.transpose(lse[own])
        for head in range(2):
            row_ref[own, 0, head : head + 1, :] = turned[:1, head * BLOCK : (head + 1) * BLOCK]
        row_ref[own, 0, 2:8, :] = jnp.zeros((6, BLOCK), F32)


def forward_scratch(blocks):
    count = blocks + 1
    rest = count - blocks // 2 - 1
    return [
        pltpu.VMEM((2, NEAR, BLOCK), BF16),
        pltpu.VMEM((count * BLOCK, BLOCK), BF16),
        pltpu.VMEM((NEAR, count * BLOCK), F32),
        pltpu.VMEM((2, NEAR, BLOCK), F32),
        pltpu.VMEM((2, NEAR, BLOCK), F32),
        pltpu.VMEM((2 * NEAR, count * BLOCK), BF16),
        pltpu.VMEM((count * BLOCK, BLOCK), BF16),
        pltpu.VMEM((rest * BLOCK, BLOCK), BF16),
    ]


def pair_specs(rows, width):
    pairs = width // BLOCK

    def column(offset):
        return pl.BlockSpec((rows, BLOCK), lambda pair, plan: (0, offset + pair))

    return [column(0), column(pairs), column(2 * pairs)]


def attend_forward(plan, qkv, base, width):
    rows = qkv.shape[0]
    own = pl.BlockSpec((NEAR, BLOCK), lambda pair, plan: (0, pair))
    return pl.pallas_call(
        forward_kernel,
        grid_spec=pltpu.PrefetchScalarGridSpec(
            num_scalar_prefetch=1,
            grid=(PAIRS,),
            in_specs=pair_specs(rows, width)
            + [pl.BlockSpec((1, 8, SPAN), lambda pair, plan: (pair, 0, 0))],
            out_specs=[
                own,
                own,
                pl.BlockSpec((1, 2, NEAR, BLOCK), lambda pair, plan: (pair, 0, 0, 0)),
                pl.BlockSpec((2, 1, 8, BLOCK), lambda pair, plan: (0, pair, 0, 0)),
            ],
            scratch_shapes=[pltpu.VMEM((NEAR, NEAR), F32), *forward_scratch(rows // BLOCK)],
        ),
        out_shape=[
            jax.ShapeDtypeStruct((NEAR, width), BF16),
            jax.ShapeDtypeStruct((NEAR, width), F32),
            jax.ShapeDtypeStruct((PAIRS, 2, NEAR, BLOCK), F32),
            jax.ShapeDtypeStruct((2, PAIRS, 8, BLOCK), F32),
        ],
        compiler_params=pltpu.CompilerParams(vmem_limit_bytes=60 << 20),
        name="attend_forward",
    )(plan, qkv, qkv, qkv, base)


def put_sums(sums_ref, place, near_ref, far):
    row_ids = lax.broadcasted_iota(jnp.int32, (BLOCK, SPAN), 0)
    for head in range(2):
        part = near_ref[head * BLOCK : (head + 1) * BLOCK, :]
        part = jnp.concatenate([part, jnp.zeros((BLOCK, BLOCK), F32)], axis=1)
        for bit in range(BLOCK.bit_length() - 1):
            moved = pltpu.roll(part, SPAN - (1 << bit), 1)
            part = jnp.where((row_ids >> bit) & 1 == 1, moved, part)
        sums_ref[place, head : head + 1, :] = jnp.sum(part, axis=0, keepdims=True)
        far_part = jnp.sum(far[head * BLOCK : (head + 1) * BLOCK], axis=0, keepdims=True)
        sums_ref[place, 2 + head : 3 + head, :] = jnp.concatenate(
            [far_part, jnp.zeros((1, NEAR), F32)], axis=1
        )
    sums_ref[place, 4:8, :] = jnp.zeros((4, SPAN), F32)


def query_kernel(
    plan_ref, q_ref, k_ref, v_ref, base_ref, do_ref, exact_ref, lse_ref, dq_ref, sums_ref, bias_ref, near_ref
):
    bias_ref[...] = near_bias(base_ref)
    lanes = lane_ids(2 * BLOCK, NEAR)
    far = jnp.zeros((2 * BLOCK, BLOCK), F32)
    for own in range(2):
        block = plan_ref[own]
        rows = pl.ds(own * BLOCK, BLOCK)
        stacked = stack_heads(q_ref[rows_at(plan_ref[SOURCE + 1 + block]), :])
        grads = stack_heads(do_ref[rows, :])
        exact = exact_ref[rows, :]
        product = grads.astype(F32) * jnp.concatenate([exact, exact], axis=0)
        delta = jnp.sum(product, axis=-1, keepdims=True)
        lse = lse_ref[0, own][:, :1]

        def grad_scores(scores, start):
            weights = jnp.exp(scores - lse)
            return weights * (dot(grads, two_tiles(v_ref, plan_ref, start), 1, 1) - delta)

        scores = dot(stacked, two_tiles(k_ref, plan_ref, block), 1, 1) + bias_ref[...]
        scores = jnp.where(lanes + block * BLOCK < BLOCK, MASKED, scores)
        near = grad_scores(scores, block)
        if own == 0:
            near_ref[...] = near
        else:
            near_ref[...] += near

        def step(chunk, carry):
            grad_q, far = carry
            start = block - 2 * chunk
            keys = two_tiles(k_ref, plan_ref, start)
            part = dot(stacked, keys, 1, 1)
            part = jnp.where(lanes + start * BLOCK < BLOCK, MASKED, part)
            grad_s = grad_scores(part, start)
            return (grad_q + dot(grad_s.astype(BF16), keys), far + fold_lanes(grad_s, jnp.add))

        grad_q, far = lax.fori_loop(
            1,
            jnp.maximum(block, 1) // 2 + 1,
            step,
            (dot(near.astype(BF16), two_tiles(k_ref, plan_ref, block)), far),
        )
        dq_ref[rows, :] = merge_heads(grad_q).astype(BF16)
    put_sums(sums_ref, 0, near_ref, far)


def attend_queries(plan, qkv, base, grad_out, exact, lse):
    rows, width = qkv.shape[0], grad_out.shape[1]
    own = pl.BlockSpec((NEAR, BLOCK), lambda pair, plan: (0, pair))
    row_spec = pl.BlockSpec((1, 8, SPAN), lambda pair, plan: (pair, 0, 0))
    return pl.pallas_call(
        query_kernel,
        grid_spec=pltpu.PrefetchScalarGridSpec(
            num_scalar_prefetch=1,
            grid=(PAIRS,),
            in_specs=pair_specs(rows, width)
            + [
                row_spec,
                own,
                own,
                pl.BlockSpec((1, 2, NEAR, BLOCK), lambda pair, plan: (pair, 0, 0, 0)),
            ],
            out_specs=[own, row_spec],
            scratch_shapes=[pltpu.VMEM((NEAR, NEAR), F32), pltpu.VMEM((NEAR, NEAR), F32)],
        ),
        out_shape=[
            jax.ShapeDtypeStruct((NEAR, width), BF16),
            jax.ShapeDtypeStruct((PAIRS, 8, SPAN), F32),
        ],
        compiler_params=pltpu.CompilerParams(vmem_limit_bytes=60 << 20),
        name="attend_queries",
    )(plan, qkv, qkv, qkv, base, grad_out, exact, lse)


def key_pair(tiles, load, stat, bias, mine, queries, grads, rest_q, rest_g, stats, grad_s, weights):
    half, count = tiles.half, tiles.count
    for place in range(2):
        for part in range(2):
            mine[part, place] = stack_heads(load(1 + part, tiles.row(tiles.own_step(place))))
    for step in range(count):
        row, place = tiles.row(step), tiles.place(step)
        for part, whole, rest in ((0, queries, rest_q), (3, grads, rest_g)):
            tile = load(part, row)
            whole[0, span(step), :] = tile
            whole[1, span(step), :] = only(place, 1, tile)
            if step > half:
                rest[span(step - half - 1), :] = only(place, 0, tile)
        stats[:, span(step)] = stat(row)
    for step, size in tiles.groups():
        place = tiles.place(step)
        scores = dot(mine[0, place], queries[0, span(step, size), :], 1, 1)
        extra = order_bias(bias, step, size, place, half)
        if extra is not None:
            scores = scores + extra
        push = dot(mine[1, place], grads[0, span(step, size), :], 1, 1)
        for head in range(2):
            rows = slice(head * BLOCK, (head + 1) * BLOCK)
            part = jnp.exp(scores[rows] - stats[head : head + 1, span(step, size)])
            weights[rows, span(step, size)] = part.astype(BF16)
            part = part * (push[rows] - stats[2 + head : 3 + head, span(step, size)])
            grad_s[rows, span(step, size)] = part.astype(BF16)
    tail = span(half + 1, count - half - 1)
    grad_k = (dot(grad_s[:, tail], rest_q[...]), dot(grad_s[...], queries[1]))
    grad_v = (dot(weights[:, tail], rest_g[...]), dot(weights[...], grads[1]))
    return [
        [merge_heads(part).astype(BF16) for part in grad] for grad in (grad_k, grad_v)
    ]


def key_kernel(plan_ref, q_ref, k_ref, v_ref, base_ref, do_ref, stats_ref, *refs):
    passed = (len(refs) - 11) // 2
    passed_in, outs, passed_out = (
        refs[:passed],
        refs[passed : passed + 2],
        refs[passed + 2 : 2 * passed + 2],
    )
    bias, *scratch = refs[2 * passed + 2 :]
    for src, dst in zip(passed_in, passed_out):
        dst[...] = src[...]
    blocks = q_ref.shape[0] // BLOCK
    tiles = Tiles(plan_ref, blocks, True)
    tile_refs = (q_ref, k_ref, v_ref, do_ref)
    bias[...] = near_bias(base_ref)

    def load(part, row):
        return tile_refs[part][rows_at(row), :]

    def stat(row):
        return stats_ref[row, 0]

    for out, grad in zip(outs, key_pair(tiles, load, stat, bias, *scratch)):
        for own, part in enumerate(in_order(tiles, grad)):
            out[own * BLOCK : (own + 1) * BLOCK, :] = part


def key_scratch(blocks):
    count = blocks + 1
    rest = count - blocks // 2 - 1
    return [
        pltpu.VMEM((2, 2, NEAR, BLOCK), BF16),
        pltpu.VMEM((2, count * BLOCK, BLOCK), BF16),
        pltpu.VMEM((2, count * BLOCK, BLOCK), BF16),
        pltpu.VMEM((rest * BLOCK, BLOCK), BF16),
        pltpu.VMEM((rest * BLOCK, BLOCK), BF16),
        pltpu.VMEM((8, count * BLOCK), F32),
        pltpu.VMEM((NEAR, count * BLOCK), BF16),
        pltpu.VMEM((NEAR, count * BLOCK), BF16),
    ]


def attend_keys(plan, qkv, base, grad_out, stats, passed):
    rows, width = grad_out.shape
    own = pl.BlockSpec((NEAR, BLOCK), lambda pair, plan: (0, pair))
    pieces = [own] + [
        pl.BlockSpec(
            (array.shape[0], array.shape[1] // PAIRS, array.shape[2]), lambda pair, plan: (0, pair, 0)
        )
        for array in passed[1:]
    ]
    return pl.pallas_call(
        key_kernel,
        grid_spec=pltpu.PrefetchScalarGridSpec(
            num_scalar_prefetch=1,
            grid=(PAIRS,),
            in_specs=pair_specs(rows, width)
            + [
                pl.BlockSpec((1, 8, SPAN), lambda pair, plan: (pair, 0, 0)),
                pl.BlockSpec((rows, BLOCK), lambda pair, plan: (0, pair)),
                pl.BlockSpec(
                    (rows // BLOCK, 1, 8, BLOCK), lambda pair, plan: (0, pair, 0, 0)
                ),
            ]
            + pieces,
            out_specs=[own, own] + pieces,
            scratch_shapes=[pltpu.VMEM((NEAR, NEAR), F32), *key_scratch(rows // BLOCK)],
        ),
        out_shape=[jax.ShapeDtypeStruct((NEAR, width), BF16)] * 2
        + [jax.ShapeDtypeStruct(array.shape, array.dtype) for array in passed],
        compiler_params=pltpu.CompilerParams(vmem_limit_bytes=60 << 20),
        name="attend_keys",
    )(plan, qkv, qkv, qkv, base, grad_out, stats, *passed)


BITS = {"core": ("wsh", 1), "x": ("wsh", 2), "y": ("ctx", 1), "near": ("ctx", 2), "far": ("ctx", 4)}
UNITS = (
    (3, 0, 6, ("core", "x", "y", "near", "far")),
    (0, 0, 6, ("core", "y", "x", "near", "far")),
    (1, 0, 4, ("core", "x", "y", "near", "far")),
    (2, 0, 4, ("core", "y", "x", "near", "far")),
    (1, 4, 2, ("core", "x", "y", "near", "far")),
    (2, 4, 2, ("core", "y", "x", "near", "far")),
)


def halved_shapes(order, share, width):
    shapes, blocks, rows, columns = [], 4, share, width
    for name in order:
        if name in ("core", "x"):
            blocks //= 2
        elif name == "y":
            columns //= 2
        else:
            rows //= 2
        shapes.append((blocks, rows, columns))
    return shapes


def partner(name):
    axis, bit = BITS[name]
    me = lax.axis_index(axis)
    side = (me // bit) % 2
    return axis, me + bit * (1 - 2 * side), side


class UnitSum:
    def __init__(self, unit, total, gathered, sends, recvs, sems):
        self.weight, first, pairs, self.order = unit
        self.first, self.columns = first * BLOCK, pairs * BLOCK
        self.total, self.gathered, self.sends, self.recvs = total, gathered, sends, recvs
        self.half_send, self.half_recv, self.whole_send, self.whole_recv = sems
        self.steps = len(self.order)
        blocks, row, column = [0, 1, 2, 3], 0, 0
        rows, columns = total.shape[1], self.columns
        self.regions = []
        for name in self.order:
            side = partner(name)[2]
            if name == "core":
                keep = ([line * 2 + side for line in range(2)], row, column)
                sent = ([line * 2 + 1 - side for line in range(2)], row, column)
            elif name == "x":
                core = partner("core")[2]
                keep = ([side * 2 + core], row, column)
                sent = ([(1 - side) * 2 + core], row, column)
            elif name == "y":
                columns //= 2
                keep = (blocks, row, column + side * columns)
                sent = (blocks, row, column + (1 - side) * columns)
            else:
                rows //= 2
                keep = (blocks, row + side * rows, column)
                sent = (blocks, row + (1 - side) * rows, column)
            blocks, row, column = keep
            self.regions.append((keep, sent))
        self.wholes = [name for name in reversed(self.order) if BITS[name][0] == "ctx"]

    def span(self, step, region, shift=0):
        shape = self.sends[step].shape
        blocks, row, column = region
        row_part = pl.ds(row if isinstance(row, int) else pl.multiple_of(row, 16), shape[1])
        column = column + shift
        column_part = pl.ds(
            column if isinstance(column, int) else pl.multiple_of(column, BLOCK), shape[2]
        )
        return blocks, row_part, column_part

    def remote(self, source, target, send, recv, name):
        axis, peer, side = partner(name)
        return pltpu.make_async_remote_copy(
            src_ref=source,
            dst_ref=target,
            send_sem=send,
            recv_sem=recv,
            device_id={axis: peer},
            device_id_type=pl.DeviceIdType.MESH,
        )

    def half_copy(self, step):
        return self.remote(
            self.sends[step],
            self.recvs[step],
            self.half_send.at[step],
            self.half_recv.at[step],
            self.order[step],
        )

    def give(self, step):
        blocks, row_part, column_part = self.span(step, self.regions[step][1])
        for place, block in enumerate(blocks):
            self.sends[step][place] = self.total[block, row_part, column_part].astype(BF16)
        self.half_copy(step).start()

    def begin(self, value):
        share = self.total.shape[1]
        for block in range(4):
            self.total[block] = value[block * share : (block + 1) * share].astype(F32)
        self.give(0)

    def whole_copy(self, back):
        name = self.wholes[back]
        step = self.order.index(name)
        blocks, row_part, column_part = self.span(step, self.regions[step][0], self.first)
        view = self.gathered.at[self.weight, row_part, column_part]
        return self.remote(
            view, view, self.whole_send.at[back], self.whole_recv.at[back], name
        )

    def advance(self, phase):
        if phase >= self.steps:
            back = phase - self.steps
            self.whole_copy(back).wait_recv()
            if back + 1 < len(self.wholes):
                self.whole_copy(back + 1).start()
            return
        self.half_copy(phase).wait_recv()
        blocks, row_part, column_part = self.span(phase, self.regions[phase][0])
        for place, block in enumerate(blocks):
            self.total[block, row_part, column_part] += self.recvs[phase][place].astype(F32)
        if phase + 1 < self.steps:
            self.give(phase + 1)
            return
        whole = self.span(phase, self.regions[phase][0], self.first)
        self.gathered[self.weight, whole[1], whole[2]] = self.total[
            blocks[0], row_part, column_part
        ].astype(BF16)
        self.whole_copy(0).start()

    def finish(self):
        for step in range(self.steps):
            self.half_copy(step).wait_send()
        for back in range(len(self.wholes)):
            self.whole_copy(back).wait_send()


def tail_kernel(
    experts,
    dq_ref,
    hidden_ref,
    grad_mid_ref,
    weights_ref,
    grad_wo_ref,
    qkv_ref,
    do_ref,
    stats_ref,
    returned_ref,
    resid_ref,
    gate_ref,
    slot_ref,
    small_ref,
    router_ref,
    gain_ref,
    sums_ref,
    hot_ref,
    base_ref,
    plan_ref,
    input_grad_out,
    output_out,
    shares_out,
    router_out,
    gains_out,
    table_out,
    weights,
    hidden,
    grad_mid,
    grad_wo,
    resid,
    returned,
    home,
    qkv,
    grad_out,
    stats,
    dk,
    dv,
    bias,
    mine,
    queries,
    grads,
    rest_q,
    rest_g,
    tile_stats,
    grad_s,
    tile_weights,
    gathered,
    pack,
    pack_recv,
    *rest,
):
    steps, count = len(BITS), len(UNITS)
    totals, rest = rest[:count], rest[count:]
    sends = [rest[unit * steps : (unit + 1) * steps] for unit in range(count)]
    rest = rest[count * steps :]
    recvs = [rest[unit * steps : (unit + 1) * steps] for unit in range(count)]
    (
        fetch_sems,
        half_send,
        half_recv,
        whole_send,
        whole_recv,
        pack_send,
        pack_sem,
        back_send,
        back_recv,
    ) = rest[count * steps :]
    tokens, width = dq_ref.shape
    share = totals[0].shape[1]
    ctx_count = lax.axis_size("ctx")
    exp_dev = experts // ctx_count
    most = returned.shape[0] // experts
    sources = (
        (hidden_ref, hidden),
        (grad_wo_ref, grad_wo),
        (returned_ref, returned),
        (qkv_ref, qkv),
        (do_ref, grad_out),
        (stats_ref, stats),
        (weights_ref.at[pl.ds(0, 3)], weights),
        (grad_mid_ref, grad_mid),
        (resid_ref, resid),
    )
    fetches = [
        pltpu.make_async_copy(src, dst, fetch_sems.at[place])
        for place, (src, dst) in enumerate(sources)
    ]
    for fetch in fetches:
        fetch.start()
    greet((ctx_count, lax.axis_size("wsh")))
    units = [
        UnitSum(
            unit,
            totals[place],
            gathered,
            sends[place],
            recvs[place],
            [sem.at[place] for sem in (half_send, half_recv, whole_send, whole_recv)],
        )
        for place, unit in enumerate(UNITS)
    ]
    wo, wq, wk_early, wv_early, wk_late, wv_late = units

    fetches[0].wait()
    rows = hidden[...].astype(F32)
    inv = lax.rsqrt(jnp.mean(rows * rows, axis=-1, keepdims=True) + epsilon)
    gain = small_ref[...].astype(F32)[experts : experts + 1, :]
    normed = (rows * inv * gain).astype(BF16)
    hidden[...] = normed
    fetches[1].wait()
    wo.begin(grad_wo[...])
    wq.begin(dot(normed, dq_ref[...], 0, 0))
    fetches[2].wait()
    back = Exchange(
        ctx_count,
        exp_dev,
        most,
        (back_send, back_recv),
        lambda expert, peer: returned.at[back.rows(expert * ctx_count + peer), :],
        lambda expert, peer: home.at[back.rows(peer * exp_dev + expert), :],
    )
    for expert in range(exp_dev):
        back.start(expert)
    for fetch in fetches[3:6]:
        fetch.wait()
    tiles = Tiles(plan_ref, qkv.shape[0], True)

    def key_step(pair, carry):
        pair_lanes = pl.ds(pl.multiple_of(pair * BLOCK, BLOCK), BLOCK)

        def load(part, row):
            if part == 3:
                return grad_out[row, :, pair_lanes]
            lanes = pl.ds(pl.multiple_of(part * width + pair * BLOCK, BLOCK), BLOCK)
            return qkv[row, :, lanes]

        bias[...] = near_bias(base_ref, pair)
        results = key_pair(
            tiles,
            load,
            lambda row: stats[row, pair],
            bias,
            mine,
            queries,
            grads,
            rest_q,
            rest_g,
            tile_stats,
            grad_s,
            tile_weights,
        )
        for out, result in zip((dk, dv), results):
            for own, part in enumerate(in_order(tiles, result)):
                out[own * BLOCK : (own + 1) * BLOCK, pair_lanes] = part

        @pl.when(pair == 0)
        def _():
            wo.advance(0)
            wq.advance(0)

        @pl.when(pair == 2)
        def _():
            wo.advance(1)
            wq.advance(1)

        @pl.when(pair == 3)
        def _():
            early = slice(wk_early.first, wk_early.first + wk_early.columns)
            wk_early.begin(dot(hidden[...], dk[:, early], 0, 0))
            wv_early.begin(dot(hidden[...], dv[:, early], 0, 0))
            wo.advance(2)
            wq.advance(2)

        @pl.when(pair == 4)
        def _():
            wk_early.advance(0)
            wv_early.advance(0)
            wo.advance(3)
            wq.advance(3)

        return carry

    lax.fori_loop(0, PAIRS, key_step, 0)
    late = slice(wk_late.first, wk_late.first + wk_late.columns)
    wk_late.begin(dot(hidden[...], dk[:, late], 0, 0))
    wv_late.begin(dot(hidden[...], dv[:, late], 0, 0))
    for unit, phase in ((wo, 4), (wq, 4), (wk_early, 1), (wv_early, 1)):
        unit.advance(phase)
    fetches[6].wait()
    grad_normed = dot(dq_ref[...], weights[0], 1, 1)
    grad_normed = grad_normed + dot(dk[...], weights[1], 1, 1)
    grad_normed = grad_normed + dot(dv[...], weights[2], 1, 1)
    for unit, phase in ((wk_late, 0), (wv_late, 0)):
        unit.advance(phase)
    gain_part = jnp.sum(grad_normed * rows * inv, axis=0, keepdims=True)
    pack[...] = jnp.zeros_like(pack)
    pack[:experts, :] = router_ref[...]
    pack[experts : experts + 1, :] = gain_part
    pack[experts + 1 : experts + 2, :] = gain_ref[0:1, :]
    last = lane_ids(2, BLOCK) == hot_ref.shape[1] - 1
    for pair in range(PAIRS):
        near = lax.dot_general(
            sums_ref[pair, 0:2, :],
            hot_ref[...],
            (((1,), (0,)), ((), ())),
            precision=HIGH,
            preferred_element_type=F32,
        )
        near = jnp.concatenate([near, jnp.zeros((2, BLOCK - near.shape[1]), F32)], axis=1)
        distant = jnp.sum(sums_ref[pair, 2:4, :], axis=1, keepdims=True)
        near = near + jnp.where(last, distant, 0.0)
        for head in range(2):
            pack[experts + 2 + head : experts + 3 + head, span(pair)] = near[head : head + 1]

    def pack_copy(step):
        return wo.remote(
            pack_recv.at[0, step],
            pack_recv.at[1, step],
            pack_send.at[step],
            pack_sem.at[step],
            list(BITS)[step],
        )

    def pack_start(step):
        pack_recv[0, step] = pack[...].astype(BF16)
        pack_copy(step).start()

    def pack_end(step):
        pack_copy(step).wait_recv()
        pack[...] = pack_recv[0, step].astype(F32) + pack_recv[1, step].astype(F32)
        if step + 1 < steps:
            pack_start(step + 1)

    pack_start(0)
    for unit, phase in ((wk_early, 2), (wv_early, 2), (wk_late, 1), (wv_late, 1), (wo, 5), (wq, 5)):
        unit.advance(phase)
    pack_end(0)
    fetches[7].wait()
    scaled = grad_normed * gain
    mean = jnp.mean(scaled * rows, axis=-1, keepdims=True)
    grad_in = grad_mid[...] + inv * scaled - rows * inv * inv * inv * mean
    input_grad_out[...] = grad_in.astype(BF16)
    for unit, phase in ((wk_early, 3), (wv_early, 3), (wk_late, 2), (wv_late, 2), (wo, 6), (wq, 6)):
        unit.advance(phase)
    pack_end(1)
    for expert in range(exp_dev):
        back.wait(expert)
    fetches[8].wait()
    token_out = dot(placement_of(slot_ref, experts * most), home[...], 0, 0)
    output_out[...] = (resid[...] + gate_ref[:, :1] * token_out).astype(BF16)
    for unit, phase in ((wk_early, 4), (wv_early, 4), (wk_late, 3), (wv_late, 3), (wo, 7), (wq, 7)):
        unit.advance(phase)
    pack_end(2)
    for unit, phase in ((wk_late, 4), (wv_late, 4), (wk_early, 5), (wv_early, 5)):
        unit.advance(phase)
    pack_end(3)
    for unit, phase in ((wk_late, 5), (wv_late, 5), (wk_early, 6), (wv_early, 6)):
        unit.advance(phase)
    pack_end(4)
    for unit, phase in ((wk_late, 6), (wv_late, 6), (wk_early, 7), (wv_early, 7)):
        unit.advance(phase)
    own = lax.axis_index("wsh")
    buckets = table_out.shape[0]
    for block in range(4):

        @pl.when(own == block)
        def _():
            part = pack[: experts + 8, block * share : (block + 1) * share]
            router_out[...] = part[:experts]
            gains_out[...] = part[experts : experts + 8]
            heads = [
                pack[experts + 2 + head : experts + 3 + head, span(pair)]
                for pair in range(PAIRS)
                for head in range(2)
            ]
            table = jnp.transpose(jnp.concatenate(heads + heads[:4], axis=0))
            table_out[...] = table[block * buckets : (block + 1) * buckets, :HEADS]

    for unit in (wk_late, wv_late):
        unit.advance(7)
    shares_out[...] = gathered[...]
    for step in range(steps):
        pack_copy(step).wait_send()
    for unit in units:
        unit.finish()
    for expert in range(exp_dev):
        back.finish(expert)


def tail(
    experts,
    dq,
    hidden,
    grad_mid,
    weights,
    grad_wo,
    qkv,
    grad_out,
    stats,
    returned,
    resid,
    gate,
    slots,
    small,
    router,
    gains,
    sums,
    hot,
    base,
    plan,
    share,
    buckets,
):
    tokens, width = dq.shape
    vmem = pl.BlockSpec(memory_space=pltpu.VMEM)
    anywhere = pl.BlockSpec(memory_space=pl.ANY)
    steps, count = len(BITS), len(UNITS)
    pieces = [
        shape for unit in UNITS for shape in halved_shapes(unit[3], share, unit[2] * BLOCK)
    ]
    buffers = [pltpu.VMEM(shape, BF16) for shape in pieces]
    ctx_count = lax.axis_size("ctx")
    rows = experts + 16
    dma = pltpu.SemaphoreType.DMA
    return pl.pallas_call(
        functools.partial(tail_kernel, experts),
        in_specs=[vmem]
        + [anywhere] * 9
        + [vmem] * 8
        + [pl.BlockSpec(memory_space=pltpu.SMEM)],
        out_specs=[vmem] * 6,
        out_shape=[
            jax.ShapeDtypeStruct((tokens, width), BF16),
            jax.ShapeDtypeStruct((tokens, width), BF16),
            jax.ShapeDtypeStruct((4, share, width), BF16),
            jax.ShapeDtypeStruct((experts, share), F32),
            jax.ShapeDtypeStruct((8, share), F32),
            jax.ShapeDtypeStruct((buckets, HEADS), F32),
        ],
        scratch_shapes=[
            pltpu.VMEM((3, width, width), BF16),
            pltpu.VMEM((tokens, width), BF16),
            pltpu.VMEM((tokens, width), F32),
            pltpu.VMEM((width, width), BF16),
            pltpu.VMEM((tokens, width), F32),
            pltpu.VMEM(returned.shape, BF16),
            pltpu.VMEM(returned.shape, BF16),
            pltpu.VMEM(qkv.shape, BF16),
            pltpu.VMEM(grad_out.shape, BF16),
            pltpu.VMEM(stats.shape, F32),
            pltpu.VMEM((tokens, width), BF16),
            pltpu.VMEM((tokens, width), BF16),
            pltpu.VMEM((NEAR, NEAR), F32),
            *key_scratch(qkv.shape[0]),
            pltpu.VMEM((4, share, width), BF16),
            pltpu.VMEM((rows, width), F32),
            pltpu.VMEM((2, steps, rows, width), BF16),
            *[pltpu.VMEM((4, share, unit[2] * BLOCK), F32) for unit in UNITS],
            *buffers,
            *buffers,
            dma((9,)),
            dma((count, steps)),
            dma((count, steps)),
            dma((count, 3)),
            dma((count, 3)),
            dma((steps,)),
            dma((steps,)),
            dma((experts // ctx_count, ctx_count - 1)),
            dma((experts // ctx_count, ctx_count - 1)),
        ],
        compiler_params=pltpu.CompilerParams(
            collective_id=2, has_side_effects=True, vmem_limit_bytes=62 << 20
        ),
        name="tail",
    )(
        dq,
        hidden,
        grad_mid,
        weights,
        grad_wo,
        qkv,
        grad_out,
        stats,
        returned,
        resid,
        gate,
        slots,
        small,
        router,
        gains,
        sums,
        hot,
        base,
        plan,
    )


def finish_kernel(
    input_ref,
    output_ref,
    shares_ref,
    router_ref,
    gains_ref,
    table_ref,
    w_in_ref,
    w_out_ref,
    input_out,
    output_out,
    wq,
    wk,
    wv,
    wo,
    router,
    gain_a,
    gain_m,
    table,
    w_in_out,
    w_out_out,
):
    w_in_out[...] = w_in_ref[...].astype(F32)
    w_out_out[...] = w_out_ref[...].astype(F32)

    @pl.when(pl.program_id(0) == 0)
    def _():
        input_out[...] = input_ref[...]
        output_out[...] = output_ref[...]
        for place, out in enumerate((wq, wk, wv, wo)):
            out[...] = shares_ref[place].astype(F32)
        router[...] = router_ref[...]
        gain_a[...] = gains_ref[0, :]
        gain_m[...] = gains_ref[1, :]
        table[...] = table_ref[...]


def finish(grad_input, output, shares, router, gains, table, w_in, w_out):
    share, width = shares.shape[1:]

    def whole(array):
        zeros = (0,) * len(array.shape)
        return pl.BlockSpec(array.shape, lambda step: zeros)

    def pieces(array):
        return pl.BlockSpec(
            (array.shape[0], array.shape[1] // 8, array.shape[2]), lambda step: (0, step, 0)
        )

    arrays = (grad_input, output, shares, router, gains, table)
    outs = [
        jax.ShapeDtypeStruct(grad_input.shape, BF16),
        jax.ShapeDtypeStruct(output.shape, BF16),
        *[jax.ShapeDtypeStruct((share, width), F32)] * 4,
        jax.ShapeDtypeStruct(router.shape, F32),
        jax.ShapeDtypeStruct((share,), F32),
        jax.ShapeDtypeStruct((share,), F32),
        jax.ShapeDtypeStruct(table.shape, F32),
    ]
    experts = [jax.ShapeDtypeStruct(array.shape, F32) for array in (w_in, w_out)]
    return pl.pallas_call(
        finish_kernel,
        grid=(8,),
        in_specs=[whole(array) for array in arrays] + [pieces(w_in), pieces(w_out)],
        out_specs=[whole(array) for array in outs] + [pieces(w_in), pieces(w_out)],
        out_shape=outs + experts,
        compiler_params=pltpu.CompilerParams(vmem_limit_bytes=60 << 20),
        name="finish",
    )(*arrays, w_in, w_out)


def rms_forward(values, gain_vec):
    inv_rms = lax.rsqrt(jnp.mean(values * values, axis=-1, keepdims=True) + epsilon)
    return (values * inv_rms * gain_vec, inv_rms)


def rms_backward(values, inv_rms, gain_vec, upstream):
    grad_gain = jnp.sum(upstream * values * inv_rms, axis=0)
    scaled = upstream * gain_vec
    grad_values = inv_rms * scaled - values * inv_rms**3 * jnp.mean(
        scaled * values, axis=-1, keepdims=True
    )
    return (grad_values, grad_gain)


def per_device(
    hidden_in,
    w_query,
    w_key,
    w_value,
    w_output,
    w_router,
    gain_attn,
    gain_moe,
    rel_bias,
    w_in,
    w_out,
    routes,
    block_pairs,
    cotangent,
):
    tokens, width = hidden_in.shape[1:]
    ctx_count, wsh_count = lax.axis_size("ctx"), lax.axis_size("wsh")
    ctx_rank, wsh_rank = lax.axis_index("ctx"), lax.axis_index("wsh")
    length = tokens * ctx_count
    blocks = length // BLOCK
    experts, exp_dev = w_router.shape[1], w_in.shape[0]
    slot_most = 2 * tokens // experts
    capacity = (9 * length // (8 * experts) + 7) // 8 * 8

    def over(axis, array, dim=0):
        return lax.all_gather(array, axis, axis=dim, tiled=True)

    share = width // wsh_count
    lanes = wrapped_lanes()
    buckets = rel_bias.shape[0] * wsh_count
    query_hot = onehot_of(BLOCK - lanes, buckets)
    key_hot = onehot_of(lanes, buckets)

    def hot_rows(hot):
        return jnp.asarray(hot.T, BF16)

    qkv, weights, small, slot_rows, targets, plan, query_base, key_base = project(
        (ctx_count, wsh_count),
        capacity,
        experts,
        slot_most,
        hidden_in[0],
        (w_query, w_key, w_value, w_output),
        (w_router.T, gain_attn, gain_moe, rel_bias),
        routes.reshape(1, tokens),
        block_pairs.T,
        hot_rows(query_hot),
        hot_rows(key_hot),
    )
    if wsh_count > 4:
        attn_low, attn_exact, lse, lse_rows = attend_forward(plan, qkv, query_base, width)
    else:
        attn_low = attn_exact = hidden_in[0]
        lse_rows = query_base
    (
        output_rows,
        returned,
        resid,
        gate,
        grad_mid,
        grad_heads,
        heads_all,
        stats,
        grad_wo,
        grad_router,
        grad_gain_m,
        grad_q,
        sums,
        grad_w_in,
        grad_w_out,
    ) = middle(
        (ctx_count, wsh_count),
        experts,
        attn_low,
        attn_exact.reshape(2, BLOCK, width),
        hidden_in[0],
        cotangent[0],
        weights,
        w_in,
        w_out,
        small,
        slot_rows,
        targets,
        lse_rows,
        routes.reshape(1, tokens),
        query_base,
        plan,
        qkv.reshape(blocks, BLOCK, 3 * width),
        capacity,
    )

    bucket_share = buckets // wsh_count
    if wsh_count <= 4:
        results = tail(
            experts,
            grad_q,
            hidden_in[0],
            grad_mid,
            weights,
            grad_wo,
            qkv.reshape(blocks, BLOCK, 3 * width),
            heads_all.reshape(blocks, BLOCK, width),
            stats.reshape(blocks, PAIRS, 8, BLOCK),
            returned,
            resid,
            gate,
            slot_rows,
            small,
            grad_router,
            grad_gain_m,
            sums,
            jnp.asarray(query_hot),
            key_base,
            plan,
            share,
            bucket_share,
        )
        grad_input, output_rows, *rest = finish(*results, grad_w_in, grad_w_out)
        rest[4] = rest[4].T
        return (output_rows[None], grad_input[None], *rest)

    heads_all = dot(over("ctx", heads_all), weights[3], 1, 1).astype(BF16)
    stats = over("ctx", stats).reshape(blocks, PAIRS, 8, BLOCK)
    grad_q, sums = attend_queries(plan, qkv, query_base, grad_heads, attn_exact, lse)
    grad_k, grad_v, output_rows, grad_w_in, grad_w_out = attend_keys(
        plan, qkv, key_base, heads_all, stats, (output_rows, grad_w_in, grad_w_out)
    )

    near_sums = sums[:, :2].reshape(HEADS, SPAN)
    far_sums = jnp.sum(sums[:, 2:4].reshape(HEADS, SPAN), axis=1)
    grad_table = jnp.dot(jnp.asarray(query_hot.T), near_sums.T, precision=HIGH)
    grad_table = grad_table.at[buckets - 1].add(far_sums)

    resid_in = hidden_in[0].astype(F32)
    full_query, full_key, full_value = (weights[place] for place in range(3))
    gain_one = small[experts].astype(F32)
    normed_one, inv_one = rms_forward(resid_in, gain_one)
    normed_one = normed_one.astype(BF16)
    grad_normed_one = dot(grad_q, full_query, 1, 1)
    grad_normed_one = grad_normed_one + dot(grad_k, full_key, 1, 1)
    grad_normed_one = grad_normed_one + dot(grad_v, full_value, 1, 1)
    grad_in_norm, grad_gain_a = rms_backward(resid_in, inv_one, gain_one, grad_normed_one)
    grad_input = (grad_mid + grad_in_norm).astype(BF16)

    def reduce_weight(grad):
        part = lax.psum_scatter(grad.astype(BF16), "wsh", scatter_dimension=0, tiled=True)
        return lax.psum(part, "ctx").astype(F32)

    grad_wq = dot(normed_one, grad_q, 0, 0)
    grad_wk = dot(normed_one, grad_k, 0, 0)
    grad_wv = dot(normed_one, grad_v, 0, 0)
    shares = [reduce_weight(grad) for grad in (grad_wq, grad_wk, grad_wv, grad_wo)]
    columns = jnp.concatenate(
        [grad_router.T, grad_gain_a[:, None], grad_gain_m[0][:, None]], axis=1
    )
    table = jnp.pad(grad_table, ((0, 0), (0, columns.shape[1] - HEADS)))
    summed = lax.psum(jnp.concatenate([columns, table], axis=0), ("ctx", "wsh"))
    own_columns = lax.dynamic_slice_in_dim(summed[:width], wsh_rank * share, share, 0)
    own_table = lax.dynamic_slice_in_dim(
        summed[width:, :HEADS], wsh_rank * bucket_share, bucket_share, 0
    )
    return (
        output_rows.astype(BF16)[None],
        grad_input[None],
        *shares,
        own_columns[:, :experts],
        own_columns[:, experts],
        own_columns[:, experts + 1],
        own_table,
        grad_w_in,
        grad_w_out,
    )


def solution(mesh):
    in_specs = (
        P("wsh", "ctx", None),
        P("wsh", None),
        P("wsh", None),
        P("wsh", None),
        P("wsh", None),
        P("wsh", None),
        P("wsh"),
        P("wsh"),
        P("wsh", None),
        P("ctx", None, "wsh"),
        P("ctx", "wsh", None),
        P("wsh", "ctx", None),
        P(),
        P("wsh", "ctx", None),
    )
    out_specs = (
        P("wsh", "ctx", None),
        P("wsh", "ctx", None),
        P("wsh", None),
        P("wsh", None),
        P("wsh", None),
        P("wsh", None),
        P("wsh", None),
        P("wsh"),
        P("wsh"),
        P("wsh", None),
        P("ctx", None, "wsh"),
        P("ctx", "wsh", None),
    )
    return jax.shard_map(
        per_device, mesh=mesh, in_specs=in_specs, out_specs=out_specs, check_vma=False
    )
```

```python
import functools
import math

import jax
import jax.numpy as jnp
import numpy as np
from jax import lax
from jax.experimental import pallas as pl
from jax.experimental.pallas import tpu as pltpu
from jax.sharding import PartitionSpec as P

HEADS = 12
HEAD_DIM = 64
BLOCK = 128
PAIRS = HEADS // 2
NEAR = 2 * BLOCK
SPAN = 3 * BLOCK
epsilon = 1e-06
MASKED = -1e30
bucket_edges = [math.ceil(16 * 8 ** (marker / 16)) for marker in range(1, 16)]
F32 = jnp.float32
BF16 = jnp.bfloat16
HIGH = lax.Precision.HIGHEST


def bucket_of(distance):
    gap = np.maximum(distance, 0)
    count = np.full(gap.shape, 16, np.int32)
    for edge in bucket_edges:
        count = count + (gap >= edge)
    return np.where(gap < 16, gap, count)


def wrapped_lanes():
    lanes = np.arange(SPAN)
    return np.where(lanes < NEAR, lanes, lanes - SPAN)


def onehot_of(distance, buckets):
    return (bucket_of(distance)[:, None] == np.arange(buckets)[None, :]).astype(np.float32)


def dot(left, right, left_dim=1, right_dim=0):
    return lax.dot_general(
        left, right, (((left_dim,), (right_dim,)), ((), ())), preferred_element_type=F32
    )


def lane_ids(rows, lanes):
    return lax.broadcasted_iota(jnp.int32, (rows, lanes), 1)


def stack_heads(rows):
    first = lane_ids(rows.shape[0], BLOCK) < HEAD_DIM
    zero = jnp.zeros_like(rows)
    return jnp.concatenate([jnp.where(first, rows, zero), jnp.where(first, zero, rows)], axis=0)


def merge_heads(stacked):
    half = stacked.shape[0] // 2
    first = lane_ids(half, BLOCK) < HEAD_DIM
    return jnp.where(first, stacked[:half], stacked[half:])


def fold_lanes(tile, combine):
    return combine(tile[:, :BLOCK], tile[:, BLOCK:])


def near_bias(base_ref, place=0):
    tiles = []
    for head in range(2):
        row = jnp.broadcast_to(base_ref[place, head : head + 1, :], (BLOCK, SPAN))
        tiles.append(pltpu.roll(row, 0, 1, stride=1, stride_axis=0)[:, :NEAR])
    return jnp.concatenate(tiles, axis=0)


def rows_at(block):
    return pl.ds(pl.multiple_of(block * BLOCK, BLOCK), BLOCK)


def two_tiles(ref, plan_ref, tile):
    tile = SOURCE + tile
    return jnp.concatenate(
        [ref[rows_at(plan_ref[tile]), :], ref[rows_at(plan_ref[tile + 1]), :]], axis=0
    )


class LineGather:
    def __init__(self, axis, lines, across, views, own, sems, crossing=None):
        self.axis, self.lines, self.across = axis, lines, across
        self.views, self.own, self.sems = views, own, sems
        self.crossing = crossing or ["all"] * len(views)
        self.me = lax.axis_index(axis)
        self.line, self.column = self.me // across, self.me % across

    def copy(self, part, block, peer, kind, place, own=False):
        send, recv = self.sems
        view = self.views[part](block)
        return pltpu.make_async_remote_copy(
            src_ref=self.own[part] if own else view,
            dst_ref=view,
            send_sem=send.at[part, kind, place],
            recv_sem=recv.at[part, kind, place],
            device_id={self.axis: peer},
            device_id_type=pl.DeviceIdType.MESH,
        )

    def line_send(self, part, way, step):
        place = self.line - way * step
        ahead = self.line + way
        there = (place >= 0) & (place < self.lines) & (ahead >= 0) & (ahead < self.lines)
        copy = self.copy(
            part,
            place * self.across + self.column,
            ahead * self.across + self.column,
            (1 - way) // 2,
            step,
            own=step == 0,
        )
        return there, copy

    def line_recv(self, part, way, step):
        place = self.line - way * (step + 1)
        there = (place >= 0) & (place < self.lines)
        block = place * self.across + self.column
        return there, block, self.copy(part, block, self.me, (1 - way) // 2, step)

    def cross_send(self, part, block, ahead, own=False):
        peer = self.line * self.across + (self.column + ahead) % self.across
        return self.copy(part, block, peer, 1 + ahead, block // self.across, own)

    def cross_recv(self, part, line, ahead):
        block = line * self.across + (self.column + self.across - ahead) % self.across
        return self.copy(part, block, self.me, 1 + ahead, line)

    def begin(self, part):
        for way in (1, -1):
            there, copy = self.line_send(part, way, 0)
            pl.when(there)(copy.start)
        if self.crossing[part] != "none":
            for ahead in range(1, self.across):
                self.cross_send(part, self.me, ahead, own=True).start()

    def advance(self, part, step):
        for way in (1, -1):
            there, block, arrived = self.line_recv(part, way, step)

            pl.when(there)(arrived.wait_recv)
            if step + 2 < self.lines:
                onward, copy = self.line_send(part, way, step + 1)
                pl.when(onward)(copy.start)
            if self.crossing[part] == "all":
                for ahead in range(1, self.across):
                    pl.when(there)(self.cross_send(part, block, ahead).start)

    def wait_cross(self, part):
        for ahead in range(1, self.across):
            for line in range(self.lines):
                self.cross_recv(part, line, ahead).wait_recv()

    def finish(self):
        for part in range(len(self.views)):
            for step in range(self.lines - 1):
                for way in (1, -1):
                    there, copy = self.line_send(part, way, step)
                    pl.when(there)(copy.wait_send)
            for ahead in range(1, self.across):
                if self.crossing[part] == "all":
                    for line in range(self.lines):
                        self.cross_send(part, line * self.across + self.column, ahead).wait_send()
                elif self.crossing[part] == "own":
                    self.cross_send(part, self.me, ahead).wait_send()


class RowGather:
    def __init__(self, counts, held, sems):
        lines, across = grid_of(counts[0])
        tokens = held.shape[1]
        self.across, self.lines = across, lines
        me = lax.axis_index("ctx")
        self.me = me
        self.balanced = across == 2 and tokens % 32 == 0
        bulk = tokens * 14 // 16 if self.balanced else tokens
        half = bulk // 32 * 16
        cuts = [(0, half), (half, bulk - half)]

        def view(start, rows, turn):
            def of(block):
                if turn:
                    block = block + 1 - 2 * (block % 2)
                return held.at[block, pl.ds(start, rows), :]

            return of

        views = [view(start, rows, False) for start, rows in cuts]
        crossing = ["all", "all"]
        if self.balanced:
            views += [view(bulk, tokens - bulk, turn) for turn in (False, True)]
            crossing += ["own", "none"]
        self.parts = len(views)
        self.gather = LineGather(
            "ctx", lines, across, views, [of(me) for of in views], sems, crossing
        )

    def begin(self):
        for part in range(min(self.parts, 3)):
            self.gather.begin(part)

    def advance(self, step):
        if self.balanced and step == 0:
            self.gather.cross_recv(2, self.gather.line, 1).wait_recv()
            self.gather.begin(3)
        for part in range(self.parts):
            self.gather.advance(part, step)

    def wait_cross(self, line, ahead):
        for part in range(2):
            self.gather.cross_recv(part, line, ahead).wait_recv()

    def finish(self):
        self.gather.finish()


def row_parts(ctx_count, tokens):
    return 4 if grid_of(ctx_count)[1] == 2 and tokens % 32 == 0 else 2


def gather_sems(parts, lines, across):
    return [pltpu.SemaphoreType.DMA((parts, 1 + across, lines))] * 2


def greet(counts):
    barrier = pltpu.get_barrier_semaphore()
    for axis, count in zip(("ctx", "wsh"), counts):
        me = lax.axis_index(axis)
        for ahead in range(1, count):
            pl.semaphore_signal(
                barrier,
                inc=1,
                device_id={axis: (me + ahead) % count},
                device_id_type=pl.DeviceIdType.MESH,
            )
    pl.semaphore_wait(barrier, sum(counts) - 2)


class Exchange:
    def __init__(self, count, experts, most, sems, source, target):
        self.count, self.experts, self.most = count, experts, most
        self.send, self.recv = sems
        self.source, self.target = source, target
        self.me = lax.axis_index("ctx")

    def rows(self, place):
        return pl.ds(pl.multiple_of(place * self.most, self.most), self.most)

    def copy(self, expert, ahead, outward):
        peer = (self.me + ahead) % self.count if outward else (self.me + self.count - ahead) % self.count
        return pltpu.make_async_remote_copy(
            src_ref=self.source(expert, peer),
            dst_ref=self.target(expert, self.me),
            send_sem=self.send.at[expert, ahead - 1],
            recv_sem=self.recv.at[expert, ahead - 1],
            device_id={"ctx": peer},
            device_id_type=pl.DeviceIdType.MESH,
        )

    def start(self, expert):
        for ahead in range(1, self.count):
            self.copy(expert, ahead, True).start()
        self.target(expert, self.me)[...] = self.source(expert, self.me)[...]

    def wait(self, expert):
        for ahead in range(1, self.count):
            peer = (self.me + self.count - ahead) % self.count
            pltpu.make_async_remote_copy(
                src_ref=self.source(expert, peer),
                dst_ref=self.target(expert, peer),
                send_sem=self.send.at[expert, ahead - 1],
                recv_sem=self.recv.at[expert, ahead - 1],
                device_id={"ctx": peer},
                device_id_type=pl.DeviceIdType.MESH,
            ).wait_recv()

    def finish(self, expert):
        for ahead in range(1, self.count):
            self.copy(expert, ahead, True).wait_send()


def exchange_sems(count, experts):
    return [pltpu.SemaphoreType.DMA((experts, count - 1))] * 2


def cap_map(target_ref, expert, capacity):
    slots = target_ref.shape[1]
    rows = lax.broadcasted_iota(jnp.int32, (capacity, slots), 0)
    return (rows == jnp.broadcast_to(target_ref[expert : expert + 1, :], rows.shape)).astype(F32).astype(BF16)


def placement_of(slot_ref, slots):
    rows = lax.broadcasted_iota(jnp.int32, (slots, slot_ref.shape[1]), 0)
    return (rows == jnp.broadcast_to(slot_ref[0:1, :], rows.shape)).astype(F32).astype(BF16)


def grid_of(count):
    lines = 4 if count % 4 == 0 else 1
    return lines, count // lines


def route_slots(routes_ref, chosen_ref, most):
    experts, tokens = chosen_ref.shape
    ids = lax.broadcasted_iota(jnp.int32, (experts, tokens), 0)
    routes = jnp.broadcast_to(routes_ref[0:1, :], ids.shape)
    chosen = (ids == routes).astype(F32)
    chosen_ref[...] = chosen
    earlier = lax.broadcasted_iota(jnp.int32, (tokens, tokens), 0) < lax.broadcasted_iota(
        jnp.int32, (tokens, tokens), 1
    )
    before = dot(chosen.astype(BF16), earlier.astype(F32).astype(BF16))
    rank = jnp.sum(chosen * before, axis=0, keepdims=True).astype(jnp.int32)
    return routes_ref[0:1, :] * most + rank, jnp.sum(chosen, axis=1, keepdims=True)


SOURCE = 2


def plan_start(blocks):
    return SOURCE + blocks + 2


def plan_size(blocks):
    return plan_start(blocks) + 4 + 3 * (blocks + 1)


def write_plan(pairs_ref, plan, me):
    blocks = 2 * pairs_ref.shape[1]
    half = blocks // 2
    own = [pairs_ref[side, me] for side in range(2)]
    plan[0], plan[1] = own[0], own[1]
    plan[SOURCE] = jnp.int32(0)
    plan[SOURCE + blocks + 1] = jnp.int32(0)

    def place(position, carry):
        found = jnp.int32(0)
        for row in range(blocks):
            found = found + jnp.where(pairs_ref[row % 2, row // 2] == position, row, 0)
        plan[SOURCE + 1 + position] = found
        return carry

    lax.fori_loop(0, blocks, place, 0)
    early, late = jnp.minimum(own[0], own[1]), jnp.maximum(own[0], own[1])
    first = jnp.where(own[0] < own[1], 0, 1).astype(jnp.int32)
    start = plan_start(blocks)
    plan[start], plan[start + 1] = first, 1 - first
    plan[start + 2], plan[start + 3] = early, late
    start = start + 4
    for step in range(blocks + 1):
        rest = step - (half + 2)
        if step <= half:
            tile, owner = late - step, jnp.int32(1)
        elif step == half + 1:
            tile, owner = early, jnp.int32(0)
        else:
            tile = jnp.where(rest < early, early - 1 - rest, late - half - 1 - (rest - early))
            owner = jnp.where(rest < early, 0, 1).astype(jnp.int32)
        tile = jnp.minimum(jnp.maximum(tile, 0), blocks - 1)
        plan[start + step] = plan[SOURCE + 1 + tile]
        plan[start + blocks + 1 + step] = owner
        plan[start + 2 * blocks + 2 + step] = plan[SOURCE + blocks - tile]


def project_kernel(
    counts,
    capacity,
    rows_ref,
    wq_ref,
    wk_ref,
    wv_ref,
    wo_ref,
    router_ref,
    gain_a_ref,
    gain_m_ref,
    bias_ref,
    routes_ref,
    pairs_in_ref,
    query_hot_ref,
    key_hot_ref,
    qkv_out,
    weights_out,
    small_out,
    slot_out,
    target_out,
    plan_out,
    query_base_out,
    key_base_out,
    held,
    weights,
    own_small,
    smalls,
    gain,
    pairs_ref,
    ready,
    chosen,
    tallies,
    row_send,
    row_recv,
    weight_send,
    weight_recv,
    tally_send,
    tally_recv,
    out_sems,
    local_sems,
):
    ctx_count, wsh_count = counts
    experts = chosen.shape[0]
    exp_dev = experts // ctx_count
    lanes = experts
    tokens, width = rows_ref.shape
    share = wq_ref.shape[0]
    lines, across = grid_of(ctx_count)
    pairs = wsh_count // 2

    def shard(block):
        return pl.ds(pl.multiple_of(block * share, 16), share)

    def weight_view(place):
        return lambda block: weights.at[place, shard(block), :]

    rows = RowGather(counts, held, (row_send, row_recv))
    mats = LineGather(
        "wsh",
        pairs,
        2,
        [lambda block: smalls.at[block]] + [weight_view(place) for place in range(4)],
        None,
        (weight_send, weight_recv),
    )
    mats.own = [view(mats.me) for view in mats.views]
    own_weights = (wq_ref, wk_ref, wv_ref, wo_ref)
    own_copies = [
        pltpu.make_async_copy(ref, view, local_sems.at[2 + place])
        for place, (ref, view) in enumerate(
            [(rows_ref, held.at[rows.me])]
            + list(zip(own_weights, mats.own[1:]))
        )
    ]
    for copy in own_copies:
        copy.start()
    pairs_copy = pltpu.make_async_copy(pairs_in_ref, pairs_ref, local_sems.at[7])
    pairs_copy.start()
    buckets = bias_ref.shape[0]
    own_small[...] = jnp.zeros_like(own_small)
    own_small[:experts, :share] = router_ref[...].astype(F32)
    own_small[experts : experts + 1, :share] = gain_a_ref[...].astype(F32).reshape(1, share)
    own_small[experts + 1 : experts + 2, :share] = gain_m_ref[...].astype(F32).reshape(1, share)
    own_small[experts + 8 : experts + 8 + buckets, :HEADS] = bias_ref[...].astype(F32)
    smalls[mats.me] = own_small[...].astype(BF16)
    greet(counts)
    own_copies[0].wait()
    rows.begin()
    mats.begin(0)
    for part in range(1, 5):
        own_copies[part].wait()
        if part < 4:
            mats.begin(part)
    most = target_out.shape[1] // ctx_count
    slot, tally = route_slots(routes_ref, chosen, most)
    slot_out[...] = jnp.broadcast_to(slot, slot_out.shape)
    tallies[rows.me] = jnp.broadcast_to(tally, (experts, BLOCK))
    counted = Exchange(
        ctx_count,
        1,
        most,
        (tally_send, tally_recv),
        lambda expert, peer: tallies.at[rows.me],
        lambda expert, peer: tallies.at[peer],
    )
    for ahead in range(1, ctx_count):
        counted.copy(0, ahead, True).start()
    pairs_copy.wait()
    write_plan(pairs_ref, plan_out, rows.me)

    def place_targets():
        counted.wait(0)
        lane = lane_ids(1, ctx_count * most)
        for expert in range(exp_dev):
            offset = jnp.zeros((1, 1), F32)
            target = jnp.full((1, ctx_count * most), capacity, jnp.int32)
            for source in range(ctx_count):
                count = tallies[source, pl.ds(rows.me * exp_dev + expert, 1), 0:1]
                inside = (lane >= source * most) & (
                    lane < source * most + jnp.broadcast_to(count.astype(jnp.int32), lane.shape)
                )
                place = lane - source * most + jnp.broadcast_to(offset.astype(jnp.int32), lane.shape)
                target = jnp.where(inside, place, target)
                offset = offset + count
            target_out[expert : expert + 1, :] = target
        target_out[exp_dev:, :] = jnp.zeros_like(target_out[exp_dev:, :])

    for step in range(lines - 2):
        rows.advance(step)
        if step == 0:
            place_targets()
    for step in range(pairs - 1):
        for part in range(4):
            mats.advance(part, step)
    mats.begin(4)
    for part in range(4):
        mats.wait_cross(part)
    parts = [smalls[block].astype(F32) for block in range(wsh_count)]
    bias_rows = [part[experts + 8 : experts + 8 + buckets, :BLOCK] for part in parts]
    bias_rows = jnp.concatenate(bias_rows, axis=0).astype(BF16)
    turned = jnp.concatenate([part[: experts + 8, :share] for part in parts], axis=1)
    spare = jnp.zeros((BLOCK - turned.shape[0], width), F32)
    turned = jnp.concatenate([turned, spare], axis=0)
    small_out[...] = turned.astype(BF16)
    gain[...] = turned[lanes : lanes + 8, :]
    for hot_ref, base_out, sign in (
        (query_hot_ref, query_base_out, -1),
        (key_hot_ref, key_base_out, 1),
    ):
        table = dot(bias_rows, hot_ref[...], 0, 0)
        lane = lane_ids(BLOCK, SPAN)
        lane = jnp.where(lane < NEAR, lane, lane - SPAN)
        gap = lane if sign > 0 else BLOCK - lane
        last = jnp.max(jnp.where(gap == NEAR - 1, table, -jnp.inf), axis=1, keepdims=True)
        table = jnp.where(gap >= 0, table - last, MASKED)
        for pair in range(PAIRS):
            base_out[pair] = jnp.zeros((8, SPAN), F32)
            base_out[pair, 0:2, :] = table[2 * pair : 2 * pair + 2]
    ahead_of_last = 5 if lines == 4 and across == 2 else 0
    if not ahead_of_last:
        rows.advance(lines - 2)
    column = rows.me % across
    upper = rows.me // across // max(lines // 2, 1)

    def put(slot, block):
        place = pl.ds(pl.multiple_of(block * tokens, tokens), tokens)
        return pltpu.make_async_copy(ready.at[slot], qkv_out.at[place, :], out_sems.at[slot])

    def order(step):
        if ahead_of_last:
            step = jnp.asarray(step)
            step = jnp.where(
                step < 3, step, jnp.where(step < 5, step + 1, jnp.where(step == 5, 3, step))
            )
        ahead, line = step // lines, step % lines
        line = line + upper * (lines - 1 - 2 * line)
        return line, ahead, line * across + (column + across - ahead) % across

    def step_body(step, carry):
        line, ahead, block = order(step)
        slot = step % 2
        for skip in range(1, across):

            @pl.when(ahead == skip)
            def _():
                rows.wait_cross(line, skip)

        @pl.when(step >= 2)
        def _():
            put(slot, order(step - 2)[2]).wait()

        values = held[block].astype(F32)
        inv = lax.rsqrt(jnp.mean(values * values, axis=-1, keepdims=True) + epsilon)
        normed = (values * inv * gain[0:1, :]).astype(BF16)
        for place in range(3):
            ready[slot, :, place * width : (place + 1) * width] = dot(
                normed, weights[place]
            ).astype(BF16)
        put(slot, block).start()
        return carry

    first = ahead_of_last or ctx_count // 2
    lax.fori_loop(0, first, step_body, 0)
    if ahead_of_last:
        rows.advance(lines - 2)
    for step in range(pairs - 1):
        mats.advance(4, step)
    lax.fori_loop(first, ctx_count, step_body, 0)
    mats.wait_cross(4)
    weights_copy = pltpu.make_async_copy(weights, weights_out, local_sems.at[0])
    weights_copy.start()
    for step in (ctx_count - 2, ctx_count - 1):
        put(step % 2, order(step)[2]).wait()
    weights_copy.wait()
    counted.finish(0)
    rows.finish()
    mats.finish()


def project(
    counts, capacity, experts, most, rows, weights, small, routes, pairs, query_hot, key_hot
):
    tokens, width = rows.shape
    ctx_count, wsh_count = counts
    length = tokens * ctx_count
    lines, across = grid_of(ctx_count)
    small_rows = -(-(experts + 8 + small[3].shape[0]) // 16) * 16
    small_lanes = -(-(width // wsh_count) // BLOCK) * BLOCK
    vmem = pl.BlockSpec(memory_space=pltpu.VMEM)
    anywhere = pl.BlockSpec(memory_space=pl.ANY)
    smem = pl.BlockSpec(memory_space=pltpu.SMEM)
    return pl.pallas_call(
        functools.partial(project_kernel, counts, capacity),
        in_specs=[anywhere] * 5 + [vmem] * 5 + [anywhere, vmem, vmem],
        out_specs=[anywhere] * 2 + [vmem] * 3 + [smem] + [vmem] * 2,
        out_shape=[
            jax.ShapeDtypeStruct((length, 3 * width), BF16),
            jax.ShapeDtypeStruct((4, width, width), BF16),
            jax.ShapeDtypeStruct((BLOCK, width), BF16),
            jax.ShapeDtypeStruct((8, tokens), jnp.int32),
            jax.ShapeDtypeStruct((8, ctx_count * most), jnp.int32),
            jax.ShapeDtypeStruct((plan_size(2 * ctx_count),), jnp.int32),
            jax.ShapeDtypeStruct((PAIRS, 8, SPAN), F32),
            jax.ShapeDtypeStruct((PAIRS, 8, SPAN), F32),
        ],
        scratch_shapes=[
            pltpu.VMEM((ctx_count, tokens, width), BF16),
            pltpu.VMEM((4, width, width), BF16),
            pltpu.VMEM((small_rows, small_lanes), F32),
            pltpu.VMEM((wsh_count, small_rows, small_lanes), BF16),
            pltpu.VMEM((8, width), F32),
            pltpu.SMEM(pairs.shape, jnp.int32),
            pltpu.VMEM((2, tokens, 3 * width), BF16),
            pltpu.VMEM((experts, tokens), F32),
            pltpu.VMEM((ctx_count, experts, BLOCK), F32),
            *gather_sems(row_parts(ctx_count, tokens), lines, across),
            *gather_sems(5, wsh_count // 2, 2),
            *exchange_sems(ctx_count, 1),
            pltpu.SemaphoreType.DMA((2,)),
            pltpu.SemaphoreType.DMA((8,)),
        ],
        compiler_params=pltpu.CompilerParams(
            collective_id=0, has_side_effects=True, vmem_limit_bytes=60 << 20
        ),
        name="project",
    )(rows, *weights, *small, routes, pairs, query_hot, key_hot)


def gelu_parts(values):
    slope, cubic = math.sqrt(2 / math.pi), 0.044715
    square = values * values
    bent = jnp.tanh(slope * (values + cubic * values * square))
    outer = 0.5 * (1.0 + bent)
    derivative = outer + 0.5 * values * (1.0 - bent * bent) * slope * (1.0 + 3 * cubic * square)
    return values * outer, derivative


def choose(rows, router, experts, expert):
    logits = dot(rows, router, 1, 1)
    lanes = lane_ids(rows.shape[0], router.shape[0])
    logits = jnp.where(lanes < experts, logits, MASKED)
    weights = jnp.exp(logits - jnp.max(logits, axis=-1, keepdims=True))
    probs = weights / jnp.sum(weights, axis=-1, keepdims=True)
    hot = (lanes == expert).astype(F32)
    return probs, hot, jnp.sum(probs * hot, axis=-1, keepdims=True)


def middle_kernel(
    counts,
    experts,
    spread_here,
    attn_ref,
    exact_ref,
    hidden_ref,
    grad_ref,
    weights_ref,
    w_in_ref,
    w_out_ref,
    small_ref,
    slot_ref,
    target_ref,
    lse_ref,
    routes_ref,
    base_ref,
    plan_ref,
    qkv_ref,
    output_out,
    returned_out,
    resid_out,
    gate_out,
    grad_mid_out,
    grad_heads_out,
    heads_all_out,
    stats_out,
    grad_wo_out,
    grad_router_out,
    grad_gain_out,
    dq_out,
    sums_out,
    grad_in_out,
    grad_out_out,
    qkv,
    lse_all,
    stacked_q,
    stacked_g,
    delta_rep,
    bias,
    near,
    tile_keys,
    scores,
    tops,
    tile_weights,
    tile_values,
    other_values,
    lse_rows,
    own_g,
    early_in,
    attn,
    heads,
    exact_blocks,
    hidden,
    grad,
    wo,
    w_in,
    w_out,
    resid,
    incoming,
    own_x,
    all_x,
    all_g,
    hid,
    du,
    parts,
    from_mate,
    from_far,
    shares,
    mate_shares,
    far_shares,
    returning,
    home,
    branch,
    stats,
    stage_in,
    stage_out,
    heads_stage,
    fetch_sems,
    out_sems,
    heads_sems,
    x_send,
    x_recv,
    g_send,
    g_recv,
    early_send,
    early_recv,
    go_send,
    go_recv,
    back_send,
    back_recv,
    mate_send,
    mate_recv,
    far_send,
    far_recv,
    branch_send,
    branch_recv,
    stat_send,
    stat_recv,
):
    ctx_count, wsh_count = counts
    tokens, width = hidden.shape
    exp_dev, capacity = own_x.shape[:2]
    most = incoming.shape[1] // ctx_count
    lines, across = grid_of(ctx_count)
    pairs = wsh_count // 2
    me = lax.axis_index("ctx")
    home_row = me if spread_here else 0
    sources = [
        (grad_ref, grad),
        (weights_ref.at[3], wo),
        (hidden_ref, hidden),
        (w_in_ref, w_in),
        (w_out_ref, w_out),
    ]
    if spread_here:
        sources.insert(1, (qkv_ref, qkv))
    else:
        sources += [(attn_ref, attn), (exact_ref, exact_blocks)]
    fetches = [
        pltpu.make_async_copy(src, dst, fetch_sems.at[place])
        for place, (src, dst) in enumerate(sources)
    ]
    for fetch in fetches:
        fetch.start()
    views = [
        (lambda buffer, expert: lambda block: buffer.at[expert, block])(buffer, expert)
        for buffer in (all_g, all_x)
        for expert in range(exp_dev)
    ]
    gather_g = LineGather(
        "wsh",
        pairs,
        2,
        views[:exp_dev],
        [own_g.at[expert] for expert in range(exp_dev)],
        (g_send, g_recv),
    )
    gather_x = LineGather(
        "wsh",
        pairs,
        2,
        views[exp_dev:],
        [own_x.at[expert] for expert in range(exp_dev)],
        (x_send, x_recv),
    )
    wsh_me, my_line, my_core = gather_x.me, gather_x.line, gather_x.column
    greet(counts)
    fetches[0].wait()
    returning[1] = dot(placement_of(slot_ref, experts * most), grad[...]).astype(BF16)
    early = Exchange(
        ctx_count,
        exp_dev,
        most,
        (early_send, early_recv),
        lambda expert, peer: returning.at[1, early.rows(peer * exp_dev + expert), :],
        lambda expert, peer: early_in.at[expert, early.rows(peer), :],
    )
    for expert in range(exp_dev):
        early.start(expert)

    def pass_on():
        for expert in range(exp_dev):
            early.wait(expert)
            own_g[expert] = dot(cap_map(target_ref, expert, capacity), early_in[expert]).astype(BF16)
            gather_g.begin(expert)
            all_g[expert, wsh_me] = own_g[expert]

    if spread_here:
        tiles = Tiles(plan_ref, 2 * ctx_count, False)
        fetches[1].wait()

        def attend(pair, carry):
            pair_lanes = pl.ds(pl.multiple_of(pair * BLOCK, BLOCK), BLOCK)

            def load(part, row):
                lanes = pl.ds(pl.multiple_of(part * width + pair * BLOCK, BLOCK), BLOCK)
                return qkv[row, :, lanes]

            near_tiles = near_bias(base_ref, pair)
            bias[...] = jnp.concatenate(
                [near_tiles[:, BLOCK:], near_tiles[:, :BLOCK]], axis=1
            )
            totals = lse_all.at[pair]
            results = forward_pair(
                tiles,
                load,
                bias,
                stacked_q,
                tile_keys,
                scores,
                tops,
                totals,
                tile_weights,
                tile_values,
                other_values,
            )
            main = in_order(tiles, [result[0] for result in results])
            whole = in_order(tiles, [result[1] for result in results])
            lse = in_order(tiles, [totals[0], totals[1]])
            for own in range(2):
                rows = pl.ds(own * BLOCK, BLOCK)
                attn[rows, pair_lanes] = main[own]
                exact_blocks[own, :, pair_lanes] = whole[own]
                turned = jnp.transpose(lse[own])
                for head in range(2):
                    lse_rows[own, pair, head : head + 1, :] = turned[
                        :1, head * BLOCK : (head + 1) * BLOCK
                    ]
                lse_rows[own, pair, 2:8, :] = jnp.zeros((6, BLOCK), F32)
            return carry

        lax.fori_loop(0, PAIRS - 1, attend, 0)
        pass_on()
        lax.fori_loop(PAIRS - 1, PAIRS, attend, 0)
    else:
        lse_rows[...] = lse_ref[...]
        pass_on()

    gain_two = small_ref[...].astype(F32)[experts + 1 : experts + 2, :]
    row_ids = lax.broadcasted_iota(jnp.int32, (BLOCK, width), 0)
    router = jnp.where(row_ids < experts, small_ref[...], jnp.zeros((BLOCK, width), BF16))
    for fetch in fetches[2 if spread_here else 1 :]:
        fetch.wait()
    resid[...] = hidden[...].astype(F32) + dot(attn[...], wo[...])
    inv_two = lax.rsqrt(jnp.mean(resid[...] * resid[...], axis=-1, keepdims=True) + epsilon)
    normed_two = (resid[...] * inv_two * gain_two).astype(BF16)
    units = w_in.shape[2]
    placement = placement_of(slot_ref, experts * most)
    returning[0] = dot(placement, normed_two).astype(BF16)
    forth = Exchange(
        ctx_count,
        exp_dev,
        most,
        (go_send, go_recv),
        lambda expert, peer: returning.at[0, forth.rows(peer * exp_dev + expert), :],
        lambda expert, peer: incoming.at[expert, forth.rows(peer), :],
    )
    forth.start(0)
    routed = jnp.broadcast_to(routes_ref[...].astype(F32), (BLOCK, tokens))
    routed = jnp.transpose(routed)[:, :1].astype(jnp.int32)
    gate = choose(normed_two, router, experts, routed)[2]
    for expert in range(exp_dev):
        for step in range(pairs - 1):
            gather_g.advance(expert, step)
    gather_g.finish()

    summed = (parts.at[0], parts.at[1], shares)
    mate_parts = (from_mate.at[0], from_mate.at[1], mate_shares)
    far_parts = (from_far.at[0], from_far.at[1], far_shares)

    def mate_copy(array, expert, line):
        mine = line * 2 + 1 - my_core
        return pltpu.make_async_remote_copy(
            src_ref=summed[array].at[expert, mine],
            dst_ref=mate_parts[array].at[expert, line],
            send_sem=mate_send.at[array, expert, line],
            recv_sem=mate_recv.at[array, expert, line],
            device_id={"wsh": my_line * 2 + 1 - my_core},
            device_id_type=pl.DeviceIdType.MESH,
        )

    def far_copy(array, expert, ahead):
        line = (my_line + ahead) % pairs
        return pltpu.make_async_remote_copy(
            src_ref=summed[array].at[expert, line * 2 + my_core],
            dst_ref=far_parts[array].at[expert, ahead - 1],
            send_sem=far_send.at[array, expert, ahead - 1],
            recv_sem=far_recv.at[array, expert, ahead - 1],
            device_id={"wsh": line * 2 + my_core},
            device_id_type=pl.DeviceIdType.MESH,
        )

    def work(expert, ahead):
        line = (my_line + ahead) % pairs
        both = pl.ds(line * 2, 2)
        gather_x.cross_recv(expert, line, 1).wait_recv()
        gather_g.cross_recv(expert, line, 1).wait_recv()
        rows = all_x[expert, both].reshape(2 * capacity, width)
        active, slope = gelu_parts(dot(rows, w_in[expert]))
        active = active.astype(BF16)
        hid[expert, both] = active.reshape(2, capacity, units)
        share = choose(rows, router, experts, exp_dev * me + expert)[2]
        grads = all_g[expert, both].reshape(2 * capacity, width).astype(F32)
        grads = (share * grads).astype(BF16)
        all_g[expert, both] = grads.reshape(2, capacity, width)
        push = dot(grads, w_out[expert], 1, 1)
        product = jnp.sum(push * active.astype(F32), axis=-1, keepdims=True)
        product = jnp.transpose(jnp.broadcast_to(product, (2 * capacity, BLOCK)))
        for core in range(2):
            shares[expert, line * 2 + core] = product[:8, core * capacity : (core + 1) * capacity]
        mate_copy(2, expert, line).start()
        grad_u = (push * slope).astype(BF16)
        du[expert, both] = grad_u.reshape(2, capacity, units)
        part = dot(grad_u, w_in[expert], 1, 1).astype(BF16)
        parts[1, expert, both] = part.reshape(2, capacity, width)
        mate_copy(1, expert, line).start()
        part = dot(active, w_out[expert]).astype(BF16)
        parts[0, expert, both] = part.reshape(2, capacity, width)
        mate_copy(0, expert, line).start()

    def fold(array, expert, ahead):
        line = (my_line + ahead) % pairs
        mate_copy(array, expert, line).wait_recv()
        both = summed[array][expert, line * 2 + my_core].astype(F32) + mate_parts[array][
            expert, line
        ].astype(F32)
        summed[array][expert, line * 2 + my_core] = both.astype(summed[array].dtype)
        far_copy(array, expert, ahead).start()

    def whole(array, expert):
        mate_copy(array, expert, my_line).wait_recv()
        total = summed[array][expert, my_line * 2 + my_core].astype(F32) + mate_parts[array][
            expert, my_line
        ].astype(F32)
        for ahead in range(1, pairs):
            far_copy(array, expert, ahead).wait_recv()
            total = total + far_parts[array][expert, ahead - 1].astype(F32)
        return total

    back = [
        Exchange(
            ctx_count,
            exp_dev,
            most,
            (back_send.at[array], back_recv.at[array]),
            (
                lambda array: lambda expert, peer: returning.at[
                    array, forth.rows(expert * ctx_count + peer), :
                ]
            )(array),
            (
                lambda array: lambda expert, peer: home.at[
                    array, forth.rows(peer * exp_dev + expert), :
                ]
            )(array),
        )
        for array in range(2)
    ]

    def settle(expert):
        expert_rows = pl.ds(expert * ctx_count * most, ctx_count * most)
        rows = own_x[expert]
        probs, hot, share = choose(rows, router, experts, exp_dev * me + expert)
        product = jnp.transpose(whole(2, expert))[:, :1]
        grad_logits = (product * (hot - probs)).astype(BF16)
        grad_rows = whole(1, expert).astype(BF16).astype(F32) + dot(grad_logits, router)
        spread = cap_map(target_ref, expert, capacity)
        returning[1, expert_rows] = dot(spread, grad_rows.astype(BF16), 0, 0).astype(BF16)
        back[1].start(expert)
        router_part = dot(grad_logits, rows, 0, 0)[:experts]
        if expert == 0:
            grad_router_out[...] = router_part
        else:
            grad_router_out[...] += router_part

    for expert in range(exp_dev):
        early.finish(expert)
    for expert in range(exp_dev):
        forth.wait(expert)
        if expert + 1 < exp_dev:
            forth.start(expert + 1)
        own_x[expert] = dot(cap_map(target_ref, expert, capacity), incoming[expert]).astype(BF16)
        gather_x.begin(expert)
        all_x[expert, wsh_me] = own_x[expert]
        work(expert, 0)
        if expert:
            settle(expert - 1)
        for step in range(pairs - 1):
            gather_x.advance(expert, step)

        def others(ahead, carry):
            work(expert, ahead)
            return carry

        if pairs == 2:
            work(expert, 1)
        else:
            lax.fori_loop(1, pairs, others, 0)
        for ahead in range(1, pairs):
            fold(2, expert, ahead)
            fold(1, expert, ahead)
    settle(exp_dev - 1)
    for expert in range(exp_dev):
        forth.finish(expert)
        for ahead in range(1, pairs):
            fold(0, expert, ahead)

    def in_copy(expert):
        return pltpu.make_async_copy(stage_in, grad_in_out.at[expert], out_sems.at[1])

    one_stage = units == width
    out_stage = stage_in if one_stage else stage_out

    def out_copy(expert):
        return pltpu.make_async_copy(out_stage, grad_out_out.at[expert], out_sems.at[0])

    group = min(wsh_count, 4)

    def slot_sum(stage, left, right, expert):
        def part(turn):
            blocks = pl.ds(turn * group, group)
            return dot(
                left[expert, blocks].reshape(group * capacity, left.shape[3]),
                right[expert, blocks].reshape(group * capacity, right.shape[3]),
                0,
                0,
            )

        stage[...] = part(0).astype(stage.dtype)
        if wsh_count > group:

            def add(turn, carry):
                stage[...] += part(turn)
                return carry

            lax.fori_loop(1, wsh_count // group, add, 0)

    def grads_of(expert):
        if expert:
            (in_copy if one_stage else out_copy)(expert - 1).wait()
        slot_sum(out_stage, hid, all_g, expert)
        out_copy(expert).start()
        if one_stage:
            out_copy(expert).wait()
        elif expert:
            in_copy(expert - 1).wait()
        slot_sum(stage_in, all_x, du, expert)
        in_copy(expert).start()

    for expert in range(exp_dev):
        grads_of(expert)
        expert_rows = pl.ds(expert * ctx_count * most, ctx_count * most)
        spread = cap_map(target_ref, expert, capacity)
        out_rows = whole(0, expert).astype(BF16)
        returning[0, expert_rows] = dot(spread, out_rows, 0, 0).astype(BF16)
    grad_up = grad[...].astype(F32)
    for expert in range(exp_dev):
        back[1].wait(expert)
    grad_normed = dot(placement_of(slot_ref, experts * most), home[1], 0, 0)
    scaled = grad_normed * gain_two
    mean = jnp.mean(scaled * resid[...], axis=-1, keepdims=True)
    gain_part = jnp.sum(grad_normed * resid[...] * inv_two, axis=0, keepdims=True)
    grad_gain_out[...] = jnp.broadcast_to(gain_part, grad_gain_out.shape)
    grad_mid = grad_up + inv_two * scaled - resid[...] * inv_two * inv_two * inv_two * mean
    grad_mid_out[...] = grad_mid
    branch[home_row] = grad_mid.astype(BF16)

    if spread_here:
        gather_d = RowGather(counts, branch, (branch_send, branch_recv))
        gather_s = LineGather(
            "ctx",
            lines,
            across,
            [lambda block: stats.at[block]],
            [stats.at[me]],
            (stat_send, stat_recv),
        )
        gather_d.begin()
    if spread_here:
        returned_out[...] = returning[0]
        resid_out[...] = resid[...]
        gate_out[...] = jnp.broadcast_to(gate, gate_out.shape)
    else:
        for expert in range(exp_dev):
            back[0].start(expert)
    grad_heads = dot(branch[home_row], wo[...], 1, 1).astype(BF16)
    grad_heads_out[...] = grad_heads
    if spread_here:
        for own in range(2):
            heads[own] = grad_heads[own * BLOCK : (own + 1) * BLOCK]
    product = grad_heads.astype(F32) * exact_blocks[...].reshape(tokens, width)
    head_of = lax.broadcasted_iota(jnp.int32, (width, BLOCK), 0) // HEAD_DIM
    head_hot = (head_of == lane_ids(width, BLOCK)).astype(F32)
    delta = jnp.transpose(
        lax.dot_general(
            product, head_hot, (((1,), (0,)), ((), ())), precision=HIGH, preferred_element_type=F32
        )
    )
    for pair in range(PAIRS):
        for own in range(2):
            stats[home_row, own, pair] = lse_rows[own, pair]
            stats[home_row, own, pair, 2:4, :] = delta[
                2 * pair : 2 * pair + 2, own * BLOCK : (own + 1) * BLOCK
            ]
    if spread_here:
        gather_s.begin(0)

    grad_wo_out[...] = dot(attn[...], branch[home_row], 0, 0).astype(BF16)

    plan_from = plan_start(2 * ctx_count)
    half = ctx_count

    def query_pair(pair, carry):
        pair_lanes = pl.ds(pl.multiple_of(pair * BLOCK, BLOCK), BLOCK)

        def tile(part, step):
            lanes = pl.ds(pl.multiple_of(part * width + pair * BLOCK, BLOCK), BLOCK)
            return qkv[plan_ref[plan_from + 4 + step], :, lanes]

        bias[...] = near_bias(base_ref, pair)
        for place in range(2):
            own = plan_ref[plan_from + place]
            stacked_q[place] = stack_heads(tile(0, 0 if place else half + 1))
            grads = stack_heads(heads[own, :, pair_lanes])
            stacked_g[place] = grads
            own_exact = exact_blocks[own, :, pair_lanes]
            product = grads.astype(F32) * jnp.concatenate([own_exact, own_exact], axis=0)
            delta_rep[place] = jnp.broadcast_to(
                jnp.sum(product, axis=-1, keepdims=True), (2 * BLOCK, BLOCK)
            )

        def score_grads(place, step, extra):
            keys = tile(1, step)
            part = dot(stacked_q[place], keys, 1, 1)
            if extra is not None:
                part = part + extra
            weights = jnp.exp(part - lse_all[pair, place])
            grad_s = weights * (dot(stacked_g[place], tile(2, step), 1, 1) - delta_rep[place])
            return grad_s, dot(grad_s.astype(BF16), keys)

        diagonal, big = score_grads(1, 0, bias[:, BLOCK:])
        beside, more = score_grads(1, 1, bias[:, :BLOCK])
        big = big + more
        far = jnp.zeros((2 * BLOCK, BLOCK), F32)
        for step in range(2, half + 1):
            grad_s, more = score_grads(1, step, None)
            far, big = far + grad_s, big + more
        grad_s, small_part = score_grads(0, half + 1, bias[:, BLOCK:])
        near[:, BLOCK:] = diagonal + grad_s
        for step in range(half + 2, 2 * half + 1):
            place = plan_ref[plan_from + 4 + 2 * half + 1 + step]
            later = place.astype(F32)
            sooner = 1.0 - later
            extra = None
            if step == half + 2:
                extra = bias[:, :BLOCK] * sooner
            grad_s, more = score_grads(place, step, extra)
            if step == half + 2:
                near[:, :BLOCK] = beside + grad_s * sooner
                far = far + grad_s * later
            else:
                far = far + grad_s
            big = big + more * later
            small_part = small_part + more * sooner
        second = plan_ref[plan_from].astype(F32)
        small_part, big = merge_heads(small_part), merge_heads(big)
        first = 1.0 - second
        dq_out[:BLOCK, pair_lanes] = (small_part * first + big * second).astype(BF16)
        dq_out[BLOCK:, pair_lanes] = (big * first + small_part * second).astype(BF16)
        put_sums(sums_out, pair, near, far)
        return carry

    def query_pairs(turn):
        share = PAIRS // (lines - 1)
        lax.fori_loop(turn * share, (turn + 1) * share, query_pair, 0)

    if spread_here:
        for step in range(lines - 1):
            query_pairs(step)
            gather_d.advance(step)
            gather_s.advance(0, step)
    if not spread_here:
        for expert in range(exp_dev):
            back[0].wait(expert)
        token_out = dot(placement_of(slot_ref, experts * most), home[0], 0, 0)
        output_out[...] = (resid[...] + gate * token_out).astype(BF16)
    column = me % across
    upper = me // across // max(lines // 2, 1)

    def order(step):
        ahead, line = step // lines, step % lines
        line = line + upper * (lines - 1 - 2 * line)
        return line, ahead, line * across + (column + across - ahead) % across

    def put(slot, block):
        place = pl.ds(pl.multiple_of(block * tokens, tokens), tokens)
        return pltpu.make_async_copy(
            heads_stage.at[slot], heads_all_out.at[place, :], heads_sems.at[slot]
        )

    def heads_step(step, carry):
        line, ahead, block = order(step)
        slot = step % 2
        for skip in range(1, across):

            @pl.when(ahead == skip)
            def _():
                gather_d.wait_cross(line, skip)
                gather_s.cross_recv(0, line, skip).wait_recv()

        @pl.when(step >= 2)
        def _():
            put(slot, order(step - 2)[2]).wait()

        heads_stage[slot] = dot(branch[block], wo[...], 1, 1).astype(BF16)
        put(slot, block).start()
        return carry

    if spread_here:
        lax.fori_loop(0, ctx_count, heads_step, 0)
    stats_copy = pltpu.make_async_copy(stats, stats_out, fetch_sems.at[0])
    stats_copy.start()
    if spread_here:
        for step in (ctx_count - 2, ctx_count - 1):
            put(step % 2, order(step)[2]).wait()
    else:
        heads_stage[0] = branch[0]
        own_branch = pltpu.make_async_copy(heads_stage.at[0], heads_all_out, heads_sems.at[0])
        own_branch.start()
        own_branch.wait()
    if not one_stage:
        out_copy(exp_dev - 1).wait()
    in_copy(exp_dev - 1).wait()
    stats_copy.wait()
    for expert in range(exp_dev):
        for array in range(1 if spread_here else 0, 2):
            back[array].finish(expert)
        for array in range(3):
            for line in range(pairs):
                mate_copy(array, expert, line).wait_send()
            for ahead in range(1, pairs):
                far_copy(array, expert, ahead).wait_send()
    gather_x.finish()
    if spread_here:
        gather_d.finish()
        gather_s.finish()


def middle(
    counts,
    experts,
    attn,
    exact,
    hidden,
    grad,
    weights,
    w_in,
    w_out,
    small,
    slots,
    targets,
    lse_rows,
    routes,
    base,
    plan,
    qkv,
    capacity,
):
    ctx_count, wsh_count = counts
    tokens, width = hidden.shape
    exp_dev = w_in.shape[0]
    units = w_in.shape[2]
    slot_count = targets.shape[1]
    all_slots = experts * (slot_count // ctx_count)
    lines, across = grid_of(ctx_count)
    pairs = wsh_count // 2
    vmem = pl.BlockSpec(memory_space=pltpu.VMEM)
    anywhere = pl.BlockSpec(memory_space=pl.ANY)
    slot_rows = (exp_dev, wsh_count, capacity)
    spread_here = wsh_count <= 4
    held = ctx_count if spread_here else 1
    kept = BF16 if spread_here else F32
    score_rows = NEAR if spread_here else 16
    forward = forward_scratch(2 * ctx_count) if spread_here else [pltpu.VMEM((8, BLOCK), F32)] * 8
    return pl.pallas_call(
        functools.partial(middle_kernel, counts, experts, spread_here),
        in_specs=[anywhere] * 7
        + [vmem] * 6
        + [pl.BlockSpec(memory_space=pltpu.SMEM), anywhere],
        out_specs=[vmem] * 6 + [anywhere] * 2 + [vmem] * 5 + [anywhere] * 2,
        out_shape=[
            jax.ShapeDtypeStruct((16 if spread_here else tokens, width), BF16),
            jax.ShapeDtypeStruct((all_slots if spread_here else 16, width), BF16),
            jax.ShapeDtypeStruct((tokens if spread_here else 8, width), F32),
            jax.ShapeDtypeStruct((tokens, BLOCK), F32),
            jax.ShapeDtypeStruct((tokens, width), F32),
            jax.ShapeDtypeStruct((tokens, width), BF16),
            jax.ShapeDtypeStruct((tokens * held, width), BF16),
            jax.ShapeDtypeStruct((held, 2, PAIRS, 8, BLOCK), F32),
            jax.ShapeDtypeStruct((width, width), BF16),
            jax.ShapeDtypeStruct((experts, width), F32),
            jax.ShapeDtypeStruct((8, width), F32),
            jax.ShapeDtypeStruct((tokens if spread_here else 16, width), BF16),
            jax.ShapeDtypeStruct((PAIRS, 8, SPAN), F32),
            jax.ShapeDtypeStruct((exp_dev, width, units), kept),
            jax.ShapeDtypeStruct((exp_dev, units, width), kept),
        ],
        scratch_shapes=[
            pltpu.VMEM(qkv.shape if spread_here else (1, 16, BLOCK), BF16),
            pltpu.VMEM((PAIRS, 2, NEAR, BLOCK) if spread_here else (1, 2, 8, BLOCK), F32),
            pltpu.VMEM((2, score_rows, BLOCK), BF16),
            pltpu.VMEM((2, score_rows, BLOCK), BF16),
            pltpu.VMEM((2, score_rows, BLOCK), F32),
            pltpu.VMEM((score_rows, NEAR), F32),
            pltpu.VMEM((score_rows, NEAR), F32),
            *forward[1:4],
            *forward[5:],
            pltpu.VMEM((2, PAIRS, 8, BLOCK), F32),
            pltpu.VMEM((exp_dev, capacity, width), BF16),
            pltpu.VMEM((exp_dev, slot_count, width), BF16),
            pltpu.VMEM((tokens, width), BF16),
            pltpu.VMEM((2, BLOCK if spread_here else 16, width), BF16),
            pltpu.VMEM((2, BLOCK, width), F32),
            pltpu.VMEM((tokens, width), BF16),
            pltpu.VMEM((tokens, width), BF16),
            pltpu.VMEM((width, width), BF16),
            pltpu.VMEM(w_in.shape, BF16),
            pltpu.VMEM(w_out.shape, BF16),
            pltpu.VMEM((tokens, width), F32),
            pltpu.VMEM((exp_dev, slot_count, width), BF16),
            pltpu.VMEM((exp_dev, capacity, width), BF16),
            pltpu.VMEM((*slot_rows, width), BF16),
            pltpu.VMEM((*slot_rows, width), BF16),
            pltpu.VMEM((*slot_rows, units), BF16),
            pltpu.VMEM((*slot_rows, units), BF16),
            pltpu.VMEM((2, *slot_rows, width), BF16),
            pltpu.VMEM((2, exp_dev, pairs, capacity, width), BF16),
            pltpu.VMEM((2, exp_dev, max(pairs - 1, 1), capacity, width), BF16),
            pltpu.VMEM((exp_dev, wsh_count, 8, capacity), F32),
            pltpu.VMEM((exp_dev, pairs, 8, capacity), F32),
            pltpu.VMEM((exp_dev, max(pairs - 1, 1), 8, capacity), F32),
            pltpu.VMEM((2, all_slots, width), BF16),
            pltpu.VMEM((2, all_slots, width), BF16),
            pltpu.VMEM((held, tokens, width), BF16),
            pltpu.VMEM((held, 2, PAIRS, 8, BLOCK), F32),
            pltpu.VMEM((width, units), kept),
            pltpu.VMEM((16, BLOCK) if units == width else (units, width), kept),
            pltpu.VMEM((2, tokens, width), BF16),
            pltpu.SemaphoreType.DMA((9,)),
            pltpu.SemaphoreType.DMA((2,)),
            pltpu.SemaphoreType.DMA((2,)),
            *gather_sems(exp_dev, pairs, 2),
            *gather_sems(exp_dev, pairs, 2),
            *exchange_sems(ctx_count, exp_dev),
            *exchange_sems(ctx_count, exp_dev),
            pltpu.SemaphoreType.DMA((2, exp_dev, ctx_count - 1)),
            pltpu.SemaphoreType.DMA((2, exp_dev, ctx_count - 1)),
            pltpu.SemaphoreType.DMA((3, exp_dev, pairs)),
            pltpu.SemaphoreType.DMA((3, exp_dev, pairs)),
            pltpu.SemaphoreType.DMA((3, exp_dev, max(pairs - 1, 1))),
            pltpu.SemaphoreType.DMA((3, exp_dev, max(pairs - 1, 1))),
            *gather_sems(row_parts(ctx_count, tokens), lines, across),
            *gather_sems(1, lines, across),
        ],
        compiler_params=pltpu.CompilerParams(
            collective_id=1, has_side_effects=True, vmem_limit_bytes=(62 if spread_here else 63) << 20
        ),
        name="middle",
    )(
        attn,
        exact,
        hidden,
        grad,
        weights,
        w_in,
        w_out,
        small,
        slots,
        targets,
        lse_rows,
        routes,
        base,
        plan,
        qkv,
    )


class Tiles:
    def __init__(self, plan_ref, blocks, keys):
        self.plan, self.blocks, self.half = plan_ref, blocks, blocks // 2
        self.start = plan_start(blocks)
        self.rows_from = self.start + 4 + (2 * (blocks + 1) if keys else 0)
        self.keys = keys
        self.count = blocks + 1

    def own(self, place):
        return self.plan[self.start + (1 - place if self.keys else place)]

    def own_step(self, place):
        return 0 if place else self.half + 1

    def row(self, step):
        return self.plan[self.rows_from + step]

    def place(self, step):
        if step <= self.half:
            return 1
        if step == self.half + 1:
            return 0
        return self.plan[self.start + 4 + self.blocks + 1 + step]

    def groups(self):
        found, step = [], 0
        while step <= self.half:
            size = 2 if step + 1 <= self.half else 1
            found.append((step, size))
            step += size
        return found + [(step, 1) for step in range(self.half + 1, self.count)]


def span(step, size=1):
    return slice(step * BLOCK, (step + size) * BLOCK)


def share_of(place, wanted):
    return place.astype(F32) if wanted else 1.0 - place.astype(F32)


def only(place, wanted, value):
    if isinstance(place, int):
        return value if place == wanted else jnp.zeros_like(value)
    return value * share_of(place, wanted).astype(value.dtype)


def order_bias(bias, step, size, place, half):
    if step == 0:
        return bias[:, : size * BLOCK]
    if step == half + 1:
        return bias[:, :BLOCK]
    if step == half + 2:
        return bias[:, BLOCK:] * share_of(place, 0)
    return None


def forward_pair(tiles, load, bias, stacked, keys, scores, tops, totals, weights, values, others):
    half, count = tiles.half, tiles.count
    lowest = jnp.full((NEAR, BLOCK), MASKED, F32)
    for place in range(2):
        stacked[place] = stack_heads(load(0, tiles.row(tiles.own_step(place))))
    for step in range(count):
        row = tiles.row(step)
        keys[span(step), :] = load(1, row)
        tile, place = load(2, row), tiles.place(step)
        values[span(step), :] = only(place, 1, tile)
        if step > half:
            others[span(step - half - 1), :] = only(place, 0, tile)
    best = [lowest, lowest]
    for step, size in tiles.groups():
        place = tiles.place(step)
        part = dot(stacked[place], keys[span(step, size), :], 1, 1)
        extra = order_bias(bias, step, size, place, half)
        if extra is not None:
            part = part + extra
        scores[:, span(step, size)] = part
        part = fold_lanes(part, jnp.maximum) if size == 2 else part
        for wanted in range(2):
            if isinstance(place, int):
                if place == wanted:
                    best[wanted] = jnp.maximum(best[wanted], part)
            else:
                share = share_of(place, wanted)
                best[wanted] = jnp.maximum(best[wanted], part * share + MASKED * (1.0 - share))
    for wanted in range(2):
        top = jnp.max(best[wanted], axis=-1, keepdims=True)
        tops[wanted] = jnp.broadcast_to(top, (NEAR, BLOCK))
    total = [jnp.zeros((NEAR, BLOCK), F32)] * 2
    for step in range(count):
        place = tiles.place(step)
        part = jnp.exp(scores[:, span(step)] - tops[place])
        high = part.astype(BF16)
        weights[:NEAR, span(step)] = high
        weights[NEAR:, span(step)] = (part - high.astype(F32)).astype(BF16)
        for wanted in range(2):
            if not isinstance(place, int) or place == wanted:
                total[wanted] = total[wanted] + only(place, wanted, part)
    results = []
    for wanted in range(2):
        whole = jnp.sum(total[wanted], axis=-1, keepdims=True)
        if wanted:
            summed = dot(weights[...], values[...])
        else:
            summed = dot(weights[:, span(half + 1, count - half - 1)], others[...])
        main = summed[:NEAR] / whole
        exact = main + summed[NEAR:] / whole
        totals[wanted] = tops[wanted] + jnp.log(jnp.broadcast_to(whole, (NEAR, BLOCK)))
        results.append((merge_heads(main).astype(BF16), merge_heads(exact)))
    return results


def in_order(tiles, pair):
    kind = pair[0].dtype
    second = tiles.own(0).astype(F32)
    first, second = (1.0 - second).astype(kind), second.astype(kind)
    return pair[0] * first + pair[1] * second, pair[1] * first + pair[0] * second


def forward_kernel(
    plan_ref, q_ref, k_ref, v_ref, base_ref, out_ref, exact_ref, lse_ref, row_ref, bias, *scratch
):
    blocks = q_ref.shape[0] // BLOCK
    tiles = Tiles(plan_ref, blocks, False)
    refs = (q_ref, k_ref, v_ref)
    near = near_bias(base_ref)
    bias[...] = jnp.concatenate([near[:, BLOCK:], near[:, :BLOCK]], axis=1)
    totals = scratch[4]

    def load(part, row):
        return refs[part][rows_at(row), :]

    results = forward_pair(tiles, load, bias, *scratch)
    main = in_order(tiles, [result[0] for result in results])
    exact = in_order(tiles, [result[1] for result in results])
    lse = in_order(tiles, [totals[0], totals[1]])
    for own in range(2):
        rows = pl.ds(own * BLOCK, BLOCK)
        out_ref[rows, :] = main[own]
        exact_ref[rows, :] = exact[own]
        lse_ref[0, own] = lse[own]
        turned = jnp.transpose(lse[own])
        for head in range(2):
            row_ref[own, 0, head : head + 1, :] = turned[:1, head * BLOCK : (head + 1) * BLOCK]
        row_ref[own, 0, 2:8, :] = jnp.zeros((6, BLOCK), F32)


def forward_scratch(blocks):
    count = blocks + 1
    rest = count - blocks // 2 - 1
    return [
        pltpu.VMEM((2, NEAR, BLOCK), BF16),
        pltpu.VMEM((count * BLOCK, BLOCK), BF16),
        pltpu.VMEM((NEAR, count * BLOCK), F32),
        pltpu.VMEM((2, NEAR, BLOCK), F32),
        pltpu.VMEM((2, NEAR, BLOCK), F32),
        pltpu.VMEM((2 * NEAR, count * BLOCK), BF16),
        pltpu.VMEM((count * BLOCK, BLOCK), BF16),
        pltpu.VMEM((rest * BLOCK, BLOCK), BF16),
    ]


def pair_specs(rows, width):
    pairs = width // BLOCK

    def column(offset):
        return pl.BlockSpec((rows, BLOCK), lambda pair, plan: (0, offset + pair))

    return [column(0), column(pairs), column(2 * pairs)]


def attend_forward(plan, qkv, base, width):
    rows = qkv.shape[0]
    own = pl.BlockSpec((NEAR, BLOCK), lambda pair, plan: (0, pair))
    return pl.pallas_call(
        forward_kernel,
        grid_spec=pltpu.PrefetchScalarGridSpec(
            num_scalar_prefetch=1,
            grid=(PAIRS,),
            in_specs=pair_specs(rows, width)
            + [pl.BlockSpec((1, 8, SPAN), lambda pair, plan: (pair, 0, 0))],
            out_specs=[
                own,
                own,
                pl.BlockSpec((1, 2, NEAR, BLOCK), lambda pair, plan: (pair, 0, 0, 0)),
                pl.BlockSpec((2, 1, 8, BLOCK), lambda pair, plan: (0, pair, 0, 0)),
            ],
            scratch_shapes=[pltpu.VMEM((NEAR, NEAR), F32), *forward_scratch(rows // BLOCK)],
        ),
        out_shape=[
            jax.ShapeDtypeStruct((NEAR, width), BF16),
            jax.ShapeDtypeStruct((NEAR, width), F32),
            jax.ShapeDtypeStruct((PAIRS, 2, NEAR, BLOCK), F32),
            jax.ShapeDtypeStruct((2, PAIRS, 8, BLOCK), F32),
        ],
        compiler_params=pltpu.CompilerParams(vmem_limit_bytes=60 << 20),
        name="attend_forward",
    )(plan, qkv, qkv, qkv, base)


def put_sums(sums_ref, place, near_ref, far):
    row_ids = lax.broadcasted_iota(jnp.int32, (BLOCK, SPAN), 0)
    for head in range(2):
        part = near_ref[head * BLOCK : (head + 1) * BLOCK, :]
        part = jnp.concatenate([part, jnp.zeros((BLOCK, BLOCK), F32)], axis=1)
        for bit in range(BLOCK.bit_length() - 1):
            moved = pltpu.roll(part, SPAN - (1 << bit), 1)
            part = jnp.where((row_ids >> bit) & 1 == 1, moved, part)
        sums_ref[place, head : head + 1, :] = jnp.sum(part, axis=0, keepdims=True)
        far_part = jnp.sum(far[head * BLOCK : (head + 1) * BLOCK], axis=0, keepdims=True)
        sums_ref[place, 2 + head : 3 + head, :] = jnp.concatenate(
            [far_part, jnp.zeros((1, NEAR), F32)], axis=1
        )
    sums_ref[place, 4:8, :] = jnp.zeros((4, SPAN), F32)


def query_kernel(
    plan_ref, q_ref, k_ref, v_ref, base_ref, do_ref, exact_ref, lse_ref, dq_ref, sums_ref, bias_ref, near_ref
):
    bias_ref[...] = near_bias(base_ref)
    lanes = lane_ids(2 * BLOCK, NEAR)
    far = jnp.zeros((2 * BLOCK, BLOCK), F32)
    for own in range(2):
        block = plan_ref[own]
        rows = pl.ds(own * BLOCK, BLOCK)
        stacked = stack_heads(q_ref[rows_at(plan_ref[SOURCE + 1 + block]), :])
        grads = stack_heads(do_ref[rows, :])
        exact = exact_ref[rows, :]
        product = grads.astype(F32) * jnp.concatenate([exact, exact], axis=0)
        delta = jnp.sum(product, axis=-1, keepdims=True)
        lse = lse_ref[0, own][:, :1]

        def grad_scores(scores, start):
            weights = jnp.exp(scores - lse)
            return weights * (dot(grads, two_tiles(v_ref, plan_ref, start), 1, 1) - delta)

        scores = dot(stacked, two_tiles(k_ref, plan_ref, block), 1, 1) + bias_ref[...]
        scores = jnp.where(lanes + block * BLOCK < BLOCK, MASKED, scores)
        near = grad_scores(scores, block)
        if own == 0:
            near_ref[...] = near
        else:
            near_ref[...] += near

        def step(chunk, carry):
            grad_q, far = carry
            start = block - 2 * chunk
            keys = two_tiles(k_ref, plan_ref, start)
            part = dot(stacked, keys, 1, 1)
            part = jnp.where(lanes + start * BLOCK < BLOCK, MASKED, part)
            grad_s = grad_scores(part, start)
            return (grad_q + dot(grad_s.astype(BF16), keys), far + fold_lanes(grad_s, jnp.add))

        grad_q, far = lax.fori_loop(
            1,
            jnp.maximum(block, 1) // 2 + 1,
            step,
            (dot(near.astype(BF16), two_tiles(k_ref, plan_ref, block)), far),
        )
        dq_ref[rows, :] = merge_heads(grad_q).astype(BF16)
    put_sums(sums_ref, 0, near_ref, far)


def attend_queries(plan, qkv, base, grad_out, exact, lse):
    rows, width = qkv.shape[0], grad_out.shape[1]
    own = pl.BlockSpec((NEAR, BLOCK), lambda pair, plan: (0, pair))
    row_spec = pl.BlockSpec((1, 8, SPAN), lambda pair, plan: (pair, 0, 0))
    return pl.pallas_call(
        query_kernel,
        grid_spec=pltpu.PrefetchScalarGridSpec(
            num_scalar_prefetch=1,
            grid=(PAIRS,),
            in_specs=pair_specs(rows, width)
            + [
                row_spec,
                own,
                own,
                pl.BlockSpec((1, 2, NEAR, BLOCK), lambda pair, plan: (pair, 0, 0, 0)),
            ],
            out_specs=[own, row_spec],
            scratch_shapes=[pltpu.VMEM((NEAR, NEAR), F32), pltpu.VMEM((NEAR, NEAR), F32)],
        ),
        out_shape=[
            jax.ShapeDtypeStruct((NEAR, width), BF16),
            jax.ShapeDtypeStruct((PAIRS, 8, SPAN), F32),
        ],
        compiler_params=pltpu.CompilerParams(vmem_limit_bytes=60 << 20),
        name="attend_queries",
    )(plan, qkv, qkv, qkv, base, grad_out, exact, lse)


def key_pair(tiles, load, stat, bias, mine, queries, grads, rest_q, rest_g, stats, grad_s, weights):
    half, count = tiles.half, tiles.count
    for place in range(2):
        for part in range(2):
            mine[part, place] = stack_heads(load(1 + part, tiles.row(tiles.own_step(place))))
    for step in range(count):
        row, place = tiles.row(step), tiles.place(step)
        for part, whole, rest in ((0, queries, rest_q), (3, grads, rest_g)):
            tile = load(part, row)
            whole[0, span(step), :] = tile
            whole[1, span(step), :] = only(place, 1, tile)
            if step > half:
                rest[span(step - half - 1), :] = only(place, 0, tile)
        stats[:, span(step)] = stat(row)
    for step, size in tiles.groups():
        place = tiles.place(step)
        scores = dot(mine[0, place], queries[0, span(step, size), :], 1, 1)
        extra = order_bias(bias, step, size, place, half)
        if extra is not None:
            scores = scores + extra
        push = dot(mine[1, place], grads[0, span(step, size), :], 1, 1)
        for head in range(2):
            rows = slice(head * BLOCK, (head + 1) * BLOCK)
            part = jnp.exp(scores[rows] - stats[head : head + 1, span(step, size)])
            weights[rows, span(step, size)] = part.astype(BF16)
            part = part * (push[rows] - stats[2 + head : 3 + head, span(step, size)])
            grad_s[rows, span(step, size)] = part.astype(BF16)
    tail = span(half + 1, count - half - 1)
    grad_k = (dot(grad_s[:, tail], rest_q[...]), dot(grad_s[...], queries[1]))
    grad_v = (dot(weights[:, tail], rest_g[...]), dot(weights[...], grads[1]))
    return [
        [merge_heads(part).astype(BF16) for part in grad] for grad in (grad_k, grad_v)
    ]


def key_kernel(plan_ref, q_ref, k_ref, v_ref, base_ref, do_ref, stats_ref, *refs):
    passed = (len(refs) - 11) // 2
    passed_in, outs, passed_out = (
        refs[:passed],
        refs[passed : passed + 2],
        refs[passed + 2 : 2 * passed + 2],
    )
    bias, *scratch = refs[2 * passed + 2 :]
    for src, dst in zip(passed_in, passed_out):
        dst[...] = src[...]
    blocks = q_ref.shape[0] // BLOCK
    tiles = Tiles(plan_ref, blocks, True)
    tile_refs = (q_ref, k_ref, v_ref, do_ref)
    bias[...] = near_bias(base_ref)

    def load(part, row):
        return tile_refs[part][rows_at(row), :]

    def stat(row):
        return stats_ref[row, 0]

    for out, grad in zip(outs, key_pair(tiles, load, stat, bias, *scratch)):
        for own, part in enumerate(in_order(tiles, grad)):
            out[own * BLOCK : (own + 1) * BLOCK, :] = part


def key_scratch(blocks):
    count = blocks + 1
    rest = count - blocks // 2 - 1
    return [
        pltpu.VMEM((2, 2, NEAR, BLOCK), BF16),
        pltpu.VMEM((2, count * BLOCK, BLOCK), BF16),
        pltpu.VMEM((2, count * BLOCK, BLOCK), BF16),
        pltpu.VMEM((rest * BLOCK, BLOCK), BF16),
        pltpu.VMEM((rest * BLOCK, BLOCK), BF16),
        pltpu.VMEM((8, count * BLOCK), F32),
        pltpu.VMEM((NEAR, count * BLOCK), BF16),
        pltpu.VMEM((NEAR, count * BLOCK), BF16),
    ]


def attend_keys(plan, qkv, base, grad_out, stats, passed):
    rows, width = grad_out.shape
    own = pl.BlockSpec((NEAR, BLOCK), lambda pair, plan: (0, pair))
    pieces = [own] + [
        pl.BlockSpec(
            (array.shape[0], array.shape[1] // PAIRS, array.shape[2]), lambda pair, plan: (0, pair, 0)
        )
        for array in passed[1:]
    ]
    return pl.pallas_call(
        key_kernel,
        grid_spec=pltpu.PrefetchScalarGridSpec(
            num_scalar_prefetch=1,
            grid=(PAIRS,),
            in_specs=pair_specs(rows, width)
            + [
                pl.BlockSpec((1, 8, SPAN), lambda pair, plan: (pair, 0, 0)),
                pl.BlockSpec((rows, BLOCK), lambda pair, plan: (0, pair)),
                pl.BlockSpec(
                    (rows // BLOCK, 1, 8, BLOCK), lambda pair, plan: (0, pair, 0, 0)
                ),
            ]
            + pieces,
            out_specs=[own, own] + pieces,
            scratch_shapes=[pltpu.VMEM((NEAR, NEAR), F32), *key_scratch(rows // BLOCK)],
        ),
        out_shape=[jax.ShapeDtypeStruct((NEAR, width), BF16)] * 2
        + [jax.ShapeDtypeStruct(array.shape, array.dtype) for array in passed],
        compiler_params=pltpu.CompilerParams(vmem_limit_bytes=60 << 20),
        name="attend_keys",
    )(plan, qkv, qkv, qkv, base, grad_out, stats, *passed)


BITS = {"core": ("wsh", 1), "x": ("wsh", 2), "y": ("ctx", 1), "near": ("ctx", 2), "far": ("ctx", 4)}
UNITS = (
    (3, 0, 6, ("core", "x", "y", "near", "far")),
    (0, 0, 6, ("core", "y", "x", "near", "far")),
    (1, 0, 4, ("core", "x", "y", "near", "far")),
    (2, 0, 4, ("core", "y", "x", "near", "far")),
    (1, 4, 2, ("core", "x", "y", "near", "far")),
    (2, 4, 2, ("core", "y", "x", "near", "far")),
)


def halved_shapes(order, share, width):
    shapes, blocks, rows, columns = [], 4, share, width
    for name in order:
        if name in ("core", "x"):
            blocks //= 2
        elif name == "y":
            columns //= 2
        else:
            rows //= 2
        shapes.append((blocks, rows, columns))
    return shapes


def partner(name):
    axis, bit = BITS[name]
    me = lax.axis_index(axis)
    side = (me // bit) % 2
    return axis, me + bit * (1 - 2 * side), side


class UnitSum:
    def __init__(self, unit, total, gathered, sends, recvs, sems):
        self.weight, first, pairs, self.order = unit
        self.first, self.columns = first * BLOCK, pairs * BLOCK
        self.total, self.gathered, self.sends, self.recvs = total, gathered, sends, recvs
        self.half_send, self.half_recv, self.whole_send, self.whole_recv = sems
        self.steps = len(self.order)
        blocks, row, column = [0, 1, 2, 3], 0, 0
        rows, columns = total.shape[1], self.columns
        self.regions = []
        for name in self.order:
            side = partner(name)[2]
            if name == "core":
                keep = ([line * 2 + side for line in range(2)], row, column)
                sent = ([line * 2 + 1 - side for line in range(2)], row, column)
            elif name == "x":
                core = partner("core")[2]
                keep = ([side * 2 + core], row, column)
                sent = ([(1 - side) * 2 + core], row, column)
            elif name == "y":
                columns //= 2
                keep = (blocks, row, column + side * columns)
                sent = (blocks, row, column + (1 - side) * columns)
            else:
                rows //= 2
                keep = (blocks, row + side * rows, column)
                sent = (blocks, row + (1 - side) * rows, column)
            blocks, row, column = keep
            self.regions.append((keep, sent))
        self.wholes = [name for name in reversed(self.order) if BITS[name][0] == "ctx"]

    def span(self, step, region, shift=0):
        shape = self.sends[step].shape
        blocks, row, column = region
        row_part = pl.ds(row if isinstance(row, int) else pl.multiple_of(row, 16), shape[1])
        column = column + shift
        column_part = pl.ds(
            column if isinstance(column, int) else pl.multiple_of(column, BLOCK), shape[2]
        )
        return blocks, row_part, column_part

    def remote(self, source, target, send, recv, name):
        axis, peer, side = partner(name)
        return pltpu.make_async_remote_copy(
            src_ref=source,
            dst_ref=target,
            send_sem=send,
            recv_sem=recv,
            device_id={axis: peer},
            device_id_type=pl.DeviceIdType.MESH,
        )

    def half_copy(self, step):
        return self.remote(
            self.sends[step],
            self.recvs[step],
            self.half_send.at[step],
            self.half_recv.at[step],
            self.order[step],
        )

    def give(self, step):
        blocks, row_part, column_part = self.span(step, self.regions[step][1])
        for place, block in enumerate(blocks):
            self.sends[step][place] = self.total[block, row_part, column_part].astype(BF16)
        self.half_copy(step).start()

    def begin(self, value):
        share = self.total.shape[1]
        for block in range(4):
            self.total[block] = value[block * share : (block + 1) * share].astype(F32)
        self.give(0)

    def whole_copy(self, back):
        name = self.wholes[back]
        step = self.order.index(name)
        blocks, row_part, column_part = self.span(step, self.regions[step][0], self.first)
        view = self.gathered.at[self.weight, row_part, column_part]
        return self.remote(
            view, view, self.whole_send.at[back], self.whole_recv.at[back], name
        )

    def advance(self, phase):
        if phase >= self.steps:
            back = phase - self.steps
            self.whole_copy(back).wait_recv()
            if back + 1 < len(self.wholes):
                self.whole_copy(back + 1).start()
            return
        self.half_copy(phase).wait_recv()
        blocks, row_part, column_part = self.span(phase, self.regions[phase][0])
        for place, block in enumerate(blocks):
            self.total[block, row_part, column_part] += self.recvs[phase][place].astype(F32)
        if phase + 1 < self.steps:
            self.give(phase + 1)
            return
        whole = self.span(phase, self.regions[phase][0], self.first)
        self.gathered[self.weight, whole[1], whole[2]] = self.total[
            blocks[0], row_part, column_part
        ].astype(BF16)
        self.whole_copy(0).start()

    def finish(self):
        for step in range(self.steps):
            self.half_copy(step).wait_send()
        for back in range(len(self.wholes)):
            self.whole_copy(back).wait_send()


def tail_kernel(
    experts,
    dq_ref,
    hidden_ref,
    grad_mid_ref,
    weights_ref,
    grad_wo_ref,
    qkv_ref,
    do_ref,
    stats_ref,
    returned_ref,
    resid_ref,
    gate_ref,
    slot_ref,
    small_ref,
    router_ref,
    gain_ref,
    sums_ref,
    hot_ref,
    base_ref,
    plan_ref,
    input_grad_out,
    output_out,
    shares_out,
    router_out,
    gains_out,
    table_out,
    weights,
    hidden,
    grad_mid,
    grad_wo,
    resid,
    returned,
    home,
    qkv,
    grad_out,
    stats,
    dk,
    dv,
    bias,
    mine,
    queries,
    grads,
    rest_q,
    rest_g,
    tile_stats,
    grad_s,
    tile_weights,
    gathered,
    pack,
    pack_recv,
    *rest,
):
    steps, count = len(BITS), len(UNITS)
    totals, rest = rest[:count], rest[count:]
    sends = [rest[unit * steps : (unit + 1) * steps] for unit in range(count)]
    rest = rest[count * steps :]
    recvs = [rest[unit * steps : (unit + 1) * steps] for unit in range(count)]
    (
        fetch_sems,
        half_send,
        half_recv,
        whole_send,
        whole_recv,
        pack_send,
        pack_sem,
        back_send,
        back_recv,
    ) = rest[count * steps :]
    tokens, width = dq_ref.shape
    share = totals[0].shape[1]
    ctx_count = lax.axis_size("ctx")
    exp_dev = experts // ctx_count
    most = returned.shape[0] // experts
    sources = (
        (hidden_ref, hidden),
        (grad_wo_ref, grad_wo),
        (returned_ref, returned),
        (qkv_ref, qkv),
        (do_ref, grad_out),
        (stats_ref, stats),
        (weights_ref.at[pl.ds(0, 3)], weights),
        (grad_mid_ref, grad_mid),
        (resid_ref, resid),
    )
    fetches = [
        pltpu.make_async_copy(src, dst, fetch_sems.at[place])
        for place, (src, dst) in enumerate(sources)
    ]
    for fetch in fetches:
        fetch.start()
    greet((ctx_count, lax.axis_size("wsh")))
    units = [
        UnitSum(
            unit,
            totals[place],
            gathered,
            sends[place],
            recvs[place],
            [sem.at[place] for sem in (half_send, half_recv, whole_send, whole_recv)],
        )
        for place, unit in enumerate(UNITS)
    ]
    wo, wq, wk_early, wv_early, wk_late, wv_late = units

    fetches[2].wait()
    back = Exchange(
        ctx_count,
        exp_dev,
        most,
        (back_send, back_recv),
        lambda expert, peer: returned.at[back.rows(expert * ctx_count + peer), :],
        lambda expert, peer: home.at[back.rows(peer * exp_dev + expert), :],
    )
    for expert in range(exp_dev):
        back.start(expert)
    fetches[0].wait()
    rows = hidden[...].astype(F32)
    inv = lax.rsqrt(jnp.mean(rows * rows, axis=-1, keepdims=True) + epsilon)
    gain = small_ref[...].astype(F32)[experts : experts + 1, :]
    normed = (rows * inv * gain).astype(BF16)
    hidden[...] = normed
    fetches[1].wait()
    wo.begin(grad_wo[...])
    wq.begin(dot(normed, dq_ref[...], 0, 0))
    for fetch in fetches[3:6]:
        fetch.wait()
    tiles = Tiles(plan_ref, qkv.shape[0], True)

    def key_step(pair, carry):
        pair_lanes = pl.ds(pl.multiple_of(pair * BLOCK, BLOCK), BLOCK)

        def load(part, row):
            if part == 3:
                return grad_out[row, :, pair_lanes]
            lanes = pl.ds(pl.multiple_of(part * width + pair * BLOCK, BLOCK), BLOCK)
            return qkv[row, :, lanes]

        bias[...] = near_bias(base_ref, pair)
        results = key_pair(
            tiles,
            load,
            lambda row: stats[row, pair],
            bias,
            mine,
            queries,
            grads,
            rest_q,
            rest_g,
            tile_stats,
            grad_s,
            tile_weights,
        )
        for out, result in zip((dk, dv), results):
            for own, part in enumerate(in_order(tiles, result)):
                out[own * BLOCK : (own + 1) * BLOCK, pair_lanes] = part

        @pl.when(pair == 0)
        def _():
            wo.advance(0)
            wq.advance(0)

        @pl.when(pair == 2)
        def _():
            wo.advance(1)
            wq.advance(1)

        @pl.when(pair == 3)
        def _():
            early = slice(wk_early.first, wk_early.first + wk_early.columns)
            wk_early.begin(dot(hidden[...], dk[:, early], 0, 0))
            wv_early.begin(dot(hidden[...], dv[:, early], 0, 0))
            wo.advance(2)
            wq.advance(2)

        @pl.when(pair == 4)
        def _():
            wk_early.advance(0)
            wv_early.advance(0)
            wo.advance(3)
            wq.advance(3)

        return carry

    lax.fori_loop(0, PAIRS, key_step, 0)
    late = slice(wk_late.first, wk_late.first + wk_late.columns)
    wk_late.begin(dot(hidden[...], dk[:, late], 0, 0))
    wv_late.begin(dot(hidden[...], dv[:, late], 0, 0))
    for unit, phase in ((wo, 4), (wq, 4), (wk_early, 1), (wv_early, 1)):
        unit.advance(phase)
    fetches[6].wait()
    grad_normed = dot(dq_ref[...], weights[0], 1, 1)
    grad_normed = grad_normed + dot(dk[...], weights[1], 1, 1)
    grad_normed = grad_normed + dot(dv[...], weights[2], 1, 1)
    for unit, phase in ((wk_late, 0), (wv_late, 0)):
        unit.advance(phase)
    gain_part = jnp.sum(grad_normed * rows * inv, axis=0, keepdims=True)
    pack[...] = jnp.zeros_like(pack)
    pack[:experts, :] = router_ref[...]
    pack[experts : experts + 1, :] = gain_part
    pack[experts + 1 : experts + 2, :] = gain_ref[0:1, :]
    last = lane_ids(2, BLOCK) == hot_ref.shape[1] - 1
    for pair in range(PAIRS):
        near = lax.dot_general(
            sums_ref[pair, 0:2, :],
            hot_ref[...],
            (((1,), (0,)), ((), ())),
            precision=HIGH,
            preferred_element_type=F32,
        )
        near = jnp.concatenate([near, jnp.zeros((2, BLOCK - near.shape[1]), F32)], axis=1)
        distant = jnp.sum(sums_ref[pair, 2:4, :], axis=1, keepdims=True)
        near = near + jnp.where(last, distant, 0.0)
        for head in range(2):
            pack[experts + 2 + head : experts + 3 + head, span(pair)] = near[head : head + 1]

    def pack_copy(step):
        return wo.remote(
            pack_recv.at[0, step],
            pack_recv.at[1, step],
            pack_send.at[step],
            pack_sem.at[step],
            list(BITS)[step],
        )

    def pack_start(step):
        pack_recv[0, step] = pack[...].astype(BF16)
        pack_copy(step).start()

    def pack_end(step):
        pack_copy(step).wait_recv()
        pack[...] = pack_recv[0, step].astype(F32) + pack_recv[1, step].astype(F32)
        if step + 1 < steps:
            pack_start(step + 1)

    pack_start(0)
    for unit, phase in ((wk_early, 2), (wv_early, 2), (wk_late, 1), (wv_late, 1), (wo, 5), (wq, 5)):
        unit.advance(phase)
    pack_end(0)
    fetches[7].wait()
    scaled = grad_normed * gain
    mean = jnp.mean(scaled * rows, axis=-1, keepdims=True)
    grad_in = grad_mid[...] + inv * scaled - rows * inv * inv * inv * mean
    input_grad_out[...] = grad_in.astype(BF16)
    for unit, phase in ((wk_early, 3), (wv_early, 3), (wk_late, 2), (wv_late, 2), (wo, 6), (wq, 6)):
        unit.advance(phase)
    pack_end(1)
    for expert in range(exp_dev):
        back.wait(expert)
    fetches[8].wait()
    token_out = dot(placement_of(slot_ref, experts * most), home[...], 0, 0)
    output_out[...] = (resid[...] + gate_ref[:, :1] * token_out).astype(BF16)
    for unit, phase in ((wk_early, 4), (wv_early, 4), (wk_late, 3), (wv_late, 3), (wo, 7), (wq, 7)):
        unit.advance(phase)
    pack_end(2)
    for unit, phase in ((wk_late, 4), (wv_late, 4), (wk_early, 5), (wv_early, 5)):
        unit.advance(phase)
    pack_end(3)
    for unit, phase in ((wk_late, 5), (wv_late, 5), (wk_early, 6), (wv_early, 6)):
        unit.advance(phase)
    pack_end(4)
    for unit, phase in ((wk_late, 6), (wv_late, 6), (wk_early, 7), (wv_early, 7)):
        unit.advance(phase)
    own = lax.axis_index("wsh")
    buckets = table_out.shape[0]
    for block in range(4):

        @pl.when(own == block)
        def _():
            part = pack[: experts + 8, block * share : (block + 1) * share]
            router_out[...] = part[:experts]
            gains_out[...] = part[experts : experts + 8]
            heads = [
                pack[experts + 2 + head : experts + 3 + head, span(pair)]
                for pair in range(PAIRS)
                for head in range(2)
            ]
            table = jnp.transpose(jnp.concatenate(heads + heads[:4], axis=0))
            table_out[...] = table[block * buckets : (block + 1) * buckets, :HEADS]

    for unit in (wk_late, wv_late):
        unit.advance(7)
    shares_out[...] = gathered[...]
    for step in range(steps):
        pack_copy(step).wait_send()
    for unit in units:
        unit.finish()
    for expert in range(exp_dev):
        back.finish(expert)


def tail(
    experts,
    dq,
    hidden,
    grad_mid,
    weights,
    grad_wo,
    qkv,
    grad_out,
    stats,
    returned,
    resid,
    gate,
    slots,
    small,
    router,
    gains,
    sums,
    hot,
    base,
    plan,
    share,
    buckets,
):
    tokens, width = dq.shape
    vmem = pl.BlockSpec(memory_space=pltpu.VMEM)
    anywhere = pl.BlockSpec(memory_space=pl.ANY)
    steps, count = len(BITS), len(UNITS)
    pieces = [
        shape for unit in UNITS for shape in halved_shapes(unit[3], share, unit[2] * BLOCK)
    ]
    buffers = [pltpu.VMEM(shape, BF16) for shape in pieces]
    ctx_count = lax.axis_size("ctx")
    rows = experts + 16
    dma = pltpu.SemaphoreType.DMA
    return pl.pallas_call(
        functools.partial(tail_kernel, experts),
        in_specs=[vmem]
        + [anywhere] * 9
        + [vmem] * 8
        + [pl.BlockSpec(memory_space=pltpu.SMEM)],
        out_specs=[vmem] * 6,
        out_shape=[
            jax.ShapeDtypeStruct((tokens, width), BF16),
            jax.ShapeDtypeStruct((tokens, width), BF16),
            jax.ShapeDtypeStruct((4, share, width), BF16),
            jax.ShapeDtypeStruct((experts, share), F32),
            jax.ShapeDtypeStruct((8, share), F32),
            jax.ShapeDtypeStruct((buckets, HEADS), F32),
        ],
        scratch_shapes=[
            pltpu.VMEM((3, width, width), BF16),
            pltpu.VMEM((tokens, width), BF16),
            pltpu.VMEM((tokens, width), F32),
            pltpu.VMEM((width, width), BF16),
            pltpu.VMEM((tokens, width), F32),
            pltpu.VMEM(returned.shape, BF16),
            pltpu.VMEM(returned.shape, BF16),
            pltpu.VMEM(qkv.shape, BF16),
            pltpu.VMEM(grad_out.shape, BF16),
            pltpu.VMEM(stats.shape, F32),
            pltpu.VMEM((tokens, width), BF16),
            pltpu.VMEM((tokens, width), BF16),
            pltpu.VMEM((NEAR, NEAR), F32),
            *key_scratch(qkv.shape[0]),
            pltpu.VMEM((4, share, width), BF16),
            pltpu.VMEM((rows, width), F32),
            pltpu.VMEM((2, steps, rows, width), BF16),
            *[pltpu.VMEM((4, share, unit[2] * BLOCK), F32) for unit in UNITS],
            *buffers,
            *buffers,
            dma((9,)),
            dma((count, steps)),
            dma((count, steps)),
            dma((count, 3)),
            dma((count, 3)),
            dma((steps,)),
            dma((steps,)),
            dma((experts // ctx_count, ctx_count - 1)),
            dma((experts // ctx_count, ctx_count - 1)),
        ],
        compiler_params=pltpu.CompilerParams(
            collective_id=2, has_side_effects=True, vmem_limit_bytes=62 << 20
        ),
        name="tail",
    )(
        dq,
        hidden,
        grad_mid,
        weights,
        grad_wo,
        qkv,
        grad_out,
        stats,
        returned,
        resid,
        gate,
        slots,
        small,
        router,
        gains,
        sums,
        hot,
        base,
        plan,
    )


def finish_kernel(
    input_ref,
    output_ref,
    shares_ref,
    router_ref,
    gains_ref,
    table_ref,
    w_in_ref,
    w_out_ref,
    input_out,
    output_out,
    wq,
    wk,
    wv,
    wo,
    router,
    gain_a,
    gain_m,
    table,
    w_in_out,
    w_out_out,
):
    w_in_out[...] = w_in_ref[...].astype(F32)
    w_out_out[...] = w_out_ref[...].astype(F32)
    input_out[...] = input_ref[...]
    output_out[...] = output_ref[...]
    for place, out in enumerate((wq, wk, wv, wo)):
        out[...] = shares_ref[place].astype(F32)

    @pl.when(pl.program_id(0) == 0)
    def _():
        router[...] = router_ref[...]
        gain_a[...] = gains_ref[0, :]
        gain_m[...] = gains_ref[1, :]
        table[...] = table_ref[...]


def finish(grad_input, output, shares, router, gains, table, w_in, w_out):
    share, width = shares.shape[1:]

    def whole(array):
        zeros = (0,) * len(array.shape)
        return pl.BlockSpec(array.shape, lambda step: zeros)

    def pieces(array):
        *outer, rows, columns = array.shape
        zeros = (0,) * len(outer)
        return pl.BlockSpec((*outer, rows // 4, columns), lambda step: (*zeros, step, 0))

    arrays = (grad_input, output, shares, router, gains, table)
    outs = [
        jax.ShapeDtypeStruct(grad_input.shape, BF16),
        jax.ShapeDtypeStruct(output.shape, BF16),
        *[jax.ShapeDtypeStruct((share, width), F32)] * 4,
        jax.ShapeDtypeStruct(router.shape, F32),
        jax.ShapeDtypeStruct((share,), F32),
        jax.ShapeDtypeStruct((share,), F32),
        jax.ShapeDtypeStruct(table.shape, F32),
    ]
    experts = [jax.ShapeDtypeStruct(array.shape, F32) for array in (w_in, w_out)]
    return pl.pallas_call(
        finish_kernel,
        grid=(4,),
        in_specs=[pieces(array) for array in arrays[:3]]
        + [whole(array) for array in arrays[3:]]
        + [pieces(w_in), pieces(w_out)],
        out_specs=[pieces(array) for array in outs[:6]]
        + [whole(array) for array in outs[6:]]
        + [pieces(w_in), pieces(w_out)],
        out_shape=outs + experts,
        compiler_params=pltpu.CompilerParams(vmem_limit_bytes=60 << 20),
        name="finish",
    )(*arrays, w_in, w_out)


def rms_forward(values, gain_vec):
    inv_rms = lax.rsqrt(jnp.mean(values * values, axis=-1, keepdims=True) + epsilon)
    return (values * inv_rms * gain_vec, inv_rms)


def rms_backward(values, inv_rms, gain_vec, upstream):
    grad_gain = jnp.sum(upstream * values * inv_rms, axis=0)
    scaled = upstream * gain_vec
    grad_values = inv_rms * scaled - values * inv_rms**3 * jnp.mean(
        scaled * values, axis=-1, keepdims=True
    )
    return (grad_values, grad_gain)


def per_device(
    hidden_in,
    w_query,
    w_key,
    w_value,
    w_output,
    w_router,
    gain_attn,
    gain_moe,
    rel_bias,
    w_in,
    w_out,
    routes,
    block_pairs,
    cotangent,
):
    tokens, width = hidden_in.shape[1:]
    ctx_count, wsh_count = lax.axis_size("ctx"), lax.axis_size("wsh")
    ctx_rank, wsh_rank = lax.axis_index("ctx"), lax.axis_index("wsh")
    length = tokens * ctx_count
    blocks = length // BLOCK
    experts, exp_dev = w_router.shape[1], w_in.shape[0]
    slot_most = 2 * tokens // experts
    capacity = (9 * length // (8 * experts) + 7) // 8 * 8

    def over(axis, array, dim=0):
        return lax.all_gather(array, axis, axis=dim, tiled=True)

    share = width // wsh_count
    lanes = wrapped_lanes()
    buckets = rel_bias.shape[0] * wsh_count
    query_hot = onehot_of(BLOCK - lanes, buckets)
    key_hot = onehot_of(lanes, buckets)

    def hot_rows(hot):
        return jnp.asarray(hot.T, BF16)

    qkv, weights, small, slot_rows, targets, plan, query_base, key_base = project(
        (ctx_count, wsh_count),
        capacity,
        experts,
        slot_most,
        hidden_in[0],
        (w_query, w_key, w_value, w_output),
        (w_router.T, gain_attn, gain_moe, rel_bias),
        routes.reshape(1, tokens),
        block_pairs.T,
        hot_rows(query_hot),
        hot_rows(key_hot),
    )
    if wsh_count > 4:
        attn_low, attn_exact, lse, lse_rows = attend_forward(plan, qkv, query_base, width)
    else:
        attn_low = attn_exact = hidden_in[0]
        lse_rows = query_base
    (
        output_rows,
        returned,
        resid,
        gate,
        grad_mid,
        grad_heads,
        heads_all,
        stats,
        grad_wo,
        grad_router,
        grad_gain_m,
        grad_q,
        sums,
        grad_w_in,
        grad_w_out,
    ) = middle(
        (ctx_count, wsh_count),
        experts,
        attn_low,
        attn_exact.reshape(2, BLOCK, width),
        hidden_in[0],
        cotangent[0],
        weights,
        w_in,
        w_out,
        small,
        slot_rows,
        targets,
        lse_rows,
        routes.reshape(1, tokens),
        query_base,
        plan,
        qkv.reshape(blocks, BLOCK, 3 * width),
        capacity,
    )

    bucket_share = buckets // wsh_count
    if wsh_count <= 4:
        results = tail(
            experts,
            grad_q,
            hidden_in[0],
            grad_mid,
            weights,
            grad_wo,
            qkv.reshape(blocks, BLOCK, 3 * width),
            heads_all.reshape(blocks, BLOCK, width),
            stats.reshape(blocks, PAIRS, 8, BLOCK),
            returned,
            resid,
            gate,
            slot_rows,
            small,
            grad_router,
            grad_gain_m,
            sums,
            jnp.asarray(query_hot),
            key_base,
            plan,
            share,
            bucket_share,
        )
        grad_input, output_rows, *rest = finish(*results, grad_w_in, grad_w_out)
        rest[4] = rest[4].T
        return (output_rows[None], grad_input[None], *rest)

    heads_all = dot(over("ctx", heads_all), weights[3], 1, 1).astype(BF16)
    stats = over("ctx", stats).reshape(blocks, PAIRS, 8, BLOCK)
    grad_q, sums = attend_queries(plan, qkv, query_base, grad_heads, attn_exact, lse)
    grad_k, grad_v, output_rows, grad_w_in, grad_w_out = attend_keys(
        plan, qkv, key_base, heads_all, stats, (output_rows, grad_w_in, grad_w_out)
    )

    near_sums = sums[:, :2].reshape(HEADS, SPAN)
    far_sums = jnp.sum(sums[:, 2:4].reshape(HEADS, SPAN), axis=1)
    grad_table = jnp.dot(jnp.asarray(query_hot.T), near_sums.T, precision=HIGH)
    grad_table = grad_table.at[buckets - 1].add(far_sums)

    resid_in = hidden_in[0].astype(F32)
    full_query, full_key, full_value = (weights[place] for place in range(3))
    gain_one = small[experts].astype(F32)
    normed_one, inv_one = rms_forward(resid_in, gain_one)
    normed_one = normed_one.astype(BF16)
    grad_normed_one = dot(grad_q, full_query, 1, 1)
    grad_normed_one = grad_normed_one + dot(grad_k, full_key, 1, 1)
    grad_normed_one = grad_normed_one + dot(grad_v, full_value, 1, 1)
    grad_in_norm, grad_gain_a = rms_backward(resid_in, inv_one, gain_one, grad_normed_one)
    grad_input = (grad_mid + grad_in_norm).astype(BF16)

    def reduce_weight(grad):
        part = lax.psum_scatter(grad.astype(BF16), "wsh", scatter_dimension=0, tiled=True)
        return lax.psum(part, "ctx").astype(F32)

    grad_wq = dot(normed_one, grad_q, 0, 0)
    grad_wk = dot(normed_one, grad_k, 0, 0)
    grad_wv = dot(normed_one, grad_v, 0, 0)
    shares = [reduce_weight(grad) for grad in (grad_wq, grad_wk, grad_wv, grad_wo)]
    columns = jnp.concatenate(
        [grad_router.T, grad_gain_a[:, None], grad_gain_m[0][:, None]], axis=1
    )
    table = jnp.pad(grad_table, ((0, 0), (0, columns.shape[1] - HEADS)))
    summed = lax.psum(jnp.concatenate([columns, table], axis=0), ("ctx", "wsh"))
    own_columns = lax.dynamic_slice_in_dim(summed[:width], wsh_rank * share, share, 0)
    own_table = lax.dynamic_slice_in_dim(
        summed[width:, :HEADS], wsh_rank * bucket_share, bucket_share, 0
    )
    return (
        output_rows.astype(BF16)[None],
        grad_input[None],
        *shares,
        own_columns[:, :experts],
        own_columns[:, experts],
        own_columns[:, experts + 1],
        own_table,
        grad_w_in,
        grad_w_out,
    )


def solution(mesh):
    in_specs = (
        P("wsh", "ctx", None),
        P("wsh", None),
        P("wsh", None),
        P("wsh", None),
        P("wsh", None),
        P("wsh", None),
        P("wsh"),
        P("wsh"),
        P("wsh", None),
        P("ctx", None, "wsh"),
        P("ctx", "wsh", None),
        P("wsh", "ctx", None),
        P(),
        P("wsh", "ctx", None),
    )
    out_specs = (
        P("wsh", "ctx", None),
        P("wsh", "ctx", None),
        P("wsh", None),
        P("wsh", None),
        P("wsh", None),
        P("wsh", None),
        P("wsh", None),
        P("wsh"),
        P("wsh"),
        P("wsh", None),
        P("ctx", None, "wsh"),
        P("ctx", "wsh", None),
    )
    return jax.shard_map(
        per_device, mesh=mesh, in_specs=in_specs, out_specs=out_specs, check_vma=False
    )
```

```python
import functools
import math

import jax
import jax.numpy as jnp
import numpy as np
from jax import lax
from jax.experimental import pallas as pl
from jax.experimental.pallas import tpu as pltpu
from jax.sharding import PartitionSpec as P

HEADS = 12
HEAD_DIM = 64
BLOCK = 128
PAIRS = HEADS // 2
NEAR = 2 * BLOCK
SPAN = 3 * BLOCK
epsilon = 1e-06
MASKED = -1e30
bucket_edges = [math.ceil(16 * 8 ** (marker / 16)) for marker in range(1, 16)]
F32 = jnp.float32
BF16 = jnp.bfloat16
HIGH = lax.Precision.HIGHEST


def bucket_of(distance):
    gap = np.maximum(distance, 0)
    count = np.full(gap.shape, 16, np.int32)
    for edge in bucket_edges:
        count = count + (gap >= edge)
    return np.where(gap < 16, gap, count)


def wrapped_lanes():
    lanes = np.arange(SPAN)
    return np.where(lanes < NEAR, lanes, lanes - SPAN)


def onehot_of(distance, buckets):
    return (bucket_of(distance)[:, None] == np.arange(buckets)[None, :]).astype(np.float32)


def dot(left, right, left_dim=1, right_dim=0):
    return lax.dot_general(
        left, right, (((left_dim,), (right_dim,)), ((), ())), preferred_element_type=F32
    )


def lane_ids(rows, lanes):
    return lax.broadcasted_iota(jnp.int32, (rows, lanes), 1)


def stack_heads(rows):
    first = lane_ids(rows.shape[0], BLOCK) < HEAD_DIM
    zero = jnp.zeros_like(rows)
    return jnp.concatenate([jnp.where(first, rows, zero), jnp.where(first, zero, rows)], axis=0)


def merge_heads(stacked):
    half = stacked.shape[0] // 2
    first = lane_ids(half, BLOCK) < HEAD_DIM
    return jnp.where(first, stacked[:half], stacked[half:])


def fold_lanes(tile, combine):
    return combine(tile[:, :BLOCK], tile[:, BLOCK:])


def near_bias(base_ref, place=0):
    tiles = []
    for head in range(2):
        row = jnp.broadcast_to(base_ref[place, head : head + 1, :], (BLOCK, SPAN))
        tiles.append(pltpu.roll(row, 0, 1, stride=1, stride_axis=0)[:, :NEAR])
    return jnp.concatenate(tiles, axis=0)


def rows_at(block):
    return pl.ds(pl.multiple_of(block * BLOCK, BLOCK), BLOCK)


def two_tiles(ref, plan_ref, tile):
    tile = SOURCE + tile
    return jnp.concatenate(
        [ref[rows_at(plan_ref[tile]), :], ref[rows_at(plan_ref[tile + 1]), :]], axis=0
    )


class LineGather:
    def __init__(self, axis, lines, across, views, own, sems, crossing=None):
        self.axis, self.lines, self.across = axis, lines, across
        self.views, self.own, self.sems = views, own, sems
        self.crossing = crossing or ["all"] * len(views)
        self.me = lax.axis_index(axis)
        self.line, self.column = self.me // across, self.me % across

    def copy(self, part, block, peer, kind, place, own=False):
        send, recv = self.sems
        view = self.views[part](block)
        return pltpu.make_async_remote_copy(
            src_ref=self.own[part] if own else view,
            dst_ref=view,
            send_sem=send.at[part, kind, place],
            recv_sem=recv.at[part, kind, place],
            device_id={self.axis: peer},
            device_id_type=pl.DeviceIdType.MESH,
        )

    def line_send(self, part, way, step):
        place = self.line - way * step
        ahead = self.line + way
        there = (place >= 0) & (place < self.lines) & (ahead >= 0) & (ahead < self.lines)
        copy = self.copy(
            part,
            place * self.across + self.column,
            ahead * self.across + self.column,
            (1 - way) // 2,
            step,
            own=step == 0,
        )
        return there, copy

    def line_recv(self, part, way, step):
        place = self.line - way * (step + 1)
        there = (place >= 0) & (place < self.lines)
        block = place * self.across + self.column
        return there, block, self.copy(part, block, self.me, (1 - way) // 2, step)

    def cross_send(self, part, block, ahead, own=False):
        peer = self.line * self.across + (self.column + ahead) % self.across
        return self.copy(part, block, peer, 1 + ahead, block // self.across, own)

    def cross_recv(self, part, line, ahead):
        block = line * self.across + (self.column + self.across - ahead) % self.across
        return self.copy(part, block, self.me, 1 + ahead, line)

    def begin(self, part):
        for way in (1, -1):
            there, copy = self.line_send(part, way, 0)
            pl.when(there)(copy.start)
        if self.crossing[part] != "none":
            for ahead in range(1, self.across):
                self.cross_send(part, self.me, ahead, own=True).start()

    def advance(self, part, step):
        for way in (1, -1):
            there, block, arrived = self.line_recv(part, way, step)

            pl.when(there)(arrived.wait_recv)
            if step + 2 < self.lines:
                onward, copy = self.line_send(part, way, step + 1)
                pl.when(onward)(copy.start)
            if self.crossing[part] == "all":
                for ahead in range(1, self.across):
                    pl.when(there)(self.cross_send(part, block, ahead).start)

    def wait_cross(self, part):
        for ahead in range(1, self.across):
            for line in range(self.lines):
                self.cross_recv(part, line, ahead).wait_recv()

    def finish(self):
        for part in range(len(self.views)):
            self.finish_part(part)

    def finish_part(self, part):
        for step in range(self.lines - 1):
            for way in (1, -1):
                there, copy = self.line_send(part, way, step)
                pl.when(there)(copy.wait_send)
        for ahead in range(1, self.across):
            if self.crossing[part] == "all":
                for line in range(self.lines):
                    self.cross_send(part, line * self.across + self.column, ahead).wait_send()
            elif self.crossing[part] == "own":
                self.cross_send(part, self.me, ahead).wait_send()


class RowGather:
    def __init__(self, counts, held, sems):
        lines, across = grid_of(counts[0])
        tokens = held.shape[1]
        self.across, self.lines = across, lines
        me = lax.axis_index("ctx")
        self.me = me
        self.balanced = across == 2 and tokens % 32 == 0
        bulk = tokens * 14 // 16 if self.balanced else tokens
        half = bulk // 32 * 16
        cuts = [(0, half), (half, bulk - half)]

        def view(start, rows, turn):
            def of(block):
                if turn:
                    block = block + 1 - 2 * (block % 2)
                return held.at[block, pl.ds(start, rows), :]

            return of

        views = [view(start, rows, False) for start, rows in cuts]
        crossing = ["all", "all"]
        if self.balanced:
            views += [view(bulk, tokens - bulk, turn) for turn in (False, True)]
            crossing += ["own", "none"]
        self.parts = len(views)
        self.gather = LineGather(
            "ctx", lines, across, views, [of(me) for of in views], sems, crossing
        )

    def begin(self):
        for part in range(min(self.parts, 3)):
            self.gather.begin(part)

    def advance(self, step):
        if self.balanced and step == 0:
            self.gather.cross_recv(2, self.gather.line, 1).wait_recv()
            self.gather.begin(3)
        for part in range(self.parts):
            self.gather.advance(part, step)

    def wait_cross(self, line, ahead):
        for part in range(2):
            self.gather.cross_recv(part, line, ahead).wait_recv()

    def finish(self):
        self.gather.finish()


def row_parts(ctx_count, tokens):
    return 4 if grid_of(ctx_count)[1] == 2 and tokens % 32 == 0 else 2


def gather_sems(parts, lines, across):
    return [pltpu.SemaphoreType.DMA((parts, 1 + across, lines))] * 2


def greet(counts):
    barrier = pltpu.get_barrier_semaphore()
    for axis, count in zip(("ctx", "wsh"), counts):
        me = lax.axis_index(axis)
        for ahead in range(1, count):
            pl.semaphore_signal(
                barrier,
                inc=1,
                device_id={axis: (me + ahead) % count},
                device_id_type=pl.DeviceIdType.MESH,
            )
    pl.semaphore_wait(barrier, sum(counts) - 2)


class Exchange:
    def __init__(self, count, experts, most, sems, source, target):
        self.count, self.experts, self.most = count, experts, most
        self.send, self.recv = sems
        self.source, self.target = source, target
        self.me = lax.axis_index("ctx")

    def rows(self, place):
        return pl.ds(pl.multiple_of(place * self.most, self.most), self.most)

    def copy(self, expert, ahead, outward):
        peer = (self.me + ahead) % self.count if outward else (self.me + self.count - ahead) % self.count
        return pltpu.make_async_remote_copy(
            src_ref=self.source(expert, peer),
            dst_ref=self.target(expert, self.me),
            send_sem=self.send.at[expert, ahead - 1],
            recv_sem=self.recv.at[expert, ahead - 1],
            device_id={"ctx": peer},
            device_id_type=pl.DeviceIdType.MESH,
        )

    def start(self, expert):
        for ahead in range(1, self.count):
            self.copy(expert, ahead, True).start()
        self.target(expert, self.me)[...] = self.source(expert, self.me)[...]

    def wait(self, expert):
        for ahead in range(1, self.count):
            peer = (self.me + self.count - ahead) % self.count
            pltpu.make_async_remote_copy(
                src_ref=self.source(expert, peer),
                dst_ref=self.target(expert, peer),
                send_sem=self.send.at[expert, ahead - 1],
                recv_sem=self.recv.at[expert, ahead - 1],
                device_id={"ctx": peer},
                device_id_type=pl.DeviceIdType.MESH,
            ).wait_recv()

    def finish(self, expert):
        for ahead in range(1, self.count):
            self.copy(expert, ahead, True).wait_send()


def exchange_sems(count, experts):
    return [pltpu.SemaphoreType.DMA((experts, count - 1))] * 2


def cap_map(target_ref, expert, capacity):
    slots = target_ref.shape[1]
    rows = lax.broadcasted_iota(jnp.int32, (capacity, slots), 0)
    return (rows == jnp.broadcast_to(target_ref[expert : expert + 1, :], rows.shape)).astype(F32).astype(BF16)


def placement_of(slot_ref, slots):
    rows = lax.broadcasted_iota(jnp.int32, (slots, slot_ref.shape[1]), 0)
    return (rows == jnp.broadcast_to(slot_ref[0:1, :], rows.shape)).astype(F32).astype(BF16)


def grid_of(count):
    lines = 4 if count % 4 == 0 else 1
    return lines, count // lines


def route_slots(routes_ref, chosen_ref, most):
    experts, tokens = chosen_ref.shape
    ids = lax.broadcasted_iota(jnp.int32, (experts, tokens), 0)
    routes = jnp.broadcast_to(routes_ref[0:1, :], ids.shape)
    chosen = (ids == routes).astype(F32)
    chosen_ref[...] = chosen
    earlier = lax.broadcasted_iota(jnp.int32, (tokens, tokens), 0) < lax.broadcasted_iota(
        jnp.int32, (tokens, tokens), 1
    )
    before = dot(chosen.astype(BF16), earlier.astype(F32).astype(BF16))
    rank = jnp.sum(chosen * before, axis=0, keepdims=True).astype(jnp.int32)
    return routes_ref[0:1, :] * most + rank, jnp.sum(chosen, axis=1, keepdims=True)


SOURCE = 2


def plan_start(blocks):
    return SOURCE + blocks + 2


def plan_size(blocks):
    return plan_start(blocks) + 4 + 3 * (blocks + 1)


def write_plan(pairs_ref, plan, me):
    blocks = 2 * pairs_ref.shape[1]
    half = blocks // 2
    own = [pairs_ref[side, me] for side in range(2)]
    plan[0], plan[1] = own[0], own[1]
    plan[SOURCE] = jnp.int32(0)
    plan[SOURCE + blocks + 1] = jnp.int32(0)

    def place(position, carry):
        found = jnp.int32(0)
        for row in range(blocks):
            found = found + jnp.where(pairs_ref[row % 2, row // 2] == position, row, 0)
        plan[SOURCE + 1 + position] = found
        return carry

    lax.fori_loop(0, blocks, place, 0)
    early, late = jnp.minimum(own[0], own[1]), jnp.maximum(own[0], own[1])
    first = jnp.where(own[0] < own[1], 0, 1).astype(jnp.int32)
    start = plan_start(blocks)
    plan[start], plan[start + 1] = first, 1 - first
    plan[start + 2], plan[start + 3] = early, late
    start = start + 4
    for step in range(blocks + 1):
        rest = step - (half + 2)
        if step <= half:
            tile, owner = late - step, jnp.int32(1)
        elif step == half + 1:
            tile, owner = early, jnp.int32(0)
        else:
            tile = jnp.where(rest < early, early - 1 - rest, late - half - 1 - (rest - early))
            owner = jnp.where(rest < early, 0, 1).astype(jnp.int32)
        tile = jnp.minimum(jnp.maximum(tile, 0), blocks - 1)
        plan[start + step] = plan[SOURCE + 1 + tile]
        plan[start + blocks + 1 + step] = owner
        plan[start + 2 * blocks + 2 + step] = plan[SOURCE + blocks - tile]


def project_kernel(
    counts,
    capacity,
    rows_ref,
    wq_ref,
    wk_ref,
    wv_ref,
    wo_ref,
    router_ref,
    gain_a_ref,
    gain_m_ref,
    bias_ref,
    routes_ref,
    pairs_in_ref,
    query_hot_ref,
    key_hot_ref,
    qkv_out,
    weights_out,
    small_out,
    slot_out,
    target_out,
    plan_out,
    query_base_out,
    key_base_out,
    held,
    weights,
    own_small,
    smalls,
    gain,
    pairs_ref,
    ready,
    chosen,
    tallies,
    row_send,
    row_recv,
    weight_send,
    weight_recv,
    tally_send,
    tally_recv,
    out_sems,
    local_sems,
):
    ctx_count, wsh_count = counts
    experts = chosen.shape[0]
    exp_dev = experts // ctx_count
    lanes = experts
    tokens, width = rows_ref.shape
    share = wq_ref.shape[0]
    lines, across = grid_of(ctx_count)
    pairs = wsh_count // 2

    def shard(block):
        return pl.ds(pl.multiple_of(block * share, 16), share)

    def weight_view(place):
        return lambda block: weights.at[place, shard(block), :]

    rows = RowGather(counts, held, (row_send, row_recv))
    mats = LineGather(
        "wsh",
        pairs,
        2,
        [lambda block: smalls.at[block]] + [weight_view(place) for place in range(4)],
        None,
        (weight_send, weight_recv),
    )
    mats.own = [view(mats.me) for view in mats.views]
    own_weights = (wq_ref, wk_ref, wv_ref, wo_ref)
    own_copies = [
        pltpu.make_async_copy(ref, view, local_sems.at[2 + place])
        for place, (ref, view) in enumerate(
            [(rows_ref, held.at[rows.me])]
            + list(zip(own_weights, mats.own[1:]))
        )
    ]
    for copy in own_copies:
        copy.start()
    pairs_copy = pltpu.make_async_copy(pairs_in_ref, pairs_ref, local_sems.at[7])
    pairs_copy.start()
    buckets = bias_ref.shape[0]
    own_small[...] = jnp.zeros_like(own_small)
    own_small[:experts, :share] = router_ref[...].astype(F32)
    own_small[experts : experts + 1, :share] = gain_a_ref[...].astype(F32).reshape(1, share)
    own_small[experts + 1 : experts + 2, :share] = gain_m_ref[...].astype(F32).reshape(1, share)
    own_small[experts + 8 : experts + 8 + buckets, :HEADS] = bias_ref[...].astype(F32)
    smalls[mats.me] = own_small[...].astype(BF16)
    greet(counts)
    own_copies[0].wait()
    rows.begin()
    mats.begin(0)
    for part in range(1, 5):
        own_copies[part].wait()
        if part < 4:
            mats.begin(part)
    most = target_out.shape[1] // ctx_count
    slot, tally = route_slots(routes_ref, chosen, most)
    slot_out[...] = jnp.broadcast_to(slot, slot_out.shape)
    tallies[rows.me] = jnp.broadcast_to(tally, (experts, BLOCK))
    counted = Exchange(
        ctx_count,
        1,
        most,
        (tally_send, tally_recv),
        lambda expert, peer: tallies.at[rows.me],
        lambda expert, peer: tallies.at[peer],
    )
    for ahead in range(1, ctx_count):
        counted.copy(0, ahead, True).start()
    pairs_copy.wait()
    write_plan(pairs_ref, plan_out, rows.me)

    def place_targets():
        counted.wait(0)
        lane = lane_ids(1, ctx_count * most)
        for expert in range(exp_dev):
            offset = jnp.zeros((1, 1), F32)
            target = jnp.full((1, ctx_count * most), capacity, jnp.int32)
            for source in range(ctx_count):
                count = tallies[source, pl.ds(rows.me * exp_dev + expert, 1), 0:1]
                inside = (lane >= source * most) & (
                    lane < source * most + jnp.broadcast_to(count.astype(jnp.int32), lane.shape)
                )
                place = lane - source * most + jnp.broadcast_to(offset.astype(jnp.int32), lane.shape)
                target = jnp.where(inside, place, target)
                offset = offset + count
            target_out[expert : expert + 1, :] = target
        target_out[exp_dev:, :] = jnp.zeros_like(target_out[exp_dev:, :])

    for step in range(lines - 2):
        rows.advance(step)
        if step == 0:
            place_targets()
    for step in range(pairs - 1):
        for part in range(4):
            mats.advance(part, step)
    mats.begin(4)
    for part in range(4):
        mats.wait_cross(part)
    parts = [smalls[block].astype(F32) for block in range(wsh_count)]
    bias_rows = [part[experts + 8 : experts + 8 + buckets, :BLOCK] for part in parts]
    bias_rows = jnp.concatenate(bias_rows, axis=0).astype(BF16)
    turned = jnp.concatenate([part[: experts + 8, :share] for part in parts], axis=1)
    spare = jnp.zeros((BLOCK - turned.shape[0], width), F32)
    turned = jnp.concatenate([turned, spare], axis=0)
    small_out[...] = turned.astype(BF16)
    gain[...] = turned[lanes : lanes + 8, :]
    for hot_ref, base_out, sign in (
        (query_hot_ref, query_base_out, -1),
        (key_hot_ref, key_base_out, 1),
    ):
        table = dot(bias_rows, hot_ref[...], 0, 0)
        lane = lane_ids(BLOCK, SPAN)
        lane = jnp.where(lane < NEAR, lane, lane - SPAN)
        gap = lane if sign > 0 else BLOCK - lane
        last = jnp.max(jnp.where(gap == NEAR - 1, table, -jnp.inf), axis=1, keepdims=True)
        table = jnp.where(gap >= 0, table - last, MASKED)
        for pair in range(PAIRS):
            base_out[pair] = jnp.zeros((8, SPAN), F32)
            base_out[pair, 0:2, :] = table[2 * pair : 2 * pair + 2]
    ahead_of_last = 5 if lines == 4 and across == 2 else 0
    if not ahead_of_last:
        rows.advance(lines - 2)
    column = rows.me % across
    upper = rows.me // across // max(lines // 2, 1)

    def put(slot, block):
        place = pl.ds(pl.multiple_of(block * tokens, tokens), tokens)
        return pltpu.make_async_copy(ready.at[slot], qkv_out.at[place, :], out_sems.at[slot])

    def order(step):
        if ahead_of_last:
            step = jnp.asarray(step)
            step = jnp.where(
                step < 3, step, jnp.where(step < 5, step + 1, jnp.where(step == 5, 3, step))
            )
        ahead, line = step // lines, step % lines
        line = line + upper * (lines - 1 - 2 * line)
        return line, ahead, line * across + (column + across - ahead) % across

    def step_body(step, carry):
        line, ahead, block = order(step)
        slot = step % 2
        for skip in range(1, across):

            @pl.when(ahead == skip)
            def _():
                rows.wait_cross(line, skip)

        @pl.when(step >= 2)
        def _():
            put(slot, order(step - 2)[2]).wait()

        values = held[block].astype(F32)
        inv = lax.rsqrt(jnp.mean(values * values, axis=-1, keepdims=True) + epsilon)
        normed = (values * inv * gain[0:1, :]).astype(BF16)
        for place in range(3):
            ready[slot, :, place * width : (place + 1) * width] = dot(
                normed, weights[place]
            ).astype(BF16)
        put(slot, block).start()
        return carry

    first = ahead_of_last or ctx_count // 2
    lax.fori_loop(0, first, step_body, 0)
    if ahead_of_last:
        rows.advance(lines - 2)
    for step in range(pairs - 1):
        mats.advance(4, step)
    lax.fori_loop(first, ctx_count, step_body, 0)
    mats.wait_cross(4)
    weights_copy = pltpu.make_async_copy(weights, weights_out, local_sems.at[0])
    weights_copy.start()
    for step in (ctx_count - 2, ctx_count - 1):
        put(step % 2, order(step)[2]).wait()
    weights_copy.wait()
    counted.finish(0)
    rows.finish()
    mats.finish()


def project(
    counts, capacity, experts, most, rows, weights, small, routes, pairs, query_hot, key_hot
):
    tokens, width = rows.shape
    ctx_count, wsh_count = counts
    length = tokens * ctx_count
    lines, across = grid_of(ctx_count)
    small_rows = -(-(experts + 8 + small[3].shape[0]) // 16) * 16
    small_lanes = -(-(width // wsh_count) // BLOCK) * BLOCK
    vmem = pl.BlockSpec(memory_space=pltpu.VMEM)
    anywhere = pl.BlockSpec(memory_space=pl.ANY)
    smem = pl.BlockSpec(memory_space=pltpu.SMEM)
    return pl.pallas_call(
        functools.partial(project_kernel, counts, capacity),
        in_specs=[anywhere] * 5 + [vmem] * 5 + [anywhere, vmem, vmem],
        out_specs=[anywhere] * 2 + [vmem] * 3 + [smem] + [vmem] * 2,
        out_shape=[
            jax.ShapeDtypeStruct((length, 3 * width), BF16),
            jax.ShapeDtypeStruct((4, width, width), BF16),
            jax.ShapeDtypeStruct((BLOCK, width), BF16),
            jax.ShapeDtypeStruct((8, tokens), jnp.int32),
            jax.ShapeDtypeStruct((8, ctx_count * most), jnp.int32),
            jax.ShapeDtypeStruct((plan_size(2 * ctx_count),), jnp.int32),
            jax.ShapeDtypeStruct((PAIRS, 8, SPAN), F32),
            jax.ShapeDtypeStruct((PAIRS, 8, SPAN), F32),
        ],
        scratch_shapes=[
            pltpu.VMEM((ctx_count, tokens, width), BF16),
            pltpu.VMEM((4, width, width), BF16),
            pltpu.VMEM((small_rows, small_lanes), F32),
            pltpu.VMEM((wsh_count, small_rows, small_lanes), BF16),
            pltpu.VMEM((8, width), F32),
            pltpu.SMEM(pairs.shape, jnp.int32),
            pltpu.VMEM((2, tokens, 3 * width), BF16),
            pltpu.VMEM((experts, tokens), F32),
            pltpu.VMEM((ctx_count, experts, BLOCK), F32),
            *gather_sems(row_parts(ctx_count, tokens), lines, across),
            *gather_sems(5, wsh_count // 2, 2),
            *exchange_sems(ctx_count, 1),
            pltpu.SemaphoreType.DMA((2,)),
            pltpu.SemaphoreType.DMA((8,)),
        ],
        compiler_params=pltpu.CompilerParams(
            collective_id=0, has_side_effects=True, vmem_limit_bytes=60 << 20
        ),
        name="project",
    )(rows, *weights, *small, routes, pairs, query_hot, key_hot)


def gelu_parts(values):
    slope, cubic = math.sqrt(2 / math.pi), 0.044715
    square = values * values
    bent = jnp.tanh(slope * (values + cubic * values * square))
    outer = 0.5 * (1.0 + bent)
    derivative = outer + 0.5 * values * (1.0 - bent * bent) * slope * (1.0 + 3 * cubic * square)
    return values * outer, derivative


def choose(rows, router, experts, expert):
    logits = dot(rows, router, 1, 1)
    lanes = lane_ids(rows.shape[0], router.shape[0])
    logits = jnp.where(lanes < experts, logits, MASKED)
    weights = jnp.exp(logits - jnp.max(logits, axis=-1, keepdims=True))
    probs = weights / jnp.sum(weights, axis=-1, keepdims=True)
    hot = (lanes == expert).astype(F32)
    return probs, hot, jnp.sum(probs * hot, axis=-1, keepdims=True)


def middle_kernel(
    counts,
    experts,
    spread_here,
    attn_ref,
    exact_ref,
    hidden_ref,
    grad_ref,
    weights_ref,
    w_in_ref,
    w_out_ref,
    small_ref,
    slot_ref,
    target_ref,
    lse_ref,
    routes_ref,
    base_ref,
    plan_ref,
    qkv_ref,
    output_out,
    returned_out,
    resid_out,
    gate_out,
    grad_mid_out,
    grad_heads_out,
    heads_all_out,
    stats_out,
    grad_wo_out,
    grad_router_out,
    grad_gain_out,
    dq_out,
    sums_out,
    grad_in_out,
    grad_out_out,
    qkv,
    lse_all,
    stacked_q,
    stacked_g,
    delta_rep,
    bias,
    near,
    tile_keys,
    scores,
    tops,
    tile_weights,
    tile_values,
    other_values,
    lse_rows,
    own_g,
    early_in,
    attn,
    heads,
    exact_blocks,
    hidden,
    grad,
    wo,
    w_in,
    w_out,
    resid,
    incoming,
    own_x,
    all_x,
    all_g,
    hid,
    du,
    parts,
    from_mate,
    from_far,
    shares,
    mate_shares,
    far_shares,
    returning,
    home,
    branch,
    stats,
    stage_in,
    stage_out,
    heads_stage,
    fetch_sems,
    out_sems,
    heads_sems,
    x_send,
    x_recv,
    g_send,
    g_recv,
    early_send,
    early_recv,
    go_send,
    go_recv,
    back_send,
    back_recv,
    mate_send,
    mate_recv,
    far_send,
    far_recv,
    branch_send,
    branch_recv,
    stat_send,
    stat_recv,
):
    ctx_count, wsh_count = counts
    tokens, width = hidden.shape
    exp_dev, capacity = own_x.shape[:2]
    most = incoming.shape[1] // ctx_count
    lines, across = grid_of(ctx_count)
    pairs = wsh_count // 2
    me = lax.axis_index("ctx")
    home_row = me if spread_here else 0
    sources = [
        (grad_ref, grad),
        (weights_ref.at[3], wo),
        (hidden_ref, hidden),
        (w_in_ref, w_in),
        (w_out_ref, w_out),
    ]
    if spread_here:
        sources.insert(1, (qkv_ref, qkv))
    else:
        sources += [(attn_ref, attn), (exact_ref, exact_blocks)]
    fetches = [
        pltpu.make_async_copy(src, dst, fetch_sems.at[place])
        for place, (src, dst) in enumerate(sources)
    ]
    for fetch in fetches:
        fetch.start()
    views = [
        (lambda buffer, expert: lambda block: buffer.at[expert, block])(buffer, expert)
        for buffer in (all_g, all_x)
        for expert in range(exp_dev)
    ]
    gather_g = LineGather(
        "wsh",
        pairs,
        2,
        views[:exp_dev],
        [own_g.at[expert] for expert in range(exp_dev)],
        (g_send, g_recv),
    )
    gather_x = LineGather(
        "wsh",
        pairs,
        2,
        views[exp_dev:],
        [own_x.at[expert] for expert in range(exp_dev)],
        (x_send, x_recv),
    )
    wsh_me, my_line, my_core = gather_x.me, gather_x.line, gather_x.column
    greet(counts)
    fetches[0].wait()
    returning[1] = dot(placement_of(slot_ref, experts * most), grad[...]).astype(BF16)
    early = Exchange(
        ctx_count,
        exp_dev,
        most,
        (early_send, early_recv),
        lambda expert, peer: returning.at[1, early.rows(peer * exp_dev + expert), :],
        lambda expert, peer: early_in.at[expert, early.rows(peer), :],
    )
    for expert in range(exp_dev):
        early.start(expert)

    def pass_on():
        for expert in range(exp_dev):
            early.wait(expert)
            own_g[expert] = dot(cap_map(target_ref, expert, capacity), early_in[expert]).astype(BF16)
            gather_g.begin(expert)
            all_g[expert, wsh_me] = own_g[expert]

    if spread_here:
        tiles = Tiles(plan_ref, 2 * ctx_count, False)
        fetches[1].wait()

        def attend(pair, carry):
            pair_lanes = pl.ds(pl.multiple_of(pair * BLOCK, BLOCK), BLOCK)

            def load(part, row):
                lanes = pl.ds(pl.multiple_of(part * width + pair * BLOCK, BLOCK), BLOCK)
                return qkv[row, :, lanes]

            near_tiles = near_bias(base_ref, pair)
            bias[...] = jnp.concatenate(
                [near_tiles[:, BLOCK:], near_tiles[:, :BLOCK]], axis=1
            )
            totals = lse_all.at[pair]
            results = forward_pair(
                tiles,
                load,
                bias,
                stacked_q,
                tile_keys,
                scores,
                tops,
                totals,
                tile_weights,
                tile_values,
                other_values,
            )
            main = in_order(tiles, [result[0] for result in results])
            whole = in_order(tiles, [result[1] for result in results])
            lse = in_order(tiles, [totals[0], totals[1]])
            for own in range(2):
                rows = pl.ds(own * BLOCK, BLOCK)
                attn[rows, pair_lanes] = main[own]
                exact_blocks[own, :, pair_lanes] = whole[own]
                turned = jnp.transpose(lse[own])
                for head in range(2):
                    lse_rows[own, pair, head : head + 1, :] = turned[
                        :1, head * BLOCK : (head + 1) * BLOCK
                    ]
                lse_rows[own, pair, 2:8, :] = jnp.zeros((6, BLOCK), F32)
            return carry

        lax.fori_loop(0, PAIRS, attend, 0)
    else:
        lse_rows[...] = lse_ref[...]

    gain_two = small_ref[...].astype(F32)[experts + 1 : experts + 2, :]
    row_ids = lax.broadcasted_iota(jnp.int32, (BLOCK, width), 0)
    router = jnp.where(row_ids < experts, small_ref[...], jnp.zeros((BLOCK, width), BF16))
    for fetch in fetches[2 if spread_here else 1 :]:
        fetch.wait()
    resid[...] = hidden[...].astype(F32) + dot(attn[...], wo[...])
    inv_two = lax.rsqrt(jnp.mean(resid[...] * resid[...], axis=-1, keepdims=True) + epsilon)
    normed_two = (resid[...] * inv_two * gain_two).astype(BF16)
    units = w_in.shape[2]
    placement = placement_of(slot_ref, experts * most)
    returning[0] = dot(placement, normed_two).astype(BF16)
    forth = Exchange(
        ctx_count,
        exp_dev,
        most,
        (go_send, go_recv),
        lambda expert, peer: returning.at[0, forth.rows(peer * exp_dev + expert), :],
        lambda expert, peer: incoming.at[expert, forth.rows(peer), :],
    )
    forth.start(0)
    routed = jnp.broadcast_to(routes_ref[...].astype(F32), (BLOCK, tokens))
    routed = jnp.transpose(routed)[:, :1].astype(jnp.int32)
    gate = choose(normed_two, router, experts, routed)[2]
    pass_on()

    summed = (parts.at[0], parts.at[1], shares)
    mate_parts = (from_mate.at[0], from_mate.at[1], mate_shares)
    far_parts = (from_far.at[0], from_far.at[1], far_shares)

    def mate_copy(array, expert, line):
        mine = line * 2 + 1 - my_core
        return pltpu.make_async_remote_copy(
            src_ref=summed[array].at[expert, mine],
            dst_ref=mate_parts[array].at[expert, line],
            send_sem=mate_send.at[array, expert, line],
            recv_sem=mate_recv.at[array, expert, line],
            device_id={"wsh": my_line * 2 + 1 - my_core},
            device_id_type=pl.DeviceIdType.MESH,
        )

    def far_copy(array, expert, ahead):
        line = (my_line + ahead) % pairs
        return pltpu.make_async_remote_copy(
            src_ref=summed[array].at[expert, line * 2 + my_core],
            dst_ref=far_parts[array].at[expert, ahead - 1],
            send_sem=far_send.at[array, expert, ahead - 1],
            recv_sem=far_recv.at[array, expert, ahead - 1],
            device_id={"wsh": line * 2 + my_core},
            device_id_type=pl.DeviceIdType.MESH,
        )

    def work(expert, ahead):
        line = (my_line + ahead) % pairs
        both = pl.ds(line * 2, 2)
        gather_x.cross_recv(expert, line, 1).wait_recv()
        gather_g.cross_recv(expert, line, 1).wait_recv()
        rows = all_x[expert, both].reshape(2 * capacity, width)
        active, slope = gelu_parts(dot(rows, w_in[expert]))
        active = active.astype(BF16)
        hid[expert, both] = active.reshape(2, capacity, units)
        share = choose(rows, router, experts, exp_dev * me + expert)[2]
        grads = all_g[expert, both].reshape(2 * capacity, width).astype(F32)
        grads = (share * grads).astype(BF16)
        all_g[expert, both] = grads.reshape(2, capacity, width)
        push = dot(grads, w_out[expert], 1, 1)
        product = jnp.sum(push * active.astype(F32), axis=-1, keepdims=True)
        product = jnp.transpose(jnp.broadcast_to(product, (2 * capacity, BLOCK)))
        for core in range(2):
            shares[expert, line * 2 + core] = product[:8, core * capacity : (core + 1) * capacity]
        mate_copy(2, expert, line).start()
        grad_u = (push * slope).astype(BF16)
        du[expert, both] = grad_u.reshape(2, capacity, units)
        part = dot(grad_u, w_in[expert], 1, 1).astype(BF16)
        parts[1, expert, both] = part.reshape(2, capacity, width)
        mate_copy(1, expert, line).start()
        part = dot(active, w_out[expert]).astype(BF16)
        parts[0, expert, both] = part.reshape(2, capacity, width)
        mate_copy(0, expert, line).start()

    def fold(array, expert, ahead):
        line = (my_line + ahead) % pairs
        mate_copy(array, expert, line).wait_recv()
        both = summed[array][expert, line * 2 + my_core].astype(F32) + mate_parts[array][
            expert, line
        ].astype(F32)
        summed[array][expert, line * 2 + my_core] = both.astype(summed[array].dtype)
        far_copy(array, expert, ahead).start()

    def whole(array, expert):
        mate_copy(array, expert, my_line).wait_recv()
        total = summed[array][expert, my_line * 2 + my_core].astype(F32) + mate_parts[array][
            expert, my_line
        ].astype(F32)
        for ahead in range(1, pairs):
            far_copy(array, expert, ahead).wait_recv()
            total = total + far_parts[array][expert, ahead - 1].astype(F32)
        return total

    back = [
        Exchange(
            ctx_count,
            exp_dev,
            most,
            (back_send.at[array], back_recv.at[array]),
            (
                lambda array: lambda expert, peer: returning.at[
                    array, forth.rows(expert * ctx_count + peer), :
                ]
            )(array),
            (
                lambda array: lambda expert, peer: home.at[
                    array, forth.rows(peer * exp_dev + expert), :
                ]
            )(array),
        )
        for array in range(2)
    ]

    def settle(expert):
        expert_rows = pl.ds(expert * ctx_count * most, ctx_count * most)
        rows = own_x[expert]
        probs, hot, share = choose(rows, router, experts, exp_dev * me + expert)
        product = jnp.transpose(whole(2, expert))[:, :1]
        grad_logits = (product * (hot - probs)).astype(BF16)
        grad_rows = whole(1, expert).astype(BF16).astype(F32) + dot(grad_logits, router)
        spread = cap_map(target_ref, expert, capacity)
        returning[1, expert_rows] = dot(spread, grad_rows.astype(BF16), 0, 0).astype(BF16)
        back[1].start(expert)
        router_part = dot(grad_logits, rows, 0, 0)[:experts]
        if expert == 0:
            grad_router_out[...] = router_part
        else:
            grad_router_out[...] += router_part

    for expert in range(exp_dev):
        early.finish(expert)
    for expert in range(exp_dev):
        forth.wait(expert)
        if expert + 1 < exp_dev:
            forth.start(expert + 1)
        own_x[expert] = dot(cap_map(target_ref, expert, capacity), incoming[expert]).astype(BF16)
        gather_x.begin(expert)
        all_x[expert, wsh_me] = own_x[expert]
        for step in range(pairs - 1):
            gather_g.advance(expert, step)
        gather_g.finish_part(expert)
        work(expert, 0)
        if expert:
            settle(expert - 1)
        for step in range(pairs - 1):
            gather_x.advance(expert, step)

        def others(ahead, carry):
            work(expert, ahead)
            return carry

        if pairs == 2:
            work(expert, 1)
        else:
            lax.fori_loop(1, pairs, others, 0)
        for ahead in range(1, pairs):
            fold(2, expert, ahead)
            fold(1, expert, ahead)
    settle(exp_dev - 1)
    for expert in range(exp_dev):
        forth.finish(expert)
        for ahead in range(1, pairs):
            fold(0, expert, ahead)

    def in_copy(expert):
        return pltpu.make_async_copy(stage_in, grad_in_out.at[expert], out_sems.at[1])

    one_stage = units == width
    out_stage = stage_in if one_stage else stage_out

    def out_copy(expert):
        return pltpu.make_async_copy(out_stage, grad_out_out.at[expert], out_sems.at[0])

    group = min(wsh_count, 4)

    def slot_sum(stage, left, right, expert):
        def part(turn):
            blocks = pl.ds(turn * group, group)
            return dot(
                left[expert, blocks].reshape(group * capacity, left.shape[3]),
                right[expert, blocks].reshape(group * capacity, right.shape[3]),
                0,
                0,
            )

        stage[...] = part(0).astype(stage.dtype)
        if wsh_count > group:

            def add(turn, carry):
                stage[...] += part(turn)
                return carry

            lax.fori_loop(1, wsh_count // group, add, 0)

    def grads_of(expert):
        if expert:
            (in_copy if one_stage else out_copy)(expert - 1).wait()
        slot_sum(out_stage, hid, all_g, expert)
        out_copy(expert).start()
        if one_stage:
            out_copy(expert).wait()
        elif expert:
            in_copy(expert - 1).wait()
        slot_sum(stage_in, all_x, du, expert)
        in_copy(expert).start()

    for expert in range(exp_dev):
        grads_of(expert)
        expert_rows = pl.ds(expert * ctx_count * most, ctx_count * most)
        spread = cap_map(target_ref, expert, capacity)
        out_rows = whole(0, expert).astype(BF16)
        returning[0, expert_rows] = dot(spread, out_rows, 0, 0).astype(BF16)
    grad_up = grad[...].astype(F32)
    for expert in range(exp_dev):
        back[1].wait(expert)
    grad_normed = dot(placement_of(slot_ref, experts * most), home[1], 0, 0)
    scaled = grad_normed * gain_two
    mean = jnp.mean(scaled * resid[...], axis=-1, keepdims=True)
    gain_part = jnp.sum(grad_normed * resid[...] * inv_two, axis=0, keepdims=True)
    grad_gain_out[...] = jnp.broadcast_to(gain_part, grad_gain_out.shape)
    grad_mid = grad_up + inv_two * scaled - resid[...] * inv_two * inv_two * inv_two * mean
    grad_mid_out[...] = grad_mid
    branch[home_row] = grad_mid.astype(BF16)

    if spread_here:
        gather_d = RowGather(counts, branch, (branch_send, branch_recv))
        gather_s = LineGather(
            "ctx",
            lines,
            across,
            [lambda block: stats.at[block]],
            [stats.at[me]],
            (stat_send, stat_recv),
        )
        gather_d.begin()
    if spread_here:
        returned_out[...] = returning[0]
        resid_out[...] = resid[...]
        gate_out[...] = jnp.broadcast_to(gate, gate_out.shape)
    else:
        for expert in range(exp_dev):
            back[0].start(expert)
    grad_heads = dot(branch[home_row], wo[...], 1, 1).astype(BF16)
    grad_heads_out[...] = grad_heads
    if spread_here:
        for own in range(2):
            heads[own] = grad_heads[own * BLOCK : (own + 1) * BLOCK]
    product = grad_heads.astype(F32) * exact_blocks[...].reshape(tokens, width)
    head_of = lax.broadcasted_iota(jnp.int32, (width, BLOCK), 0) // HEAD_DIM
    head_hot = (head_of == lane_ids(width, BLOCK)).astype(F32)
    delta = jnp.transpose(
        lax.dot_general(
            product, head_hot, (((1,), (0,)), ((), ())), precision=HIGH, preferred_element_type=F32
        )
    )
    for pair in range(PAIRS):
        for own in range(2):
            stats[home_row, own, pair] = lse_rows[own, pair]
            stats[home_row, own, pair, 2:4, :] = delta[
                2 * pair : 2 * pair + 2, own * BLOCK : (own + 1) * BLOCK
            ]
    if spread_here:
        gather_s.begin(0)

    grad_wo_out[...] = dot(attn[...], branch[home_row], 0, 0).astype(BF16)

    plan_from = plan_start(2 * ctx_count)
    half = ctx_count

    def query_pair(pair, carry):
        pair_lanes = pl.ds(pl.multiple_of(pair * BLOCK, BLOCK), BLOCK)

        def tile(part, step):
            lanes = pl.ds(pl.multiple_of(part * width + pair * BLOCK, BLOCK), BLOCK)
            return qkv[plan_ref[plan_from + 4 + step], :, lanes]

        bias[...] = near_bias(base_ref, pair)
        for place in range(2):
            own = plan_ref[plan_from + place]
            stacked_q[place] = stack_heads(tile(0, 0 if place else half + 1))
            grads = stack_heads(heads[own, :, pair_lanes])
            stacked_g[place] = grads
            own_exact = exact_blocks[own, :, pair_lanes]
            product = grads.astype(F32) * jnp.concatenate([own_exact, own_exact], axis=0)
            delta_rep[place] = jnp.broadcast_to(
                jnp.sum(product, axis=-1, keepdims=True), (2 * BLOCK, BLOCK)
            )

        def score_grads(place, step, extra):
            keys = tile(1, step)
            part = dot(stacked_q[place], keys, 1, 1)
            if extra is not None:
                part = part + extra
            weights = jnp.exp(part - lse_all[pair, place])
            grad_s = weights * (dot(stacked_g[place], tile(2, step), 1, 1) - delta_rep[place])
            return grad_s, dot(grad_s.astype(BF16), keys)

        diagonal, big = score_grads(1, 0, bias[:, BLOCK:])
        beside, more = score_grads(1, 1, bias[:, :BLOCK])
        big = big + more
        far = jnp.zeros((2 * BLOCK, BLOCK), F32)
        for step in range(2, half + 1):
            grad_s, more = score_grads(1, step, None)
            far, big = far + grad_s, big + more
        grad_s, small_part = score_grads(0, half + 1, bias[:, BLOCK:])
        near[:, BLOCK:] = diagonal + grad_s
        for step in range(half + 2, 2 * half + 1):
            place = plan_ref[plan_from + 4 + 2 * half + 1 + step]
            later = place.astype(F32)
            sooner = 1.0 - later
            extra = None
            if step == half + 2:
                extra = bias[:, :BLOCK] * sooner
            grad_s, more = score_grads(place, step, extra)
            if step == half + 2:
                near[:, :BLOCK] = beside + grad_s * sooner
                far = far + grad_s * later
            else:
                far = far + grad_s
            big = big + more * later
            small_part = small_part + more * sooner
        second = plan_ref[plan_from].astype(F32)
        small_part, big = merge_heads(small_part), merge_heads(big)
        first = 1.0 - second
        dq_out[:BLOCK, pair_lanes] = (small_part * first + big * second).astype(BF16)
        dq_out[BLOCK:, pair_lanes] = (big * first + small_part * second).astype(BF16)
        put_sums(sums_out, pair, near, far)
        return carry

    def query_pairs(turn):
        share = PAIRS // (lines - 1)
        lax.fori_loop(turn * share, (turn + 1) * share, query_pair, 0)

    if spread_here:
        for step in range(lines - 1):
            query_pairs(step)
            gather_d.advance(step)
            gather_s.advance(0, step)
    if not spread_here:
        for expert in range(exp_dev):
            back[0].wait(expert)
        token_out = dot(placement_of(slot_ref, experts * most), home[0], 0, 0)
        output_out[...] = (resid[...] + gate * token_out).astype(BF16)
    column = me % across
    upper = me // across // max(lines // 2, 1)

    def order(step):
        ahead, line = step // lines, step % lines
        line = line + upper * (lines - 1 - 2 * line)
        return line, ahead, line * across + (column + across - ahead) % across

    def put(slot, block):
        place = pl.ds(pl.multiple_of(block * tokens, tokens), tokens)
        return pltpu.make_async_copy(
            heads_stage.at[slot], heads_all_out.at[place, :], heads_sems.at[slot]
        )

    def heads_step(step, carry):
        line, ahead, block = order(step)
        slot = step % 2
        for skip in range(1, across):

            @pl.when(ahead == skip)
            def _():
                gather_d.wait_cross(line, skip)
                gather_s.cross_recv(0, line, skip).wait_recv()

        @pl.when(step >= 2)
        def _():
            put(slot, order(step - 2)[2]).wait()

        heads_stage[slot] = dot(branch[block], wo[...], 1, 1).astype(BF16)
        put(slot, block).start()
        return carry

    if spread_here:
        lax.fori_loop(0, ctx_count, heads_step, 0)
    stats_copy = pltpu.make_async_copy(stats, stats_out, fetch_sems.at[0])
    stats_copy.start()
    if spread_here:
        for step in (ctx_count - 2, ctx_count - 1):
            put(step % 2, order(step)[2]).wait()
    else:
        heads_stage[0] = branch[0]
        own_branch = pltpu.make_async_copy(heads_stage.at[0], heads_all_out, heads_sems.at[0])
        own_branch.start()
        own_branch.wait()
    if not one_stage:
        out_copy(exp_dev - 1).wait()
    in_copy(exp_dev - 1).wait()
    stats_copy.wait()
    for expert in range(exp_dev):
        for array in range(1 if spread_here else 0, 2):
            back[array].finish(expert)
        for array in range(3):
            for line in range(pairs):
                mate_copy(array, expert, line).wait_send()
            for ahead in range(1, pairs):
                far_copy(array, expert, ahead).wait_send()
    gather_x.finish()
    if spread_here:
        gather_d.finish()
        gather_s.finish()


def middle(
    counts,
    experts,
    attn,
    exact,
    hidden,
    grad,
    weights,
    w_in,
    w_out,
    small,
    slots,
    targets,
    lse_rows,
    routes,
    base,
    plan,
    qkv,
    capacity,
):
    ctx_count, wsh_count = counts
    tokens, width = hidden.shape
    exp_dev = w_in.shape[0]
    units = w_in.shape[2]
    slot_count = targets.shape[1]
    all_slots = experts * (slot_count // ctx_count)
    lines, across = grid_of(ctx_count)
    pairs = wsh_count // 2
    vmem = pl.BlockSpec(memory_space=pltpu.VMEM)
    anywhere = pl.BlockSpec(memory_space=pl.ANY)
    slot_rows = (exp_dev, wsh_count, capacity)
    spread_here = wsh_count <= 4
    held = ctx_count if spread_here else 1
    kept = BF16 if spread_here else F32
    score_rows = NEAR if spread_here else 16
    forward = forward_scratch(2 * ctx_count) if spread_here else [pltpu.VMEM((8, BLOCK), F32)] * 8
    return pl.pallas_call(
        functools.partial(middle_kernel, counts, experts, spread_here),
        in_specs=[anywhere] * 7
        + [vmem] * 6
        + [pl.BlockSpec(memory_space=pltpu.SMEM), anywhere],
        out_specs=[vmem] * 6 + [anywhere] * 2 + [vmem] * 5 + [anywhere] * 2,
        out_shape=[
            jax.ShapeDtypeStruct((16 if spread_here else tokens, width), BF16),
            jax.ShapeDtypeStruct((all_slots if spread_here else 16, width), BF16),
            jax.ShapeDtypeStruct((tokens if spread_here else 8, width), F32),
            jax.ShapeDtypeStruct((tokens, BLOCK), F32),
            jax.ShapeDtypeStruct((tokens, width), F32),
            jax.ShapeDtypeStruct((tokens, width), BF16),
            jax.ShapeDtypeStruct((tokens * held, width), BF16),
            jax.ShapeDtypeStruct((held, 2, PAIRS, 8, BLOCK), F32),
            jax.ShapeDtypeStruct((width, width), BF16),
            jax.ShapeDtypeStruct((experts, width), F32),
            jax.ShapeDtypeStruct((8, width), F32),
            jax.ShapeDtypeStruct((tokens if spread_here else 16, width), BF16),
            jax.ShapeDtypeStruct((PAIRS, 8, SPAN), F32),
            jax.ShapeDtypeStruct((exp_dev, width, units), kept),
            jax.ShapeDtypeStruct((exp_dev, units, width), kept),
        ],
        scratch_shapes=[
            pltpu.VMEM(qkv.shape if spread_here else (1, 16, BLOCK), BF16),
            pltpu.VMEM((PAIRS, 2, NEAR, BLOCK) if spread_here else (1, 2, 8, BLOCK), F32),
            pltpu.VMEM((2, score_rows, BLOCK), BF16),
            pltpu.VMEM((2, score_rows, BLOCK), BF16),
            pltpu.VMEM((2, score_rows, BLOCK), F32),
            pltpu.VMEM((score_rows, NEAR), F32),
            pltpu.VMEM((score_rows, NEAR), F32),
            *forward[1:4],
            *forward[5:],
            pltpu.VMEM((2, PAIRS, 8, BLOCK), F32),
            pltpu.VMEM((exp_dev, capacity, width), BF16),
            pltpu.VMEM((exp_dev, slot_count, width), BF16),
            pltpu.VMEM((tokens, width), BF16),
            pltpu.VMEM((2, BLOCK if spread_here else 16, width), BF16),
            pltpu.VMEM((2, BLOCK, width), F32),
            pltpu.VMEM((tokens, width), BF16),
            pltpu.VMEM((tokens, width), BF16),
            pltpu.VMEM((width, width), BF16),
            pltpu.VMEM(w_in.shape, BF16),
            pltpu.VMEM(w_out.shape, BF16),
            pltpu.VMEM((tokens, width), F32),
            pltpu.VMEM((exp_dev, slot_count, width), BF16),
            pltpu.VMEM((exp_dev, capacity, width), BF16),
            pltpu.VMEM((*slot_rows, width), BF16),
            pltpu.VMEM((*slot_rows, width), BF16),
            pltpu.VMEM((*slot_rows, units), BF16),
            pltpu.VMEM((*slot_rows, units), BF16),
            pltpu.VMEM((2, *slot_rows, width), BF16),
            pltpu.VMEM((2, exp_dev, pairs, capacity, width), BF16),
            pltpu.VMEM((2, exp_dev, max(pairs - 1, 1), capacity, width), BF16),
            pltpu.VMEM((exp_dev, wsh_count, 8, capacity), F32),
            pltpu.VMEM((exp_dev, pairs, 8, capacity), F32),
            pltpu.VMEM((exp_dev, max(pairs - 1, 1), 8, capacity), F32),
            pltpu.VMEM((2, all_slots, width), BF16),
            pltpu.VMEM((2, all_slots, width), BF16),
            pltpu.VMEM((held, tokens, width), BF16),
            pltpu.VMEM((held, 2, PAIRS, 8, BLOCK), F32),
            pltpu.VMEM((width, units), kept),
            pltpu.VMEM((16, BLOCK) if units == width else (units, width), kept),
            pltpu.VMEM((2, tokens, width), BF16),
            pltpu.SemaphoreType.DMA((9,)),
            pltpu.SemaphoreType.DMA((2,)),
            pltpu.SemaphoreType.DMA((2,)),
            *gather_sems(exp_dev, pairs, 2),
            *gather_sems(exp_dev, pairs, 2),
            *exchange_sems(ctx_count, exp_dev),
            *exchange_sems(ctx_count, exp_dev),
            pltpu.SemaphoreType.DMA((2, exp_dev, ctx_count - 1)),
            pltpu.SemaphoreType.DMA((2, exp_dev, ctx_count - 1)),
            pltpu.SemaphoreType.DMA((3, exp_dev, pairs)),
            pltpu.SemaphoreType.DMA((3, exp_dev, pairs)),
            pltpu.SemaphoreType.DMA((3, exp_dev, max(pairs - 1, 1))),
            pltpu.SemaphoreType.DMA((3, exp_dev, max(pairs - 1, 1))),
            *gather_sems(row_parts(ctx_count, tokens), lines, across),
            *gather_sems(1, lines, across),
        ],
        compiler_params=pltpu.CompilerParams(
            collective_id=1, has_side_effects=True, vmem_limit_bytes=(62 if spread_here else 63) << 20
        ),
        name="middle",
    )(
        attn,
        exact,
        hidden,
        grad,
        weights,
        w_in,
        w_out,
        small,
        slots,
        targets,
        lse_rows,
        routes,
        base,
        plan,
        qkv,
    )


class Tiles:
    def __init__(self, plan_ref, blocks, keys):
        self.plan, self.blocks, self.half = plan_ref, blocks, blocks // 2
        self.start = plan_start(blocks)
        self.rows_from = self.start + 4 + (2 * (blocks + 1) if keys else 0)
        self.keys = keys
        self.count = blocks + 1

    def own(self, place):
        return self.plan[self.start + (1 - place if self.keys else place)]

    def own_step(self, place):
        return 0 if place else self.half + 1

    def row(self, step):
        return self.plan[self.rows_from + step]

    def place(self, step):
        if step <= self.half:
            return 1
        if step == self.half + 1:
            return 0
        return self.plan[self.start + 4 + self.blocks + 1 + step]

    def groups(self):
        found, step = [], 0
        while step <= self.half:
            size = 2 if step + 1 <= self.half else 1
            found.append((step, size))
            step += size
        return found + [(step, 1) for step in range(self.half + 1, self.count)]


def span(step, size=1):
    return slice(step * BLOCK, (step + size) * BLOCK)


def share_of(place, wanted):
    return place.astype(F32) if wanted else 1.0 - place.astype(F32)


def only(place, wanted, value):
    if isinstance(place, int):
        return value if place == wanted else jnp.zeros_like(value)
    return value * share_of(place, wanted).astype(value.dtype)


def order_bias(bias, step, size, place, half):
    if step == 0:
        return bias[:, : size * BLOCK]
    if step == half + 1:
        return bias[:, :BLOCK]
    if step == half + 2:
        return bias[:, BLOCK:] * share_of(place, 0)
    return None


def forward_pair(tiles, load, bias, stacked, keys, scores, tops, totals, weights, values, others):
    half, count = tiles.half, tiles.count
    lowest = jnp.full((NEAR, BLOCK), MASKED, F32)
    for place in range(2):
        stacked[place] = stack_heads(load(0, tiles.row(tiles.own_step(place))))
    for step in range(count):
        row = tiles.row(step)
        keys[span(step), :] = load(1, row)
        tile, place = load(2, row), tiles.place(step)
        values[span(step), :] = only(place, 1, tile)
        if step > half:
            others[span(step - half - 1), :] = only(place, 0, tile)
    best = [lowest, lowest]
    for step, size in tiles.groups():
        place = tiles.place(step)
        part = dot(stacked[place], keys[span(step, size), :], 1, 1)
        extra = order_bias(bias, step, size, place, half)
        if extra is not None:
            part = part + extra
        scores[:, span(step, size)] = part
        part = fold_lanes(part, jnp.maximum) if size == 2 else part
        for wanted in range(2):
            if isinstance(place, int):
                if place == wanted:
                    best[wanted] = jnp.maximum(best[wanted], part)
            else:
                share = share_of(place, wanted)
                best[wanted] = jnp.maximum(best[wanted], part * share + MASKED * (1.0 - share))
    for wanted in range(2):
        top = jnp.max(best[wanted], axis=-1, keepdims=True)
        tops[wanted] = jnp.broadcast_to(top, (NEAR, BLOCK))
    total = [jnp.zeros((NEAR, BLOCK), F32)] * 2
    for step in range(count):
        place = tiles.place(step)
        part = jnp.exp(scores[:, span(step)] - tops[place])
        high = part.astype(BF16)
        weights[:NEAR, span(step)] = high
        weights[NEAR:, span(step)] = (part - high.astype(F32)).astype(BF16)
        for wanted in range(2):
            if not isinstance(place, int) or place == wanted:
                total[wanted] = total[wanted] + only(place, wanted, part)
    results = []
    for wanted in range(2):
        whole = jnp.sum(total[wanted], axis=-1, keepdims=True)
        if wanted:
            summed = dot(weights[...], values[...])
        else:
            summed = dot(weights[:, span(half + 1, count - half - 1)], others[...])
        main = summed[:NEAR] / whole
        exact = main + summed[NEAR:] / whole
        totals[wanted] = tops[wanted] + jnp.log(jnp.broadcast_to(whole, (NEAR, BLOCK)))
        results.append((merge_heads(main).astype(BF16), merge_heads(exact)))
    return results


def in_order(tiles, pair):
    kind = pair[0].dtype
    second = tiles.own(0).astype(F32)
    first, second = (1.0 - second).astype(kind), second.astype(kind)
    return pair[0] * first + pair[1] * second, pair[1] * first + pair[0] * second


def forward_kernel(
    plan_ref, q_ref, k_ref, v_ref, base_ref, out_ref, exact_ref, lse_ref, row_ref, bias, *scratch
):
    blocks = q_ref.shape[0] // BLOCK
    tiles = Tiles(plan_ref, blocks, False)
    refs = (q_ref, k_ref, v_ref)
    near = near_bias(base_ref)
    bias[...] = jnp.concatenate([near[:, BLOCK:], near[:, :BLOCK]], axis=1)
    totals = scratch[4]

    def load(part, row):
        return refs[part][rows_at(row), :]

    results = forward_pair(tiles, load, bias, *scratch)
    main = in_order(tiles, [result[0] for result in results])
    exact = in_order(tiles, [result[1] for result in results])
    lse = in_order(tiles, [totals[0], totals[1]])
    for own in range(2):
        rows = pl.ds(own * BLOCK, BLOCK)
        out_ref[rows, :] = main[own]
        exact_ref[rows, :] = exact[own]
        lse_ref[0, own] = lse[own]
        turned = jnp.transpose(lse[own])
        for head in range(2):
            row_ref[own, 0, head : head + 1, :] = turned[:1, head * BLOCK : (head + 1) * BLOCK]
        row_ref[own, 0, 2:8, :] = jnp.zeros((6, BLOCK), F32)


def forward_scratch(blocks):
    count = blocks + 1
    rest = count - blocks // 2 - 1
    return [
        pltpu.VMEM((2, NEAR, BLOCK), BF16),
        pltpu.VMEM((count * BLOCK, BLOCK), BF16),
        pltpu.VMEM((NEAR, count * BLOCK), F32),
        pltpu.VMEM((2, NEAR, BLOCK), F32),
        pltpu.VMEM((2, NEAR, BLOCK), F32),
        pltpu.VMEM((2 * NEAR, count * BLOCK), BF16),
        pltpu.VMEM((count * BLOCK, BLOCK), BF16),
        pltpu.VMEM((rest * BLOCK, BLOCK), BF16),
    ]


def pair_specs(rows, width):
    pairs = width // BLOCK

    def column(offset):
        return pl.BlockSpec((rows, BLOCK), lambda pair, plan: (0, offset + pair))

    return [column(0), column(pairs), column(2 * pairs)]


def attend_forward(plan, qkv, base, width):
    rows = qkv.shape[0]
    own = pl.BlockSpec((NEAR, BLOCK), lambda pair, plan: (0, pair))
    return pl.pallas_call(
        forward_kernel,
        grid_spec=pltpu.PrefetchScalarGridSpec(
            num_scalar_prefetch=1,
            grid=(PAIRS,),
            in_specs=pair_specs(rows, width)
            + [pl.BlockSpec((1, 8, SPAN), lambda pair, plan: (pair, 0, 0))],
            out_specs=[
                own,
                own,
                pl.BlockSpec((1, 2, NEAR, BLOCK), lambda pair, plan: (pair, 0, 0, 0)),
                pl.BlockSpec((2, 1, 8, BLOCK), lambda pair, plan: (0, pair, 0, 0)),
            ],
            scratch_shapes=[pltpu.VMEM((NEAR, NEAR), F32), *forward_scratch(rows // BLOCK)],
        ),
        out_shape=[
            jax.ShapeDtypeStruct((NEAR, width), BF16),
            jax.ShapeDtypeStruct((NEAR, width), F32),
            jax.ShapeDtypeStruct((PAIRS, 2, NEAR, BLOCK), F32),
            jax.ShapeDtypeStruct((2, PAIRS, 8, BLOCK), F32),
        ],
        compiler_params=pltpu.CompilerParams(vmem_limit_bytes=60 << 20),
        name="attend_forward",
    )(plan, qkv, qkv, qkv, base)


def put_sums(sums_ref, place, near_ref, far):
    row_ids = lax.broadcasted_iota(jnp.int32, (BLOCK, SPAN), 0)
    for head in range(2):
        part = near_ref[head * BLOCK : (head + 1) * BLOCK, :]
        part = jnp.concatenate([part, jnp.zeros((BLOCK, BLOCK), F32)], axis=1)
        for bit in range(BLOCK.bit_length() - 1):
            moved = pltpu.roll(part, SPAN - (1 << bit), 1)
            part = jnp.where((row_ids >> bit) & 1 == 1, moved, part)
        sums_ref[place, head : head + 1, :] = jnp.sum(part, axis=0, keepdims=True)
        far_part = jnp.sum(far[head * BLOCK : (head + 1) * BLOCK], axis=0, keepdims=True)
        sums_ref[place, 2 + head : 3 + head, :] = jnp.concatenate(
            [far_part, jnp.zeros((1, NEAR), F32)], axis=1
        )
    sums_ref[place, 4:8, :] = jnp.zeros((4, SPAN), F32)


def query_kernel(
    plan_ref, q_ref, k_ref, v_ref, base_ref, do_ref, exact_ref, lse_ref, dq_ref, sums_ref, bias_ref, near_ref
):
    bias_ref[...] = near_bias(base_ref)
    lanes = lane_ids(2 * BLOCK, NEAR)
    far = jnp.zeros((2 * BLOCK, BLOCK), F32)
    for own in range(2):
        block = plan_ref[own]
        rows = pl.ds(own * BLOCK, BLOCK)
        stacked = stack_heads(q_ref[rows_at(plan_ref[SOURCE + 1 + block]), :])
        grads = stack_heads(do_ref[rows, :])
        exact = exact_ref[rows, :]
        product = grads.astype(F32) * jnp.concatenate([exact, exact], axis=0)
        delta = jnp.sum(product, axis=-1, keepdims=True)
        lse = lse_ref[0, own][:, :1]

        def grad_scores(scores, start):
            weights = jnp.exp(scores - lse)
            return weights * (dot(grads, two_tiles(v_ref, plan_ref, start), 1, 1) - delta)

        scores = dot(stacked, two_tiles(k_ref, plan_ref, block), 1, 1) + bias_ref[...]
        scores = jnp.where(lanes + block * BLOCK < BLOCK, MASKED, scores)
        near = grad_scores(scores, block)
        if own == 0:
            near_ref[...] = near
        else:
            near_ref[...] += near

        def step(chunk, carry):
            grad_q, far = carry
            start = block - 2 * chunk
            keys = two_tiles(k_ref, plan_ref, start)
            part = dot(stacked, keys, 1, 1)
            part = jnp.where(lanes + start * BLOCK < BLOCK, MASKED, part)
            grad_s = grad_scores(part, start)
            return (grad_q + dot(grad_s.astype(BF16), keys), far + fold_lanes(grad_s, jnp.add))

        grad_q, far = lax.fori_loop(
            1,
            jnp.maximum(block, 1) // 2 + 1,
            step,
            (dot(near.astype(BF16), two_tiles(k_ref, plan_ref, block)), far),
        )
        dq_ref[rows, :] = merge_heads(grad_q).astype(BF16)
    put_sums(sums_ref, 0, near_ref, far)


def attend_queries(plan, qkv, base, grad_out, exact, lse):
    rows, width = qkv.shape[0], grad_out.shape[1]
    own = pl.BlockSpec((NEAR, BLOCK), lambda pair, plan: (0, pair))
    row_spec = pl.BlockSpec((1, 8, SPAN), lambda pair, plan: (pair, 0, 0))
    return pl.pallas_call(
        query_kernel,
        grid_spec=pltpu.PrefetchScalarGridSpec(
            num_scalar_prefetch=1,
            grid=(PAIRS,),
            in_specs=pair_specs(rows, width)
            + [
                row_spec,
                own,
                own,
                pl.BlockSpec((1, 2, NEAR, BLOCK), lambda pair, plan: (pair, 0, 0, 0)),
            ],
            out_specs=[own, row_spec],
            scratch_shapes=[pltpu.VMEM((NEAR, NEAR), F32), pltpu.VMEM((NEAR, NEAR), F32)],
        ),
        out_shape=[
            jax.ShapeDtypeStruct((NEAR, width), BF16),
            jax.ShapeDtypeStruct((PAIRS, 8, SPAN), F32),
        ],
        compiler_params=pltpu.CompilerParams(vmem_limit_bytes=60 << 20),
        name="attend_queries",
    )(plan, qkv, qkv, qkv, base, grad_out, exact, lse)


def key_pair(tiles, load, stat, bias, mine, queries, grads, rest_q, rest_g, stats, grad_s, weights):
    half, count = tiles.half, tiles.count
    for place in range(2):
        for part in range(2):
            mine[part, place] = stack_heads(load(1 + part, tiles.row(tiles.own_step(place))))
    for step in range(count):
        row, place = tiles.row(step), tiles.place(step)
        for part, whole, rest in ((0, queries, rest_q), (3, grads, rest_g)):
            tile = load(part, row)
            whole[0, span(step), :] = tile
            whole[1, span(step), :] = only(place, 1, tile)
            if step > half:
                rest[span(step - half - 1), :] = only(place, 0, tile)
        stats[:, span(step)] = stat(row)
    for step, size in tiles.groups():
        place = tiles.place(step)
        scores = dot(mine[0, place], queries[0, span(step, size), :], 1, 1)
        extra = order_bias(bias, step, size, place, half)
        if extra is not None:
            scores = scores + extra
        push = dot(mine[1, place], grads[0, span(step, size), :], 1, 1)
        for head in range(2):
            rows = slice(head * BLOCK, (head + 1) * BLOCK)
            part = jnp.exp(scores[rows] - stats[head : head + 1, span(step, size)])
            weights[rows, span(step, size)] = part.astype(BF16)
            part = part * (push[rows] - stats[2 + head : 3 + head, span(step, size)])
            grad_s[rows, span(step, size)] = part.astype(BF16)
    tail = span(half + 1, count - half - 1)
    grad_k = (dot(grad_s[:, tail], rest_q[...]), dot(grad_s[...], queries[1]))
    grad_v = (dot(weights[:, tail], rest_g[...]), dot(weights[...], grads[1]))
    return [
        [merge_heads(part).astype(BF16) for part in grad] for grad in (grad_k, grad_v)
    ]


def key_kernel(plan_ref, q_ref, k_ref, v_ref, base_ref, do_ref, stats_ref, *refs):
    passed = (len(refs) - 11) // 2
    passed_in, outs, passed_out = (
        refs[:passed],
        refs[passed : passed + 2],
        refs[passed + 2 : 2 * passed + 2],
    )
    bias, *scratch = refs[2 * passed + 2 :]
    for src, dst in zip(passed_in, passed_out):
        dst[...] = src[...]
    blocks = q_ref.shape[0] // BLOCK
    tiles = Tiles(plan_ref, blocks, True)
    tile_refs = (q_ref, k_ref, v_ref, do_ref)
    bias[...] = near_bias(base_ref)

    def load(part, row):
        return tile_refs[part][rows_at(row), :]

    def stat(row):
        return stats_ref[row, 0]

    for out, grad in zip(outs, key_pair(tiles, load, stat, bias, *scratch)):
        for own, part in enumerate(in_order(tiles, grad)):
            out[own * BLOCK : (own + 1) * BLOCK, :] = part


def key_scratch(blocks):
    count = blocks + 1
    rest = count - blocks // 2 - 1
    return [
        pltpu.VMEM((2, 2, NEAR, BLOCK), BF16),
        pltpu.VMEM((2, count * BLOCK, BLOCK), BF16),
        pltpu.VMEM((2, count * BLOCK, BLOCK), BF16),
        pltpu.VMEM((rest * BLOCK, BLOCK), BF16),
        pltpu.VMEM((rest * BLOCK, BLOCK), BF16),
        pltpu.VMEM((8, count * BLOCK), F32),
        pltpu.VMEM((NEAR, count * BLOCK), BF16),
        pltpu.VMEM((NEAR, count * BLOCK), BF16),
    ]


def attend_keys(plan, qkv, base, grad_out, stats, passed):
    rows, width = grad_out.shape
    own = pl.BlockSpec((NEAR, BLOCK), lambda pair, plan: (0, pair))
    pieces = [own] + [
        pl.BlockSpec(
            (array.shape[0], array.shape[1] // PAIRS, array.shape[2]), lambda pair, plan: (0, pair, 0)
        )
        for array in passed[1:]
    ]
    return pl.pallas_call(
        key_kernel,
        grid_spec=pltpu.PrefetchScalarGridSpec(
            num_scalar_prefetch=1,
            grid=(PAIRS,),
            in_specs=pair_specs(rows, width)
            + [
                pl.BlockSpec((1, 8, SPAN), lambda pair, plan: (pair, 0, 0)),
                pl.BlockSpec((rows, BLOCK), lambda pair, plan: (0, pair)),
                pl.BlockSpec(
                    (rows // BLOCK, 1, 8, BLOCK), lambda pair, plan: (0, pair, 0, 0)
                ),
            ]
            + pieces,
            out_specs=[own, own] + pieces,
            scratch_shapes=[pltpu.VMEM((NEAR, NEAR), F32), *key_scratch(rows // BLOCK)],
        ),
        out_shape=[jax.ShapeDtypeStruct((NEAR, width), BF16)] * 2
        + [jax.ShapeDtypeStruct(array.shape, array.dtype) for array in passed],
        compiler_params=pltpu.CompilerParams(vmem_limit_bytes=60 << 20),
        name="attend_keys",
    )(plan, qkv, qkv, qkv, base, grad_out, stats, *passed)


BITS = {"core": ("wsh", 1), "x": ("wsh", 2), "y": ("ctx", 1), "near": ("ctx", 2), "far": ("ctx", 4)}
UNITS = (
    (3, 0, 6, ("core", "x", "y", "near", "far")),
    (0, 0, 6, ("core", "y", "x", "near", "far")),
    (1, 0, 4, ("core", "x", "y", "near", "far")),
    (2, 0, 4, ("core", "y", "x", "near", "far")),
    (1, 4, 2, ("core", "x", "y", "near", "far")),
    (2, 4, 2, ("core", "y", "x", "near", "far")),
)


def halved_shapes(order, share, width):
    shapes, blocks, rows, columns = [], 4, share, width
    for name in order:
        if name in ("core", "x"):
            blocks //= 2
        elif name == "y":
            columns //= 2
        else:
            rows //= 2
        shapes.append((blocks, rows, columns))
    return shapes


def partner(name):
    axis, bit = BITS[name]
    me = lax.axis_index(axis)
    side = (me // bit) % 2
    return axis, me + bit * (1 - 2 * side), side


class UnitSum:
    def __init__(self, unit, total, gathered, sends, recvs, sems):
        self.weight, first, pairs, self.order = unit
        self.first, self.columns = first * BLOCK, pairs * BLOCK
        self.total, self.gathered, self.sends, self.recvs = total, gathered, sends, recvs
        self.half_send, self.half_recv, self.whole_send, self.whole_recv = sems
        self.steps = len(self.order)
        blocks, row, column = [0, 1, 2, 3], 0, 0
        rows, columns = total.shape[1], self.columns
        self.regions = []
        for name in self.order:
            side = partner(name)[2]
            if name == "core":
                keep = ([line * 2 + side for line in range(2)], row, column)
                sent = ([line * 2 + 1 - side for line in range(2)], row, column)
            elif name == "x":
                core = partner("core")[2]
                keep = ([side * 2 + core], row, column)
                sent = ([(1 - side) * 2 + core], row, column)
            elif name == "y":
                columns //= 2
                keep = (blocks, row, column + side * columns)
                sent = (blocks, row, column + (1 - side) * columns)
            else:
                rows //= 2
                keep = (blocks, row + side * rows, column)
                sent = (blocks, row + (1 - side) * rows, column)
            blocks, row, column = keep
            self.regions.append((keep, sent))
        self.wholes = [name for name in reversed(self.order) if BITS[name][0] == "ctx"]

    def span(self, step, region, shift=0):
        shape = self.sends[step].shape
        blocks, row, column = region
        row_part = pl.ds(row if isinstance(row, int) else pl.multiple_of(row, 16), shape[1])
        column = column + shift
        column_part = pl.ds(
            column if isinstance(column, int) else pl.multiple_of(column, BLOCK), shape[2]
        )
        return blocks, row_part, column_part

    def remote(self, source, target, send, recv, name):
        axis, peer, side = partner(name)
        return pltpu.make_async_remote_copy(
            src_ref=source,
            dst_ref=target,
            send_sem=send,
            recv_sem=recv,
            device_id={axis: peer},
            device_id_type=pl.DeviceIdType.MESH,
        )

    def half_copy(self, step):
        return self.remote(
            self.sends[step],
            self.recvs[step],
            self.half_send.at[step],
            self.half_recv.at[step],
            self.order[step],
        )

    def give(self, step):
        blocks, row_part, column_part = self.span(step, self.regions[step][1])
        for place, block in enumerate(blocks):
            self.sends[step][place] = self.total[block, row_part, column_part].astype(BF16)
        self.half_copy(step).start()

    def begin(self, value):
        share = self.total.shape[1]
        for block in range(4):
            self.total[block] = value[block * share : (block + 1) * share].astype(F32)
        self.give(0)

    def whole_copy(self, back):
        name = self.wholes[back]
        step = self.order.index(name)
        blocks, row_part, column_part = self.span(step, self.regions[step][0], self.first)
        view = self.gathered.at[self.weight, row_part, column_part]
        return self.remote(
            view, view, self.whole_send.at[back], self.whole_recv.at[back], name
        )

    def advance(self, phase):
        if phase >= self.steps:
            back = phase - self.steps
            self.whole_copy(back).wait_recv()
            if back + 1 < len(self.wholes):
                self.whole_copy(back + 1).start()
            return
        self.half_copy(phase).wait_recv()
        blocks, row_part, column_part = self.span(phase, self.regions[phase][0])
        for place, block in enumerate(blocks):
            self.total[block, row_part, column_part] += self.recvs[phase][place].astype(F32)
        if phase + 1 < self.steps:
            self.give(phase + 1)
            return
        whole = self.span(phase, self.regions[phase][0], self.first)
        self.gathered[self.weight, whole[1], whole[2]] = self.total[
            blocks[0], row_part, column_part
        ].astype(BF16)
        self.whole_copy(0).start()

    def finish(self):
        for step in range(self.steps):
            self.half_copy(step).wait_send()
        for back in range(len(self.wholes)):
            self.whole_copy(back).wait_send()


def tail_kernel(
    experts,
    dq_ref,
    hidden_ref,
    grad_mid_ref,
    weights_ref,
    grad_wo_ref,
    qkv_ref,
    do_ref,
    stats_ref,
    returned_ref,
    resid_ref,
    gate_ref,
    slot_ref,
    small_ref,
    router_ref,
    gain_ref,
    sums_ref,
    hot_ref,
    base_ref,
    plan_ref,
    input_grad_out,
    output_out,
    shares_out,
    router_out,
    gains_out,
    table_out,
    weights,
    hidden,
    grad_mid,
    grad_wo,
    resid,
    returned,
    home,
    qkv,
    grad_out,
    stats,
    dk,
    dv,
    bias,
    mine,
    queries,
    grads,
    rest_q,
    rest_g,
    tile_stats,
    grad_s,
    tile_weights,
    gathered,
    pack,
    pack_recv,
    *rest,
):
    steps, count = len(BITS), len(UNITS)
    totals, rest = rest[:count], rest[count:]
    sends = [rest[unit * steps : (unit + 1) * steps] for unit in range(count)]
    rest = rest[count * steps :]
    recvs = [rest[unit * steps : (unit + 1) * steps] for unit in range(count)]
    (
        fetch_sems,
        half_send,
        half_recv,
        whole_send,
        whole_recv,
        pack_send,
        pack_sem,
        back_send,
        back_recv,
    ) = rest[count * steps :]
    tokens, width = dq_ref.shape
    share = totals[0].shape[1]
    ctx_count = lax.axis_size("ctx")
    exp_dev = experts // ctx_count
    most = returned.shape[0] // experts
    sources = (
        (hidden_ref, hidden),
        (grad_wo_ref, grad_wo),
        (returned_ref, returned),
        (qkv_ref, qkv),
        (do_ref, grad_out),
        (stats_ref, stats),
        (weights_ref.at[pl.ds(0, 3)], weights),
        (grad_mid_ref, grad_mid),
        (resid_ref, resid),
    )
    fetches = [
        pltpu.make_async_copy(src, dst, fetch_sems.at[place])
        for place, (src, dst) in enumerate(sources)
    ]
    for fetch in fetches:
        fetch.start()
    greet((ctx_count, lax.axis_size("wsh")))
    units = [
        UnitSum(
            unit,
            totals[place],
            gathered,
            sends[place],
            recvs[place],
            [sem.at[place] for sem in (half_send, half_recv, whole_send, whole_recv)],
        )
        for place, unit in enumerate(UNITS)
    ]
    wo, wq, wk_early, wv_early, wk_late, wv_late = units

    fetches[2].wait()
    back = Exchange(
        ctx_count,
        exp_dev,
        most,
        (back_send, back_recv),
        lambda expert, peer: returned.at[back.rows(expert * ctx_count + peer), :],
        lambda expert, peer: home.at[back.rows(peer * exp_dev + expert), :],
    )
    for expert in range(exp_dev):
        back.start(expert)
    fetches[0].wait()
    rows = hidden[...].astype(F32)
    inv = lax.rsqrt(jnp.mean(rows * rows, axis=-1, keepdims=True) + epsilon)
    gain = small_ref[...].astype(F32)[experts : experts + 1, :]
    normed = (rows * inv * gain).astype(BF16)
    hidden[...] = normed
    fetches[1].wait()
    wo.begin(grad_wo[...])
    wq.begin(dot(normed, dq_ref[...], 0, 0))
    for fetch in fetches[3:6]:
        fetch.wait()
    tiles = Tiles(plan_ref, qkv.shape[0], True)

    def key_step(pair, carry):
        pair_lanes = pl.ds(pl.multiple_of(pair * BLOCK, BLOCK), BLOCK)

        def load(part, row):
            if part == 3:
                return grad_out[row, :, pair_lanes]
            lanes = pl.ds(pl.multiple_of(part * width + pair * BLOCK, BLOCK), BLOCK)
            return qkv[row, :, lanes]

        bias[...] = near_bias(base_ref, pair)
        results = key_pair(
            tiles,
            load,
            lambda row: stats[row, pair],
            bias,
            mine,
            queries,
            grads,
            rest_q,
            rest_g,
            tile_stats,
            grad_s,
            tile_weights,
        )
        for out, result in zip((dk, dv), results):
            for own, part in enumerate(in_order(tiles, result)):
                out[own * BLOCK : (own + 1) * BLOCK, pair_lanes] = part

        @pl.when(pair == 0)
        def _():
            wo.advance(0)
            wq.advance(0)

        @pl.when(pair == 2)
        def _():
            wo.advance(1)
            wq.advance(1)

        @pl.when(pair == 3)
        def _():
            early = slice(wk_early.first, wk_early.first + wk_early.columns)
            wk_early.begin(dot(hidden[...], dk[:, early], 0, 0))
            wv_early.begin(dot(hidden[...], dv[:, early], 0, 0))
            wo.advance(2)
            wq.advance(2)

        @pl.when(pair == 4)
        def _():
            wk_early.advance(0)
            wv_early.advance(0)
            wo.advance(3)
            wq.advance(3)

        return carry

    lax.fori_loop(0, PAIRS, key_step, 0)
    late = slice(wk_late.first, wk_late.first + wk_late.columns)
    wk_late.begin(dot(hidden[...], dk[:, late], 0, 0))
    wv_late.begin(dot(hidden[...], dv[:, late], 0, 0))
    for unit, phase in ((wo, 4), (wq, 4), (wk_early, 1), (wv_early, 1)):
        unit.advance(phase)
    fetches[6].wait()
    grad_normed = dot(dq_ref[...], weights[0], 1, 1)
    grad_normed = grad_normed + dot(dk[...], weights[1], 1, 1)
    grad_normed = grad_normed + dot(dv[...], weights[2], 1, 1)
    for unit, phase in ((wk_late, 0), (wv_late, 0)):
        unit.advance(phase)
    gain_part = jnp.sum(grad_normed * rows * inv, axis=0, keepdims=True)
    pack[...] = jnp.zeros_like(pack)
    pack[:experts, :] = router_ref[...]
    pack[experts : experts + 1, :] = gain_part
    pack[experts + 1 : experts + 2, :] = gain_ref[0:1, :]
    last = lane_ids(2, BLOCK) == hot_ref.shape[1] - 1
    for pair in range(PAIRS):
        near = lax.dot_general(
            sums_ref[pair, 0:2, :],
            hot_ref[...],
            (((1,), (0,)), ((), ())),
            precision=HIGH,
            preferred_element_type=F32,
        )
        near = jnp.concatenate([near, jnp.zeros((2, BLOCK - near.shape[1]), F32)], axis=1)
        distant = jnp.sum(sums_ref[pair, 2:4, :], axis=1, keepdims=True)
        near = near + jnp.where(last, distant, 0.0)
        for head in range(2):
            pack[experts + 2 + head : experts + 3 + head, span(pair)] = near[head : head + 1]

    def pack_copy(step):
        return wo.remote(
            pack_recv.at[0, step],
            pack_recv.at[1, step],
            pack_send.at[step],
            pack_sem.at[step],
            list(BITS)[step],
        )

    def pack_start(step):
        pack_recv[0, step] = pack[...].astype(BF16)
        pack_copy(step).start()

    def pack_end(step):
        pack_copy(step).wait_recv()
        pack[...] = pack_recv[0, step].astype(F32) + pack_recv[1, step].astype(F32)
        if step + 1 < steps:
            pack_start(step + 1)

    pack_start(0)
    for unit, phase in ((wk_early, 2), (wv_early, 2), (wk_late, 1), (wv_late, 1), (wo, 5), (wq, 5)):
        unit.advance(phase)
    pack_end(0)
    fetches[7].wait()
    scaled = grad_normed * gain
    mean = jnp.mean(scaled * rows, axis=-1, keepdims=True)
    grad_in = grad_mid[...] + inv * scaled - rows * inv * inv * inv * mean
    input_grad_out[...] = grad_in.astype(BF16)
    for unit, phase in ((wk_early, 3), (wv_early, 3), (wk_late, 2), (wv_late, 2), (wo, 6), (wq, 6)):
        unit.advance(phase)
    pack_end(1)
    for expert in range(exp_dev):
        back.wait(expert)
    fetches[8].wait()
    token_out = dot(placement_of(slot_ref, experts * most), home[...], 0, 0)
    output_out[...] = (resid[...] + gate_ref[:, :1] * token_out).astype(BF16)
    for unit, phase in ((wk_early, 4), (wv_early, 4), (wk_late, 3), (wv_late, 3), (wo, 7), (wq, 7)):
        unit.advance(phase)
    pack_end(2)
    for unit, phase in ((wk_late, 4), (wv_late, 4), (wk_early, 5), (wv_early, 5)):
        unit.advance(phase)
    pack_end(3)
    for unit, phase in ((wk_late, 5), (wv_late, 5), (wk_early, 6), (wv_early, 6)):
        unit.advance(phase)
    pack_end(4)
    for unit, phase in ((wk_late, 6), (wv_late, 6), (wk_early, 7), (wv_early, 7)):
        unit.advance(phase)
    own = lax.axis_index("wsh")
    buckets = table_out.shape[0]
    for block in range(4):

        @pl.when(own == block)
        def _():
            part = pack[: experts + 8, block * share : (block + 1) * share]
            router_out[...] = part[:experts]
            gains_out[...] = part[experts : experts + 8]
            heads = [
                pack[experts + 2 + head : experts + 3 + head, span(pair)]
                for pair in range(PAIRS)
                for head in range(2)
            ]
            table = jnp.transpose(jnp.concatenate(heads + heads[:4], axis=0))
            table_out[...] = table[block * buckets : (block + 1) * buckets, :HEADS]

    for unit in (wk_late, wv_late):
        unit.advance(7)
    shares_out[...] = gathered[...]
    for step in range(steps):
        pack_copy(step).wait_send()
    for unit in units:
        unit.finish()
    for expert in range(exp_dev):
        back.finish(expert)


def tail(
    experts,
    dq,
    hidden,
    grad_mid,
    weights,
    grad_wo,
    qkv,
    grad_out,
    stats,
    returned,
    resid,
    gate,
    slots,
    small,
    router,
    gains,
    sums,
    hot,
    base,
    plan,
    share,
    buckets,
):
    tokens, width = dq.shape
    vmem = pl.BlockSpec(memory_space=pltpu.VMEM)
    anywhere = pl.BlockSpec(memory_space=pl.ANY)
    steps, count = len(BITS), len(UNITS)
    pieces = [
        shape for unit in UNITS for shape in halved_shapes(unit[3], share, unit[2] * BLOCK)
    ]
    buffers = [pltpu.VMEM(shape, BF16) for shape in pieces]
    ctx_count = lax.axis_size("ctx")
    rows = experts + 16
    dma = pltpu.SemaphoreType.DMA
    return pl.pallas_call(
        functools.partial(tail_kernel, experts),
        in_specs=[vmem]
        + [anywhere] * 9
        + [vmem] * 8
        + [pl.BlockSpec(memory_space=pltpu.SMEM)],
        out_specs=[vmem] * 6,
        out_shape=[
            jax.ShapeDtypeStruct((tokens, width), BF16),
            jax.ShapeDtypeStruct((tokens, width), BF16),
            jax.ShapeDtypeStruct((4, share, width), BF16),
            jax.ShapeDtypeStruct((experts, share), F32),
            jax.ShapeDtypeStruct((8, share), F32),
            jax.ShapeDtypeStruct((buckets, HEADS), F32),
        ],
        scratch_shapes=[
            pltpu.VMEM((3, width, width), BF16),
            pltpu.VMEM((tokens, width), BF16),
            pltpu.VMEM((tokens, width), F32),
            pltpu.VMEM((width, width), BF16),
            pltpu.VMEM((tokens, width), F32),
            pltpu.VMEM(returned.shape, BF16),
            pltpu.VMEM(returned.shape, BF16),
            pltpu.VMEM(qkv.shape, BF16),
            pltpu.VMEM(grad_out.shape, BF16),
            pltpu.VMEM(stats.shape, F32),
            pltpu.VMEM((tokens, width), BF16),
            pltpu.VMEM((tokens, width), BF16),
            pltpu.VMEM((NEAR, NEAR), F32),
            *key_scratch(qkv.shape[0]),
            pltpu.VMEM((4, share, width), BF16),
            pltpu.VMEM((rows, width), F32),
            pltpu.VMEM((2, steps, rows, width), BF16),
            *[pltpu.VMEM((4, share, unit[2] * BLOCK), F32) for unit in UNITS],
            *buffers,
            *buffers,
            dma((9,)),
            dma((count, steps)),
            dma((count, steps)),
            dma((count, 3)),
            dma((count, 3)),
            dma((steps,)),
            dma((steps,)),
            dma((experts // ctx_count, ctx_count - 1)),
            dma((experts // ctx_count, ctx_count - 1)),
        ],
        compiler_params=pltpu.CompilerParams(
            collective_id=2, has_side_effects=True, vmem_limit_bytes=62 << 20
        ),
        name="tail",
    )(
        dq,
        hidden,
        grad_mid,
        weights,
        grad_wo,
        qkv,
        grad_out,
        stats,
        returned,
        resid,
        gate,
        slots,
        small,
        router,
        gains,
        sums,
        hot,
        base,
        plan,
    )


def finish_kernel(
    input_ref,
    output_ref,
    shares_ref,
    router_ref,
    gains_ref,
    table_ref,
    w_in_ref,
    w_out_ref,
    input_out,
    output_out,
    wq,
    wk,
    wv,
    wo,
    router,
    gain_a,
    gain_m,
    table,
    w_in_out,
    w_out_out,
):
    w_in_out[...] = w_in_ref[...].astype(F32)
    w_out_out[...] = w_out_ref[...].astype(F32)
    input_out[...] = input_ref[...]
    output_out[...] = output_ref[...]
    for place, out in enumerate((wq, wk, wv, wo)):
        out[...] = shares_ref[place].astype(F32)

    @pl.when(pl.program_id(0) == 0)
    def _():
        router[...] = router_ref[...]
        gain_a[...] = gains_ref[0, :]
        gain_m[...] = gains_ref[1, :]
        table[...] = table_ref[...]


def finish(grad_input, output, shares, router, gains, table, w_in, w_out):
    share, width = shares.shape[1:]

    def whole(array):
        zeros = (0,) * len(array.shape)
        return pl.BlockSpec(array.shape, lambda step: zeros)

    def pieces(array):
        *outer, rows, columns = array.shape
        zeros = (0,) * len(outer)
        return pl.BlockSpec((*outer, rows // 4, columns), lambda step: (*zeros, step, 0))

    arrays = (grad_input, output, shares, router, gains, table)
    outs = [
        jax.ShapeDtypeStruct(grad_input.shape, BF16),
        jax.ShapeDtypeStruct(output.shape, BF16),
        *[jax.ShapeDtypeStruct((share, width), F32)] * 4,
        jax.ShapeDtypeStruct(router.shape, F32),
        jax.ShapeDtypeStruct((share,), F32),
        jax.ShapeDtypeStruct((share,), F32),
        jax.ShapeDtypeStruct(table.shape, F32),
    ]
    experts = [jax.ShapeDtypeStruct(array.shape, F32) for array in (w_in, w_out)]
    return pl.pallas_call(
        finish_kernel,
        grid=(4,),
        in_specs=[pieces(array) for array in arrays[:3]]
        + [whole(array) for array in arrays[3:]]
        + [pieces(w_in), pieces(w_out)],
        out_specs=[pieces(array) for array in outs[:6]]
        + [whole(array) for array in outs[6:]]
        + [pieces(w_in), pieces(w_out)],
        out_shape=outs + experts,
        compiler_params=pltpu.CompilerParams(vmem_limit_bytes=60 << 20),
        name="finish",
    )(*arrays, w_in, w_out)


def rms_forward(values, gain_vec):
    inv_rms = lax.rsqrt(jnp.mean(values * values, axis=-1, keepdims=True) + epsilon)
    return (values * inv_rms * gain_vec, inv_rms)


def rms_backward(values, inv_rms, gain_vec, upstream):
    grad_gain = jnp.sum(upstream * values * inv_rms, axis=0)
    scaled = upstream * gain_vec
    grad_values = inv_rms * scaled - values * inv_rms**3 * jnp.mean(
        scaled * values, axis=-1, keepdims=True
    )
    return (grad_values, grad_gain)


def per_device(
    hidden_in,
    w_query,
    w_key,
    w_value,
    w_output,
    w_router,
    gain_attn,
    gain_moe,
    rel_bias,
    w_in,
    w_out,
    routes,
    block_pairs,
    cotangent,
):
    tokens, width = hidden_in.shape[1:]
    ctx_count, wsh_count = lax.axis_size("ctx"), lax.axis_size("wsh")
    ctx_rank, wsh_rank = lax.axis_index("ctx"), lax.axis_index("wsh")
    length = tokens * ctx_count
    blocks = length // BLOCK
    experts, exp_dev = w_router.shape[1], w_in.shape[0]
    slot_most = 2 * tokens // experts
    capacity = (9 * length // (8 * experts) + 7) // 8 * 8

    def over(axis, array, dim=0):
        return lax.all_gather(array, axis, axis=dim, tiled=True)

    share = width // wsh_count
    lanes = wrapped_lanes()
    buckets = rel_bias.shape[0] * wsh_count
    query_hot = onehot_of(BLOCK - lanes, buckets)
    key_hot = onehot_of(lanes, buckets)

    def hot_rows(hot):
        return jnp.asarray(hot.T, BF16)

    qkv, weights, small, slot_rows, targets, plan, query_base, key_base = project(
        (ctx_count, wsh_count),
        capacity,
        experts,
        slot_most,
        hidden_in[0],
        (w_query, w_key, w_value, w_output),
        (w_router.T, gain_attn, gain_moe, rel_bias),
        routes.reshape(1, tokens),
        block_pairs.T,
        hot_rows(query_hot),
        hot_rows(key_hot),
    )
    if wsh_count > 4:
        attn_low, attn_exact, lse, lse_rows = attend_forward(plan, qkv, query_base, width)
    else:
        attn_low = attn_exact = hidden_in[0]
        lse_rows = query_base
    (
        output_rows,
        returned,
        resid,
        gate,
        grad_mid,
        grad_heads,
        heads_all,
        stats,
        grad_wo,
        grad_router,
        grad_gain_m,
        grad_q,
        sums,
        grad_w_in,
        grad_w_out,
    ) = middle(
        (ctx_count, wsh_count),
        experts,
        attn_low,
        attn_exact.reshape(2, BLOCK, width),
        hidden_in[0],
        cotangent[0],
        weights,
        w_in,
        w_out,
        small,
        slot_rows,
        targets,
        lse_rows,
        routes.reshape(1, tokens),
        query_base,
        plan,
        qkv.reshape(blocks, BLOCK, 3 * width),
        capacity,
    )

    bucket_share = buckets // wsh_count
    if wsh_count <= 4:
        results = tail(
            experts,
            grad_q,
            hidden_in[0],
            grad_mid,
            weights,
            grad_wo,
            qkv.reshape(blocks, BLOCK, 3 * width),
            heads_all.reshape(blocks, BLOCK, width),
            stats.reshape(blocks, PAIRS, 8, BLOCK),
            returned,
            resid,
            gate,
            slot_rows,
            small,
            grad_router,
            grad_gain_m,
            sums,
            jnp.asarray(query_hot),
            key_base,
            plan,
            share,
            bucket_share,
        )
        grad_input, output_rows, *rest = finish(*results, grad_w_in, grad_w_out)
        rest[4] = rest[4].T
        return (output_rows[None], grad_input[None], *rest)

    heads_all = dot(over("ctx", heads_all), weights[3], 1, 1).astype(BF16)
    stats = over("ctx", stats).reshape(blocks, PAIRS, 8, BLOCK)
    grad_q, sums = attend_queries(plan, qkv, query_base, grad_heads, attn_exact, lse)
    grad_k, grad_v, output_rows, grad_w_in, grad_w_out = attend_keys(
        plan, qkv, key_base, heads_all, stats, (output_rows, grad_w_in, grad_w_out)
    )

    near_sums = sums[:, :2].reshape(HEADS, SPAN)
    far_sums = jnp.sum(sums[:, 2:4].reshape(HEADS, SPAN), axis=1)
    grad_table = jnp.dot(jnp.asarray(query_hot.T), near_sums.T, precision=HIGH)
    grad_table = grad_table.at[buckets - 1].add(far_sums)

    resid_in = hidden_in[0].astype(F32)
    full_query, full_key, full_value = (weights[place] for place in range(3))
    gain_one = small[experts].astype(F32)
    normed_one, inv_one = rms_forward(resid_in, gain_one)
    normed_one = normed_one.astype(BF16)
    grad_normed_one = dot(grad_q, full_query, 1, 1)
    grad_normed_one = grad_normed_one + dot(grad_k, full_key, 1, 1)
    grad_normed_one = grad_normed_one + dot(grad_v, full_value, 1, 1)
    grad_in_norm, grad_gain_a = rms_backward(resid_in, inv_one, gain_one, grad_normed_one)
    grad_input = (grad_mid + grad_in_norm).astype(BF16)

    def reduce_weight(grad):
        part = lax.psum_scatter(grad.astype(BF16), "wsh", scatter_dimension=0, tiled=True)
        return lax.psum(part, "ctx").astype(F32)

    grad_wq = dot(normed_one, grad_q, 0, 0)
    grad_wk = dot(normed_one, grad_k, 0, 0)
    grad_wv = dot(normed_one, grad_v, 0, 0)
    shares = [reduce_weight(grad) for grad in (grad_wq, grad_wk, grad_wv, grad_wo)]
    columns = jnp.concatenate(
        [grad_router.T, grad_gain_a[:, None], grad_gain_m[0][:, None]], axis=1
    )
    table = jnp.pad(grad_table, ((0, 0), (0, columns.shape[1] - HEADS)))
    summed = lax.psum(jnp.concatenate([columns, table], axis=0), ("ctx", "wsh"))
    own_columns = lax.dynamic_slice_in_dim(summed[:width], wsh_rank * share, share, 0)
    own_table = lax.dynamic_slice_in_dim(
        summed[width:, :HEADS], wsh_rank * bucket_share, bucket_share, 0
    )
    return (
        output_rows.astype(BF16)[None],
        grad_input[None],
        *shares,
        own_columns[:, :experts],
        own_columns[:, experts],
        own_columns[:, experts + 1],
        own_table,
        grad_w_in,
        grad_w_out,
    )


def solution(mesh):
    in_specs = (
        P("wsh", "ctx", None),
        P("wsh", None),
        P("wsh", None),
        P("wsh", None),
        P("wsh", None),
        P("wsh", None),
        P("wsh"),
        P("wsh"),
        P("wsh", None),
        P("ctx", None, "wsh"),
        P("ctx", "wsh", None),
        P("wsh", "ctx", None),
        P(),
        P("wsh", "ctx", None),
    )
    out_specs = (
        P("wsh", "ctx", None),
        P("wsh", "ctx", None),
        P("wsh", None),
        P("wsh", None),
        P("wsh", None),
        P("wsh", None),
        P("wsh", None),
        P("wsh"),
        P("wsh"),
        P("wsh", None),
        P("ctx", None, "wsh"),
        P("ctx", "wsh", None),
    )
    return jax.shard_map(
        per_device, mesh=mesh, in_specs=in_specs, out_specs=out_specs, check_vma=False
    )
```
